32 devices in a mesh: dp: 4 (over y, x), fsdp: 8 (over z, core).
Axes of the slice: x: 2, y: 2, z: 4, core: 2. Of those that a mesh axis runs over, the one named last changes fastest.
Arguments:
- inputs: bfloat16 [32768, 1024], P(('dp', 'fsdp')), may hold values from -6 to 6
- skip_in: bfloat16 [32768, 1024], P(('dp', 'fsdp')), may hold values from -6 to 6
- time_emb: bfloat16 [32, 4, 1024], P(('dp', 'fsdp')), may hold values from -3 to 3
- seg_ids: int32 [32, 1024], P(('dp', 'fsdp')), may hold values from 0 to 3, as said below
- positions: int32 [32, 1024], P(('dp', 'fsdp')), may hold values from 0 to 639, as said below
- pad_mask: int32 [32, 1024], P(('dp', 'fsdp')), may hold values from 0 to 1, as said below
- w_skip: bfloat16 [2048, 1024], P('dp', 'fsdp'), may hold values from -0.125 to 0.125
- w_ada1: bfloat16 [1024, 1024], P('dp', 'fsdp'), may hold values from -0.1875 to 0.1875
- w_qkv: bfloat16 [1024, 3072], P('dp', 'fsdp'), may hold values from -0.1875 to 0.1875
- w_out: bfloat16 [1024, 1024], P('dp', 'fsdp'), may hold values from -0.75 to 0.75
- w_ada2: bfloat16 [1024, 1024], P('dp', 'fsdp'), may hold values from -0.1875 to 0.1875
- w_up: bfloat16 [1024, 4096], P('dp', 'fsdp'), may hold values from -0.1875 to 0.1875
- w_down: bfloat16 [4096, 1024], P('dp', 'fsdp'), may hold values from -0.09375 to 0.09375
- cotangent: bfloat16 [32768, 1024], P(('dp', 'fsdp')), may hold values from -6 to 6
Outputs:
- output: bfloat16 [32768, 1024], P(('dp', 'fsdp'))
- d_input: float32 [32768, 1024], P(('dp', 'fsdp'))
- d_skip: float32 [32768, 1024], P(('dp', 'fsdp'))
- d_time: float32 [32, 4, 1024], P(('dp', 'fsdp'))
- grad_w_skip: float32 [2048, 1024], P('dp', 'fsdp')
- grad_w_ada1: float32 [1024, 1024], P('dp', 'fsdp')
- grad_w_qkv: float32 [1024, 3072], P('dp', 'fsdp')
- grad_w_out: float32 [1024, 1024], P('dp', 'fsdp')
- grad_w_ada2: float32 [1024, 1024], P('dp', 'fsdp')
- grad_w_up: float32 [1024, 4096], P('dp', 'fsdp')
- grad_w_down: float32 [4096, 1024], P('dp', 'fsdp')
The draws below stay inside these ranges and needn't reach their ends.
Inputs may be any that keep to these rules, and one draw needn't show every extreme that they name: `seg_ids`: each row of 1024 frames is cut into 4 utterances in order, numbered 0 to 3, none empty; one of them, at a place drawn from the seed, has 640 frames and is the longest. `positions`: A frame's index within its utterance, counted from 0. `pad_mask`: zeros only on the last 0 to 128 frames of a row.
All inputs are finite; a program needn't handle non-finite values.
Results may differ from the reference program's by a relative error of at most 0.022.
Values may be sent and summed in bfloat16 or wider, within the bound.
A program may use at most 256 MiB of HBM per device.

```python
import jax
import jax.numpy as jnp
from jax import lax

D = 1024
HD = 64
FF = 4096
ROW_LEN = 1024
SEGS = 4
ROWS = 32
TOKENS = 32768


def packing(key):
    keys = jax.random.split(key, 2)
    longest = ROW_LEN * 5 // 8
    others_count = SEGS - 1
    rest = ROW_LEN - longest - others_count
    drawn = jax.random.randint(keys[0], (ROWS, others_count - 1), 0, rest // others_count + 1)
    final = rest - jnp.sum(drawn, axis=1, keepdims=True)
    others = jnp.concatenate([drawn, final], axis=1) + 1
    spot = jax.random.randint(keys[1], (ROWS, 1), 0, SEGS)
    slots = jnp.arange(SEGS, dtype=jnp.int32)[None, :]
    pick = jnp.clip(slots - (slots > spot).astype(jnp.int32), 0, others_count - 1)
    lengths = jnp.where(slots == spot, longest, jnp.take_along_axis(others, pick, axis=1))
    ends = jnp.cumsum(lengths, axis=1)
    starts = ends - lengths
    places = jnp.arange(ROW_LEN, dtype=jnp.int32)[None, :]
    segment = jnp.sum((places[:, :, None] >= ends[:, None, :]).astype(jnp.int32), axis=-1)
    begin = jnp.take_along_axis(starts, segment, axis=1)
    return (segment.astype(jnp.int32), (places - begin).astype(jnp.int32))


def draw_seg_ids(key, part):
    segment, places = packing(key)
    return segment


def draw_positions(key, part):
    segment, places = packing(key)
    return places


def draw_pad_mask(key, part):
    key = jax.random.fold_in(key, 7)
    padded = jax.random.randint(key, (ROWS, 1), 0, ROW_LEN // 8 + 1)
    places = jnp.arange(ROW_LEN, dtype=jnp.int32)[None, :]
    return (places < ROW_LEN - padded).astype(jnp.int32)


def with_spikes(values, key, source, target, blocks, factor):
    owner, partner = [(jnp.arange(values.shape[dim]) // (values.shape[dim] // blocks)).reshape([-1 if axis == dim else 1 for axis in range(values.ndim)]) for dim in (source, target)]
    chosen = jax.random.permutation(key, blocks)[partner]
    strong = (owner == chosen) | (owner == (partner + blocks // 2) % blocks)
    return jnp.where(strong, factor * values, values)


def block_scale(rng, shape, shards, smallest, high):
    level = 1.0
    for position, shards_of in shards:
        steps = jax.random.uniform(jax.random.fold_in(jax.random.fold_in(rng, 6), position), (shards_of,), jnp.float32, smallest / len(shards), high / len(shards))
        level = level * jnp.repeat(jnp.exp(steps), shape[position] // shards_of).reshape((-1,) + (1,) * (len(shape) - 1 - position))
    return level


def gaussian(stream_key, shape, scale, limit, cuts=(), kind=jnp.bfloat16):
    values = jax.random.normal(stream_key, shape, jnp.float32) * scale
    if len(cuts) > 0:
        values = block_scale(stream_key, shape, cuts, -0.22, 0.18) * values
    return jnp.clip(values, min=-limit, max=limit).astype(kind)


def bell_draw_with(rng, dims, deviation, bound, pieces, heavy, kind=jnp.bfloat16):
    values = deviation * jax.random.normal(rng, dims, jnp.float32)
    if pieces:
        values = values * block_scale(rng, dims, pieces, -0.22, 0.18)
    return jnp.clip(with_spikes(values, jax.random.fold_in(rng, 3), *heavy), -bound, bound).astype(kind)


def setup_inputs(seed: int = 0) -> dict:
    arg_keys = jax.random.split(jax.random.key(seed), 15)
    inputs = gaussian(arg_keys[0], (TOKENS, D), 1.0, 6.0, ((0, 32),))
    skip_in = gaussian(arg_keys[1], (TOKENS, D), 1.0, 6.0, ((0, 32),))
    time_emb = gaussian(arg_keys[2], (ROWS, SEGS, D), 0.5, 3.0, ((0, 32),))
    seg_ids = draw_seg_ids(jax.random.fold_in(arg_keys[14], 71), 0)
    positions = draw_positions(jax.random.fold_in(arg_keys[14], 71), 0)
    pad_mask = draw_pad_mask(jax.random.fold_in(arg_keys[14], 71), 0)
    w_skip = gaussian(arg_keys[6], (2 * D, D), (2 * D) ** -0.5, 0.125, ((0, 4), (1, 8)))
    w_ada1 = gaussian(arg_keys[7], (D, D), D ** -0.5, 0.1875, ((0, 4), (1, 8)))
    w_qkv = gaussian(arg_keys[8], (D, 3 * D), D ** -0.5, 0.1875, ((0, 4), (1, 8)))
    w_out = gaussian(arg_keys[9], (D, D), (D // 16) ** -0.5, 0.75, ((0, 4), (1, 8)))
    w_ada2 = gaussian(arg_keys[10], (D, D), D ** -0.5, 0.1875, ((0, 4), (1, 8)))
    w_up = gaussian(arg_keys[11], (D, FF), D ** -0.5, 0.1875, ((0, 4), (1, 8)))
    w_down = gaussian(arg_keys[12], (FF, D), FF ** -0.5, 0.09375, ((0, 4), (1, 8)))
    cotangent = bell_draw_with(arg_keys[13], (TOKENS, D), 1.0, 6.0, ((0, 32),), (0, 1, 32, 2.75))
    return dict(inputs=inputs, skip_in=skip_in, time_emb=time_emb, seg_ids=seg_ids, positions=positions, pad_mask=pad_mask, w_skip=w_skip, w_ada1=w_ada1, w_qkv=w_qkv, w_out=w_out, w_ada2=w_ada2, w_up=w_up, w_down=w_down, cotangent=cotangent)


@jax.custom_vjp
def low(v):
    return lax.optimization_barrier(v.astype(jnp.bfloat16)).astype(jnp.float32)

@jax.custom_vjp
def low_back(v):
    return v

def low_keep(v):
    return (low(v), None)

def low_pass(kept, grad):
    return (grad,)

def back_keep(v):
    return (v, None)

def back_low(kept, grad):
    return (low(grad),)
low.defvjp(low_keep, low_pass)
low_back.defvjp(back_keep, back_low)
eps = 1e-06
masked = -1e+30

def product(former, latter):
    return jnp.dot(former, latter, precision=lax.Precision.HIGHEST)

def angles(positions):
    halfway = HD // 2
    frequency = 10000.0 ** (-2.0 * jnp.arange(halfway, dtype=jnp.float32) / HD)
    phases = positions.astype(jnp.float32)[..., None] * frequency
    phases = jnp.concatenate([phases, phases], axis=-1).reshape(-1, 1, HD)
    return (jnp.cos(phases), jnp.sin(phases))

def rotate(array, cosine, sine):
    halfway = array.shape[-1] // 2
    turned = jnp.concatenate([-array[..., halfway:], array[..., :halfway]], axis=-1)
    return array * cosine + turned * sine

def normalize(stream, gain):
    inverse = lax.rsqrt(lax.optimization_barrier(jnp.mean(stream * stream, axis=-1, keepdims=True)) + eps)
    return stream * inverse * (1.0 + gain)

def spread(gamma, segments):

    def select(lookup, chosen):
        return lookup[chosen]
    return jax.vmap(select)(gamma, segments).reshape(-1, gamma.shape[-1])

def row_attention(bundle):
    query_rows, key_rows, value_rows, segment, padding = bundle
    factor = HD ** (-0.5)
    scores = low_back(jnp.einsum('qhd,khd->hqk', query_rows, key_rows, precision=lax.Precision.HIGHEST) * factor)
    places = jnp.arange(segment.shape[0])
    allowed = (segment[:, None] == segment[None, :]) & ((padding[None, :] > 0) | (places[:, None] == places[None, :]))
    scores = jnp.where(allowed[None], scores, masked)
    largest = lax.optimization_barrier(jnp.max(scores, axis=-1, keepdims=True))
    exponent = jnp.exp(scores - largest)
    softened = low(exponent / lax.optimization_barrier(jnp.sum(exponent, axis=-1, keepdims=True)))
    return jnp.einsum('hqk,khd->qhd', softened, value_rows, precision=lax.Precision.HIGHEST)

def forward_group(frames, skipped, timing, matrices, segments, places, padding):
    w_skip, w_ada1, w_qkv, w_out, w_ada2, w_up, w_down = matrices
    group_rows = segments.shape[0]
    features = frames.shape[1]
    stream0 = low_back(product(jnp.concatenate([frames, skipped], axis=1), w_skip))
    flat_time = timing.reshape(-1, features)
    gamma1 = low_back(product(flat_time, w_ada1)).reshape(group_rows, -1, features)
    gamma2 = low_back(product(flat_time, w_ada2)).reshape(group_rows, -1, features)
    normed1 = low(normalize(stream0, spread(gamma1, segments)))
    projected = low_back(product(normed1, w_qkv))
    cosine, sine = angles(places)
    head_shape = (-1, features // HD, HD)
    queries = low(rotate(projected[:, :features].reshape(head_shape), cosine, sine))
    key_rows = low(rotate(projected[:, features:2 * features].reshape(head_shape), cosine, sine))
    value_rows = low(projected[:, 2 * features:].reshape(head_shape))
    row_shape = (group_rows, -1, features // HD, HD)
    context = lax.map(jax.checkpoint(row_attention), (queries.reshape(row_shape), key_rows.reshape(row_shape), value_rows.reshape(row_shape), segments, padding))
    context = low_back(low(context.reshape(-1, features)))
    stream1 = stream0 + low_back(product(context, w_out))
    normed2 = low(normalize(stream1, spread(gamma2, segments)))
    activated = low(jax.nn.gelu(low_back(product(normed2, w_up))))
    return stream1 + product(activated, w_down)

def reference(inputs, skip_in, time_emb, seg_ids, positions, pad_mask, w_skip, w_ada1, w_qkv, w_out, w_ada2, w_up, w_down, cotangent):
    weights = tuple((weight.astype(jnp.float32) for weight in (w_skip, w_ada1, w_qkv, w_out, w_ada2, w_up, w_down)))
    group_rows = 4 if ROWS % 4 == 0 else 1
    block_count = ROWS // group_rows

    def blocked(array):
        return array.reshape((block_count, -1) + array.shape[1:])

    def advance(totals, bundle):
        frames, skipped, timing, segments, places, padding, grad_out = bundle

        def forward(frames, skipped, timing, *matrices):
            return forward_group(frames, skipped, timing, matrices, segments, places, padding)
        result, pullback = jax.vjp(forward, frames, skipped, timing, *weights)
        grads = pullback(grad_out)
        totals = tuple((total + extra for total, extra in zip(totals, grads[3:])))
        return (totals, (result.astype(jnp.bfloat16), grads[0], grads[1], grads[2]))
    initial = tuple((jnp.zeros_like(weight) for weight in weights))
    bundles = (blocked(inputs.astype(jnp.float32)), blocked(skip_in.astype(jnp.float32)), blocked(time_emb.astype(jnp.float32)), blocked(seg_ids), blocked(positions), blocked(pad_mask), blocked(cotangent.astype(jnp.float32)))
    totals, (outputs, grad_input, grad_skip, grad_time) = lax.scan(advance, initial, bundles)
    return (outputs.reshape(inputs.shape), grad_input.reshape(inputs.shape), grad_skip.reshape(inputs.shape), grad_time.reshape(time_emb.shape), totals[0], totals[1], totals[2], totals[3], totals[4], totals[5], totals[6])
```

```python
import functools

import jax
import jax.numpy as jnp
from jax import lax
from jax.experimental import pallas as pl
from jax.experimental.pallas import tpu as pltpu
from jax.sharding import PartitionSpec as P

HD = 64
NB = 8
EPS = 1e-06
MASKED = -1e30
BF = jnp.bfloat16
F32 = jnp.float32
NN = (((1,), (0,)), ((), ()))
NT = (((1,), (1,)), ((), ()))
TN = (((0,), (0,)), ((), ()))
ROOT = 0.7978845608028654
CUBE = 0.044715


def dot(left, right, form=NN):
    return lax.dot_general(left, right, form, preferred_element_type=F32)


def params(**extra):
    return pltpu.CompilerParams(vmem_limit_bytes=60 << 20, **extra)


def whole(shape):
    return pl.BlockSpec(shape, lambda *_: (0,) * len(shape))


def shaped(shape, kind):
    return jax.ShapeDtypeStruct(shape, kind)


def columns(ref, first, count, rows=slice(None)):
    return jnp.concatenate([ref[first + i, rows, :] for i in range(count)], axis=1)


def token_gain(seg, gamma):
    gain = gamma[0:1, :]
    for slot in range(1, 4):
        gain = jnp.where(seg == slot, gamma[slot : slot + 1, :], gain)
    return gain


def segment_sum(seg_row, values):
    slots = lax.broadcasted_iota(jnp.int32, (8, seg_row.shape[1]), 0)
    picked = (slots == seg_row).astype(BF)
    high = values.astype(BF)
    low = (values - high.astype(F32)).astype(BF)
    return dot(picked, high) + dot(picked, low)


def norm_back(grad, stream, gain):
    inverse = lax.rsqrt(jnp.mean(stream * stream, axis=-1, keepdims=True) + EPS)
    unit = stream * inverse
    scaled = grad * (1.0 + gain)
    d_stream = inverse * (scaled - unit * jnp.mean(scaled * unit, axis=-1, keepdims=True))
    return d_stream, grad * unit


def norm(stream, gain):
    inverse = lax.rsqrt(jnp.mean(stream * stream, axis=-1, keepdims=True) + EPS)
    return (stream * inverse * (1.0 + gain)).astype(BF)


def front_body(x_ref, s_ref, w_ref, time_ref, ada_ref, seg_ref, stream_ref, normed_ref, g1_ref, g2_ref):
    length, width = x_ref.shape
    per = ada_ref.shape[2] // 2
    for f in range(NB):
        both = dot(time_ref[...], ada_ref[f])
        g1_ref[:, f * per : (f + 1) * per] = both[:, :per]
        g2_ref[:, f * per : (f + 1) * per] = both[:, per:]
    for i in range(NB // 2):
        tile = columns(w_ref, 2 * i, 2)
        part = dot(x_ref[...], tile[:width]) + dot(s_ref[...], tile[width:])
        stream_ref[:, i * part.shape[1] : (i + 1) * part.shape[1]] = part

    @pl.loop(0, length // 128)
    def _(t):
        rows = pl.ds(pl.multiple_of(t * 128, 128), 128)
        gain = token_gain(seg_ref[rows, :], g1_ref)
        normed_ref[rows, :] = norm(stream_ref[rows, :], gain)


def front(inputs, skip_in, w_skip, time8, ada, seg_col):
    length, width = inputs.shape
    return pl.pallas_call(
        front_body,
        out_shape=(
            shaped((length, width), F32),
            shaped((length, width), BF),
            shaped((8, width), F32),
            shaped((8, width), F32),
        ),
        compiler_params=params(),
        name="front",
    )(inputs, skip_in, w_skip, time8, ada, seg_col)


def key_bias(seg_col, pad_col, seg_row, length):
    keys = lax.broadcasted_iota(jnp.int32, (length, length), 0)
    queries = lax.broadcasted_iota(jnp.int32, (length, length), 1)
    allowed = (seg_col == seg_row) & ((pad_col > 0) | (keys == queries))
    return jnp.where(allowed, 0.0, MASKED)


def fill_bias(bias_ref, seg_ref, pad_ref, row_ref):
    length = seg_ref.shape[0]
    for t in range(length // 128):
        rows = slice(t * 128, (t + 1) * 128)
        keys = lax.broadcasted_iota(jnp.int32, (128, length), 0) + t * 128
        queries = lax.broadcasted_iota(jnp.int32, (128, length), 1)
        allowed = (seg_ref[rows, :] == row_ref[0:1, :]) & (
            (pad_ref[rows, :] > 0) | (keys == queries)
        )
        bias_ref[rows, :] = jnp.where(allowed, 0.0, MASKED)


def turn(unit, cosine, before, after):
    return (
        unit * cosine
        + pltpu.roll(unit, 96, 1) * before
        + pltpu.roll(unit, 32, 1) * after
    )


def attend_body(
    n_ref, qa, qb, ka, kb, va, vb, cos_ref, lo_ref, hi_ref, seg_ref, pad_ref, row_ref,
    q_ref, k_ref, v_ref, c_ref, lse_ref, bias_ref,
):
    @pl.when(pl.program_id(0) == 0)
    def _():
        fill_bias(bias_ref, seg_ref, pad_ref, row_ref)

    normed = n_ref[...]
    for out, first, second, scale in ((q_ref, qa, qb, HD**-0.5), (k_ref, ka, kb, 1.0)):
        made = dot(normed, jnp.concatenate([first[0], second[0]], axis=1))
        for half in range(2):
            unit = made[:, half * 128 : (half + 1) * 128]
            turned = turn(unit, cos_ref[...], lo_ref[...], hi_ref[...])
            out[:, half * 128 : (half + 1) * 128] = (turned.astype(BF) * scale).astype(BF)
    v_ref[...] = dot(normed, jnp.concatenate([va[0], vb[0]], axis=1)).astype(BF)
    for head in range(4):
        lanes = slice(head * HD, (head + 1) * HD)
        scores = dot(k_ref[:, lanes], q_ref[:, lanes], NT) + bias_ref[...]
        largest = jnp.max(scores, axis=0, keepdims=True)
        exponent = jnp.exp(scores - largest)
        total = jnp.sum(exponent, axis=0, keepdims=True)
        mixed = dot(v_ref[:, lanes].T, exponent.astype(BF)) * (1.0 / total)
        c_ref[:, lanes] = mixed.T.astype(BF)
        lse_ref[head : head + 1, :] = largest + jnp.log(total)


def unit_spec(rows, base):
    def index(j):
        unit = base + 2 * j
        return (unit // 3, 0, unit % 3)

    return pl.BlockSpec((1, rows, 128), index)


def attend(normed, w_qkv, tables, seg_col, pad_col, seg_row):
    length, width = normed.shape
    groups = width // 256
    units = [unit_spec(width, part * (width // 128) + e) for part in range(3) for e in range(2)]
    column = pl.BlockSpec((length, 256), lambda j: (0, j))
    wide = shaped((length, width), BF)
    return pl.pallas_call(
        attend_body,
        grid=(groups,),
        in_specs=[whole((length, width))]
        + units
        + [whole((length, 128))] * 3
        + [whole((length, 1))] * 2
        + [whole((1, length))],
        out_specs=(column,) * 4 + (pl.BlockSpec((8, length), lambda j: (j, 0)),),
        out_shape=(wide,) * 4 + (shaped((8 * groups, length), F32),),
        scratch_shapes=[pltpu.VMEM((length, length), F32)],
        compiler_params=params(),
        name="attend",
    )(normed, *([w_qkv] * 6), *tables, seg_col, pad_col, seg_row)


def mlp_body(
    stream0_ref, ctx_ref, wout_ref, g2_ref, seg_ref, row_ref, up_ref, down_ref, cot_ref,
    out_ref, gdown_ref, gup_ref, gout_ref, ds1_ref, dctx_ref, dg2_ref,
    s1_ref, n2_ref, acc_ref, dn_ref,
):
    step = pl.program_id(0)
    length, width = ctx_ref.shape
    tiles = length // 128

    @pl.when(step == 0)
    def _():
        @pl.loop(0, NB // 2)
        def _(i):
            lanes = pl.ds(pl.multiple_of(i * 256, 256), 256)
            s1_ref[:, lanes] = stream0_ref[:, lanes] + dot(ctx_ref[...], columns(wout_ref, 2 * i, 2))

        @pl.loop(0, tiles)
        def _(t):
            rows = pl.ds(pl.multiple_of(t * 128, 128), 128)
            n2_ref[rows, :] = norm(s1_ref[rows, :], token_gain(seg_ref[rows, :], g2_ref))

        acc_ref[...] = jnp.zeros_like(acc_ref)
        dn_ref[...] = jnp.zeros_like(dn_ref)

    cot = cot_ref[...]
    up = up_ref[0]
    down = columns(down_ref, 0, NB)
    hidden = dot(n2_ref[...], up)
    square = hidden * hidden
    tanh = jnp.tanh(ROOT * hidden * (1.0 + CUBE * square))
    active = (0.5 * hidden * (1.0 + tanh)).astype(BF)
    slope = 0.5 * (1.0 + tanh) + 0.5 * hidden * (1.0 - tanh * tanh) * (
        ROOT * (1.0 + 3.0 * CUBE * square)
    )
    d_pre = (dot(cot, down, NT) * slope).astype(BF)
    acc_ref[...] += dot(active, down)
    dn_ref[...] += dot(d_pre, up, NT)
    grad = dot(active, cot, TN).astype(BF)
    for f in range(NB):
        gdown_ref[f] = grad[:, f * gdown_ref.shape[2] : (f + 1) * gdown_ref.shape[2]]
    gup_ref[0] = dot(n2_ref[...], d_pre, TN).astype(BF)

    @pl.when(step == pl.num_programs(0) - 1)
    def _():
        dg2_ref[...] = jnp.zeros_like(dg2_ref)

        @pl.loop(0, tiles)
        def _(t):
            rows = pl.ds(pl.multiple_of(t * 128, 128), 128)
            stream = s1_ref[rows, :]
            out_ref[rows, :] = (stream + acc_ref[rows, :]).astype(BF)
            gain = token_gain(seg_ref[rows, :], g2_ref)
            term, d_gain = norm_back(dn_ref[rows, :], stream, gain)
            d_stream = cot_ref[rows, :].astype(F32) + term
            ds1_ref[rows, :] = d_stream
            n2_ref[rows, :] = d_stream.astype(BF)
            dg2_ref[...] += segment_sum(row_ref[:, rows], d_gain)

        @pl.loop(0, NB // 2)
        def _(i):
            lanes = pl.ds(pl.multiple_of(i * 256, 256), 256)
            part = dot(ctx_ref[...], n2_ref[:, lanes], TN).astype(BF)
            gout_ref[2 * i] = part[:, :128]
            gout_ref[2 * i + 1] = part[:, 128:]

        acc_ref[...] = jnp.zeros_like(acc_ref)

        @pl.loop(0, NB // 2)
        def _(i):
            lanes = pl.ds(pl.multiple_of(i * 256, 256), 256)
            acc_ref[...] += dot(n2_ref[:, lanes], columns(wout_ref, 2 * i, 2), NT)

        dctx_ref[...] = acc_ref[...].astype(BF)


def mlp(stream0, ctx, w_out, gamma2, seg_col, seg_row, w_up, w_down, cotangent):
    length, width = ctx.shape
    hidden = w_down.shape[1]
    piece = hidden // NB
    per = width // NB
    full = whole((length, width))
    return pl.pallas_call(
        mlp_body,
        grid=(NB,),
        in_specs=[
            full,
            full,
            whole((NB, width, per)),
            whole((8, width)),
            whole((length, 1)),
            whole((1, length)),
            pl.BlockSpec((1, width, piece), lambda j: (j, 0, 0)),
            pl.BlockSpec((NB, piece, per), lambda j: (0, j, 0)),
            full,
        ],
        out_specs=(
            full,
            pl.BlockSpec((NB, piece, per), lambda j: (0, j, 0)),
            pl.BlockSpec((1, width, piece), lambda j: (j, 0, 0)),
            whole((NB, width, per)),
            full,
            full,
            whole((8, width)),
        ),
        out_shape=(
            shaped((length, width), BF),
            shaped((NB, hidden, per), BF),
            shaped((NB, width, piece), BF),
            shaped((NB, width, per), BF),
            shaped((length, width), F32),
            shaped((length, width), BF),
            shaped((8, width), F32),
        ),
        scratch_shapes=[
            pltpu.VMEM((length, width), F32),
            pltpu.VMEM((length, width), BF),
            pltpu.VMEM((length, width), F32),
            pltpu.VMEM((length, width), F32),
        ],
        compiler_params=params(),
        name="mlp",
    )(stream0, ctx, w_out, gamma2, seg_col, seg_row, w_up, w_down, cotangent)


def attend_back_body(
    n_ref, qa, qb, ka, kb, va, vb, cos_ref, lo_ref, hi_ref, seg_ref, pad_ref, row_ref,
    q_ref, k_ref, v_ref, g_ref, c_ref, lse_ref, s0_ref, g1_ref, ds1_ref,
    gw_ref, dlow_ref, dg1_ref, bias_ref, dn_ref, dq_ref, dk_ref, dv_ref,
):
    step = pl.program_id(0)
    length, width = n_ref.shape

    @pl.when(step == 0)
    def _():
        fill_bias(bias_ref, seg_ref, pad_ref, row_ref)
        dn_ref[...] = jnp.zeros_like(dn_ref)

    ones = jnp.ones((8, HD), BF)
    for head in range(4):
        lanes = slice(head * HD, (head + 1) * HD)
        query, key, value = q_ref[:, lanes], k_ref[:, lanes], v_ref[:, lanes]
        grad = g_ref[:, lanes]
        both = grad.astype(F32) * c_ref[:, lanes].astype(F32)
        high = both.astype(BF)
        low = (both - high.astype(F32)).astype(BF)
        delta = (dot(ones, high, NT) + dot(ones, low, NT))[0:1, :]
        probs = jnp.exp(dot(key, query, NT) + bias_ref[...] - lse_ref[head : head + 1, :])
        d_scores = (probs * (dot(value, grad, NT) - delta)).astype(BF)
        dv_ref[:, lanes] = dot(probs.astype(BF), grad)
        dk_ref[:, lanes] = dot(d_scores, query)
        dq_ref[:, lanes] = dot(key.T, d_scores).T * HD**-0.5
    for part, (src, first, second) in enumerate(
        ((dq_ref, qa, qb), (dk_ref, ka, kb), (dv_ref, va, vb))
    ):
        if part < 2:
            made = jnp.concatenate(
                [
                    turn(src[:, half * 128 : (half + 1) * 128], cos_ref[...], -lo_ref[...], -hi_ref[...])
                    for half in range(2)
                ],
                axis=1,
            ).astype(BF)
        else:
            made = src[...].astype(BF)
        grad = dot(n_ref[...], made, TN).astype(BF)
        gw_ref[part, 0] = grad[:, :128]
        gw_ref[part, 1] = grad[:, 128:]
        dn_ref[...] += dot(made, jnp.concatenate([first[0], second[0]], axis=1), NT)

    @pl.when(step == pl.num_programs(0) - 1)
    def _():
        dg1_ref[...] = jnp.zeros_like(dg1_ref)

        @pl.loop(0, length // 128)
        def _(t):
            rows = pl.ds(pl.multiple_of(t * 128, 128), 128)
            gain = token_gain(seg_ref[rows, :], g1_ref)
            term, d_gain = norm_back(dn_ref[rows, :], s0_ref[rows, :], gain)
            dlow_ref[rows, :] = (ds1_ref[rows, :] + term).astype(BF)
            dg1_ref[...] += segment_sum(row_ref[:, rows], d_gain)


def attend_back(
    normed, w_qkv, tables, seg_col, pad_col, seg_row, q, k, v, d_ctx, ctx, lse, stream0, gamma1, d_stream1
):
    length, width = normed.shape
    groups = width // 256
    units = [unit_spec(width, part * (width // 128) + e) for part in range(3) for e in range(2)]
    column = pl.BlockSpec((length, 256), lambda j: (0, j))
    full = whole((length, width))
    return pl.pallas_call(
        attend_back_body,
        grid=(groups,),
        in_specs=[full]
        + units
        + [whole((length, 128))] * 3
        + [whole((length, 1))] * 2
        + [whole((1, length))]
        + [column] * 5
        + [pl.BlockSpec((8, length), lambda j: (j, 0)), full, whole((8, width)), full],
        out_specs=(
            pl.BlockSpec((3, 2, width, 128), lambda j: (0, j, 0, 0)),
            full,
            whole((8, width)),
        ),
        out_shape=(
            shaped((3, width // 128, width, 128), BF),
            shaped((length, width), BF),
            shaped((8, width), F32),
        ),
        scratch_shapes=[pltpu.VMEM((length, length), F32), pltpu.VMEM((length, width), F32)]
        + [pltpu.VMEM((length, 256), F32)] * 3,
        compiler_params=params(),
        name="attend_back",
    )(
        normed, *([w_qkv] * 6), *tables, seg_col, pad_col, seg_row, q, k, v, d_ctx, ctx, lse,
        stream0, gamma1, d_stream1,
    )


def skip_back_body(x_ref, s_ref, d_ref, w_ref, gw_ref, dx_ref, ds_ref):
    low = d_ref[...]
    per = 256
    width = x_ref.shape[1]

    @pl.loop(0, width // per)
    def _(i):
        lanes = pl.ds(pl.multiple_of(i * per, per), per)
        part = d_ref[:, lanes]
        top = dot(x_ref[...], part, TN).astype(BF)
        end = dot(s_ref[...], part, TN).astype(BF)
        for e in range(2):
            gw_ref[2 * i + e, :width, :] = top[:, e * 128 : (e + 1) * 128]
            gw_ref[2 * i + e, width:, :] = end[:, e * 128 : (e + 1) * 128]

    tall = 256

    @pl.loop(0, width // tall)
    def _(i):
        rows = pl.ds(pl.multiple_of(i * tall, tall), tall)
        rest = pl.ds(pl.multiple_of(width + i * tall, tall), tall)
        dx_ref[:, rows] = dot(low, columns(w_ref, 0, NB, rows), NT)
        ds_ref[:, rows] = dot(low, columns(w_ref, 0, NB, rest), NT)


def skip_back(inputs, skip_in, d_low, w_skip):
    length, width = inputs.shape
    return pl.pallas_call(
        skip_back_body,
        out_shape=(
            shaped(w_skip.shape, BF),
            shaped((length, width), F32),
            shaped((length, width), F32),
        ),
        compiler_params=params(),
        name="skip_back",
    )(inputs, skip_in, d_low, w_skip)


def rotary(positions):
    half = HD // 2
    lane = jnp.arange(128)
    frequency = 10000.0 ** (-2.0 * (lane % half).astype(F32) / HD)
    phase = positions.reshape(-1, 1).astype(F32) * frequency[None, :]
    cosine, sine = jnp.cos(phase), jnp.sin(phase)
    early = (lane % HD < half)[None, :]
    return cosine, jnp.where(early, -sine, 0.0), jnp.where(early, 0.0, sine)


def gathered(shard):
    blocks = lax.all_gather(shard, "fsdp", axis=0, tiled=False)
    blocks = lax.all_gather(blocks, "dp", axis=1, tiled=True)
    count, rows, per = blocks.shape
    if count == NB:
        return blocks
    flat = jnp.transpose(blocks, (1, 0, 2)).reshape(rows, count * per)
    return jnp.transpose(flat.reshape(rows, NB, count * per // NB), (1, 0, 2))


def scattered(blocks):
    count, rows, per = blocks.shape
    flat = jnp.transpose(blocks, (1, 0, 2)).reshape(rows, count * per)
    part = lax.psum_scatter(flat, "fsdp", scatter_dimension=1, tiled=True)
    return lax.psum_scatter(part, "dp", scatter_dimension=0, tiled=True).astype(F32)


def shards(
    inputs, skip_in, time_emb, seg_ids, positions, pad_mask,
    w_skip, w_ada1, w_qkv, w_out, w_ada2, w_up, w_down, cotangent,
):
    slots = time_emb.shape[1]
    seg_col, seg_row = seg_ids.reshape(-1, 1), seg_ids.reshape(1, -1)
    pad_col = pad_mask.reshape(-1, 1)
    tables = rotary(positions)
    flat_time = time_emb.reshape(slots, -1)
    time8 = jnp.pad(flat_time, ((0, 8 - slots), (0, 0)))
    f_skip, f_qkv, f_out = gathered(w_skip), gathered(w_qkv), gathered(w_out)
    f_up, f_down = gathered(w_up), gathered(w_down)
    f_ada1, f_ada2 = gathered(w_ada1), gathered(w_ada2)
    ada = jnp.concatenate([f_ada1, f_ada2], axis=2)
    stream0, normed1, gamma1, gamma2 = front(inputs, skip_in, f_skip, time8, ada, seg_col)
    q, k, v, ctx, lse = attend(normed1, f_qkv, tables, seg_col, pad_col, seg_row)
    output, g_down, g_up, g_out, d_stream1, d_ctx, d_gamma2 = mlp(
        stream0, ctx, f_out, gamma2, seg_col, seg_row, f_up, f_down, cotangent
    )
    g_qkv, d_low, d_gamma1 = attend_back(
        normed1, f_qkv, tables, seg_col, pad_col, seg_row, q, k, v, d_ctx, ctx, lse,
        stream0, gamma1, d_stream1,
    )
    width = inputs.shape[1]
    g_qkv = jnp.transpose(
        g_qkv.reshape(NB, 3, width, 128), (0, 2, 1, 3)
    ).reshape(NB, width, 3 * width // NB)
    g_skip, d_input, d_skip = skip_back(inputs, skip_in, d_low, f_skip)
    d_gammas = [d[:slots].astype(BF) for d in (d_gamma1, d_gamma2)]
    d_time = 0.0
    g_ada = []
    for d_gamma, full in zip(d_gammas, (f_ada1, f_ada2)):
        flat = jnp.transpose(full, (1, 0, 2)).reshape(width, width)
        d_time = d_time + jnp.einsum("ne,de->nd", d_gamma, flat, preferred_element_type=F32)
        g = jnp.einsum("nd,ne->de", flat_time, d_gamma, preferred_element_type=F32).astype(BF)
        g_ada.append(jnp.transpose(g.reshape(width, NB, width // NB), (1, 0, 2)))
    return (
        output,
        d_input,
        d_skip,
        d_time.reshape(time_emb.shape),
        scattered(g_skip),
        scattered(g_ada[0]),
        scattered(g_qkv),
        scattered(g_out),
        scattered(g_ada[1]),
        scattered(g_up),
        scattered(g_down),
    )


def solution(mesh):
    rows = P(("dp", "fsdp"), None)
    cube = P(("dp", "fsdp"), None, None)
    tile = P("dp", "fsdp")
    return jax.shard_map(
        shards,
        mesh=mesh,
        in_specs=(rows, rows, cube) + (rows,) * 3 + (tile,) * 7 + (rows,),
        out_specs=(rows, rows, rows, cube) + (tile,) * 7,
        check_vma=False,
    )
```

```python
import functools

import jax
import jax.numpy as jnp
from jax import lax
from jax.experimental import pallas as pl
from jax.experimental.pallas import tpu as pltpu
from jax.sharding import PartitionSpec as P

HD = 64
NB = 8
EPS = 1e-06
MASKED = -1e30
BF = jnp.bfloat16
F32 = jnp.float32
NN = (((1,), (0,)), ((), ()))
NT = (((1,), (1,)), ((), ()))
TN = (((0,), (0,)), ((), ()))
ROOT = 0.7978845608028654
CUBE = 0.044715


def dot(left, right, form=NN):
    return lax.dot_general(left, right, form, preferred_element_type=F32)


def params(**extra):
    return pltpu.CompilerParams(vmem_limit_bytes=60 << 20, **extra)


def whole(shape):
    return pl.BlockSpec(shape, lambda *_: (0,) * len(shape))


def shaped(shape, kind):
    return jax.ShapeDtypeStruct(shape, kind)


def columns(ref, first, count, rows=slice(None)):
    return jnp.concatenate([ref[first + i, rows, :] for i in range(count)], axis=1)


def token_gain(seg, gamma):
    gain = gamma[0:1, :]
    for slot in range(1, 4):
        gain = jnp.where(seg == slot, gamma[slot : slot + 1, :], gain)
    return gain


def segment_sum(seg_row, values):
    slots = lax.broadcasted_iota(jnp.int32, (8, seg_row.shape[1]), 0)
    picked = (slots == seg_row).astype(BF)
    high = values.astype(BF)
    low = (values - high.astype(F32)).astype(BF)
    return dot(picked, high) + dot(picked, low)


def norm_back(grad, stream, gain):
    inverse = lax.rsqrt(jnp.mean(stream * stream, axis=-1, keepdims=True) + EPS)
    unit = stream * inverse
    scaled = grad * (1.0 + gain)
    d_stream = inverse * (scaled - unit * jnp.mean(scaled * unit, axis=-1, keepdims=True))
    return d_stream, grad * unit


def norm(stream, gain):
    inverse = lax.rsqrt(jnp.mean(stream * stream, axis=-1, keepdims=True) + EPS)
    return (stream * inverse * (1.0 + gain)).astype(BF)


def front_body(x_ref, s_ref, w_ref, time_ref, ada_ref, seg_ref, stream_ref, normed_ref, g1_ref, g2_ref):
    length, width = x_ref.shape
    per = ada_ref.shape[2] // 2
    for f in range(NB):
        both = dot(time_ref[...], ada_ref[f])
        g1_ref[:, f * per : (f + 1) * per] = both[:, :per]
        g2_ref[:, f * per : (f + 1) * per] = both[:, per:]
    for i in range(NB // 2):
        tile = columns(w_ref, 2 * i, 2)
        part = dot(x_ref[...], tile[:width]) + dot(s_ref[...], tile[width:])
        stream_ref[:, i * part.shape[1] : (i + 1) * part.shape[1]] = part

    @pl.loop(0, length // 128)
    def _(t):
        rows = pl.ds(pl.multiple_of(t * 128, 128), 128)
        gain = token_gain(seg_ref[rows, :], g1_ref)
        normed_ref[rows, :] = norm(stream_ref[rows, :], gain)


def front(inputs, skip_in, w_skip, time8, ada, seg_col):
    length, width = inputs.shape
    return pl.pallas_call(
        front_body,
        out_shape=(
            shaped((length, width), F32),
            shaped((length, width), BF),
            shaped((8, width), F32),
            shaped((8, width), F32),
        ),
        compiler_params=params(),
        name="front",
    )(inputs, skip_in, w_skip, time8, ada, seg_col)


def key_bias(seg_col, pad_col, seg_row, length):
    keys = lax.broadcasted_iota(jnp.int32, (length, length), 0)
    queries = lax.broadcasted_iota(jnp.int32, (length, length), 1)
    allowed = (seg_col == seg_row) & ((pad_col > 0) | (keys == queries))
    return jnp.where(allowed, 0.0, MASKED)


def fill_bias(bias_ref, seg_ref, pad_ref, row_ref):
    length = seg_ref.shape[0]
    for t in range(length // 128):
        rows = slice(t * 128, (t + 1) * 128)
        keys = lax.broadcasted_iota(jnp.int32, (128, length), 0) + t * 128
        queries = lax.broadcasted_iota(jnp.int32, (128, length), 1)
        allowed = (seg_ref[rows, :] == row_ref[0:1, :]) & (
            (pad_ref[rows, :] > 0) | (keys == queries)
        )
        bias_ref[rows, :] = jnp.where(allowed, 0.0, MASKED)


def turn(unit, cosine, before, after):
    return (
        unit * cosine
        + pltpu.roll(unit, 96, 1) * before
        + pltpu.roll(unit, 32, 1) * after
    )


def attend_body(
    n_ref, qa, qb, ka, kb, va, vb, cos_ref, lo_ref, hi_ref, seg_ref, pad_ref, row_ref,
    q_ref, k_ref, v_ref, c_ref, lse_ref, bias_ref,
):
    @pl.when(pl.program_id(0) == 0)
    def _():
        fill_bias(bias_ref, seg_ref, pad_ref, row_ref)

    normed = n_ref[...]
    for out, first, second, scale in ((q_ref, qa, qb, HD**-0.5), (k_ref, ka, kb, 1.0)):
        made = dot(normed, jnp.concatenate([first[0], second[0]], axis=1))
        for half in range(2):
            unit = made[:, half * 128 : (half + 1) * 128]
            turned = turn(unit, cos_ref[...], lo_ref[...], hi_ref[...])
            out[:, half * 128 : (half + 1) * 128] = (turned.astype(BF) * scale).astype(BF)
    v_ref[...] = dot(normed, jnp.concatenate([va[0], vb[0]], axis=1)).astype(BF)
    for head in range(4):
        lanes = slice(head * HD, (head + 1) * HD)
        scores = dot(k_ref[:, lanes], q_ref[:, lanes], NT) + bias_ref[...]
        largest = jnp.max(scores, axis=0, keepdims=True)
        exponent = jnp.exp(scores - largest)
        total = jnp.sum(exponent, axis=0, keepdims=True)
        mixed = dot(v_ref[:, lanes].T, exponent.astype(BF)) * (1.0 / total)
        c_ref[:, lanes] = mixed.T.astype(BF)
        lse_ref[head : head + 1, :] = largest + jnp.log(total)


def unit_spec(rows, base):
    def index(j):
        unit = base + 2 * j
        return (unit // 3, 0, unit % 3)

    return pl.BlockSpec((1, rows, 128), index)


def attend(normed, w_qkv, tables, seg_col, pad_col, seg_row):
    length, width = normed.shape
    groups = width // 256
    units = [unit_spec(width, part * (width // 128) + e) for part in range(3) for e in range(2)]
    column = pl.BlockSpec((length, 256), lambda j: (0, j))
    wide = shaped((length, width), BF)
    return pl.pallas_call(
        attend_body,
        grid=(groups,),
        in_specs=[whole((length, width))]
        + units
        + [whole((length, 128))] * 3
        + [whole((length, 1))] * 2
        + [whole((1, length))],
        out_specs=(column,) * 4 + (pl.BlockSpec((8, length), lambda j: (j, 0)),),
        out_shape=(wide,) * 4 + (shaped((8 * groups, length), F32),),
        scratch_shapes=[pltpu.VMEM((length, length), F32)],
        compiler_params=params(),
        name="attend",
    )(normed, *([w_qkv] * 6), *tables, seg_col, pad_col, seg_row)


def mlp_body(
    stream0_ref, ctx_ref, wout_ref, g2_ref, seg_ref, row_ref, up_ref, down_ref, cot_ref,
    out_ref, gdown_ref, gup_ref, gout_ref, ds1_ref, dctx_ref, dg2_ref,
    s1_ref, n2_ref, acc_ref, dn_ref,
):
    step = pl.program_id(0)
    length, width = ctx_ref.shape
    tiles = length // 128

    @pl.when(step == 0)
    def _():
        @pl.loop(0, NB // 2)
        def _(i):
            lanes = pl.ds(pl.multiple_of(i * 256, 256), 256)
            s1_ref[:, lanes] = stream0_ref[:, lanes] + dot(ctx_ref[...], columns(wout_ref, 2 * i, 2))

        @pl.loop(0, tiles)
        def _(t):
            rows = pl.ds(pl.multiple_of(t * 128, 128), 128)
            n2_ref[rows, :] = norm(s1_ref[rows, :], token_gain(seg_ref[rows, :], g2_ref))

        acc_ref[...] = jnp.zeros_like(acc_ref)
        dn_ref[...] = jnp.zeros_like(dn_ref)

    cot = cot_ref[...]
    up = up_ref[0]
    down = columns(down_ref, 0, NB)
    hidden = dot(n2_ref[...], up)
    square = hidden * hidden
    tanh = jnp.tanh(ROOT * hidden * (1.0 + CUBE * square))
    active = (0.5 * hidden * (1.0 + tanh)).astype(BF)
    slope = 0.5 * (1.0 + tanh) + 0.5 * hidden * (1.0 - tanh * tanh) * (
        ROOT * (1.0 + 3.0 * CUBE * square)
    )
    d_pre = (dot(cot, down, NT) * slope).astype(BF)
    acc_ref[...] += dot(active, down)
    dn_ref[...] += dot(d_pre, up, NT)
    grad = dot(active, cot, TN).astype(BF)
    for f in range(NB):
        gdown_ref[f] = grad[:, f * gdown_ref.shape[2] : (f + 1) * gdown_ref.shape[2]]
    gup_ref[0] = dot(n2_ref[...], d_pre, TN).astype(BF)

    @pl.when(step == pl.num_programs(0) - 1)
    def _():
        dg2_ref[...] = jnp.zeros_like(dg2_ref)

        @pl.loop(0, tiles)
        def _(t):
            rows = pl.ds(pl.multiple_of(t * 128, 128), 128)
            stream = s1_ref[rows, :]
            out_ref[rows, :] = (stream + acc_ref[rows, :]).astype(BF)
            gain = token_gain(seg_ref[rows, :], g2_ref)
            term, d_gain = norm_back(dn_ref[rows, :], stream, gain)
            d_stream = cot_ref[rows, :].astype(F32) + term
            ds1_ref[rows, :] = d_stream
            n2_ref[rows, :] = d_stream.astype(BF)
            dg2_ref[...] += segment_sum(row_ref[:, rows], d_gain)

        @pl.loop(0, NB // 2)
        def _(i):
            lanes = pl.ds(pl.multiple_of(i * 256, 256), 256)
            part = dot(ctx_ref[...], n2_ref[:, lanes], TN).astype(BF)
            gout_ref[2 * i] = part[:, :128]
            gout_ref[2 * i + 1] = part[:, 128:]

        acc_ref[...] = jnp.zeros_like(acc_ref)

        @pl.loop(0, NB // 2)
        def _(i):
            lanes = pl.ds(pl.multiple_of(i * 256, 256), 256)
            acc_ref[...] += dot(n2_ref[:, lanes], columns(wout_ref, 2 * i, 2), NT)

        dctx_ref[...] = acc_ref[...].astype(BF)


def mlp(stream0, ctx, w_out, gamma2, seg_col, seg_row, w_up, w_down, cotangent):
    length, width = ctx.shape
    hidden = w_down.shape[1]
    piece = hidden // NB
    per = width // NB
    full = whole((length, width))
    return pl.pallas_call(
        mlp_body,
        grid=(NB,),
        in_specs=[
            full,
            full,
            whole((NB, width, per)),
            whole((8, width)),
            whole((length, 1)),
            whole((1, length)),
            pl.BlockSpec((1, width, piece), lambda j: (j, 0, 0)),
            pl.BlockSpec((NB, piece, per), lambda j: (0, j, 0)),
            full,
        ],
        out_specs=(
            full,
            pl.BlockSpec((NB, piece, per), lambda j: (0, j, 0)),
            pl.BlockSpec((1, width, piece), lambda j: (j, 0, 0)),
            whole((NB, width, per)),
            full,
            full,
            whole((8, width)),
        ),
        out_shape=(
            shaped((length, width), BF),
            shaped((NB, hidden, per), BF),
            shaped((NB, width, piece), BF),
            shaped((NB, width, per), BF),
            shaped((length, width), F32),
            shaped((length, width), BF),
            shaped((8, width), F32),
        ),
        scratch_shapes=[
            pltpu.VMEM((length, width), F32),
            pltpu.VMEM((length, width), BF),
            pltpu.VMEM((length, width), F32),
            pltpu.VMEM((length, width), F32),
        ],
        compiler_params=params(),
        name="mlp",
    )(stream0, ctx, w_out, gamma2, seg_col, seg_row, w_up, w_down, cotangent)


def attend_back_body(
    n_ref, qa, qb, ka, kb, va, vb, cos_ref, lo_ref, hi_ref, seg_ref, pad_ref, row_ref,
    q_ref, k_ref, v_ref, g_ref, c_ref, lse_ref, s0_ref, g1_ref, ds1_ref,
    gw_ref, dlow_ref, dg1_ref, bias_ref, dn_ref, dq_ref, dk_ref, dv_ref,
):
    step = pl.program_id(0)
    length, width = n_ref.shape

    @pl.when(step == 0)
    def _():
        fill_bias(bias_ref, seg_ref, pad_ref, row_ref)
        dn_ref[...] = jnp.zeros_like(dn_ref)

    ones = jnp.ones((8, HD), BF)
    for head in range(4):
        lanes = slice(head * HD, (head + 1) * HD)
        query, key, value = q_ref[:, lanes], k_ref[:, lanes], v_ref[:, lanes]
        grad = g_ref[:, lanes]
        both = grad.astype(F32) * c_ref[:, lanes].astype(F32)
        high = both.astype(BF)
        low = (both - high.astype(F32)).astype(BF)
        delta = (dot(ones, high, NT) + dot(ones, low, NT))[0:1, :]
        probs = jnp.exp(dot(key, query, NT) + bias_ref[...] - lse_ref[head : head + 1, :])
        d_scores = (probs * (dot(value, grad, NT) - delta)).astype(BF)
        dv_ref[:, lanes] = dot(probs.astype(BF), grad)
        dk_ref[:, lanes] = dot(d_scores, query)
        dq_ref[:, lanes] = dot(key.T, d_scores).T * HD**-0.5
    for part, (src, first, second) in enumerate(
        ((dq_ref, qa, qb), (dk_ref, ka, kb), (dv_ref, va, vb))
    ):
        if part < 2:
            made = jnp.concatenate(
                [
                    turn(src[:, half * 128 : (half + 1) * 128], cos_ref[...], -lo_ref[...], -hi_ref[...])
                    for half in range(2)
                ],
                axis=1,
            ).astype(BF)
        else:
            made = src[...].astype(BF)
        grad = dot(n_ref[...], made, TN).astype(BF)
        gw_ref[part, 0] = grad[:, :128]
        gw_ref[part, 1] = grad[:, 128:]
        dn_ref[...] += dot(made, jnp.concatenate([first[0], second[0]], axis=1), NT)

    @pl.when(step == pl.num_programs(0) - 1)
    def _():
        dg1_ref[...] = jnp.zeros_like(dg1_ref)

        @pl.loop(0, length // 128)
        def _(t):
            rows = pl.ds(pl.multiple_of(t * 128, 128), 128)
            gain = token_gain(seg_ref[rows, :], g1_ref)
            term, d_gain = norm_back(dn_ref[rows, :], s0_ref[rows, :], gain)
            dlow_ref[rows, :] = (ds1_ref[rows, :] + term).astype(BF)
            dg1_ref[...] += segment_sum(row_ref[:, rows], d_gain)


def attend_back(
    normed, w_qkv, tables, seg_col, pad_col, seg_row, q, k, v, d_ctx, ctx, lse, stream0, gamma1, d_stream1
):
    length, width = normed.shape
    groups = width // 256
    units = [unit_spec(width, part * (width // 128) + e) for part in range(3) for e in range(2)]
    column = pl.BlockSpec((length, 256), lambda j: (0, j))
    full = whole((length, width))
    return pl.pallas_call(
        attend_back_body,
        grid=(groups,),
        in_specs=[full]
        + units
        + [whole((length, 128))] * 3
        + [whole((length, 1))] * 2
        + [whole((1, length))]
        + [column] * 5
        + [pl.BlockSpec((8, length), lambda j: (j, 0)), full, whole((8, width)), full],
        out_specs=(
            pl.BlockSpec((3, 2, width, 128), lambda j: (0, j, 0, 0)),
            full,
            whole((8, width)),
        ),
        out_shape=(
            shaped((3, width // 128, width, 128), BF),
            shaped((length, width), BF),
            shaped((8, width), F32),
        ),
        scratch_shapes=[pltpu.VMEM((length, length), F32), pltpu.VMEM((length, width), F32)]
        + [pltpu.VMEM((length, 256), F32)] * 3,
        compiler_params=params(),
        name="attend_back",
    )(
        normed, *([w_qkv] * 6), *tables, seg_col, pad_col, seg_row, q, k, v, d_ctx, ctx, lse,
        stream0, gamma1, d_stream1,
    )


def skip_back_body(x_ref, s_ref, d_ref, w_ref, gw_ref, dx_ref, ds_ref):
    low = d_ref[...]
    per = 256
    width = x_ref.shape[1]

    @pl.loop(0, width // per)
    def _(i):
        lanes = pl.ds(pl.multiple_of(i * per, per), per)
        part = d_ref[:, lanes]
        top = dot(x_ref[...], part, TN).astype(BF)
        end = dot(s_ref[...], part, TN).astype(BF)
        for e in range(2):
            gw_ref[2 * i + e, :width, :] = top[:, e * 128 : (e + 1) * 128]
            gw_ref[2 * i + e, width:, :] = end[:, e * 128 : (e + 1) * 128]

    tall = 256

    @pl.loop(0, width // tall)
    def _(i):
        rows = pl.ds(pl.multiple_of(i * tall, tall), tall)
        rest = pl.ds(pl.multiple_of(width + i * tall, tall), tall)
        dx_ref[:, rows] = dot(low, columns(w_ref, 0, NB, rows), NT)
        ds_ref[:, rows] = dot(low, columns(w_ref, 0, NB, rest), NT)


def skip_back(inputs, skip_in, d_low, w_skip):
    length, width = inputs.shape
    return pl.pallas_call(
        skip_back_body,
        out_shape=(
            shaped(w_skip.shape, BF),
            shaped((length, width), F32),
            shaped((length, width), F32),
        ),
        compiler_params=params(),
        name="skip_back",
    )(inputs, skip_in, d_low, w_skip)


def rotary(positions):
    half = HD // 2
    lane = jnp.arange(128)
    frequency = 10000.0 ** (-2.0 * (lane % half).astype(F32) / HD)
    phase = positions.reshape(-1, 1).astype(F32) * frequency[None, :]
    cosine, sine = jnp.cos(phase), jnp.sin(phase)
    early = (lane % HD < half)[None, :]
    return cosine, jnp.where(early, -sine, 0.0), jnp.where(early, 0.0, sine)


class Place:
    def __init__(self):
        dp, fs = lax.axis_index("dp"), lax.axis_index("fsdp")
        self.y, self.x, self.z, self.c = dp // 2, dp % 2, fs // 2, fs % 2
        self.dp, self.fs = dp, fs

    def across_x(self):
        return (self.y * 2 + 1 - self.x, self.fs)

    def across_y(self):
        return ((1 - self.y) * 2 + self.x, self.fs)

    def sibling(self):
        return (self.dp, self.z * 2 + 1 - self.c)

    def along_z(self, hop):
        return (self.dp, ((self.z + hop) % 4) * 2 + self.c)

    def greet(self):
        barrier = pltpu.get_barrier_semaphore()
        peers = [self.across_x(), self.across_y(), self.sibling()]
        peers += [self.along_z(hop) for hop in (1, 2, 3)]
        for peer in peers:
            pl.semaphore_signal(barrier, inc=1, device_id=peer, device_id_type=pl.DeviceIdType.MESH)
        pl.semaphore_wait(barrier, len(peers))


def remote(src, dst, send, recv, peer):
    return pltpu.make_async_remote_copy(
        src_ref=src, dst_ref=dst, send_sem=send, recv_sem=recv,
        device_id=peer, device_id_type=pl.DeviceIdType.MESH,
    )


class Lazy:
    def __init__(self, plan, send, recv):
        self.plan, self.send, self.recv = plan, send, recv

    def __len__(self):
        return len(self.plan)

    def __getitem__(self, i):
        if isinstance(i, slice):
            return [self[k] for k in range(*i.indices(len(self)))]
        if i >= len(self.plan):
            raise IndexError
        src, dst, peer = self.plan[i]
        return remote(src, dst, self.send.at[i], self.recv.at[i], peer)


class Gather:
    slots = 8
    stages = 5

    def __init__(self, place, shard, full, first, count, flip, send, recv, local):
        self.me, self.shard, self.full = place, shard, full
        self.rows = pl.ds(first, count)
        self.flip, self.send, self.recv, self.local = flip, send, recv, local

    def copies(self):
        me, full, rows = self.me, self.full, self.rows
        own = self.shard.at[rows, :]
        spot = full.at[me.z, me.c, me.y, me.x, rows, :]
        line = full.at[:, me.c, me.y, me.x, rows, :]
        if self.flip:
            pair = full.at[:, me.c, :, me.x, rows, :]
            near, far = me.across_y(), me.across_x()
            got = full.at[:, me.c, 1 - me.y, me.x, rows, :]
            late = full.at[:, me.c, :, 1 - me.x, rows, :]
        else:
            pair = full.at[:, me.c, me.y, :, rows, :]
            near, far = me.across_x(), me.across_y()
            got = full.at[:, me.c, me.y, 1 - me.x, rows, :]
            late = full.at[:, me.c, 1 - me.y, :, rows, :]
        sib = me.sibling()
        plan = [(own, spot, me.along_z(hop)) for hop in (1, 2, 3)]
        plan += [(line, line, near), (pair, pair, far), (line, line, sib), (got, got, sib), (late, late, sib)]
        return Lazy(plan, self.send, self.recv), (own, spot, self.local)

    def stage(self, number):
        made, keep = self.copies()
        if number == 0:
            pltpu.make_async_copy(*keep).start()
            for copy in made[:3]:
                copy.start()
        elif number == 1:
            pltpu.make_async_copy(*keep).wait()
            for copy in made[:3]:
                copy.wait_recv()
            made[3].start()
            made[5].start()
        elif number == 2:
            made[3].wait_recv()
            made[4].start()
            made[6].start()
        elif number == 3:
            made[4].wait_recv()
            made[7].start()
        else:
            for copy in made[5:]:
                copy.wait_recv()
            for copy in made:
                copy.wait_send()


class Reduce:
    slots = 6
    stages = 5

    def __init__(self, place, grad, out, first, count, flip, send, recv, local, own, half, quarter, parts):
        self.me, self.grad, self.out = place, grad, out
        self.rows = pl.ds(first, count)
        self.flip, self.send, self.recv, self.local = flip, send, recv, local
        self.own, self.other = own
        self.half, self.quarter, self.parts = half, quarter, parts

    @staticmethod
    def scratch(count, per):
        return [
            pltpu.VMEM((2, 4, 2, 2, count, per), BF),
            pltpu.VMEM((4, 2, count, per), BF),
            pltpu.VMEM((4, count, per), BF),
            pltpu.VMEM((3, count, per), BF),
        ]

    def copies(self):
        me, rows = self.me, self.rows
        theirs = self.grad.at[:, 1 - me.c, :, :, rows, :]
        mine = self.grad.at[:, me.c, :, :, rows, :]
        if self.flip:
            give, near = self.own.at[:, :, 1 - me.x], me.across_x()
            give2, far = self.half.at[:, 1 - me.y], me.across_y()
        else:
            give, near = self.own.at[:, 1 - me.y], me.across_y()
            give2, far = self.half.at[:, 1 - me.x], me.across_x()
        plan = [(theirs, self.other, me.sibling()), (give, self.half, near), (give2, self.quarter, far)]
        plan += [
            (self.quarter.at[(me.z + hop) % 4], self.parts.at[hop - 1], me.along_z(hop)) for hop in (1, 2, 3)
        ]
        return Lazy(plan, self.send, self.recv), (mine, self.own, self.local)

    def stage(self, number):
        me = self.me
        made, load = self.copies()
        if number == 0:
            made[0].start()
            pltpu.make_async_copy(*load).start()
        elif number == 1:
            pltpu.make_async_copy(*load).wait()
            made[0].wait_recv()
            self.own[...] = self.own[...] + self.other[...]
            made[1].start()
        elif number == 2:
            made[1].wait_recv()
            if self.flip:
                self.half[...] = self.half[...] + self.own[:, :, me.x]
            else:
                self.half[...] = self.half[...] + self.own[:, me.y]
            made[2].start()
        elif number == 3:
            made[2].wait_recv()
            kept = me.y if self.flip else me.x
            self.quarter[...] = self.quarter[...] + self.half[:, kept]
            for copy in made[3:]:
                copy.start()
        else:
            for copy in made[3:]:
                copy.wait_recv()
            total = self.quarter[me.z].astype(F32)
            for i in range(3):
                total = total + self.parts[i].astype(F32)
            self.out[self.rows, :] = total
            for copy in made:
                copy.wait_send()


def run_ticks(pieces, tick):
    for i in range(len(pieces)):
        stage = tick - i // 2
        if 0 <= stage < pieces[i].stages:
            pieces[i].stage(stage)


def ticks_of(count):
    return (count + 1) // 2 + 4


ANY = pl.BlockSpec(memory_space=pl.ANY)
PIECE = 1 << 19


def cut(shapes):
    made = []
    for which, (tall, per) in enumerate(shapes):
        count = 4 if tall * per * 32 >= 4 * PIECE else 2
        for i in range(count):
            made.append((which, i * tall // count, tall // count, i % 2 == 1))
    return made


def gather_body(plan, count, *refs):
    shard, full, (send, recv, local) = refs[:count], refs[count : 2 * count], refs[2 * count :]
    me = Place()
    me.greet()
    pieces = [
        Gather(me, shard[w], full[w], first, rows, flip, send.at[i], recv.at[i], local.at[i])
        for i, (w, first, rows, flip) in enumerate(plan)
    ]
    for tick in range(ticks_of(len(pieces))):
        run_ticks(pieces, tick)


def gather_all(*weights):
    plan = cut([w.shape for w in weights])
    sems = [pltpu.SemaphoreType.DMA((len(plan), 8))] * 2 + [pltpu.SemaphoreType.DMA((len(plan),))]
    full = pl.pallas_call(
        functools.partial(gather_body, plan, len(weights)),
        in_specs=[ANY] * len(weights),
        out_specs=(ANY,) * len(weights),
        out_shape=tuple(shaped((4, 2, 2, 2) + w.shape, BF) for w in weights),
        scratch_shapes=sems,
        compiler_params=params(collective_id=0, has_side_effects=True),
        name="gather_all",
    )(*weights)
    return [f.reshape(NB, 4 * w.shape[0], w.shape[1]) for f, w in zip(full, weights)]


def reduce_body(plan, count, *refs):
    grad, out, (send, recv, local) = refs[:count], refs[count : 2 * count], refs[2 * count : 2 * count + 3]
    room = refs[2 * count + 3 :]
    me = Place()
    me.greet()
    pieces = [
        Reduce(
            me, grad[w], out[w], first, rows, flip, send.at[i], recv.at[i], local.at[i],
            (room[4 * i].at[0], room[4 * i].at[1]), *room[4 * i + 1 : 4 * i + 4],
        )
        for i, (w, first, rows, flip) in enumerate(plan)
    ]
    for tick in range(ticks_of(len(pieces))):
        run_ticks(pieces, tick)


def reduce_all(*grads):
    tops = [(g.shape[1] // 4, g.shape[2]) for g in grads]
    plan = cut(tops)
    sems = [pltpu.SemaphoreType.DMA((len(plan), 6))] * 2 + [pltpu.SemaphoreType.DMA((len(plan),))]
    room = [buffer for w, _, rows, _ in plan for buffer in Reduce.scratch(rows, tops[w][1])]
    return pl.pallas_call(
        functools.partial(reduce_body, plan, len(grads)),
        in_specs=[ANY] * len(grads),
        out_shape=tuple(shaped(top, F32) for top in tops),
        scratch_shapes=sems + room,
        compiler_params=params(collective_id=1, has_side_effects=True),
        name="reduce_all",
    )(*[g.reshape((4, 2, 2, 2) + top) for g, top in zip(grads, tops)])


def gathered(shard):
    blocks = lax.all_gather(shard, "fsdp", axis=0, tiled=False)
    blocks = lax.all_gather(blocks, "dp", axis=1, tiled=True)
    count, rows, per = blocks.shape
    if count == NB:
        return blocks
    flat = jnp.transpose(blocks, (1, 0, 2)).reshape(rows, count * per)
    return jnp.transpose(flat.reshape(rows, NB, count * per // NB), (1, 0, 2))


def scattered(blocks):
    count, rows, per = blocks.shape
    flat = jnp.transpose(blocks, (1, 0, 2)).reshape(rows, count * per)
    part = lax.psum_scatter(flat, "fsdp", scatter_dimension=1, tiled=True)
    return lax.psum_scatter(part, "dp", scatter_dimension=0, tiled=True).astype(F32)


def shards(
    fast, inputs, skip_in, time_emb, seg_ids, positions, pad_mask,
    w_skip, w_ada1, w_qkv, w_out, w_ada2, w_up, w_down, cotangent,
):
    slots = time_emb.shape[1]
    seg_col, seg_row = seg_ids.reshape(-1, 1), seg_ids.reshape(1, -1)
    pad_col = pad_mask.reshape(-1, 1)
    tables = rotary(positions)
    flat_time = time_emb.reshape(slots, -1)
    time8 = jnp.pad(flat_time, ((0, 8 - slots), (0, 0)))
    if fast:
        w_ada = jnp.concatenate([w_ada1, w_ada2], axis=1)
        f_skip, ada, f_qkv, f_out, f_up, f_down = gather_all(w_skip, w_ada, w_qkv, w_out, w_up, w_down)
    else:
        f_skip, f_qkv, f_out = gathered(w_skip), gathered(w_qkv), gathered(w_out)
        f_up, f_down = gathered(w_up), gathered(w_down)
        ada = jnp.concatenate([gathered(w_ada1), gathered(w_ada2)], axis=2)
    stream0, normed1, gamma1, gamma2 = front(inputs, skip_in, f_skip, time8, ada, seg_col)
    q, k, v, ctx, lse = attend(normed1, f_qkv, tables, seg_col, pad_col, seg_row)
    output, g_down, g_up, g_out, d_stream1, d_ctx, d_gamma2 = mlp(
        stream0, ctx, f_out, gamma2, seg_col, seg_row, f_up, f_down, cotangent
    )
    g_qkv, d_low, d_gamma1 = attend_back(
        normed1, f_qkv, tables, seg_col, pad_col, seg_row, q, k, v, d_ctx, ctx, lse,
        stream0, gamma1, d_stream1,
    )
    width = inputs.shape[1]
    g_qkv = jnp.transpose(
        g_qkv.reshape(NB, 3, width, 128), (0, 2, 1, 3)
    ).reshape(NB, width, 3 * width // NB)
    g_skip, d_input, d_skip = skip_back(inputs, skip_in, d_low, f_skip)
    d_gammas = [d[:slots].astype(BF) for d in (d_gamma1, d_gamma2)]
    per = width // NB
    d_time = 0.0
    for d_gamma, part in zip(d_gammas, (ada[:, :, :per], ada[:, :, per:])):
        flat = jnp.transpose(part, (1, 0, 2)).reshape(width, width)
        d_time = d_time + jnp.einsum("ne,de->nd", d_gamma, flat, preferred_element_type=F32)
    axes = ("dp", "fsdp")
    all_time = lax.all_gather(flat_time, axes, axis=0, tiled=True)
    tall, thin = w_ada1.shape
    all_time = lax.dynamic_slice_in_dim(all_time, lax.axis_index("dp") * tall, tall, 1)
    all_gamma = lax.all_gather(jnp.concatenate(d_gammas, axis=1), axes, axis=0, tiled=True)
    g_ada = []
    for i in range(2):
        mine = lax.dynamic_slice_in_dim(all_gamma, i * width + lax.axis_index("fsdp") * thin, thin, 1)
        g_ada.append(jnp.einsum("nd,ne->de", all_time, mine, preferred_element_type=F32))
    if fast:
        s_down, s_up, s_out, s_qkv, s_skip = reduce_all(g_down, g_up, g_out, g_qkv, g_skip)
    else:
        s_down, s_up, s_out, s_qkv, s_skip = [scattered(g) for g in (g_down, g_up, g_out, g_qkv, g_skip)]
    return (
        output,
        d_input,
        d_skip,
        d_time.reshape(time_emb.shape),
        s_skip,
        g_ada[0],
        s_qkv,
        s_out,
        g_ada[1],
        s_up,
        s_down,
    )


def solution(mesh):
    rows = P(("dp", "fsdp"), None)
    cube = P(("dp", "fsdp"), None, None)
    tile = P("dp", "fsdp")
    fast = mesh.shape["dp"] == 4 and mesh.shape["fsdp"] == NB
    return jax.shard_map(
        functools.partial(shards, fast),
        mesh=mesh,
        in_specs=(rows, rows, cube) + (rows,) * 3 + (tile,) * 7 + (rows,),
        out_specs=(rows, rows, rows, cube) + (tile,) * 7,
        check_vma=False,
    )
```

```python
import functools

import jax
import jax.numpy as jnp
from jax import lax
from jax.experimental import pallas as pl
from jax.experimental.pallas import tpu as pltpu
from jax.sharding import PartitionSpec as P

HD = 64
NB = 8
EPS = 1e-06
MASKED = -1e30
BF = jnp.bfloat16
F32 = jnp.float32
NN = (((1,), (0,)), ((), ()))
NT = (((1,), (1,)), ((), ()))
TN = (((0,), (0,)), ((), ()))
ROOT = 0.7978845608028654
CUBE = 0.044715


def dot(left, right, form=NN):
    return lax.dot_general(left, right, form, preferred_element_type=F32)


def params(**extra):
    return pltpu.CompilerParams(vmem_limit_bytes=60 << 20, **extra)


def whole(shape):
    return pl.BlockSpec(shape, lambda *_: (0,) * len(shape), pipeline_mode=pl.Buffered(1))


ANY = pl.BlockSpec(memory_space=pl.ANY)
UNIT = 128


def shaped(shape, kind):
    return jax.ShapeDtypeStruct(shape, kind)


def columns(ref, first, count, rows=slice(None)):
    return jnp.concatenate([ref[first + i, rows, :] for i in range(count)], axis=1)


def token_gain(seg, gamma):
    gain = gamma[0:1, :]
    for slot in range(1, 4):
        gain = jnp.where(seg == slot, gamma[slot : slot + 1, :], gain)
    return gain


def segment_sum(seg_row, values):
    slots = lax.broadcasted_iota(jnp.int32, (8, seg_row.shape[1]), 0)
    picked = (slots == seg_row).astype(BF)
    high = values.astype(BF)
    low = (values - high.astype(F32)).astype(BF)
    return dot(picked, high) + dot(picked, low)


def norm_back(grad, stream, gain):
    inverse = lax.rsqrt(jnp.mean(stream * stream, axis=-1, keepdims=True) + EPS)
    unit = stream * inverse
    scaled = grad * (1.0 + gain)
    d_stream = inverse * (scaled - unit * jnp.mean(scaled * unit, axis=-1, keepdims=True))
    return d_stream, grad * unit


def norm(stream, gain):
    inverse = lax.rsqrt(jnp.mean(stream * stream, axis=-1, keepdims=True) + EPS)
    return (stream * inverse * (1.0 + gain)).astype(BF)


def fill_bias(bias_ref, seg_ref, pad_ref, row_ref):
    length = seg_ref.shape[0]
    for t in range(length // 128):
        rows = slice(t * 128, (t + 1) * 128)
        keys = lax.broadcasted_iota(jnp.int32, (128, length), 0) + t * 128
        queries = lax.broadcasted_iota(jnp.int32, (128, length), 1)
        allowed = (seg_ref[rows, :] == row_ref[0:1, :]) & (
            (pad_ref[rows, :] > 0) | (keys == queries)
        )
        bias_ref[rows, :] = jnp.where(allowed, 0.0, MASKED)


def turn(unit, cosine, before, after):
    return (
        unit * cosine
        + pltpu.roll(unit, 96, 1) * before
        + pltpu.roll(unit, 32, 1) * after
    )


def unit_spec(rows, base):
    def index(j):
        unit = base + 2 * j
        return (unit // 3, 0, unit % 3)

    return pl.BlockSpec((1, rows, 128), index)


def plain_front_body(x_ref, s_ref, w_ref, time_ref, ada_ref, seg_ref, stream_ref, normed_ref, g1_ref, g2_ref):
    length, width = x_ref.shape
    per = ada_ref.shape[2] // 2
    for f in range(NB):
        both = dot(time_ref[...], ada_ref[f])
        g1_ref[:, f * per : (f + 1) * per] = both[:, :per]
        g2_ref[:, f * per : (f + 1) * per] = both[:, per:]
    for i in range(NB // 2):
        tile = columns(w_ref, 2 * i, 2)
        part = dot(x_ref[...], tile[:width]) + dot(s_ref[...], tile[width:])
        stream_ref[:, i * part.shape[1] : (i + 1) * part.shape[1]] = part

    @pl.loop(0, length // 128)
    def _(t):
        rows = pl.ds(pl.multiple_of(t * 128, 128), 128)
        gain = token_gain(seg_ref[rows, :], g1_ref)
        normed_ref[rows, :] = norm(stream_ref[rows, :], gain)


def plain_front(inputs, skip_in, w_skip, time8, ada, seg_col):
    length, width = inputs.shape
    return pl.pallas_call(
        plain_front_body,
        out_shape=(
            shaped((length, width), F32),
            shaped((length, width), BF),
            shaped((8, width), F32),
            shaped((8, width), F32),
        ),
        compiler_params=params(),
        name="front",
    )(inputs, skip_in, w_skip, time8, ada, seg_col)


def plain_attend_body(
    n_ref, qa, qb, ka, kb, va, vb, cos_ref, lo_ref, hi_ref, seg_ref, pad_ref, row_ref,
    q_ref, k_ref, v_ref, c_ref, lse_ref, bias_ref,
):
    @pl.when(pl.program_id(0) == 0)
    def _():
        fill_bias(bias_ref, seg_ref, pad_ref, row_ref)

    normed = n_ref[...]
    for out, first, second, scale in ((q_ref, qa, qb, HD**-0.5), (k_ref, ka, kb, 1.0)):
        made = dot(normed, jnp.concatenate([first[0], second[0]], axis=1))
        for half in range(2):
            unit = made[:, half * 128 : (half + 1) * 128]
            turned = turn(unit, cos_ref[...], lo_ref[...], hi_ref[...])
            out[:, half * 128 : (half + 1) * 128] = (turned.astype(BF) * scale).astype(BF)
    v_ref[...] = dot(normed, jnp.concatenate([va[0], vb[0]], axis=1)).astype(BF)
    for head in range(4):
        lanes = slice(head * HD, (head + 1) * HD)
        scores = dot(k_ref[:, lanes], q_ref[:, lanes], NT) + bias_ref[...]
        largest = jnp.max(scores, axis=0, keepdims=True)
        exponent = jnp.exp(scores - largest)
        total = jnp.sum(exponent, axis=0, keepdims=True)
        mixed = dot(v_ref[:, lanes].T, exponent.astype(BF)) * (1.0 / total)
        c_ref[:, lanes] = mixed.T.astype(BF)
        lse_ref[head : head + 1, :] = largest + jnp.log(total)


def plain_attend(normed, w_qkv, tables, seg_col, pad_col, seg_row):
    length, width = normed.shape
    groups = width // 256
    units = [unit_spec(width, part * (width // 128) + e) for part in range(3) for e in range(2)]
    column = pl.BlockSpec((length, 256), lambda j: (0, j))
    wide = shaped((length, width), BF)
    return pl.pallas_call(
        plain_attend_body,
        grid=(groups,),
        in_specs=[whole((length, width))]
        + units
        + [whole((length, 128))] * 3
        + [whole((length, 1))] * 2
        + [whole((1, length))],
        out_specs=(column,) * 4 + (pl.BlockSpec((8, length), lambda j: (j, 0)),),
        out_shape=(wide,) * 4 + (shaped((8 * groups, length), F32),),
        scratch_shapes=[pltpu.VMEM((length, length), F32)],
        compiler_params=params(),
        name="attend",
    )(normed, *([w_qkv] * 6), *tables, seg_col, pad_col, seg_row)


def plain_mlp_body(
    stream0_ref, ctx_ref, wout_ref, g2_ref, seg_ref, row_ref, up_ref, down_ref, cot_ref,
    out_ref, gdown_ref, gup_ref, gout_ref, ds1_ref, dctx_ref, dg2_ref,
    s1_ref, n2_ref, acc_ref, dn_ref,
):
    step = pl.program_id(0)
    length, width = ctx_ref.shape
    tiles = length // 128

    @pl.when(step == 0)
    def _():
        @pl.loop(0, NB // 2)
        def _(i):
            lanes = pl.ds(pl.multiple_of(i * 256, 256), 256)
            s1_ref[:, lanes] = stream0_ref[:, lanes] + dot(ctx_ref[...], columns(wout_ref, 2 * i, 2))

        @pl.loop(0, tiles)
        def _(t):
            rows = pl.ds(pl.multiple_of(t * 128, 128), 128)
            n2_ref[rows, :] = norm(s1_ref[rows, :], token_gain(seg_ref[rows, :], g2_ref))

        acc_ref[...] = jnp.zeros_like(acc_ref)
        dn_ref[...] = jnp.zeros_like(dn_ref)

    cot = cot_ref[...]
    up = up_ref[0]
    down = columns(down_ref, 0, NB)
    hidden = dot(n2_ref[...], up)
    square = hidden * hidden
    tanh = jnp.tanh(ROOT * hidden * (1.0 + CUBE * square))
    active = (0.5 * hidden * (1.0 + tanh)).astype(BF)
    slope = 0.5 * (1.0 + tanh) + 0.5 * hidden * (1.0 - tanh * tanh) * (
        ROOT * (1.0 + 3.0 * CUBE * square)
    )
    d_pre = (dot(cot, down, NT) * slope).astype(BF)
    acc_ref[...] += dot(active, down)
    dn_ref[...] += dot(d_pre, up, NT)
    grad = dot(active, cot, TN).astype(BF)
    for f in range(NB):
        gdown_ref[f] = grad[:, f * gdown_ref.shape[2] : (f + 1) * gdown_ref.shape[2]]
    gup_ref[0] = dot(n2_ref[...], d_pre, TN).astype(BF)

    @pl.when(step == pl.num_programs(0) - 1)
    def _():
        dg2_ref[...] = jnp.zeros_like(dg2_ref)

        @pl.loop(0, tiles)
        def _(t):
            rows = pl.ds(pl.multiple_of(t * 128, 128), 128)
            stream = s1_ref[rows, :]
            out_ref[rows, :] = (stream + acc_ref[rows, :]).astype(BF)
            gain = token_gain(seg_ref[rows, :], g2_ref)
            term, d_gain = norm_back(dn_ref[rows, :], stream, gain)
            d_stream = cot_ref[rows, :].astype(F32) + term
            ds1_ref[rows, :] = d_stream
            n2_ref[rows, :] = d_stream.astype(BF)
            dg2_ref[...] += segment_sum(row_ref[:, rows], d_gain)

        @pl.loop(0, NB // 2)
        def _(i):
            lanes = pl.ds(pl.multiple_of(i * 256, 256), 256)
            part = dot(ctx_ref[...], n2_ref[:, lanes], TN).astype(BF)
            gout_ref[2 * i] = part[:, :128]
            gout_ref[2 * i + 1] = part[:, 128:]

        acc_ref[...] = jnp.zeros_like(acc_ref)

        @pl.loop(0, NB // 2)
        def _(i):
            lanes = pl.ds(pl.multiple_of(i * 256, 256), 256)
            acc_ref[...] += dot(n2_ref[:, lanes], columns(wout_ref, 2 * i, 2), NT)

        dctx_ref[...] = acc_ref[...].astype(BF)


def plain_mlp(stream0, ctx, w_out, gamma2, seg_col, seg_row, w_up, w_down, cotangent):
    length, width = ctx.shape
    hidden = w_down.shape[1]
    piece = hidden // NB
    per = width // NB
    full = whole((length, width))
    return pl.pallas_call(
        plain_mlp_body,
        grid=(NB,),
        in_specs=[
            full,
            full,
            whole((NB, width, per)),
            whole((8, width)),
            whole((length, 1)),
            whole((1, length)),
            pl.BlockSpec((1, width, piece), lambda j: (j, 0, 0)),
            pl.BlockSpec((NB, piece, per), lambda j: (0, j, 0)),
            full,
        ],
        out_specs=(
            full,
            pl.BlockSpec((NB, piece, per), lambda j: (0, j, 0)),
            pl.BlockSpec((1, width, piece), lambda j: (j, 0, 0)),
            whole((NB, width, per)),
            full,
            full,
            whole((8, width)),
        ),
        out_shape=(
            shaped((length, width), BF),
            shaped((NB, hidden, per), BF),
            shaped((NB, width, piece), BF),
            shaped((NB, width, per), BF),
            shaped((length, width), F32),
            shaped((length, width), BF),
            shaped((8, width), F32),
        ),
        scratch_shapes=[
            pltpu.VMEM((length, width), F32),
            pltpu.VMEM((length, width), BF),
            pltpu.VMEM((length, width), F32),
            pltpu.VMEM((length, width), F32),
        ],
        compiler_params=params(),
        name="mlp",
    )(stream0, ctx, w_out, gamma2, seg_col, seg_row, w_up, w_down, cotangent)


def plain_attend_back_body(
    n_ref, qa, qb, ka, kb, va, vb, cos_ref, lo_ref, hi_ref, seg_ref, pad_ref, row_ref,
    q_ref, k_ref, v_ref, g_ref, c_ref, lse_ref, s0_ref, g1_ref, ds1_ref,
    gw_ref, dlow_ref, dg1_ref, bias_ref, dn_ref, dq_ref, dk_ref, dv_ref,
):
    step = pl.program_id(0)
    length, width = n_ref.shape

    @pl.when(step == 0)
    def _():
        fill_bias(bias_ref, seg_ref, pad_ref, row_ref)
        dn_ref[...] = jnp.zeros_like(dn_ref)

    ones = jnp.ones((8, HD), BF)
    for head in range(4):
        lanes = slice(head * HD, (head + 1) * HD)
        query, key, value = q_ref[:, lanes], k_ref[:, lanes], v_ref[:, lanes]
        grad = g_ref[:, lanes]
        both = grad.astype(F32) * c_ref[:, lanes].astype(F32)
        high = both.astype(BF)
        low = (both - high.astype(F32)).astype(BF)
        delta = (dot(ones, high, NT) + dot(ones, low, NT))[0:1, :]
        probs = jnp.exp(dot(key, query, NT) + bias_ref[...] - lse_ref[head : head + 1, :])
        d_scores = (probs * (dot(value, grad, NT) - delta)).astype(BF)
        dv_ref[:, lanes] = dot(probs.astype(BF), grad)
        dk_ref[:, lanes] = dot(d_scores, query)
        dq_ref[:, lanes] = dot(key.T, d_scores).T * HD**-0.5
    for part, (src, first, second) in enumerate(
        ((dq_ref, qa, qb), (dk_ref, ka, kb), (dv_ref, va, vb))
    ):
        if part < 2:
            made = jnp.concatenate(
                [
                    turn(src[:, half * 128 : (half + 1) * 128], cos_ref[...], -lo_ref[...], -hi_ref[...])
                    for half in range(2)
                ],
                axis=1,
            ).astype(BF)
        else:
            made = src[...].astype(BF)
        grad = dot(n_ref[...], made, TN).astype(BF)
        gw_ref[part, 0] = grad[:, :128]
        gw_ref[part, 1] = grad[:, 128:]
        dn_ref[...] += dot(made, jnp.concatenate([first[0], second[0]], axis=1), NT)

    @pl.when(step == pl.num_programs(0) - 1)
    def _():
        dg1_ref[...] = jnp.zeros_like(dg1_ref)

        @pl.loop(0, length // 128)
        def _(t):
            rows = pl.ds(pl.multiple_of(t * 128, 128), 128)
            gain = token_gain(seg_ref[rows, :], g1_ref)
            term, d_gain = norm_back(dn_ref[rows, :], s0_ref[rows, :], gain)
            dlow_ref[rows, :] = (ds1_ref[rows, :] + term).astype(BF)
            dg1_ref[...] += segment_sum(row_ref[:, rows], d_gain)


def plain_attend_back(
    normed, w_qkv, tables, seg_col, pad_col, seg_row, q, k, v, d_ctx, ctx, lse, stream0, gamma1, d_stream1
):
    length, width = normed.shape
    groups = width // 256
    units = [unit_spec(width, part * (width // 128) + e) for part in range(3) for e in range(2)]
    column = pl.BlockSpec((length, 256), lambda j: (0, j))
    full = whole((length, width))
    return pl.pallas_call(
        plain_attend_back_body,
        grid=(groups,),
        in_specs=[full]
        + units
        + [whole((length, 128))] * 3
        + [whole((length, 1))] * 2
        + [whole((1, length))]
        + [column] * 5
        + [pl.BlockSpec((8, length), lambda j: (j, 0)), full, whole((8, width)), full],
        out_specs=(
            pl.BlockSpec((3, 2, width, 128), lambda j: (0, j, 0, 0)),
            full,
            whole((8, width)),
        ),
        out_shape=(
            shaped((3, width // 128, width, 128), BF),
            shaped((length, width), BF),
            shaped((8, width), F32),
        ),
        scratch_shapes=[pltpu.VMEM((length, length), F32), pltpu.VMEM((length, width), F32)]
        + [pltpu.VMEM((length, 256), F32)] * 3,
        compiler_params=params(),
        name="attend_back",
    )(
        normed, *([w_qkv] * 6), *tables, seg_col, pad_col, seg_row, q, k, v, d_ctx, ctx, lse,
        stream0, gamma1, d_stream1,
    )


def plain_skip_back_body(x_ref, s_ref, d_ref, w_ref, gw_ref, dx_ref, ds_ref):
    low = d_ref[...]
    per = 256
    width = x_ref.shape[1]

    @pl.loop(0, width // per)
    def _(i):
        lanes = pl.ds(pl.multiple_of(i * per, per), per)
        part = d_ref[:, lanes]
        top = dot(x_ref[...], part, TN).astype(BF)
        end = dot(s_ref[...], part, TN).astype(BF)
        for e in range(2):
            gw_ref[2 * i + e, :width, :] = top[:, e * 128 : (e + 1) * 128]
            gw_ref[2 * i + e, width:, :] = end[:, e * 128 : (e + 1) * 128]

    tall = 256

    @pl.loop(0, width // tall)
    def _(i):
        rows = pl.ds(pl.multiple_of(i * tall, tall), tall)
        rest = pl.ds(pl.multiple_of(width + i * tall, tall), tall)
        dx_ref[:, rows] = dot(low, columns(w_ref, 0, NB, rows), NT)
        ds_ref[:, rows] = dot(low, columns(w_ref, 0, NB, rest), NT)


def plain_skip_back(inputs, skip_in, d_low, w_skip):
    length, width = inputs.shape
    return pl.pallas_call(
        plain_skip_back_body,
        out_shape=(
            shaped(w_skip.shape, BF),
            shaped((length, width), F32),
            shaped((length, width), F32),
        ),
        compiler_params=params(),
        name="skip_back",
    )(inputs, skip_in, d_low, w_skip)


class Place:
    def __init__(self):
        dp, fs = lax.axis_index("dp"), lax.axis_index("fsdp")
        self.y, self.x, self.z, self.c = dp // 2, dp % 2, fs // 2, fs % 2
        self.dp, self.fs = dp, fs

    def across_x(self):
        return (self.y * 2 + 1 - self.x, self.fs)

    def across_y(self):
        return ((1 - self.y) * 2 + self.x, self.fs)

    def sibling(self):
        return (self.dp, self.z * 2 + 1 - self.c)

    def along_z(self, hop):
        return (self.dp, ((self.z + hop) % 4) * 2 + self.c)

    def greet(self):
        barrier = pltpu.get_barrier_semaphore()
        peers = [self.across_x(), self.across_y(), self.sibling()]
        peers += [self.along_z(hop) for hop in (1, 2, 3)]
        for peer in peers:
            pl.semaphore_signal(barrier, inc=1, device_id=peer, device_id_type=pl.DeviceIdType.MESH)
        pl.semaphore_wait(barrier, len(peers))


def remote(src, dst, send, recv, peer):
    return pltpu.make_async_remote_copy(
        src_ref=src, dst_ref=dst, send_sem=send, recv_sem=recv,
        device_id=peer, device_id_type=pl.DeviceIdType.MESH,
    )


class Lazy:
    def __init__(self, plan, send, recv):
        self.plan, self.send, self.recv = plan, send, recv

    def __len__(self):
        return len(self.plan)

    def __getitem__(self, i):
        if isinstance(i, slice):
            return [self[k] for k in range(*i.indices(len(self)))]
        if i >= len(self.plan):
            raise IndexError
        src, dst, peer = self.plan[i]
        return remote(src, dst, self.send.at[i], self.recv.at[i], peer)


def flow(*copy):
    return pltpu.make_async_copy(*copy)


class Gather:
    sems = 8

    def __init__(self, place, source, full, rows, flip):
        self.me, self.source, self.full, self.rows, self.flip = place, source, full, rows, flip

    def bind(self, send, recv, local):
        self.send, self.recv, self.local = send, recv, local

    def copies(self):
        me, full, rows = self.me, self.full, self.rows
        spot = full.at[me.z, me.c, me.y, me.x, rows, :]
        line = full.at[:, me.c, me.y, me.x, rows, :]
        if self.flip:
            pair = full.at[:, me.c, :, me.x, rows, :]
            near, far = me.across_y(), me.across_x()
            got = full.at[:, me.c, 1 - me.y, me.x, rows, :]
            late = full.at[:, me.c, :, 1 - me.x, rows, :]
        else:
            pair = full.at[:, me.c, me.y, :, rows, :]
            near, far = me.across_x(), me.across_y()
            got = full.at[:, me.c, me.y, 1 - me.x, rows, :]
            late = full.at[:, me.c, 1 - me.y, :, rows, :]
        sib = me.sibling()
        plan = [(self.source, spot, me.along_z(hop)) for hop in (1, 2, 3)]
        plan += [(line, line, near), (pair, pair, far), (line, line, sib), (got, got, sib), (late, late, sib)]
        return Lazy(plan, self.send, self.recv), (self.source, spot, self.local)

    def stage(self, number):
        made, keep = self.copies()
        if number == 0:
            flow(*keep).start()
            for copy in made[:3]:
                copy.start()
        elif number == 1:
            flow(*keep).wait()
            for copy in made[:3]:
                copy.wait_recv()
            made[3].start()
            made[5].start()
        elif number == 2:
            made[3].wait_recv()
            made[4].start()
            made[6].start()
        elif number == 3:
            made[4].wait_recv()
            made[7].start()
        else:
            for copy in made[5:]:
                copy.wait_recv()
            for copy in made[:]:
                copy.wait_send()


class Reduce:
    sems = 6

    def __init__(self, place, theirs, mine, own, room, out, flip, load):
        self.me, self.theirs, self.mine, self.own = place, theirs, mine, own
        self.other, self.half, self.quarter, self.parts = room
        self.out, self.flip, self.load = out, flip, load

    @staticmethod
    def room(count, per):
        return [
            pltpu.VMEM((4, 2, 2, count, per), BF),
            pltpu.VMEM((4, 2, count, per), BF),
            pltpu.VMEM((4, count, per), BF),
            pltpu.VMEM((3, count, per), BF),
        ]

    def bind(self, send, recv, local):
        self.send, self.recv, self.local = send, recv, local

    def copies(self):
        me = self.me
        if self.flip:
            give, near = self.own.at[:, :, 1 - me.x], me.across_x()
            give2, far = self.half.at[:, 1 - me.y], me.across_y()
        else:
            give, near = self.own.at[:, 1 - me.y], me.across_y()
            give2, far = self.half.at[:, 1 - me.x], me.across_x()
        plan = [(self.theirs, self.other, me.sibling()), (give, self.half, near), (give2, self.quarter, far)]
        plan += [
            (self.quarter.at[(me.z + hop) % 4], self.parts.at[hop - 1], me.along_z(hop)) for hop in (1, 2, 3)
        ]
        return Lazy(plan, self.send, self.recv), (self.mine, self.own, self.local)

    def stage(self, number):
        me = self.me
        made, load = self.copies()
        if number == 0:
            made[0].start()
            if self.load:
                flow(*load).start()
        elif number == 1:
            if self.load:
                flow(*load).wait()
            made[0].wait_recv()
            self.own[...] = self.own[...] + self.other[...]
            made[1].start()
        elif number == 2:
            made[1].wait_recv()
            if self.flip:
                self.half[...] = self.half[...] + self.own[:, :, me.x]
            else:
                self.half[...] = self.half[...] + self.own[:, me.y]
            made[2].start()
        elif number == 3:
            made[0].wait_send()
            made[1].wait_send()
            made[2].wait_recv()
            kept = me.y if self.flip else me.x
            self.quarter[...] = self.quarter[...] + self.half[:, kept]
            for copy in made[3:]:
                copy.start()
        else:
            for copy in made[3:]:
                copy.wait_recv()
            total = self.quarter[me.z].astype(F32)
            for i in range(3):
                total = total + self.parts[i].astype(F32)
            self.out[...] = total
            for copy in made[2:]:
                copy.wait_send()


class Traffic:
    def __init__(self):
        self.todo, self.pieces = {}, []

    def add(self, first, *pieces, gap=1):
        self.pieces += pieces
        for piece in pieces:
            for stage in range(5):
                self.todo.setdefault(first + stage * gap, []).append((stage, piece))

    def bind(self, send, recv, local):
        for i, piece in enumerate(self.pieces):
            piece.bind(send.at[i], recv.at[i], local.at[i])

    def at(self, hook):
        for stage, piece in sorted(self.todo.pop(hook, []), key=lambda item: -item[0]):
            piece.stage(stage)

    def fire(self, step, steps, per, hook):
        for s in range(steps):
            if s * per + hook in self.todo:
                pl.when(step == s)(functools.partial(self.at, s * per + hook))

    def drain(self):
        for hook in sorted(self.todo):
            self.at(hook)


def semaphores(count, kind):
    return [pltpu.SemaphoreType.DMA((count, kind))] * 2 + [pltpu.SemaphoreType.DMA((count,))]


def full_of(rows, per):
    return shaped((4, 2, 2, 2, rows, per), BF)


def halves(rows):
    return [(pl.ds(e * (rows // 2), rows // 2), e == 1) for e in range(2)]


def up_pair(me, shard, full, q):
    lanes = pl.ds(q * UNIT, UNIT)
    return [Gather(me, shard.at[rows, lanes], full, rows, flip) for rows, flip in halves(shard.shape[0])]


def down_pair(me, shard, full, q):
    tall = shard.shape[0] // 2
    step = tall // 4
    return [
        Gather(me, shard.at[pl.ds(e * tall + q * step, step), :], full, pl.ds(e * step, step), e == 1)
        for e in range(2)
    ]


def row_pairs(me, shard, full, count):
    tall = shard.shape[0] // count
    made = [
        Gather(me, shard.at[pl.ds(i * tall, tall), :], full, pl.ds(i * tall, tall), i % 2 == 1)
        for i in range(count)
    ]
    return [made[i : i + 2] for i in range(0, count, 2)]


def front_body(
    x_ref, s_ref, time_ref, seg_ref, skip_ref, ada_ref, qkv_ref,
    stream_ref, normed_ref, g1_ref, g2_ref, fskip_ref, fada_ref, fqkv_ref,
    w_ref, a_ref, w_sem, send, recv, local,
):
    length, width = x_ref.shape
    per = ada_ref.shape[1] // 2
    me = Place()
    me.greet()
    traffic = Traffic()
    plan = row_pairs(me, skip_ref, fskip_ref, 4) + row_pairs(me, ada_ref, fada_ref, 2)
    need = len(plan) + 4
    plan += row_pairs(me, qkv_ref, fqkv_ref, 4)
    for i, pair in enumerate(plan):
        traffic.add(i, *pair)
    traffic.bind(send, recv, local)
    for hook in range(need):
        traffic.at(hook)
    loads = [flow(fskip_ref, w_ref, w_sem.at[0]), flow(fada_ref, a_ref, w_sem.at[1])]
    for load in loads:
        load.start()
    for load in loads:
        load.wait()
    for i in range(4):
        tile = jnp.concatenate([w_ref[i, c].reshape(2 * width, UNIT) for c in range(2)], axis=1)
        part = dot(x_ref[...], tile[:width]) + dot(s_ref[...], tile[width:])
        stream_ref[:, i * 2 * UNIT : (i + 1) * 2 * UNIT] = part
        if i % 2 == 1:
            traffic.at(need + i // 2)
    for f in range(NB):
        both = dot(time_ref[...], a_ref[f // 2, f % 2].reshape(width, 2 * per))
        g1_ref[:, f * per : (f + 1) * per] = both[:, :per]
        g2_ref[:, f * per : (f + 1) * per] = both[:, per:]

    @pl.loop(0, length // UNIT)
    def _(t):
        rows = pl.ds(pl.multiple_of(t * UNIT, UNIT), UNIT)
        gain = token_gain(seg_ref[rows, :], g1_ref)
        normed_ref[rows, :] = norm(stream_ref[rows, :], gain)

    traffic.drain()


def front(inputs, skip_in, time8, seg_col, w_skip, w_ada, w_qkv):
    length, width = inputs.shape
    fulls = [full_of(*w.shape) for w in (w_skip, w_ada, w_qkv)]
    vmem = pl.BlockSpec(memory_space=pltpu.VMEM)
    return pl.pallas_call(
        front_body,
        in_specs=[vmem] * 4 + [ANY] * 3,
        out_specs=(vmem,) * 4 + (ANY,) * 3,
        out_shape=(
            shaped((length, width), F32),
            shaped((length, width), BF),
            shaped((8, width), F32),
            shaped((8, width), F32),
            *fulls,
        ),
        scratch_shapes=[pltpu.VMEM(f.shape, BF) for f in fulls[:2]]
        + [pltpu.SemaphoreType.DMA((2,))]
        + semaphores(10, Gather.sems),
        compiler_params=params(collective_id=0, has_side_effects=True),
        name="front",
    )(inputs, skip_in, time8, seg_col, w_skip, w_ada, w_qkv)


def attend_body(
    n_ref, qa, qb, ka, kb, va, vb, cos_ref, lo_ref, hi_ref, seg_ref, pad_ref, row_ref, out_ref, up_ref, down_ref,
    q_ref, k_ref, v_ref, c_ref, lse_ref, fout_ref, fup0_ref, fdn0_ref, fup1_ref,
    bias_ref, send, recv, local,
):
    step = pl.program_id(0)
    last = pl.num_programs(0) - 1
    me = Place()
    traffic = Traffic()
    pairs = row_pairs(me, out_ref, fout_ref, 2) + [
        up_pair(me, up_ref, fup0_ref, 0),
        down_pair(me, down_ref, fdn0_ref, 0),
        up_pair(me, up_ref, fup1_ref, 1),
    ]
    for i, pair in enumerate(pairs):
        traffic.add(2 * i, *pair, gap=2)
    traffic.bind(send, recv, local)
    fire = functools.partial(traffic.fire, step, 4, 4)

    @pl.when(step == 0)
    def _():
        me.greet()
        traffic.at(0)
        fill_bias(bias_ref, seg_ref, pad_ref, row_ref)

    normed = n_ref[...]
    for out, first, second, scale in ((q_ref, qa, qb, HD**-0.5), (k_ref, ka, kb, 1.0)):
        made = dot(normed, jnp.concatenate([first[0], second[0]], axis=1))
        for half in range(2):
            unit = made[:, half * 128 : (half + 1) * 128]
            turned = turn(unit, cos_ref[...], lo_ref[...], hi_ref[...])
            out[:, half * 128 : (half + 1) * 128] = (turned.astype(BF) * scale).astype(BF)
    v_ref[...] = dot(normed, jnp.concatenate([va[0], vb[0]], axis=1)).astype(BF)
    for head in range(4):
        fire(head)
        lanes = slice(head * HD, (head + 1) * HD)
        scores = dot(k_ref[:, lanes], q_ref[:, lanes], NT) + bias_ref[...]
        largest = jnp.max(scores, axis=0, keepdims=True)
        exponent = jnp.exp(scores - largest)
        total = jnp.sum(exponent, axis=0, keepdims=True)
        mixed = dot(v_ref[:, lanes].T, exponent.astype(BF)) * (1.0 / total)
        c_ref[:, lanes] = mixed.T.astype(BF)
        lse_ref[head : head + 1, :] = largest + jnp.log(total)
    pl.when(step == last)(traffic.drain)


def attend(normed, w_qkv, tables, seg_col, pad_col, seg_row, w_out, w_up, w_down):
    length, width = normed.shape
    groups = width // 256
    units = [unit_spec(width, part * (width // 128) + e) for part in range(3) for e in range(2)]
    column = pl.BlockSpec((length, 256), lambda j: (0, j))
    wide = shaped((length, width), BF)
    quarter = full_of(w_up.shape[0], UNIT)
    return pl.pallas_call(
        attend_body,
        grid=(groups,),
        in_specs=[whole((length, width))]
        + units
        + [whole((length, 128))] * 3
        + [whole((length, 1))] * 2
        + [whole((1, length))]
        + [ANY] * 3,
        out_specs=(column,) * 4 + (pl.BlockSpec((8, length), lambda j: (j, 0)),) + (ANY,) * 4,
        out_shape=(wide,) * 4
        + (shaped((8 * groups, length), F32), full_of(*w_out.shape), quarter, quarter, quarter),
        scratch_shapes=[pltpu.VMEM((length, length), F32)] + semaphores(8, Gather.sems),
        compiler_params=params(collective_id=1, has_side_effects=True),
        name="attend",
    )(normed, *([w_qkv] * 6), *tables, seg_col, pad_col, seg_row, w_out, w_up, w_down)


def mlp_body(
    stream0_ref, ctx_ref, wout_ref, g2_ref, seg_ref, row_ref, cot_ref,
    up_ref, down_ref, fup0, fdn0, fup1,
    out_ref, gout_ref, ds1_ref, dctx_ref, dg2_ref, sup0, sdn0, sup1, sdn1, gup2, gdn2, gup3, gdn3,
    fdn1, fup2, fdn2, fup3, fdn3,
    s1_ref, n2_ref, acc_ref, dn_ref, up_tile, dn_tile, act_ref, pre_ref, stage_up, stage_dn,
    sem, gsend, grecv, glocal, rsend, rrecv, rlocal, *room,
):
    step = pl.program_id(0)
    steps = 8
    length, width = ctx_ref.shape
    tiles = length // UNIT
    me = Place()
    gather, reduce = Traffic(), Traffic()
    gather.add(0, *down_pair(me, down_ref, fdn1, 1))
    gather.add(2, *up_pair(me, up_ref, fup2, 2))
    gather.add(4, *down_pair(me, down_ref, fdn2, 2))
    gather.add(6, *up_pair(me, up_ref, fup3, 3))
    gather.add(8, *down_pair(me, down_ref, fdn3, 3))
    gather.bind(gsend, grecv, glocal)
    count = 0
    for q, (sup, sdn) in enumerate(((sup0, sdn0), (sup1, sdn1))):
        made = []
        for rows, flip in halves(2 * UNIT):
            theirs = stage_up.at[q, 1 - me.c, :, :, :, rows, :]
            mine = stage_up.at[q, me.c, :, :, :, rows, :]
            made.append(Reduce(me, theirs, mine, mine, room[4 * count : 4 * count + 4], sup.at[rows, :], flip, False))
            count += 1
        for e in range(2):
            theirs = stage_dn.at[q, e, :, 1 - me.c]
            mine = stage_dn.at[q, e, :, me.c]
            rows = pl.ds(e * UNIT, UNIT)
            made.append(Reduce(me, theirs, mine, mine, room[4 * count : 4 * count + 4], sdn.at[rows, :], e == 1, False))
            count += 1
        reduce.add(4 + 4 * q, *made[2:])
        reduce.add(5 + 4 * q, *made[:2])
    reduce.bind(rsend, rrecv, rlocal)
    ups, downs = (fup0, fup1, fup2, fup3), (fdn0, fdn1, fdn2, fdn3)
    saves = {4: (gup2, gdn2), 6: (gup3, gdn3)}

    def tile_loads(s):
        q, e = s // 2, s % 2
        return (
            flow(ups[q].at[:, e], up_tile.at[s % 2], sem.at[0, s % 2]),
            flow(downs[q].at[:, :, :, :, pl.ds(e * UNIT, UNIT), :], dn_tile.at[s % 2], sem.at[1, s % 2]),
        )

    def grad_saves(s):
        q, e = s // 2, s % 2
        gup, gdn = saves[2 * q]
        return (
            flow(stage_up.at[q % 2, e], gup.at[e], sem.at[2, s - 4]),
            flow(stage_dn.at[q % 2, e], gdn.at[e], sem.at[3, s - 4]),
        )

    def hook(which):
        gather.fire(step, steps, 2, which)
        reduce.fire(step, steps, 2, which)

    @pl.when(step == 0)
    def _():
        me.greet()
        gather.at(0)
        for load in tile_loads(0):
            load.start()
        first = flow(stream0_ref, s1_ref, sem.at[2, 0])
        first.start()
        first.wait()
        for i in range(4):
            lanes = slice(i * 2 * UNIT, (i + 1) * 2 * UNIT)
            tile = jnp.concatenate([wout_ref[i, c].reshape(width, UNIT) for c in range(2)], axis=1)
            s1_ref[:, lanes] += dot(ctx_ref[...], tile)

        @pl.loop(0, tiles)
        def _(t):
            rows = pl.ds(pl.multiple_of(t * UNIT, UNIT), UNIT)
            n2_ref[rows, :] = norm(s1_ref[rows, :], token_gain(seg_ref[rows, :], g2_ref))

        acc_ref[...] = jnp.zeros_like(acc_ref)
        dn_ref[...] = jnp.zeros_like(dn_ref)

    hook(0)
    for s in range(steps):

        @pl.when(step == s)
        def _(s=s):
            if s in (2, 4, 6):
                for load in tile_loads(s):
                    load.start()
            for load in tile_loads(s):
                load.wait()
            if s % 2 == 0:
                for load in tile_loads(s + 1):
                    load.start()

    slot = step % 2
    up = jnp.concatenate([up_tile[slot, z].reshape(width, UNIT) for z in range(4)], axis=1)
    down = jnp.concatenate([dn_tile[slot, f // 2, f % 2].reshape(4 * UNIT, UNIT) for f in range(NB)], axis=1)
    hidden = dot(n2_ref[...], up)
    square = hidden * hidden
    tanh = jnp.tanh(ROOT * hidden * (1.0 + CUBE * square))
    active = (0.5 * hidden * (1.0 + tanh)).astype(BF)
    act_ref[...] = active
    slope = 0.5 * (1.0 + tanh) + 0.5 * hidden * (1.0 - tanh * tanh) * (
        ROOT * (1.0 + 3.0 * CUBE * square)
    )
    d_pre = (dot(cot_ref[...], down, NT) * slope).astype(BF)
    pre_ref[...] = d_pre
    acc_ref[...] += dot(active, down)
    dn_ref[...] += dot(d_pre, up, NT)
    hook(1)
    par = (step // 2) % 2
    grad = dot(act_ref[...], cot_ref[...], TN).astype(BF)
    for f in range(NB):
        stage_dn[par, slot, f // 2, f % 2] = grad[:, f * UNIT : (f + 1) * UNIT].reshape(2, 2, UNIT, UNIT)
    grad = dot(n2_ref[...], pre_ref[...], TN).astype(BF)
    for z in range(4):
        stage_up[par, slot, z] = grad[:, z * UNIT : (z + 1) * UNIT].reshape(2, 2, 2 * UNIT, UNIT)
    for s in range(4, steps):

        @pl.when(step == s)
        def _(s=s):
            for save in grad_saves(s):
                save.start()

    @pl.when(step == steps - 1)
    def _():
        dg2_ref[...] = jnp.zeros_like(dg2_ref)

        @pl.loop(0, tiles)
        def _(t):
            rows = pl.ds(pl.multiple_of(t * UNIT, UNIT), UNIT)
            stream = s1_ref[rows, :]
            out_ref[rows, :] = (stream + acc_ref[rows, :]).astype(BF)
            gain = token_gain(seg_ref[rows, :], g2_ref)
            term, d_gain = norm_back(dn_ref[rows, :], stream, gain)
            d_stream = cot_ref[rows, :].astype(F32) + term
            s1_ref[rows, :] = d_stream
            n2_ref[rows, :] = d_stream.astype(BF)
            dg2_ref[...] += segment_sum(row_ref[:, rows], d_gain)

        keep = flow(s1_ref, ds1_ref, sem.at[0, 0])
        keep.start()
        for i in range(4):
            lanes = slice(i * 2 * UNIT, (i + 1) * 2 * UNIT)
            part = dot(ctx_ref[...], n2_ref[:, lanes], TN).astype(BF)
            for c in range(2):
                gout_ref[i, c] = part[:, c * UNIT : (c + 1) * UNIT].reshape(2, 2, 2 * UNIT, UNIT)
        for i in range(4):
            lanes = slice(i * 2 * UNIT, (i + 1) * 2 * UNIT)
            tile = jnp.concatenate([wout_ref[i, c].reshape(width, UNIT) for c in range(2)], axis=1)
            part = dot(n2_ref[:, lanes], tile, NT)
            acc_ref[...] = part if i == 0 else acc_ref[...] + part
        dctx_ref[...] = acc_ref[...].astype(BF)
        gather.drain()
        reduce.drain()
        for s in range(4, steps):
            for save in grad_saves(s):
                save.wait()
        keep.wait()


def mlp(stream0, ctx, w_out, gamma2, seg_col, seg_row, cotangent, s_up, s_down, fup0, fdn0, fup1):
    length, width = ctx.shape
    full = whole((length, width))
    part = pl.BlockSpec((2 * UNIT, UNIT), lambda j: (0, 0))
    quarter = full_of(2 * UNIT, UNIT)
    grads = (shaped((2, 4, 2, 2, 2 * UNIT, UNIT), BF), shaped((2, 4, 2, 2, 2, UNIT, UNIT), BF))
    pieces = 8
    return pl.pallas_call(
        mlp_body,
        grid=(8,),
        in_specs=[
            ANY,
            full,
            whole(w_out.shape),
            whole((8, width)),
            whole((length, 1)),
            whole((1, length)),
            full,
        ]
        + [ANY] * 5,
        out_specs=(full, whole(w_out.shape), ANY, full, whole((8, width))) + (part,) * 4 + (ANY,) * 9,
        out_shape=(
            shaped((length, width), BF),
            shaped(w_out.shape, BF),
            shaped((length, width), F32),
            shaped((length, width), BF),
            shaped((8, width), F32),
        )
        + (shaped((2 * UNIT, UNIT), F32),) * 4
        + grads * 2
        + (quarter,) * 5,
        scratch_shapes=[
            pltpu.VMEM((length, width), F32),
            pltpu.VMEM((length, width), BF),
            pltpu.VMEM((length, width), F32),
            pltpu.VMEM((length, width), F32),
            pltpu.VMEM((2, 4, 2, 2, 2 * UNIT, UNIT), BF),
            pltpu.VMEM((2, 4, 2, 2, 2, UNIT, UNIT), BF),
            pltpu.VMEM((length, 4 * UNIT), BF),
            pltpu.VMEM((length, 4 * UNIT), BF),
            pltpu.VMEM((2, 2, 4, 2, 2, 2 * UNIT, UNIT), BF),
            pltpu.VMEM((2, 2, 4, 2, 2, 2, UNIT, UNIT), BF),
            pltpu.SemaphoreType.DMA((4, 4)),
        ]
        + semaphores(10, Gather.sems)
        + semaphores(pieces, Reduce.sems)
        + Reduce.room(UNIT, UNIT) * pieces,
        compiler_params=params(collective_id=2, has_side_effects=True),
        name="mlp",
    )(stream0, ctx, w_out, gamma2, seg_col, seg_row, cotangent, s_up, s_down, fup0, fdn0, fup1)


def attend_back_body(
    n_ref, qa, qb, ka, kb, va, vb, cos_ref, lo_ref, hi_ref, seg_ref, pad_ref, row_ref,
    q_ref, k_ref, v_ref, g_ref, c_ref, lse_ref, g1_ref, s0_ref, ds1_ref, gup2, gdn2, gup3, gdn3, gout,
    gw_ref, dlow_ref, dg1_ref, sup2, sdn2, sup3, sdn3, sout,
    bias_ref, dn_ref, dq_ref, dk_ref, dv_ref, s0_buf, sem, send, recv, local, *room,
):
    step = pl.program_id(0)
    last = pl.num_programs(0) - 1
    length, width = n_ref.shape
    me = Place()
    traffic = Traffic()
    count = 0
    for q, (gup, gdn, sup, sdn) in enumerate(((gup2, gdn2, sup2, sdn2), (gup3, gdn3, sup3, sdn3))):
        ups, downs = [], []
        for e, (rows, flip) in enumerate(halves(2 * UNIT)):
            own, *rest = room[5 * count : 5 * count + 5]
            ups.append(
                Reduce(
                    me, gup.at[1 - me.c, :, :, :, rows, :], gup.at[me.c, :, :, :, rows, :], own, rest,
                    sup.at[rows, :], flip, True,
                )
            )
            count += 1
            own, *rest = room[5 * count : 5 * count + 5]
            downs.append(
                Reduce(
                    me, gdn.at[e, :, 1 - me.c], gdn.at[e, :, me.c], own, rest,
                    sdn.at[pl.ds(e * UNIT, UNIT), :], flip, True,
                )
            )
            count += 1
        traffic.add(6 * q, *ups, gap=2)
        traffic.add(6 * q + 3, *downs, gap=2)
    outs = []
    for rows, flip in halves(2 * UNIT):
        own, *rest = room[5 * count : 5 * count + 5]
        theirs, mine = gout.at[:, 1 - me.c, :, :, rows, :], gout.at[:, me.c, :, :, rows, :]
        outs.append(Reduce(me, theirs, mine, own, rest, sout.at[rows, :], flip, True))
        count += 1
    traffic.add(11, *outs, gap=2)
    traffic.bind(send, recv, local)
    fire = functools.partial(traffic.fire, step, 4, 5)

    @pl.when(step == 0)
    def _():
        me.greet()
        traffic.at(0)
        flow(s0_ref, s0_buf, sem.at[0]).start()
        fill_bias(bias_ref, seg_ref, pad_ref, row_ref)
        dn_ref[...] = jnp.zeros_like(dn_ref)

    ones = jnp.ones((8, HD), BF)
    for head in range(4):
        fire(head)
        lanes = slice(head * HD, (head + 1) * HD)
        query, key, value = q_ref[:, lanes], k_ref[:, lanes], v_ref[:, lanes]
        grad = g_ref[:, lanes]
        both = grad.astype(F32) * c_ref[:, lanes].astype(F32)
        high = both.astype(BF)
        low = (both - high.astype(F32)).astype(BF)
        delta = (dot(ones, high, NT) + dot(ones, low, NT))[0:1, :]
        probs = jnp.exp(dot(key, query, NT) + bias_ref[...] - lse_ref[head : head + 1, :])
        d_scores = (probs * (dot(value, grad, NT) - delta)).astype(BF)
        dv_ref[:, lanes] = dot(probs.astype(BF), grad)
        dk_ref[:, lanes] = dot(d_scores, query)
        dq_ref[:, lanes] = dot(key.T, d_scores).T * HD**-0.5

    @pl.when(step == last)
    def _():
        flow(ds1_ref, bias_ref, sem.at[1]).start()

    fire(4)
    for part, (src, first, second) in enumerate(
        ((dq_ref, qa, qb), (dk_ref, ka, kb), (dv_ref, va, vb))
    ):
        if part < 2:
            made = jnp.concatenate(
                [
                    turn(src[:, half * 128 : (half + 1) * 128], cos_ref[...], -lo_ref[...], -hi_ref[...])
                    for half in range(2)
                ],
                axis=1,
            ).astype(BF)
        else:
            made = src[...].astype(BF)
        grad = dot(n_ref[...], made, TN).astype(BF)
        gw_ref[part, 0] = grad[:, :128]
        gw_ref[part, 1] = grad[:, 128:]
        dn_ref[...] += dot(made, jnp.concatenate([first[0], second[0]], axis=1), NT)

    @pl.when(step == last)
    def _():
        dg1_ref[...] = jnp.zeros_like(dg1_ref)
        flow(s0_ref, s0_buf, sem.at[0]).wait()
        flow(ds1_ref, bias_ref, sem.at[1]).wait()

        @pl.loop(0, length // UNIT)
        def _(t):
            rows = pl.ds(pl.multiple_of(t * UNIT, UNIT), UNIT)
            gain = token_gain(seg_ref[rows, :], g1_ref)
            term, d_gain = norm_back(dn_ref[rows, :], s0_buf[rows, :], gain)
            dlow_ref[rows, :] = (bias_ref[rows, :] + term).astype(BF)
            dg1_ref[...] += segment_sum(row_ref[:, rows], d_gain)

        traffic.drain()


def attend_back(
    normed, w_qkv, tables, seg_col, pad_col, seg_row, q, k, v, d_ctx, ctx, lse, gamma1, stream0, d_stream1, grads
):
    length, width = normed.shape
    groups = width // 256
    units = [unit_spec(width, part * (width // 128) + e) for part in range(3) for e in range(2)]
    column = pl.BlockSpec((length, 256), lambda j: (0, j))
    full = whole((length, width))
    part = whole((2 * UNIT, UNIT))
    pieces = 10
    return pl.pallas_call(
        attend_back_body,
        grid=(groups,),
        in_specs=[full]
        + units
        + [whole((length, 128))] * 3
        + [whole((length, 1))] * 2
        + [whole((1, length))]
        + [column] * 5
        + [pl.BlockSpec((8, length), lambda j: (j, 0)), whole((8, width))]
        + [ANY] * 7,
        out_specs=(
            pl.BlockSpec((3, 2, width, 128), lambda j: (0, j, 0, 0)),
            full,
            whole((8, width)),
        )
        + (part,) * 5,
        out_shape=(
            shaped((3, width // 128, width, 128), BF),
            shaped((length, width), BF),
            shaped((8, width), F32),
        )
        + (shaped((2 * UNIT, UNIT), F32),) * 5,
        scratch_shapes=[pltpu.VMEM((length, length), F32), pltpu.VMEM((length, width), F32)]
        + [pltpu.VMEM((length, 256), F32)] * 3
        + [pltpu.VMEM((length, width), F32), pltpu.SemaphoreType.DMA((2,))]
        + semaphores(pieces, Reduce.sems)
        + ([pltpu.VMEM((4, 2, 2, UNIT, UNIT), BF)] + Reduce.room(UNIT, UNIT)) * pieces,
        compiler_params=params(collective_id=3, has_side_effects=True),
        name="attend_back",
    )(
        normed, *([w_qkv] * 6), *tables, seg_col, pad_col, seg_row, q, k, v, d_ctx, ctx, lse,
        gamma1, stream0, d_stream1, *grads,
    )


def skip_back_body(
    x_ref, s_ref, d_ref, w_ref, ada_ref, dg_ref, gw_ref,
    dx_ref, ds_ref, time_ref, sskip, sqkv, stage, send, recv, local, *room,
):
    low = d_ref[...]
    width = x_ref.shape[1]
    per = ada_ref.shape[5] // 2
    me = Place()
    me.greet()
    traffic = Traffic()
    count = 0
    pairs = []
    for sub in range(3):
        made = []
        for rows, flip in halves(2 * UNIT):
            own, *rest = room[5 * count : 5 * count + 5]
            theirs, mine = gw_ref.at[:, 1 - me.c, sub, :, :, rows, :], gw_ref.at[:, me.c, sub, :, :, rows, :]
            out = sqkv.at[rows, pl.ds(sub * UNIT, UNIT)]
            made.append(Reduce(me, theirs, mine, own, rest, out, flip, True))
            count += 1
        pairs.append(made)
    tall = 512
    for i in range(2):
        made = []
        for e in range(2):
            rows = pl.ds((2 * i + e) * UNIT, UNIT)
            own, *rest = room[5 * count : 5 * count + 5]
            theirs, mine = stage.at[:, 1 - me.c, :, :, rows, :], stage.at[:, me.c, :, :, rows, :]
            made.append(Reduce(me, theirs, mine, own, rest, sskip.at[rows, :], e == 1, True))
            count += 1
        pairs.append(made)
    for i, made in enumerate(pairs):
        traffic.add(i if i < 3 else i + 1, *made)
    traffic.bind(send, recv, local)
    traffic.at(0)
    for i in range(4):
        lanes = slice(i * 2 * UNIT, (i + 1) * 2 * UNIT)
        part = d_ref[:, lanes]
        top = dot(x_ref[...], part, TN).astype(BF)
        end = dot(s_ref[...], part, TN).astype(BF)
        for c in range(2):
            cols = slice(c * UNIT, (c + 1) * UNIT)
            stage[i, c, 0] = top[:, cols].reshape(2, tall, UNIT)
            stage[i, c, 1] = end[:, cols].reshape(2, tall, UNIT)
        if i < 3:
            traffic.at(i + 1)
    traffic.at(4)
    for i in range(4):
        rows = slice((i % 2) * tall, (i % 2 + 1) * tall)
        tile = jnp.concatenate([w_ref[f // 2, f % 2, i // 2, i % 2] for f in range(NB)], axis=1)
        out = (dx_ref, ds_ref)[i // 2]
        out[:, rows] = dot(low, tile, NT)
        traffic.at(5 + i)
    total = jnp.zeros((8, width), F32)
    for f in range(NB):
        block = ada_ref[f // 2, f % 2].reshape(width, 2 * per)
        cols = slice(f * per, (f + 1) * per)
        total += dot(dg_ref[0, :, cols], block[:, :per], NT) + dot(dg_ref[1, :, cols], block[:, per:], NT)
    time_ref[...] = total
    traffic.drain()


def skip_back(inputs, skip_in, d_low, w_skip, ada, d_gammas, g_qkv):
    length, width = inputs.shape
    vmem = pl.BlockSpec(memory_space=pltpu.VMEM)
    pieces = 10
    return pl.pallas_call(
        skip_back_body,
        in_specs=[vmem] * 6 + [ANY],
        out_shape=(
            shaped((length, width), F32),
            shaped((length, width), F32),
            shaped((8, width), F32),
            shaped((4 * UNIT, UNIT), F32),
            shaped((2 * UNIT, 3 * UNIT), F32),
        ),
        scratch_shapes=[pltpu.VMEM(w_skip.shape, BF)]
        + semaphores(pieces, Reduce.sems)
        + ([pltpu.VMEM((4, 2, 2, UNIT, UNIT), BF)] + Reduce.room(UNIT, UNIT)) * pieces,
        compiler_params=params(collective_id=4, has_side_effects=True),
        name="skip_back",
    )(inputs, skip_in, d_low, w_skip, ada, d_gammas, g_qkv)


def rotary(positions):
    half = HD // 2
    lane = jnp.arange(128)
    frequency = 10000.0 ** (-2.0 * (lane % half).astype(F32) / HD)
    phase = positions.reshape(-1, 1).astype(F32) * frequency[None, :]
    cosine, sine = jnp.cos(phase), jnp.sin(phase)
    early = (lane % HD < half)[None, :]
    return cosine, jnp.where(early, -sine, 0.0), jnp.where(early, 0.0, sine)


def gathered(shard):
    blocks = lax.all_gather(shard, "fsdp", axis=0, tiled=False)
    blocks = lax.all_gather(blocks, "dp", axis=1, tiled=True)
    count, rows, per = blocks.shape
    if count == NB:
        return blocks
    flat = jnp.transpose(blocks, (1, 0, 2)).reshape(rows, count * per)
    return jnp.transpose(flat.reshape(rows, NB, count * per // NB), (1, 0, 2))


def scattered(blocks):
    count, rows, per = blocks.shape
    flat = jnp.transpose(blocks, (1, 0, 2)).reshape(rows, count * per)
    part = lax.psum_scatter(flat, "fsdp", scatter_dimension=1, tiled=True)
    return lax.psum_scatter(part, "dp", scatter_dimension=0, tiled=True).astype(F32)


def ada_grads(flat_time, d_gammas, tall, thin):
    every = lax.all_gather(flat_time, "fsdp", axis=0, tiled=True)
    every = lax.all_gather(every, "dp", axis=0, tiled=True)
    every = lax.dynamic_slice_in_dim(every, lax.axis_index("dp") * tall, tall, 1)
    gammas = lax.all_gather(d_gammas, "fsdp", axis=1, tiled=True)
    gammas = lax.all_gather(gammas, "dp", axis=1, tiled=True)
    gammas = lax.dynamic_slice_in_dim(gammas, lax.axis_index("fsdp") * thin, thin, 2)
    return [jnp.einsum("nd,ne->de", every, part, preferred_element_type=F32) for part in gammas]


def fused(
    inputs, skip_in, time_emb, seg_ids, positions, pad_mask,
    w_skip, w_ada1, w_qkv, w_out, w_ada2, w_up, w_down, cotangent,
):
    slots = time_emb.shape[1]
    length, width = inputs.shape
    seg_col, seg_row = seg_ids.reshape(-1, 1), seg_ids.reshape(1, -1)
    pad_col = pad_mask.reshape(-1, 1)
    tables = rotary(positions)
    flat_time = time_emb.reshape(slots, -1)
    time8 = jnp.pad(flat_time, ((0, 8 - slots), (0, 0)))
    w_ada = jnp.concatenate([w_ada1, w_ada2], axis=1)
    stream0, normed1, gamma1, gamma2, f_skip, f_ada, f_qkv = front(
        inputs, skip_in, time8, seg_col, w_skip, w_ada, w_qkv
    )
    f_qkv = f_qkv.reshape(NB, width, -1)
    q, k, v, ctx, lse, f_out, fup0, fdn0, fup1 = attend(
        normed1, f_qkv, tables, seg_col, pad_col, seg_row, w_out, w_up, w_down
    )
    output, g_out, d_stream1, d_ctx, d_gamma2, sup0, sdn0, sup1, sdn1, *rest = mlp(
        stream0, ctx, f_out, gamma2, seg_col, seg_row, cotangent, w_up, w_down, fup0, fdn0, fup1
    )
    g_qkv, d_low, d_gamma1, sup2, sdn2, sup3, sdn3, s_out = attend_back(
        normed1, f_qkv, tables, seg_col, pad_col, seg_row, q, k, v, d_ctx, ctx, lse, gamma1,
        stream0, d_stream1, (*rest[:4], g_out),
    )
    d_gammas = jnp.stack([d_gamma1, d_gamma2]).astype(BF)
    d_input, d_skip, d_time, s_skip, s_qkv = skip_back(
        inputs, skip_in, d_low, f_skip, f_ada, d_gammas, g_qkv.reshape(4, 2, 3, 2, 2, -1, UNIT)
    )
    g_ada = ada_grads(flat_time, d_gammas[:, :slots], *w_ada1.shape)
    s_up = jnp.concatenate([sup0, sup1, sup2, sup3], axis=1)
    s_down = jnp.stack([sdn0, sdn1, sdn2, sdn3]).reshape(4, 2, UNIT, UNIT)
    s_down = jnp.transpose(s_down, (1, 0, 2, 3)).reshape(w_down.shape)
    return (
        output, d_input, d_skip, d_time[:slots].reshape(time_emb.shape),
        s_skip, g_ada[0], s_qkv, s_out, g_ada[1], s_up, s_down,
    )


def plain(
    inputs, skip_in, time_emb, seg_ids, positions, pad_mask,
    w_skip, w_ada1, w_qkv, w_out, w_ada2, w_up, w_down, cotangent,
):
    slots = time_emb.shape[1]
    width = inputs.shape[1]
    seg_col, seg_row = seg_ids.reshape(-1, 1), seg_ids.reshape(1, -1)
    pad_col = pad_mask.reshape(-1, 1)
    tables = rotary(positions)
    flat_time = time_emb.reshape(slots, -1)
    time8 = jnp.pad(flat_time, ((0, 8 - slots), (0, 0)))
    f_skip, f_qkv, f_out, f_up, f_down, f_ada1, f_ada2 = [
        gathered(w) for w in (w_skip, w_qkv, w_out, w_up, w_down, w_ada1, w_ada2)
    ]
    ada = jnp.concatenate([f_ada1, f_ada2], axis=2)
    stream0, normed1, gamma1, gamma2 = plain_front(inputs, skip_in, f_skip, time8, ada, seg_col)
    q, k, v, ctx, lse = plain_attend(normed1, f_qkv, tables, seg_col, pad_col, seg_row)
    output, g_down, g_up, g_out, d_stream1, d_ctx, d_gamma2 = plain_mlp(
        stream0, ctx, f_out, gamma2, seg_col, seg_row, f_up, f_down, cotangent
    )
    g_qkv, d_low, d_gamma1 = plain_attend_back(
        normed1, f_qkv, tables, seg_col, pad_col, seg_row, q, k, v, d_ctx, ctx, lse,
        stream0, gamma1, d_stream1,
    )
    g_qkv = jnp.transpose(
        g_qkv.reshape(NB, 3, width, 128), (0, 2, 1, 3)
    ).reshape(NB, width, 3 * width // NB)
    g_skip, d_input, d_skip = plain_skip_back(inputs, skip_in, d_low, f_skip)
    d_gammas = jnp.stack([d_gamma1, d_gamma2]).astype(BF)[:, :slots]
    d_time = 0.0
    for d_gamma, part in zip(d_gammas, (f_ada1, f_ada2)):
        flat = jnp.transpose(part, (1, 0, 2)).reshape(width, width)
        d_time = d_time + jnp.einsum("ne,de->nd", d_gamma, flat, preferred_element_type=F32)
    g_ada = ada_grads(flat_time, d_gammas, *w_ada1.shape)
    return (
        output, d_input, d_skip, d_time.reshape(time_emb.shape),
        scattered(g_skip), g_ada[0], scattered(g_qkv), scattered(g_out), g_ada[1],
        scattered(g_up), scattered(g_down),
    )


def solution(mesh):
    rows = P(("dp", "fsdp"), None)
    cube = P(("dp", "fsdp"), None, None)
    tile = P("dp", "fsdp")
    fits = mesh.shape["dp"] == 4 and mesh.shape["fsdp"] == NB
    return jax.shard_map(
        fused if fits else plain,
        mesh=mesh,
        in_specs=(rows, rows, cube) + (rows,) * 3 + (tile,) * 7 + (rows,),
        out_specs=(rows, rows, rows, cube) + (tile,) * 7,
        check_vma=False,
    )
```

```python
import functools

import jax
import jax.numpy as jnp
from jax import lax
from jax.experimental import pallas as pl
from jax.experimental.pallas import tpu as pltpu
from jax.sharding import PartitionSpec as P

HD = 64
NB = 8
EPS = 1e-06
MASKED = -1e30
BF = jnp.bfloat16
F32 = jnp.float32
NN = (((1,), (0,)), ((), ()))
NT = (((1,), (1,)), ((), ()))
TN = (((0,), (0,)), ((), ()))
ROOT = 0.7978845608028654
CUBE = 0.044715


def dot(left, right, form=NN):
    return lax.dot_general(left, right, form, preferred_element_type=F32)


def params(**extra):
    return pltpu.CompilerParams(vmem_limit_bytes=60 << 20, **extra)


def whole(shape):
    return pl.BlockSpec(shape, lambda *_: (0,) * len(shape), pipeline_mode=pl.Buffered(1))


ANY = pl.BlockSpec(memory_space=pl.ANY)
UNIT = 128


def shaped(shape, kind):
    return jax.ShapeDtypeStruct(shape, kind)


def columns(ref, first, count, rows=slice(None)):
    return jnp.concatenate([ref[first + i, rows, :] for i in range(count)], axis=1)


def token_gain(seg, gamma):
    gain = gamma[0:1, :]
    for slot in range(1, 4):
        gain = jnp.where(seg == slot, gamma[slot : slot + 1, :], gain)
    return gain


def segment_sum(seg_row, values):
    slots = lax.broadcasted_iota(jnp.int32, (8, seg_row.shape[1]), 0)
    picked = (slots == seg_row).astype(BF)
    high = values.astype(BF)
    low = (values - high.astype(F32)).astype(BF)
    return dot(picked, high) + dot(picked, low)


def norm_back(grad, stream, gain):
    inverse = lax.rsqrt(jnp.mean(stream * stream, axis=-1, keepdims=True) + EPS)
    unit = stream * inverse
    scaled = grad * (1.0 + gain)
    d_stream = inverse * (scaled - unit * jnp.mean(scaled * unit, axis=-1, keepdims=True))
    return d_stream, grad * unit


def norm(stream, gain):
    inverse = lax.rsqrt(jnp.mean(stream * stream, axis=-1, keepdims=True) + EPS)
    return (stream * inverse * (1.0 + gain)).astype(BF)


def fill_bias(bias_ref, seg_ref, pad_ref, row_ref):
    length = seg_ref.shape[0]

    @pl.loop(0, length // UNIT)
    def _(t):
        rows = pl.ds(pl.multiple_of(t * UNIT, UNIT), UNIT)
        keys = lax.broadcasted_iota(jnp.int32, (UNIT, length), 0) + t * UNIT
        queries = lax.broadcasted_iota(jnp.int32, (UNIT, length), 1)
        allowed = (seg_ref[rows, :] == row_ref[0:1, :]) & (
            (pad_ref[rows, :] > 0) | (keys == queries)
        )
        bias_ref[rows, :] = jnp.where(allowed, 0.0, MASKED)


def turn(unit, cosine, before, after):
    return (
        unit * cosine
        + pltpu.roll(unit, 96, 1) * before
        + pltpu.roll(unit, 32, 1) * after
    )


def unit_spec(rows, base):
    def index(j):
        unit = base + 2 * j
        return (unit // 3, 0, unit % 3)

    return pl.BlockSpec((1, rows, 128), index)


def plain_front_body(x_ref, s_ref, w_ref, time_ref, ada_ref, seg_ref, stream_ref, normed_ref, g1_ref, g2_ref):
    length, width = x_ref.shape
    per = ada_ref.shape[2] // 2
    for f in range(NB):
        both = dot(time_ref[...], ada_ref[f])
        g1_ref[:, f * per : (f + 1) * per] = both[:, :per]
        g2_ref[:, f * per : (f + 1) * per] = both[:, per:]
    for i in range(NB // 2):
        tile = columns(w_ref, 2 * i, 2)
        part = dot(x_ref[...], tile[:width]) + dot(s_ref[...], tile[width:])
        stream_ref[:, i * part.shape[1] : (i + 1) * part.shape[1]] = part

    @pl.loop(0, length // 128)
    def _(t):
        rows = pl.ds(pl.multiple_of(t * 128, 128), 128)
        gain = token_gain(seg_ref[rows, :], g1_ref)
        normed_ref[rows, :] = norm(stream_ref[rows, :], gain)


def plain_front(inputs, skip_in, w_skip, time8, ada, seg_col):
    length, width = inputs.shape
    return pl.pallas_call(
        plain_front_body,
        out_shape=(
            shaped((length, width), F32),
            shaped((length, width), BF),
            shaped((8, width), F32),
            shaped((8, width), F32),
        ),
        compiler_params=params(),
        name="front",
    )(inputs, skip_in, w_skip, time8, ada, seg_col)


def plain_attend_body(
    n_ref, qa, qb, ka, kb, va, vb, cos_ref, lo_ref, hi_ref, seg_ref, pad_ref, row_ref,
    q_ref, k_ref, v_ref, c_ref, lse_ref, bias_ref,
):
    @pl.when(pl.program_id(0) == 0)
    def _():
        fill_bias(bias_ref, seg_ref, pad_ref, row_ref)

    normed = n_ref[...]
    for out, first, second, scale in ((q_ref, qa, qb, HD**-0.5), (k_ref, ka, kb, 1.0)):
        made = dot(normed, jnp.concatenate([first[0], second[0]], axis=1))
        for half in range(2):
            unit = made[:, half * 128 : (half + 1) * 128]
            turned = turn(unit, cos_ref[...], lo_ref[...], hi_ref[...])
            out[:, half * 128 : (half + 1) * 128] = (turned.astype(BF) * scale).astype(BF)
    v_ref[...] = dot(normed, jnp.concatenate([va[0], vb[0]], axis=1)).astype(BF)
    for head in range(4):
        lanes = slice(head * HD, (head + 1) * HD)
        scores = dot(k_ref[:, lanes], q_ref[:, lanes], NT) + bias_ref[...]
        largest = jnp.max(scores, axis=0, keepdims=True)
        exponent = jnp.exp(scores - largest)
        total = jnp.sum(exponent, axis=0, keepdims=True)
        mixed = dot(v_ref[:, lanes].T, exponent.astype(BF)) * (1.0 / total)
        c_ref[:, lanes] = mixed.T.astype(BF)
        lse_ref[head : head + 1, :] = largest + jnp.log(total)


def plain_attend(normed, w_qkv, tables, seg_col, pad_col, seg_row):
    length, width = normed.shape
    groups = width // 256
    units = [unit_spec(width, part * (width // 128) + e) for part in range(3) for e in range(2)]
    column = pl.BlockSpec((length, 256), lambda j: (0, j))
    wide = shaped((length, width), BF)
    return pl.pallas_call(
        plain_attend_body,
        grid=(groups,),
        in_specs=[whole((length, width))]
        + units
        + [whole((length, 128))] * 3
        + [whole((length, 1))] * 2
        + [whole((1, length))],
        out_specs=(column,) * 4 + (pl.BlockSpec((8, length), lambda j: (j, 0)),),
        out_shape=(wide,) * 4 + (shaped((8 * groups, length), F32),),
        scratch_shapes=[pltpu.VMEM((length, length), F32)],
        compiler_params=params(),
        name="attend",
    )(normed, *([w_qkv] * 6), *tables, seg_col, pad_col, seg_row)


def plain_mlp_body(
    stream0_ref, ctx_ref, wout_ref, g2_ref, seg_ref, row_ref, up_ref, down_ref, cot_ref,
    out_ref, gdown_ref, gup_ref, gout_ref, ds1_ref, dctx_ref, dg2_ref,
    s1_ref, n2_ref, acc_ref, dn_ref,
):
    step = pl.program_id(0)
    length, width = ctx_ref.shape
    tiles = length // 128

    @pl.when(step == 0)
    def _():
        @pl.loop(0, NB // 2)
        def _(i):
            lanes = pl.ds(pl.multiple_of(i * 256, 256), 256)
            s1_ref[:, lanes] = stream0_ref[:, lanes] + dot(ctx_ref[...], columns(wout_ref, 2 * i, 2))

        @pl.loop(0, tiles)
        def _(t):
            rows = pl.ds(pl.multiple_of(t * 128, 128), 128)
            n2_ref[rows, :] = norm(s1_ref[rows, :], token_gain(seg_ref[rows, :], g2_ref))

        acc_ref[...] = jnp.zeros_like(acc_ref)
        dn_ref[...] = jnp.zeros_like(dn_ref)

    cot = cot_ref[...]
    up = up_ref[0]
    down = columns(down_ref, 0, NB)
    hidden = dot(n2_ref[...], up)
    square = hidden * hidden
    tanh = jnp.tanh(ROOT * hidden * (1.0 + CUBE * square))
    active = (0.5 * hidden * (1.0 + tanh)).astype(BF)
    slope = 0.5 * (1.0 + tanh) + 0.5 * hidden * (1.0 - tanh * tanh) * (
        ROOT * (1.0 + 3.0 * CUBE * square)
    )
    d_pre = (dot(cot, down, NT) * slope).astype(BF)
    acc_ref[...] += dot(active, down)
    dn_ref[...] += dot(d_pre, up, NT)
    grad = dot(active, cot, TN).astype(BF)
    for f in range(NB):
        gdown_ref[f] = grad[:, f * gdown_ref.shape[2] : (f + 1) * gdown_ref.shape[2]]
    gup_ref[0] = dot(n2_ref[...], d_pre, TN).astype(BF)

    @pl.when(step == pl.num_programs(0) - 1)
    def _():
        dg2_ref[...] = jnp.zeros_like(dg2_ref)

        @pl.loop(0, tiles)
        def _(t):
            rows = pl.ds(pl.multiple_of(t * 128, 128), 128)
            stream = s1_ref[rows, :]
            out_ref[rows, :] = (stream + acc_ref[rows, :]).astype(BF)
            gain = token_gain(seg_ref[rows, :], g2_ref)
            term, d_gain = norm_back(dn_ref[rows, :], stream, gain)
            d_stream = cot_ref[rows, :].astype(F32) + term
            ds1_ref[rows, :] = d_stream
            n2_ref[rows, :] = d_stream.astype(BF)
            dg2_ref[...] += segment_sum(row_ref[:, rows], d_gain)

        @pl.loop(0, NB // 2)
        def _(i):
            lanes = pl.ds(pl.multiple_of(i * 256, 256), 256)
            part = dot(ctx_ref[...], n2_ref[:, lanes], TN).astype(BF)
            gout_ref[2 * i] = part[:, :128]
            gout_ref[2 * i + 1] = part[:, 128:]

        acc_ref[...] = jnp.zeros_like(acc_ref)

        @pl.loop(0, NB // 2)
        def _(i):
            lanes = pl.ds(pl.multiple_of(i * 256, 256), 256)
            acc_ref[...] += dot(n2_ref[:, lanes], columns(wout_ref, 2 * i, 2), NT)

        dctx_ref[...] = acc_ref[...].astype(BF)


def plain_mlp(stream0, ctx, w_out, gamma2, seg_col, seg_row, w_up, w_down, cotangent):
    length, width = ctx.shape
    hidden = w_down.shape[1]
    piece = hidden // NB
    per = width // NB
    full = whole((length, width))
    return pl.pallas_call(
        plain_mlp_body,
        grid=(NB,),
        in_specs=[
            full,
            full,
            whole((NB, width, per)),
            whole((8, width)),
            whole((length, 1)),
            whole((1, length)),
            pl.BlockSpec((1, width, piece), lambda j: (j, 0, 0)),
            pl.BlockSpec((NB, piece, per), lambda j: (0, j, 0)),
            full,
        ],
        out_specs=(
            full,
            pl.BlockSpec((NB, piece, per), lambda j: (0, j, 0)),
            pl.BlockSpec((1, width, piece), lambda j: (j, 0, 0)),
            whole((NB, width, per)),
            full,
            full,
            whole((8, width)),
        ),
        out_shape=(
            shaped((length, width), BF),
            shaped((NB, hidden, per), BF),
            shaped((NB, width, piece), BF),
            shaped((NB, width, per), BF),
            shaped((length, width), F32),
            shaped((length, width), BF),
            shaped((8, width), F32),
        ),
        scratch_shapes=[
            pltpu.VMEM((length, width), F32),
            pltpu.VMEM((length, width), BF),
            pltpu.VMEM((length, width), F32),
            pltpu.VMEM((length, width), F32),
        ],
        compiler_params=params(),
        name="mlp",
    )(stream0, ctx, w_out, gamma2, seg_col, seg_row, w_up, w_down, cotangent)


def plain_attend_back_body(
    n_ref, qa, qb, ka, kb, va, vb, cos_ref, lo_ref, hi_ref, seg_ref, pad_ref, row_ref,
    q_ref, k_ref, v_ref, g_ref, c_ref, lse_ref, s0_ref, g1_ref, ds1_ref,
    gw_ref, dlow_ref, dg1_ref, bias_ref, dn_ref, dq_ref, dk_ref, dv_ref,
):
    step = pl.program_id(0)
    length, width = n_ref.shape

    @pl.when(step == 0)
    def _():
        fill_bias(bias_ref, seg_ref, pad_ref, row_ref)
        dn_ref[...] = jnp.zeros_like(dn_ref)

    ones = jnp.ones((8, HD), BF)
    for head in range(4):
        lanes = slice(head * HD, (head + 1) * HD)
        query, key, value = q_ref[:, lanes], k_ref[:, lanes], v_ref[:, lanes]
        grad = g_ref[:, lanes]
        both = grad.astype(F32) * c_ref[:, lanes].astype(F32)
        high = both.astype(BF)
        low = (both - high.astype(F32)).astype(BF)
        delta = (dot(ones, high, NT) + dot(ones, low, NT))[0:1, :]
        probs = jnp.exp(dot(key, query, NT) + bias_ref[...] - lse_ref[head : head + 1, :])
        d_scores = (probs * (dot(value, grad, NT) - delta)).astype(BF)
        dv_ref[:, lanes] = dot(probs.astype(BF), grad)
        dk_ref[:, lanes] = dot(d_scores, query)
        dq_ref[:, lanes] = dot(key.T, d_scores).T * HD**-0.5
    for part, (src, first, second) in enumerate(
        ((dq_ref, qa, qb), (dk_ref, ka, kb), (dv_ref, va, vb))
    ):
        if part < 2:
            made = jnp.concatenate(
                [
                    turn(src[:, half * 128 : (half + 1) * 128], cos_ref[...], -lo_ref[...], -hi_ref[...])
                    for half in range(2)
                ],
                axis=1,
            ).astype(BF)
        else:
            made = src[...].astype(BF)
        grad = dot(n_ref[...], made, TN).astype(BF)
        gw_ref[part, 0] = grad[:, :128]
        gw_ref[part, 1] = grad[:, 128:]
        dn_ref[...] += dot(made, jnp.concatenate([first[0], second[0]], axis=1), NT)

    @pl.when(step == pl.num_programs(0) - 1)
    def _():
        dg1_ref[...] = jnp.zeros_like(dg1_ref)

        @pl.loop(0, length // 128)
        def _(t):
            rows = pl.ds(pl.multiple_of(t * 128, 128), 128)
            gain = token_gain(seg_ref[rows, :], g1_ref)
            term, d_gain = norm_back(dn_ref[rows, :], s0_ref[rows, :], gain)
            dlow_ref[rows, :] = (ds1_ref[rows, :] + term).astype(BF)
            dg1_ref[...] += segment_sum(row_ref[:, rows], d_gain)


def plain_attend_back(
    normed, w_qkv, tables, seg_col, pad_col, seg_row, q, k, v, d_ctx, ctx, lse, stream0, gamma1, d_stream1
):
    length, width = normed.shape
    groups = width // 256
    units = [unit_spec(width, part * (width // 128) + e) for part in range(3) for e in range(2)]
    column = pl.BlockSpec((length, 256), lambda j: (0, j))
    full = whole((length, width))
    return pl.pallas_call(
        plain_attend_back_body,
        grid=(groups,),
        in_specs=[full]
        + units
        + [whole((length, 128))] * 3
        + [whole((length, 1))] * 2
        + [whole((1, length))]
        + [column] * 5
        + [pl.BlockSpec((8, length), lambda j: (j, 0)), full, whole((8, width)), full],
        out_specs=(
            pl.BlockSpec((3, 2, width, 128), lambda j: (0, j, 0, 0)),
            full,
            whole((8, width)),
        ),
        out_shape=(
            shaped((3, width // 128, width, 128), BF),
            shaped((length, width), BF),
            shaped((8, width), F32),
        ),
        scratch_shapes=[pltpu.VMEM((length, length), F32), pltpu.VMEM((length, width), F32)]
        + [pltpu.VMEM((length, 256), F32)] * 3,
        compiler_params=params(),
        name="attend_back",
    )(
        normed, *([w_qkv] * 6), *tables, seg_col, pad_col, seg_row, q, k, v, d_ctx, ctx, lse,
        stream0, gamma1, d_stream1,
    )


def plain_skip_back_body(x_ref, s_ref, d_ref, w_ref, gw_ref, dx_ref, ds_ref):
    low = d_ref[...]
    per = 256
    width = x_ref.shape[1]

    @pl.loop(0, width // per)
    def _(i):
        lanes = pl.ds(pl.multiple_of(i * per, per), per)
        part = d_ref[:, lanes]
        top = dot(x_ref[...], part, TN).astype(BF)
        end = dot(s_ref[...], part, TN).astype(BF)
        for e in range(2):
            gw_ref[2 * i + e, :width, :] = top[:, e * 128 : (e + 1) * 128]
            gw_ref[2 * i + e, width:, :] = end[:, e * 128 : (e + 1) * 128]

    tall = 256

    @pl.loop(0, width // tall)
    def _(i):
        rows = pl.ds(pl.multiple_of(i * tall, tall), tall)
        rest = pl.ds(pl.multiple_of(width + i * tall, tall), tall)
        dx_ref[:, rows] = dot(low, columns(w_ref, 0, NB, rows), NT)
        ds_ref[:, rows] = dot(low, columns(w_ref, 0, NB, rest), NT)


def plain_skip_back(inputs, skip_in, d_low, w_skip):
    length, width = inputs.shape
    return pl.pallas_call(
        plain_skip_back_body,
        out_shape=(
            shaped(w_skip.shape, BF),
            shaped((length, width), F32),
            shaped((length, width), F32),
        ),
        compiler_params=params(),
        name="skip_back",
    )(inputs, skip_in, d_low, w_skip)


class Place:
    def __init__(self):
        dp, fs = lax.axis_index("dp"), lax.axis_index("fsdp")
        self.y, self.x, self.z, self.c = dp // 2, dp % 2, fs // 2, fs % 2
        self.dp, self.fs = dp, fs

    def across_x(self):
        return (self.y * 2 + 1 - self.x, self.fs)

    def across_y(self):
        return ((1 - self.y) * 2 + self.x, self.fs)

    def sibling(self):
        return (self.dp, self.z * 2 + 1 - self.c)

    def along_z(self, hop):
        return (self.dp, ((self.z + hop) % 4) * 2 + self.c)

    def on_dp(self, index):
        return (index, self.fs)

    def on_fsdp(self, index):
        return (self.dp, index)

    def greet(self, wide=False):
        barrier = pltpu.get_barrier_semaphore()
        if wide:
            peers = [self.on_dp((self.dp + hop) % 4) for hop in range(1, 4)]
            peers += [self.on_fsdp((self.fs + hop) % NB) for hop in range(1, NB)]
        else:
            peers = [self.across_x(), self.across_y(), self.sibling()]
            peers += [self.along_z(hop) for hop in (1, 2, 3)]
        for peer in peers:
            pl.semaphore_signal(barrier, inc=1, device_id=peer, device_id_type=pl.DeviceIdType.MESH)
        pl.semaphore_wait(barrier, len(peers))


def remote(src, dst, send, recv, peer):
    return pltpu.make_async_remote_copy(
        src_ref=src, dst_ref=dst, send_sem=send, recv_sem=recv,
        device_id=peer, device_id_type=pl.DeviceIdType.MESH,
    )


class Lazy:
    def __init__(self, plan, send, recv):
        self.plan, self.send, self.recv = plan, send, recv

    def __len__(self):
        return len(self.plan)

    def __getitem__(self, i):
        if isinstance(i, slice):
            return [self[k] for k in range(*i.indices(len(self)))]
        if i >= len(self.plan):
            raise IndexError
        src, dst, peer = self.plan[i]
        return remote(src, dst, self.send.at[i], self.recv.at[i], peer)


def flow(*copy):
    return pltpu.make_async_copy(*copy)


class Gather:
    sems = 8

    def __init__(self, place, source, full, rows, flip):
        self.me, self.source, self.full, self.rows, self.flip = place, source, full, rows, flip

    def bind(self, send, recv, local):
        self.send, self.recv, self.local = send, recv, local

    def copies(self):
        me, full, rows = self.me, self.full, self.rows
        spot = full.at[me.z, me.c, me.y, me.x, rows, :]
        line = full.at[:, me.c, me.y, me.x, rows, :]
        if self.flip:
            pair = full.at[:, me.c, :, me.x, rows, :]
            near, far = me.across_y(), me.across_x()
            got = full.at[:, me.c, 1 - me.y, me.x, rows, :]
            late = full.at[:, me.c, :, 1 - me.x, rows, :]
        else:
            pair = full.at[:, me.c, me.y, :, rows, :]
            near, far = me.across_x(), me.across_y()
            got = full.at[:, me.c, me.y, 1 - me.x, rows, :]
            late = full.at[:, me.c, 1 - me.y, :, rows, :]
        sib = me.sibling()
        plan = [(self.source, spot, me.along_z(hop)) for hop in (1, 2, 3)]
        plan += [(line, line, near), (pair, pair, far), (line, line, sib), (got, got, sib), (late, late, sib)]
        return Lazy(plan, self.send, self.recv), (self.source, spot, self.local)

    def stage(self, number):
        made, keep = self.copies()
        if number == 0:
            flow(*keep).start()
            for copy in made[:3]:
                copy.start()
        elif number == 1:
            flow(*keep).wait()
            for copy in made[:3]:
                copy.wait_recv()
            made[3].start()
            made[5].start()
        elif number == 2:
            made[3].wait_recv()
            made[4].start()
            made[6].start()
        elif number == 3:
            made[4].wait_recv()
            made[7].start()
        else:
            for copy in made[5:]:
                copy.wait_recv()
            for copy in made[:]:
                copy.wait_send()


class Reduce:
    sems = 6

    def __init__(self, place, theirs, mine, own, room, out, flip, load):
        self.me, self.theirs, self.mine, self.own = place, theirs, mine, own
        self.other, self.half, self.quarter, self.parts = room
        self.out, self.flip, self.load = out, flip, load

    @staticmethod
    def room(count, per):
        return [
            pltpu.VMEM((4, 2, 2, count, per), BF),
            pltpu.VMEM((4, 2, count, per), BF),
            pltpu.VMEM((4, count, per), BF),
            pltpu.VMEM((3, count, per), BF),
        ]

    def bind(self, send, recv, local):
        self.send, self.recv, self.local = send, recv, local

    def copies(self):
        me = self.me
        if self.flip:
            give, near = self.own.at[:, :, 1 - me.x], me.across_x()
            give2, far = self.half.at[:, 1 - me.y], me.across_y()
        else:
            give, near = self.own.at[:, 1 - me.y], me.across_y()
            give2, far = self.half.at[:, 1 - me.x], me.across_x()
        plan = [(self.theirs, self.other, me.sibling()), (give, self.half, near), (give2, self.quarter, far)]
        plan += [
            (self.quarter.at[(me.z + hop) % 4], self.parts.at[hop - 1], me.along_z(hop)) for hop in (1, 2, 3)
        ]
        return Lazy(plan, self.send, self.recv), (self.mine, self.own, self.local)

    def stage(self, number):
        me = self.me
        made, load = self.copies()
        if number == 0:
            made[0].start()
            if self.load:
                flow(*load).start()
        elif number == 1:
            if self.load:
                flow(*load).wait()
            made[0].wait_recv()

            @pl.loop(0, 4)
            def _(z):
                self.own[z] = self.own[z] + self.other[z]

            made[1].start()
        elif number == 2:
            made[1].wait_recv()

            @pl.loop(0, 4)
            def _(z):
                kept = self.own[z, :, me.x] if self.flip else self.own[z, me.y]
                self.half[z] = self.half[z] + kept

            made[2].start()
        elif number == 3:
            made[0].wait_send()
            made[1].wait_send()
            made[2].wait_recv()
            kept = me.y if self.flip else me.x

            @pl.loop(0, 4)
            def _(z):
                self.quarter[z] = self.quarter[z] + self.half[z, kept]

            for copy in made[3:]:
                copy.start()
        else:
            for copy in made[3:]:
                copy.wait_recv()
            total = self.quarter[me.z].astype(F32)
            for i in range(3):
                total = total + self.parts[i].astype(F32)
            self.out[...] = total
            for copy in made[2:]:
                copy.wait_send()


class Swap:
    def __init__(self, place, axis, what, into, send, recv):
        count = 4 if axis == "dp" else NB
        at = place.dp if axis == "dp" else place.fs
        find = place.on_dp if axis == "dp" else place.on_fsdp
        self.at, self.what, self.into = at, what, into
        self.plan = []
        for hop in range(1, count):
            peer = (at + hop) % count
            self.plan.append((what(peer), into(at), send.at[hop - 1], recv.at[hop - 1], find(peer)))

    def start(self):
        for copy in self.plan:
            remote(*copy).start()

    def wait(self):
        for copy in self.plan:
            remote(*copy).wait()


class Traffic:
    def __init__(self):
        self.todo, self.pieces = {}, []

    def add(self, first, *pieces, gap=2):
        self.pieces += pieces
        hooks = first if isinstance(first, tuple) else [first + stage * gap for stage in range(5)]
        for piece in pieces:
            for stage, hook in enumerate(hooks):
                self.todo.setdefault(hook, []).append((stage, piece))

    def bind(self, send, recv, local):
        for i, piece in enumerate(self.pieces):
            piece.bind(send.at[i], recv.at[i], local.at[i])

    def at(self, hook):
        for stage, piece in sorted(self.todo.pop(hook, []), key=lambda item: -item[0]):
            piece.stage(stage)

    def fire(self, step, steps, per, hook):
        for s in range(steps):
            if s * per + hook in self.todo:
                pl.when(step == s)(functools.partial(self.at, s * per + hook))

    def drain(self):
        for hook in sorted(self.todo):
            self.at(hook)


def semaphores(count, kind):
    return [pltpu.SemaphoreType.DMA((count, kind))] * 2 + [pltpu.SemaphoreType.DMA((count,))]


def full_of(rows, per):
    return shaped((4, 2, 2, 2, rows, per), BF)


def halves(rows):
    return [(pl.ds(e * (rows // 2), rows // 2), e == 1) for e in range(2)]


def up_pair(me, shard, full, q):
    lanes = pl.ds(q * UNIT, UNIT)
    return [Gather(me, shard.at[rows, lanes], full, rows, flip) for rows, flip in halves(shard.shape[0])]


def down_pair(me, shard, full, q):
    tall = shard.shape[0] // 2
    step = tall // 4
    return [
        Gather(me, shard.at[pl.ds(e * tall + q * step, step), :], full, pl.ds(e * step, step), e == 1)
        for e in range(2)
    ]


def row_pairs(me, shard, full, count):
    tall = shard.shape[0] // count
    made = [
        Gather(me, shard.at[pl.ds(i * tall, tall), :], full, pl.ds(i * tall, tall), i % 2 == 1)
        for i in range(count)
    ]
    return [made[i : i + 2] for i in range(0, count, 2)]


def front_body(
    x_ref, s_ref, time_ref, seg_ref, ada_ref, skip_ref, qkv_ref,
    stream_ref, normed_ref, g1_ref, g2_ref, slots, fskip_ref, fqkv_ref,
    w_ref, part, got, summed, gam, w_sem, sends, recvs, send, recv, local,
):
    length, width = x_ref.shape
    per = ada_ref.shape[1] // 2
    me = Place()
    me.greet(True)
    traffic = Traffic()
    plan = row_pairs(me, skip_ref, fskip_ref, 8)
    need = len(plan) + 8
    plan += row_pairs(me, qkv_ref, fqkv_ref, 8)
    for i, pair in enumerate(plan):
        traffic.add(i, *pair)
    traffic.bind(send, recv, local)
    lay = functools.partial(pl.ds, 0)
    swaps = [
        Swap(me, "dp", lambda p: time_ref.at[p], lambda m: slots.at[m, me.fs], sends.at[0], recvs.at[0]),
        Swap(me, "fsdp", lambda p: slots.at[:, me.fs], lambda m: slots.at[:, m], sends.at[1], recvs.at[1]),
        Swap(me, "dp", lambda p: part.at[p, :, lay(8), :], lambda m: got.at[m], sends.at[2], recvs.at[2]),
        Swap(me, "fsdp", lambda p: summed.at[p], lambda m: gam.at[m], sends.at[3], recvs.at[3]),
    ]
    slots[me.dp, me.fs] = time_ref[me.dp]
    swaps[0].start()
    traffic.at(0)
    swaps[0].wait()
    swaps[1].start()
    traffic.at(1)
    swaps[1].wait()
    made = dot(slots[...].reshape(4 * NB * 16, -1), ada_ref[...])
    part[...] = made.reshape(part.shape)
    got[me.dp] = part[me.dp, :, :8, :]
    swaps[2].start()
    traffic.at(2)
    swaps[2].wait()
    summed[...] = got[0] + got[1] + got[2] + got[3]
    gam[me.fs] = summed[me.fs]
    swaps[3].start()
    for hook in range(3, need):
        traffic.at(hook)
    load = flow(fskip_ref, w_ref, w_sem)
    load.start()
    swaps[3].wait()
    for f in range(NB):
        g1_ref[:, f * per : (f + 1) * per] = gam[f, :, :per]
        g2_ref[:, f * per : (f + 1) * per] = gam[f, :, per:]
    load.wait()

    def stream(i):
        tile = jnp.concatenate([w_ref[i, c].reshape(2 * width, UNIT) for c in range(2)], axis=1)
        lanes = pl.ds(pl.multiple_of(i * 2 * UNIT, 2 * UNIT), 2 * UNIT)
        stream_ref[:, lanes] = dot(x_ref[...], tile[:width]) + dot(s_ref[...], tile[width:])

    def normalise(t):
        rows = pl.ds(pl.multiple_of(t * UNIT, UNIT), UNIT)
        gain = token_gain(seg_ref[rows, :], g1_ref)
        normed_ref[rows, :] = norm(stream_ref[rows, :], gain)

    pl.loop(0, 2)(stream)
    traffic.at(need)
    pl.loop(2, 4)(stream)
    traffic.at(need + 1)
    half = length // UNIT // 2
    pl.loop(0, half)(normalise)
    traffic.at(need + 2)
    pl.loop(half, 2 * half)(normalise)
    traffic.drain()


def front(inputs, skip_in, time_cut, seg_col, w_ada, w_skip, w_qkv):
    length, width = inputs.shape
    fulls = [full_of(*w.shape) for w in (w_skip, w_qkv)]
    vmem = pl.BlockSpec(memory_space=pltpu.VMEM)
    per = w_ada.shape[1]
    return pl.pallas_call(
        front_body,
        in_specs=[vmem] * 5 + [ANY] * 2,
        out_specs=(vmem,) * 5 + (ANY,) * 2,
        out_shape=(
            shaped((length, width), F32),
            shaped((length, width), BF),
            shaped((8, width), F32),
            shaped((8, width), F32),
            shaped((4, NB, 16, w_ada.shape[0]), BF),
            *fulls,
        ),
        scratch_shapes=[
            pltpu.VMEM(fulls[0].shape, BF),
            pltpu.VMEM((4, NB, 16, per), F32),
            pltpu.VMEM((4, NB, 8, per), F32),
            pltpu.VMEM((NB, 8, per), F32),
            pltpu.VMEM((NB, 8, per), F32),
            pltpu.SemaphoreType.DMA,
            pltpu.SemaphoreType.DMA((4, NB - 1)),
            pltpu.SemaphoreType.DMA((4, NB - 1)),
        ]
        + semaphores(16, Gather.sems),
        compiler_params=params(collective_id=0, has_side_effects=True),
        name="front",
    )(inputs, skip_in, time_cut, seg_col, w_ada, w_skip, w_qkv)


def attend_body(
    n_ref, qa, qb, ka, kb, va, vb, cos_ref, lo_ref, hi_ref, seg_ref, pad_ref, row_ref, out_ref, up_ref, down_ref,
    q_ref, k_ref, v_ref, c_ref, lse_ref, fout_ref, fup0_ref, fdn0_ref, fup1_ref,
    bias_ref, send, recv, local,
):
    step = pl.program_id(0)
    last = pl.num_programs(0) - 1
    me = Place()
    traffic = Traffic()
    pairs = row_pairs(me, out_ref, fout_ref, 2) + [
        up_pair(me, up_ref, fup0_ref, 0),
        down_pair(me, down_ref, fdn0_ref, 0),
        up_pair(me, up_ref, fup1_ref, 1),
    ]
    for i, pair in enumerate(pairs):
        traffic.add(2 * i, *pair, gap=3)
    traffic.bind(send, recv, local)
    fire = functools.partial(traffic.fire, step, 4, 4)

    @pl.when(step == 0)
    def _():
        me.greet()
        traffic.at(0)
        fill_bias(bias_ref, seg_ref, pad_ref, row_ref)

    normed = n_ref[...]
    for out, first, second, scale in ((q_ref, qa, qb, HD**-0.5), (k_ref, ka, kb, 1.0)):
        made = dot(normed, jnp.concatenate([first[0], second[0]], axis=1))
        for half in range(2):
            unit = made[:, half * 128 : (half + 1) * 128]
            turned = turn(unit, cos_ref[...], lo_ref[...], hi_ref[...])
            out[:, half * 128 : (half + 1) * 128] = (turned.astype(BF) * scale).astype(BF)
    v_ref[...] = dot(normed, jnp.concatenate([va[0], vb[0]], axis=1)).astype(BF)
    for head in range(4):
        fire(head)
        lanes = slice(head * HD, (head + 1) * HD)
        scores = dot(k_ref[:, lanes], q_ref[:, lanes], NT) + bias_ref[...]
        largest = jnp.max(scores, axis=0, keepdims=True)
        exponent = jnp.exp(scores - largest)
        total = jnp.sum(exponent, axis=0, keepdims=True)
        mixed = dot(v_ref[:, lanes].T, exponent.astype(BF)) * (1.0 / total)
        c_ref[:, lanes] = mixed.T.astype(BF)
        lse_ref[head : head + 1, :] = largest + jnp.log(total)
    pl.when(step == last)(traffic.drain)


def attend(normed, w_qkv, tables, seg_col, pad_col, seg_row, w_out, w_up, w_down):
    length, width = normed.shape
    groups = width // 256
    units = [unit_spec(width, part * (width // 128) + e) for part in range(3) for e in range(2)]
    column = pl.BlockSpec((length, 256), lambda j: (0, j))
    wide = shaped((length, width), BF)
    quarter = full_of(w_up.shape[0], UNIT)
    return pl.pallas_call(
        attend_body,
        grid=(groups,),
        in_specs=[whole((length, width))]
        + units
        + [whole((length, 128))] * 3
        + [whole((length, 1))] * 2
        + [whole((1, length))]
        + [ANY] * 3,
        out_specs=(column,) * 4 + (pl.BlockSpec((8, length), lambda j: (j, 0)),) + (ANY,) * 4,
        out_shape=(wide,) * 4
        + (shaped((8 * groups, length), F32), full_of(*w_out.shape), quarter, quarter, quarter),
        scratch_shapes=[pltpu.VMEM((length, length), F32)] + semaphores(8, Gather.sems),
        compiler_params=params(collective_id=1, has_side_effects=True),
        name="attend",
    )(normed, *([w_qkv] * 6), *tables, seg_col, pad_col, seg_row, w_out, w_up, w_down)


def mlp_body(
    stream0_ref, ctx_ref, wout_ref, g2_ref, seg_ref, row_ref, cot_ref,
    up_ref, down_ref, fup0, fdn0, fup1,
    out_ref, gout_ref, ds1_ref, dctx_ref, dg2_ref, sup0, sdn0, gup1, gdn1, gup2, gdn2, gup3, gdn3,
    fdn1, fup2, fdn2, fup3, fdn3,
    s1_ref, n2_ref, acc_ref, dn_ref, up_tile, dn_tile, act_ref, pre_ref, stage_up, stage_dn,
    sem, gsend, grecv, glocal, rsend, rrecv, rlocal, *room,
):
    step = pl.program_id(0)
    steps = 8
    length, width = ctx_ref.shape
    tiles = length // UNIT
    me = Place()
    gather, reduce = Traffic(), Traffic()
    gather.add((0, 1, 3, 5, 6), *down_pair(me, down_ref, fdn1, 1))
    gather.add(2, *up_pair(me, up_ref, fup2, 2))
    gather.add(4, *down_pair(me, down_ref, fdn2, 2))
    gather.add(7, *up_pair(me, up_ref, fup3, 3))
    gather.add(10, *down_pair(me, down_ref, fdn3, 3))
    gather.bind(gsend, grecv, glocal)
    count = 0
    for q, (sup, sdn) in enumerate(((sup0, sdn0),)):
        made = []
        for rows, flip in halves(2 * UNIT):
            theirs = stage_up.at[q, 1 - me.c, :, :, :, rows, :]
            mine = stage_up.at[q, me.c, :, :, :, rows, :]
            made.append(Reduce(me, theirs, mine, mine, room[4 * count : 4 * count + 4], sup.at[rows, :], flip, False))
            count += 1
        for e in range(2):
            theirs = stage_dn.at[q, e, :, 1 - me.c]
            mine = stage_dn.at[q, e, :, me.c]
            rows = pl.ds(e * UNIT, UNIT)
            made.append(Reduce(me, theirs, mine, mine, room[4 * count : 4 * count + 4], sdn.at[rows, :], e == 1, False))
            count += 1
        reduce.add(6, *made[2:])
        reduce.add(7, *made[:2])
    reduce.bind(rsend, rrecv, rlocal)
    ups, downs = (fup0, fup1, fup2, fup3), (fdn0, fdn1, fdn2, fdn3)
    saves = {2: (gup1, gdn1), 4: (gup2, gdn2), 6: (gup3, gdn3)}

    def tile_loads(s):
        q, e = s // 2, s % 2
        return (
            flow(ups[q].at[:, e], up_tile.at[s % 2], sem.at[0, s % 2]),
            flow(downs[q].at[:, :, :, :, pl.ds(e * UNIT, UNIT), :], dn_tile.at[s % 2], sem.at[1, s % 2]),
        )

    def grad_saves(s):
        q, e = s // 2, s % 2
        gup, gdn = saves[2 * q]
        return (
            flow(stage_up.at[q % 2, e], gup.at[e], sem.at[2, s - 2]),
            flow(stage_dn.at[q % 2, e], gdn.at[e], sem.at[3, s - 2]),
        )

    def hook(which):
        gather.fire(step, steps, 3, which)
        reduce.fire(step, steps, 3, which)

    @pl.when(step == 0)
    def _():
        me.greet()
        gather.at(0)
        for load in tile_loads(0):
            load.start()
        first = flow(stream0_ref, s1_ref, sem.at[2, 0])
        first.start()
        first.wait()
        for i in range(4):
            lanes = slice(i * 2 * UNIT, (i + 1) * 2 * UNIT)
            tile = jnp.concatenate([wout_ref[i, c].reshape(width, UNIT) for c in range(2)], axis=1)
            s1_ref[:, lanes] += dot(ctx_ref[...], tile)

        @pl.loop(0, tiles)
        def _(t):
            rows = pl.ds(pl.multiple_of(t * UNIT, UNIT), UNIT)
            n2_ref[rows, :] = norm(s1_ref[rows, :], token_gain(seg_ref[rows, :], g2_ref))

        acc_ref[...] = jnp.zeros_like(acc_ref)
        dn_ref[...] = jnp.zeros_like(dn_ref)

    hook(0)
    for s in range(steps):

        @pl.when(step == s)
        def _(s=s):
            if s in (2, 4, 6):
                for load in tile_loads(s):
                    load.start()
            for load in tile_loads(s):
                load.wait()
            if s % 2 == 0:
                for load in tile_loads(s + 1):
                    load.start()

    slot = step % 2
    up = jnp.concatenate([up_tile[slot, z].reshape(width, UNIT) for z in range(4)], axis=1)
    down = jnp.concatenate([dn_tile[slot, f // 2, f % 2].reshape(4 * UNIT, UNIT) for f in range(NB)], axis=1)
    hidden = dot(n2_ref[...], up)
    square = hidden * hidden
    tanh = jnp.tanh(ROOT * hidden * (1.0 + CUBE * square))
    active = (0.5 * hidden * (1.0 + tanh)).astype(BF)
    act_ref[...] = active
    slope = 0.5 * (1.0 + tanh) + 0.5 * hidden * (1.0 - tanh * tanh) * (
        ROOT * (1.0 + 3.0 * CUBE * square)
    )
    d_pre = (dot(cot_ref[...], down, NT) * slope).astype(BF)
    pre_ref[...] = d_pre
    acc_ref[...] += dot(active, down)
    dn_ref[...] += dot(d_pre, up, NT)
    hook(1)
    par = (step // 2) % 2
    grad = dot(act_ref[...], cot_ref[...], TN).astype(BF)
    for f in range(NB):
        stage_dn[par, slot, f // 2, f % 2] = grad[:, f * UNIT : (f + 1) * UNIT].reshape(2, 2, UNIT, UNIT)
    hook(2)
    grad = dot(n2_ref[...], pre_ref[...], TN).astype(BF)
    for z in range(4):
        stage_up[par, slot, z] = grad[:, z * UNIT : (z + 1) * UNIT].reshape(2, 2, 2 * UNIT, UNIT)
    for s in range(2, steps):

        @pl.when(step == s)
        def _(s=s):
            for save in grad_saves(s):
                save.start()
            if s == 5:
                for save in grad_saves(2) + grad_saves(3):
                    save.wait()

    @pl.when(step == steps - 1)
    def _():
        dg2_ref[...] = jnp.zeros_like(dg2_ref)

        @pl.loop(0, tiles)
        def _(t):
            rows = pl.ds(pl.multiple_of(t * UNIT, UNIT), UNIT)
            stream = s1_ref[rows, :]
            out_ref[rows, :] = (stream + acc_ref[rows, :]).astype(BF)
            gain = token_gain(seg_ref[rows, :], g2_ref)
            term, d_gain = norm_back(dn_ref[rows, :], stream, gain)
            d_stream = cot_ref[rows, :].astype(F32) + term
            s1_ref[rows, :] = d_stream
            n2_ref[rows, :] = d_stream.astype(BF)
            dg2_ref[...] += segment_sum(row_ref[:, rows], d_gain)

        keep = flow(s1_ref, ds1_ref, sem.at[0, 0])
        keep.start()
        for i in range(4):
            lanes = slice(i * 2 * UNIT, (i + 1) * 2 * UNIT)
            part = dot(ctx_ref[...], n2_ref[:, lanes], TN).astype(BF)
            for c in range(2):
                gout_ref[i, c] = part[:, c * UNIT : (c + 1) * UNIT].reshape(2, 2, 2 * UNIT, UNIT)
        for i in range(4):
            lanes = slice(i * 2 * UNIT, (i + 1) * 2 * UNIT)
            tile = jnp.concatenate([wout_ref[i, c].reshape(width, UNIT) for c in range(2)], axis=1)
            part = dot(n2_ref[:, lanes], tile, NT)
            acc_ref[...] = part if i == 0 else acc_ref[...] + part
        dctx_ref[...] = acc_ref[...].astype(BF)
        gather.drain()
        reduce.drain()
        for s in range(4, steps):
            for save in grad_saves(s):
                save.wait()
        keep.wait()


def mlp(stream0, ctx, w_out, gamma2, seg_col, seg_row, cotangent, s_up, s_down, fup0, fdn0, fup1):
    length, width = ctx.shape
    full = whole((length, width))
    part = pl.BlockSpec((2 * UNIT, UNIT), lambda j: (0, 0))
    quarter = full_of(2 * UNIT, UNIT)
    grads = (shaped((2, 4, 2, 2, 2 * UNIT, UNIT), BF), shaped((2, 4, 2, 2, 2, UNIT, UNIT), BF))
    pieces = 4
    return pl.pallas_call(
        mlp_body,
        grid=(8,),
        in_specs=[
            ANY,
            full,
            whole(w_out.shape),
            whole((8, width)),
            whole((length, 1)),
            whole((1, length)),
            full,
        ]
        + [ANY] * 5,
        out_specs=(full, whole(w_out.shape), ANY, full, whole((8, width))) + (part,) * 2 + (ANY,) * 11,
        out_shape=(
            shaped((length, width), BF),
            shaped(w_out.shape, BF),
            shaped((length, width), F32),
            shaped((length, width), BF),
            shaped((8, width), F32),
        )
        + (shaped((2 * UNIT, UNIT), F32),) * 2
        + grads * 3
        + (quarter,) * 5,
        scratch_shapes=[
            pltpu.VMEM((length, width), F32),
            pltpu.VMEM((length, width), BF),
            pltpu.VMEM((length, width), F32),
            pltpu.VMEM((length, width), F32),
            pltpu.VMEM((2, 4, 2, 2, 2 * UNIT, UNIT), BF),
            pltpu.VMEM((2, 4, 2, 2, 2, UNIT, UNIT), BF),
            pltpu.VMEM((length, 4 * UNIT), BF),
            pltpu.VMEM((length, 4 * UNIT), BF),
            pltpu.VMEM((2, 2, 4, 2, 2, 2 * UNIT, UNIT), BF),
            pltpu.VMEM((2, 2, 4, 2, 2, 2, UNIT, UNIT), BF),
            pltpu.SemaphoreType.DMA((4, 6)),
        ]
        + semaphores(10, Gather.sems)
        + semaphores(pieces, Reduce.sems)
        + Reduce.room(UNIT, UNIT) * pieces,
        compiler_params=params(collective_id=2, has_side_effects=True),
        name="mlp",
    )(stream0, ctx, w_out, gamma2, seg_col, seg_row, cotangent, s_up, s_down, fup0, fdn0, fup1)


def attend_back_body(
    n_ref, qa, qb, ka, kb, va, vb, cos_ref, lo_ref, hi_ref, seg_ref, pad_ref, row_ref,
    q_ref, k_ref, v_ref, g_ref, c_ref, lse_ref, g1_ref, s0_ref, ds1_ref, gup1, gdn1, gup2, gdn2, gup3, gdn3, gout,
    gw_ref, dlow_ref, dg1_ref, sup1, sdn1, sup2, sdn2, sup3, sdn3, sout,
    bias_ref, dn_ref, dq_ref, dk_ref, dv_ref, s0_buf, sem, send, recv, local, *room,
):
    step = pl.program_id(0)
    last = pl.num_programs(0) - 1
    length, width = n_ref.shape
    me = Place()
    traffic = Traffic()
    count = 0
    for q, (gup, gdn, sup, sdn) in enumerate(
        ((gup1, gdn1, sup1, sdn1), (gup2, gdn2, sup2, sdn2), (gup3, gdn3, sup3, sdn3))
    ):
        ups, downs = [], []
        for e, (rows, flip) in enumerate(halves(2 * UNIT)):
            own, rest = room[count % 10], room[10 + 4 * count : 14 + 4 * count]
            ups.append(
                Reduce(
                    me, gup.at[1 - me.c, :, :, :, rows, :], gup.at[me.c, :, :, :, rows, :], own, rest,
                    sup.at[rows, :], flip, True,
                )
            )
            count += 1
            own, rest = room[count % 10], room[10 + 4 * count : 14 + 4 * count]
            downs.append(
                Reduce(
                    me, gdn.at[e, :, 1 - me.c], gdn.at[e, :, me.c], own, rest,
                    sdn.at[pl.ds(e * UNIT, UNIT), :], flip, True,
                )
            )
            count += 1
        traffic.add(4 * q, *ups)
        traffic.add(4 * q + 2, *downs)
    outs = []
    for rows, flip in halves(2 * UNIT):
        own, rest = room[count % 10], room[10 + 4 * count : 14 + 4 * count]
        theirs, mine = gout.at[:, 1 - me.c, :, :, rows, :], gout.at[:, me.c, :, :, rows, :]
        outs.append(Reduce(me, theirs, mine, own, rest, sout.at[rows, :], flip, True))
        count += 1
    traffic.add(12, *outs)
    traffic.bind(send, recv, local)
    fire = functools.partial(traffic.fire, step, 4, 5)

    @pl.when(step == 0)
    def _():
        me.greet()
        traffic.at(0)
        flow(s0_ref, s0_buf, sem.at[0]).start()
        fill_bias(bias_ref, seg_ref, pad_ref, row_ref)
        dn_ref[...] = jnp.zeros_like(dn_ref)

    ones = jnp.ones((8, HD), BF)
    for head in range(4):
        fire(head)
        lanes = slice(head * HD, (head + 1) * HD)
        query, key, value = q_ref[:, lanes], k_ref[:, lanes], v_ref[:, lanes]
        grad = g_ref[:, lanes]
        both = grad.astype(F32) * c_ref[:, lanes].astype(F32)
        high = both.astype(BF)
        low = (both - high.astype(F32)).astype(BF)
        delta = (dot(ones, high, NT) + dot(ones, low, NT))[0:1, :]
        probs = jnp.exp(dot(key, query, NT) + bias_ref[...] - lse_ref[head : head + 1, :])
        d_scores = (probs * (dot(value, grad, NT) - delta)).astype(BF)
        dv_ref[:, lanes] = dot(probs.astype(BF), grad)
        dk_ref[:, lanes] = dot(d_scores, query)
        dq_ref[:, lanes] = dot(key.T, d_scores).T * HD**-0.5

    @pl.when(step == last)
    def _():
        flow(ds1_ref, bias_ref, sem.at[1]).start()

    fire(4)
    for part, (src, first, second) in enumerate(
        ((dq_ref, qa, qb), (dk_ref, ka, kb), (dv_ref, va, vb))
    ):
        if part < 2:
            made = jnp.concatenate(
                [
                    turn(src[:, half * 128 : (half + 1) * 128], cos_ref[...], -lo_ref[...], -hi_ref[...])
                    for half in range(2)
                ],
                axis=1,
            ).astype(BF)
        else:
            made = src[...].astype(BF)
        grad = dot(n_ref[...], made, TN).astype(BF)
        gw_ref[part, 0] = grad[:, :128]
        gw_ref[part, 1] = grad[:, 128:]
        dn_ref[...] += dot(made, jnp.concatenate([first[0], second[0]], axis=1), NT)

    @pl.when(step == last)
    def _():
        dg1_ref[...] = jnp.zeros_like(dg1_ref)
        flow(s0_ref, s0_buf, sem.at[0]).wait()
        flow(ds1_ref, bias_ref, sem.at[1]).wait()

        @pl.loop(0, length // UNIT)
        def _(t):
            rows = pl.ds(pl.multiple_of(t * UNIT, UNIT), UNIT)
            gain = token_gain(seg_ref[rows, :], g1_ref)
            term, d_gain = norm_back(dn_ref[rows, :], s0_buf[rows, :], gain)
            dlow_ref[rows, :] = (bias_ref[rows, :] + term).astype(BF)
            dg1_ref[...] += segment_sum(row_ref[:, rows], d_gain)

        traffic.drain()


def attend_back(
    normed, w_qkv, tables, seg_col, pad_col, seg_row, q, k, v, d_ctx, ctx, lse, gamma1, stream0, d_stream1, grads
):
    length, width = normed.shape
    groups = width // 256
    units = [unit_spec(width, part * (width // 128) + e) for part in range(3) for e in range(2)]
    column = pl.BlockSpec((length, 256), lambda j: (0, j))
    full = whole((length, width))
    part = whole((2 * UNIT, UNIT))
    pieces = 14
    return pl.pallas_call(
        attend_back_body,
        grid=(groups,),
        in_specs=[full]
        + units
        + [whole((length, 128))] * 3
        + [whole((length, 1))] * 2
        + [whole((1, length))]
        + [column] * 5
        + [pl.BlockSpec((8, length), lambda j: (j, 0)), whole((8, width))]
        + [ANY] * 9,
        out_specs=(
            pl.BlockSpec((3, 2, width, 128), lambda j: (0, j, 0, 0)),
            full,
            whole((8, width)),
        )
        + (part,) * 7,
        out_shape=(
            shaped((3, width // 128, width, 128), BF),
            shaped((length, width), BF),
            shaped((8, width), F32),
        )
        + (shaped((2 * UNIT, UNIT), F32),) * 7,
        scratch_shapes=[pltpu.VMEM((length, length), F32), pltpu.VMEM((length, width), F32)]
        + [pltpu.VMEM((length, 256), F32)] * 3
        + [pltpu.VMEM((length, width), F32), pltpu.SemaphoreType.DMA((2,))]
        + semaphores(pieces, Reduce.sems)
        + [pltpu.VMEM((4, 2, 2, UNIT, UNIT), BF)] * 10
        + Reduce.room(UNIT, UNIT) * pieces,
        compiler_params=params(collective_id=3, has_side_effects=True),
        name="attend_back",
    )(
        normed, *([w_qkv] * 6), *tables, seg_col, pad_col, seg_row, q, k, v, d_ctx, ctx, lse,
        gamma1, stream0, d_stream1, *grads,
    )


def skip_back_body(
    x_ref, s_ref, d_ref, w_ref, ada_ref, dg_ref, every_ref, gw_ref,
    dx_ref, ds_ref, time_ref, gada_ref, sskip, sqkv,
    stage, slots, part, got, summed, tim, sends, recvs, send, recv, local, *room,
):
    width = x_ref.shape[1]
    me = Place()
    me.greet(True)
    traffic = Traffic()
    count = 0
    pairs = []
    for sub in range(3):
        made = []
        for rows, flip in halves(2 * UNIT):
            own, *rest = room[5 * count : 5 * count + 5]
            theirs, mine = gw_ref.at[:, 1 - me.c, sub, :, :, rows, :], gw_ref.at[:, me.c, sub, :, :, rows, :]
            out = sqkv.at[rows, pl.ds(sub * UNIT, UNIT)]
            made.append(Reduce(me, theirs, mine, own, rest, out, flip, True))
            count += 1
        pairs.append(made)
    tall = 512
    for i in range(2):
        made = []
        for e in range(2):
            rows = pl.ds((2 * i + e) * UNIT, UNIT)
            own, *rest = room[5 * count : 5 * count + 5]
            theirs, mine = stage.at[:, 1 - me.c, :, :, rows, :], stage.at[:, me.c, :, :, rows, :]
            made.append(Reduce(me, theirs, mine, own, rest, sskip.at[rows, :], e == 1, True))
            count += 1
        pairs.append(made)
    for i, made in enumerate(pairs):
        traffic.add(i if i < 3 else i + 1, *made)
    traffic.bind(send, recv, local)
    lay = functools.partial(pl.ds, 0)
    swaps = [
        Swap(me, "fsdp", lambda p: dg_ref.at[p], lambda m: slots.at[me.dp, m], sends.at[0], recvs.at[0]),
        Swap(me, "dp", lambda p: slots.at[me.dp], lambda m: slots.at[m], sends.at[1], recvs.at[1]),
        Swap(me, "fsdp", lambda p: part.at[:, p, lay(8), :], lambda m: got.at[m], sends.at[2], recvs.at[2]),
        Swap(me, "dp", lambda p: summed.at[p], lambda m: tim.at[m], sends.at[3], recvs.at[3]),
    ]
    slots[me.dp, me.fs] = dg_ref[me.fs]
    swaps[0].start()
    traffic.at(0)

    def grads(i):
        lanes = pl.ds(pl.multiple_of(i * 2 * UNIT, 2 * UNIT), 2 * UNIT)
        part = d_ref[:, lanes]
        top = dot(x_ref[...], part, TN).astype(BF)
        end = dot(s_ref[...], part, TN).astype(BF)
        for c in range(2):
            cols = slice(c * UNIT, (c + 1) * UNIT)
            stage[i, c, 0] = top[:, cols].reshape(2, tall, UNIT)
            stage[i, c, 1] = end[:, cols].reshape(2, tall, UNIT)

    pl.loop(0, 1)(grads)
    traffic.at(1)
    swaps[0].wait()
    swaps[1].start()
    pl.loop(1, 2)(grads)
    traffic.at(2)
    pl.loop(2, 4)(grads)
    traffic.at(3)
    traffic.at(4)
    swaps[1].wait()
    every = slots[...].reshape(4 * NB * 16, -1)
    gada_ref[...] = dot(every_ref[...].reshape(4 * NB * 16, -1), every, TN)
    part[...] = dot(every, ada_ref[...], NT).reshape(part.shape)
    got[me.fs] = part[:, me.fs, :8, :]
    swaps[2].start()

    def back(which, out):
        @pl.loop(0, 2)
        def _(i):
            rows = pl.ds(pl.multiple_of(i * tall, tall), tall)
            tile = jnp.concatenate([w_ref[f // 2, f % 2, which, i] for f in range(NB)], axis=1)
            out[:, rows] = dot(d_ref[...], tile, NT)

    back(0, dx_ref)
    traffic.at(5)
    swaps[2].wait()
    total = got[0]
    for f in range(1, NB):
        total = total + got[f]
    summed[...] = total
    tim[me.dp] = summed[me.dp]
    swaps[3].start()
    traffic.at(6)
    back(1, ds_ref)
    swaps[3].wait()
    for d in range(4):
        time_ref[:, d * 2 * UNIT : (d + 1) * 2 * UNIT] = tim[d]
    traffic.drain()


def skip_back(inputs, skip_in, d_low, w_skip, w_ada, dg_cut, every, g_qkv):
    length, width = inputs.shape
    vmem = pl.BlockSpec(memory_space=pltpu.VMEM)
    tall, per = w_ada.shape
    pieces = 10
    return pl.pallas_call(
        skip_back_body,
        in_specs=[vmem] * 7 + [ANY],
        out_shape=(
            shaped((length, width), F32),
            shaped((length, width), F32),
            shaped((8, width), F32),
            shaped((tall, per), F32),
            shaped((4 * UNIT, UNIT), F32),
            shaped((2 * UNIT, 3 * UNIT), F32),
        ),
        scratch_shapes=[
            pltpu.VMEM(w_skip.shape, BF),
            pltpu.VMEM((4, NB, 16, per), BF),
            pltpu.VMEM((4, NB, 16, tall), F32),
            pltpu.VMEM((NB, 4, 8, tall), F32),
            pltpu.VMEM((4, 8, tall), F32),
            pltpu.VMEM((4, 8, tall), F32),
            pltpu.SemaphoreType.DMA((4, NB - 1)),
            pltpu.SemaphoreType.DMA((4, NB - 1)),
        ]
        + semaphores(pieces, Reduce.sems)
        + ([pltpu.VMEM((4, 2, 2, UNIT, UNIT), BF)] + Reduce.room(UNIT, UNIT)) * pieces,
        compiler_params=params(collective_id=4, has_side_effects=True),
        name="skip_back",
    )(inputs, skip_in, d_low, w_skip, w_ada, dg_cut, every, g_qkv)


def rotary(positions):
    half = HD // 2
    lane = jnp.arange(128)
    frequency = 10000.0 ** (-2.0 * (lane % half).astype(F32) / HD)
    phase = positions.reshape(-1, 1).astype(F32) * frequency[None, :]
    cosine, sine = jnp.cos(phase), jnp.sin(phase)
    early = (lane % HD < half)[None, :]
    return cosine, jnp.where(early, -sine, 0.0), jnp.where(early, 0.0, sine)


def gathered(shard):
    blocks = lax.all_gather(shard, "fsdp", axis=0, tiled=False)
    blocks = lax.all_gather(blocks, "dp", axis=1, tiled=True)
    count, rows, per = blocks.shape
    if count == NB:
        return blocks
    flat = jnp.transpose(blocks, (1, 0, 2)).reshape(rows, count * per)
    return jnp.transpose(flat.reshape(rows, NB, count * per // NB), (1, 0, 2))


def scattered(blocks):
    count, rows, per = blocks.shape
    flat = jnp.transpose(blocks, (1, 0, 2)).reshape(rows, count * per)
    part = lax.psum_scatter(flat, "fsdp", scatter_dimension=1, tiled=True)
    return lax.psum_scatter(part, "dp", scatter_dimension=0, tiled=True).astype(F32)


def ada_grads(flat_time, d_gammas, tall, thin):
    every = lax.all_gather(flat_time, "fsdp", axis=0, tiled=True)
    every = lax.all_gather(every, "dp", axis=0, tiled=True)
    every = lax.dynamic_slice_in_dim(every, lax.axis_index("dp") * tall, tall, 1)
    gammas = lax.all_gather(d_gammas, "fsdp", axis=1, tiled=True)
    gammas = lax.all_gather(gammas, "dp", axis=1, tiled=True)
    gammas = lax.dynamic_slice_in_dim(gammas, lax.axis_index("fsdp") * thin, thin, 2)
    return [jnp.einsum("nd,ne->de", every, part, preferred_element_type=F32) for part in gammas]


def fused(
    inputs, skip_in, time_emb, seg_ids, positions, pad_mask,
    w_skip, w_ada1, w_qkv, w_out, w_ada2, w_up, w_down, cotangent,
):
    slots = time_emb.shape[1]
    length, width = inputs.shape
    seg_col, seg_row = seg_ids.reshape(-1, 1), seg_ids.reshape(1, -1)
    pad_col = pad_mask.reshape(-1, 1)
    tables = rotary(positions)
    flat_time = time_emb.reshape(slots, -1)
    time_cut = jnp.pad(flat_time, ((0, 16 - slots), (0, 0)))
    time_cut = jnp.transpose(time_cut.reshape(16, 4, -1), (1, 0, 2))
    w_ada = jnp.concatenate([w_ada1, w_ada2], axis=1)
    stream0, normed1, gamma1, gamma2, every, f_skip, f_qkv = front(
        inputs, skip_in, time_cut, seg_col, w_ada, w_skip, w_qkv
    )
    f_qkv = f_qkv.reshape(NB, width, -1)
    q, k, v, ctx, lse, f_out, fup0, fdn0, fup1 = attend(
        normed1, f_qkv, tables, seg_col, pad_col, seg_row, w_out, w_up, w_down
    )
    output, g_out, d_stream1, d_ctx, d_gamma2, sup0, sdn0, *rest = mlp(
        stream0, ctx, f_out, gamma2, seg_col, seg_row, cotangent, w_up, w_down, fup0, fdn0, fup1
    )
    g_qkv, d_low, d_gamma1, sup1, sdn1, sup2, sdn2, sup3, sdn3, s_out = attend_back(
        normed1, f_qkv, tables, seg_col, pad_col, seg_row, q, k, v, d_ctx, ctx, lse, gamma1,
        stream0, d_stream1, (*rest[:6], g_out),
    )
    dg_cut = jnp.concatenate([d.reshape(8, NB, -1) for d in (d_gamma1, d_gamma2)], axis=2)
    dg_cut = jnp.pad(jnp.transpose(dg_cut, (1, 0, 2)).astype(BF), ((0, 0), (0, 8), (0, 0)))
    d_input, d_skip, d_time, g_ada, s_skip, s_qkv = skip_back(
        inputs, skip_in, d_low, f_skip, w_ada, dg_cut, every, g_qkv.reshape(4, 2, 3, 2, 2, -1, UNIT)
    )
    s_up = jnp.concatenate([sup0, sup1, sup2, sup3], axis=1)
    s_down = jnp.stack([sdn0, sdn1, sdn2, sdn3]).reshape(4, 2, UNIT, UNIT)
    s_down = jnp.transpose(s_down, (1, 0, 2, 3)).reshape(w_down.shape)
    return (
        output, d_input, d_skip, d_time[:slots].reshape(time_emb.shape),
        s_skip, g_ada[:, :UNIT], s_qkv, s_out, g_ada[:, UNIT:], s_up, s_down,
    )


def plain(
    inputs, skip_in, time_emb, seg_ids, positions, pad_mask,
    w_skip, w_ada1, w_qkv, w_out, w_ada2, w_up, w_down, cotangent,
):
    slots = time_emb.shape[1]
    width = inputs.shape[1]
    seg_col, seg_row = seg_ids.reshape(-1, 1), seg_ids.reshape(1, -1)
    pad_col = pad_mask.reshape(-1, 1)
    tables = rotary(positions)
    flat_time = time_emb.reshape(slots, -1)
    time8 = jnp.pad(flat_time, ((0, 8 - slots), (0, 0)))
    f_skip, f_qkv, f_out, f_up, f_down, f_ada1, f_ada2 = [
        gathered(w) for w in (w_skip, w_qkv, w_out, w_up, w_down, w_ada1, w_ada2)
    ]
    ada = jnp.concatenate([f_ada1, f_ada2], axis=2)
    stream0, normed1, gamma1, gamma2 = plain_front(inputs, skip_in, f_skip, time8, ada, seg_col)
    q, k, v, ctx, lse = plain_attend(normed1, f_qkv, tables, seg_col, pad_col, seg_row)
    output, g_down, g_up, g_out, d_stream1, d_ctx, d_gamma2 = plain_mlp(
        stream0, ctx, f_out, gamma2, seg_col, seg_row, f_up, f_down, cotangent
    )
    g_qkv, d_low, d_gamma1 = plain_attend_back(
        normed1, f_qkv, tables, seg_col, pad_col, seg_row, q, k, v, d_ctx, ctx, lse,
        stream0, gamma1, d_stream1,
    )
    g_qkv = jnp.transpose(
        g_qkv.reshape(NB, 3, width, 128), (0, 2, 1, 3)
    ).reshape(NB, width, 3 * width // NB)
    g_skip, d_input, d_skip = plain_skip_back(inputs, skip_in, d_low, f_skip)
    d_gammas = jnp.stack([d_gamma1, d_gamma2]).astype(BF)[:, :slots]
    d_time = 0.0
    for d_gamma, part in zip(d_gammas, (f_ada1, f_ada2)):
        flat = jnp.transpose(part, (1, 0, 2)).reshape(width, width)
        d_time = d_time + jnp.einsum("ne,de->nd", d_gamma, flat, preferred_element_type=F32)
    g_ada = ada_grads(flat_time, d_gammas, *w_ada1.shape)
    return (
        output, d_input, d_skip, d_time.reshape(time_emb.shape),
        scattered(g_skip), g_ada[0], scattered(g_qkv), scattered(g_out), g_ada[1],
        scattered(g_up), scattered(g_down),
    )


def solution(mesh):
    rows = P(("dp", "fsdp"), None)
    cube = P(("dp", "fsdp"), None, None)
    tile = P("dp", "fsdp")
    fits = mesh.shape["dp"] == 4 and mesh.shape["fsdp"] == NB
    return jax.shard_map(
        fused if fits else plain,
        mesh=mesh,
        in_specs=(rows, rows, cube) + (rows,) * 3 + (tile,) * 7 + (rows,),
        out_specs=(rows, rows, rows, cube) + (tile,) * 7,
        check_vma=False,
    )
```

```python
import functools

import jax
import jax.numpy as jnp
from jax import lax
from jax.experimental import pallas as pl
from jax.experimental.pallas import tpu as pltpu
from jax.sharding import PartitionSpec as P

HD = 64
NB = 8
EPS = 1e-06
MASKED = -1e30
BF = jnp.bfloat16
F32 = jnp.float32
NN = (((1,), (0,)), ((), ()))
NT = (((1,), (1,)), ((), ()))
TN = (((0,), (0,)), ((), ()))
ROOT = 0.7978845608028654
CUBE = 0.044715


def dot(left, right, form=NN):
    return lax.dot_general(left, right, form, preferred_element_type=F32)


def params(**extra):
    return pltpu.CompilerParams(vmem_limit_bytes=60 << 20, **extra)


def whole(shape):
    return pl.BlockSpec(shape, lambda *_: (0,) * len(shape), pipeline_mode=pl.Buffered(1))


ANY = pl.BlockSpec(memory_space=pl.ANY)
UNIT = 128


def shaped(shape, kind):
    return jax.ShapeDtypeStruct(shape, kind)


def columns(ref, first, count, rows=slice(None)):
    return jnp.concatenate([ref[first + i, rows, :] for i in range(count)], axis=1)


def token_gain(seg, gamma):
    gain = gamma[0:1, :]
    for slot in range(1, 4):
        gain = jnp.where(seg == slot, gamma[slot : slot + 1, :], gain)
    return gain


def segment_sum(seg_row, values):
    slots = lax.broadcasted_iota(jnp.int32, (8, seg_row.shape[1]), 0)
    picked = (slots == seg_row).astype(BF)
    high = values.astype(BF)
    low = (values - high.astype(F32)).astype(BF)
    return dot(picked, high) + dot(picked, low)


def norm_back(grad, stream, gain):
    inverse = lax.rsqrt(jnp.mean(stream * stream, axis=-1, keepdims=True) + EPS)
    unit = stream * inverse
    scaled = grad * (1.0 + gain)
    d_stream = inverse * (scaled - unit * jnp.mean(scaled * unit, axis=-1, keepdims=True))
    return d_stream, grad * unit


def norm(stream, gain):
    inverse = lax.rsqrt(jnp.mean(stream * stream, axis=-1, keepdims=True) + EPS)
    return (stream * inverse * (1.0 + gain)).astype(BF)


def fill_bias(bias_ref, seg_ref, pad_ref, row_ref):
    length = seg_ref.shape[0]

    @pl.loop(0, length // UNIT)
    def _(t):
        rows = pl.ds(pl.multiple_of(t * UNIT, UNIT), UNIT)
        keys = lax.broadcasted_iota(jnp.int32, (UNIT, length), 0) + t * UNIT
        queries = lax.broadcasted_iota(jnp.int32, (UNIT, length), 1)
        allowed = (seg_ref[rows, :] == row_ref[0:1, :]) & (
            (pad_ref[rows, :] > 0) | (keys == queries)
        )
        bias_ref[rows, :] = jnp.where(allowed, 0.0, MASKED)


def turn(unit, cosine, before, after):
    return (
        unit * cosine
        + pltpu.roll(unit, 96, 1) * before
        + pltpu.roll(unit, 32, 1) * after
    )


def unit_spec(rows, base):
    def index(j):
        unit = base + 2 * j
        return (unit // 3, 0, unit % 3)

    return pl.BlockSpec((1, rows, 128), index)


def plain_front_body(x_ref, s_ref, w_ref, time_ref, ada_ref, seg_ref, stream_ref, normed_ref, g1_ref, g2_ref):
    length, width = x_ref.shape
    per = ada_ref.shape[2] // 2
    for f in range(NB):
        both = dot(time_ref[...], ada_ref[f])
        g1_ref[:, f * per : (f + 1) * per] = both[:, :per]
        g2_ref[:, f * per : (f + 1) * per] = both[:, per:]
    for i in range(NB // 2):
        tile = columns(w_ref, 2 * i, 2)
        part = dot(x_ref[...], tile[:width]) + dot(s_ref[...], tile[width:])
        stream_ref[:, i * part.shape[1] : (i + 1) * part.shape[1]] = part

    @pl.loop(0, length // 128)
    def _(t):
        rows = pl.ds(pl.multiple_of(t * 128, 128), 128)
        gain = token_gain(seg_ref[rows, :], g1_ref)
        normed_ref[rows, :] = norm(stream_ref[rows, :], gain)


def plain_front(inputs, skip_in, w_skip, time8, ada, seg_col):
    length, width = inputs.shape
    return pl.pallas_call(
        plain_front_body,
        out_shape=(
            shaped((length, width), F32),
            shaped((length, width), BF),
            shaped((8, width), F32),
            shaped((8, width), F32),
        ),
        compiler_params=params(),
        name="front",
    )(inputs, skip_in, w_skip, time8, ada, seg_col)


def plain_attend_body(
    n_ref, qa, qb, ka, kb, va, vb, cos_ref, lo_ref, hi_ref, seg_ref, pad_ref, row_ref,
    q_ref, k_ref, v_ref, c_ref, lse_ref, bias_ref,
):
    @pl.when(pl.program_id(0) == 0)
    def _():
        fill_bias(bias_ref, seg_ref, pad_ref, row_ref)

    normed = n_ref[...]
    for out, first, second, scale in ((q_ref, qa, qb, HD**-0.5), (k_ref, ka, kb, 1.0)):
        made = dot(normed, jnp.concatenate([first[0], second[0]], axis=1))
        for half in range(2):
            unit = made[:, half * 128 : (half + 1) * 128]
            turned = turn(unit, cos_ref[...], lo_ref[...], hi_ref[...])
            out[:, half * 128 : (half + 1) * 128] = (turned.astype(BF) * scale).astype(BF)
    v_ref[...] = dot(normed, jnp.concatenate([va[0], vb[0]], axis=1)).astype(BF)
    for head in range(4):
        lanes = slice(head * HD, (head + 1) * HD)
        scores = dot(k_ref[:, lanes], q_ref[:, lanes], NT) + bias_ref[...]
        largest = jnp.max(scores, axis=0, keepdims=True)
        exponent = jnp.exp(scores - largest)
        total = jnp.sum(exponent, axis=0, keepdims=True)
        mixed = dot(v_ref[:, lanes].T, exponent.astype(BF)) * (1.0 / total)
        c_ref[:, lanes] = mixed.T.astype(BF)
        lse_ref[head : head + 1, :] = largest + jnp.log(total)


def plain_attend(normed, w_qkv, tables, seg_col, pad_col, seg_row):
    length, width = normed.shape
    groups = width // 256
    units = [unit_spec(width, part * (width // 128) + e) for part in range(3) for e in range(2)]
    column = pl.BlockSpec((length, 256), lambda j: (0, j))
    wide = shaped((length, width), BF)
    return pl.pallas_call(
        plain_attend_body,
        grid=(groups,),
        in_specs=[whole((length, width))]
        + units
        + [whole((length, 128))] * 3
        + [whole((length, 1))] * 2
        + [whole((1, length))],
        out_specs=(column,) * 4 + (pl.BlockSpec((8, length), lambda j: (j, 0)),),
        out_shape=(wide,) * 4 + (shaped((8 * groups, length), F32),),
        scratch_shapes=[pltpu.VMEM((length, length), F32)],
        compiler_params=params(),
        name="attend",
    )(normed, *([w_qkv] * 6), *tables, seg_col, pad_col, seg_row)


def plain_mlp_body(
    stream0_ref, ctx_ref, wout_ref, g2_ref, seg_ref, row_ref, up_ref, down_ref, cot_ref,
    out_ref, gdown_ref, gup_ref, gout_ref, ds1_ref, dctx_ref, dg2_ref,
    s1_ref, n2_ref, acc_ref, dn_ref,
):
    step = pl.program_id(0)
    length, width = ctx_ref.shape
    tiles = length // 128

    @pl.when(step == 0)
    def _():
        @pl.loop(0, NB // 2)
        def _(i):
            lanes = pl.ds(pl.multiple_of(i * 256, 256), 256)
            s1_ref[:, lanes] = stream0_ref[:, lanes] + dot(ctx_ref[...], columns(wout_ref, 2 * i, 2))

        @pl.loop(0, tiles)
        def _(t):
            rows = pl.ds(pl.multiple_of(t * 128, 128), 128)
            n2_ref[rows, :] = norm(s1_ref[rows, :], token_gain(seg_ref[rows, :], g2_ref))

        acc_ref[...] = jnp.zeros_like(acc_ref)
        dn_ref[...] = jnp.zeros_like(dn_ref)

    cot = cot_ref[...]
    up = up_ref[0]
    down = columns(down_ref, 0, NB)
    hidden = dot(n2_ref[...], up)
    square = hidden * hidden
    tanh = jnp.tanh(ROOT * hidden * (1.0 + CUBE * square))
    active = (0.5 * hidden * (1.0 + tanh)).astype(BF)
    slope = 0.5 * (1.0 + tanh) + 0.5 * hidden * (1.0 - tanh * tanh) * (
        ROOT * (1.0 + 3.0 * CUBE * square)
    )
    d_pre = (dot(cot, down, NT) * slope).astype(BF)
    acc_ref[...] += dot(active, down)
    dn_ref[...] += dot(d_pre, up, NT)
    grad = dot(active, cot, TN).astype(BF)
    for f in range(NB):
        gdown_ref[f] = grad[:, f * gdown_ref.shape[2] : (f + 1) * gdown_ref.shape[2]]
    gup_ref[0] = dot(n2_ref[...], d_pre, TN).astype(BF)

    @pl.when(step == pl.num_programs(0) - 1)
    def _():
        dg2_ref[...] = jnp.zeros_like(dg2_ref)

        @pl.loop(0, tiles)
        def _(t):
            rows = pl.ds(pl.multiple_of(t * 128, 128), 128)
            stream = s1_ref[rows, :]
            out_ref[rows, :] = (stream + acc_ref[rows, :]).astype(BF)
            gain = token_gain(seg_ref[rows, :], g2_ref)
            term, d_gain = norm_back(dn_ref[rows, :], stream, gain)
            d_stream = cot_ref[rows, :].astype(F32) + term
            ds1_ref[rows, :] = d_stream
            n2_ref[rows, :] = d_stream.astype(BF)
            dg2_ref[...] += segment_sum(row_ref[:, rows], d_gain)

        @pl.loop(0, NB // 2)
        def _(i):
            lanes = pl.ds(pl.multiple_of(i * 256, 256), 256)
            part = dot(ctx_ref[...], n2_ref[:, lanes], TN).astype(BF)
            gout_ref[2 * i] = part[:, :128]
            gout_ref[2 * i + 1] = part[:, 128:]

        acc_ref[...] = jnp.zeros_like(acc_ref)

        @pl.loop(0, NB // 2)
        def _(i):
            lanes = pl.ds(pl.multiple_of(i * 256, 256), 256)
            acc_ref[...] += dot(n2_ref[:, lanes], columns(wout_ref, 2 * i, 2), NT)

        dctx_ref[...] = acc_ref[...].astype(BF)


def plain_mlp(stream0, ctx, w_out, gamma2, seg_col, seg_row, w_up, w_down, cotangent):
    length, width = ctx.shape
    hidden = w_down.shape[1]
    piece = hidden // NB
    per = width // NB
    full = whole((length, width))
    return pl.pallas_call(
        plain_mlp_body,
        grid=(NB,),
        in_specs=[
            full,
            full,
            whole((NB, width, per)),
            whole((8, width)),
            whole((length, 1)),
            whole((1, length)),
            pl.BlockSpec((1, width, piece), lambda j: (j, 0, 0)),
            pl.BlockSpec((NB, piece, per), lambda j: (0, j, 0)),
            full,
        ],
        out_specs=(
            full,
            pl.BlockSpec((NB, piece, per), lambda j: (0, j, 0)),
            pl.BlockSpec((1, width, piece), lambda j: (j, 0, 0)),
            whole((NB, width, per)),
            full,
            full,
            whole((8, width)),
        ),
        out_shape=(
            shaped((length, width), BF),
            shaped((NB, hidden, per), BF),
            shaped((NB, width, piece), BF),
            shaped((NB, width, per), BF),
            shaped((length, width), F32),
            shaped((length, width), BF),
            shaped((8, width), F32),
        ),
        scratch_shapes=[
            pltpu.VMEM((length, width), F32),
            pltpu.VMEM((length, width), BF),
            pltpu.VMEM((length, width), F32),
            pltpu.VMEM((length, width), F32),
        ],
        compiler_params=params(),
        name="mlp",
    )(stream0, ctx, w_out, gamma2, seg_col, seg_row, w_up, w_down, cotangent)


def plain_attend_back_body(
    n_ref, qa, qb, ka, kb, va, vb, cos_ref, lo_ref, hi_ref, seg_ref, pad_ref, row_ref,
    q_ref, k_ref, v_ref, g_ref, c_ref, lse_ref, s0_ref, g1_ref, ds1_ref,
    gw_ref, dlow_ref, dg1_ref, bias_ref, dn_ref, dq_ref, dk_ref, dv_ref,
):
    step = pl.program_id(0)
    length, width = n_ref.shape

    @pl.when(step == 0)
    def _():
        fill_bias(bias_ref, seg_ref, pad_ref, row_ref)
        dn_ref[...] = jnp.zeros_like(dn_ref)

    ones = jnp.ones((8, HD), BF)
    for head in range(4):
        lanes = slice(head * HD, (head + 1) * HD)
        query, key, value = q_ref[:, lanes], k_ref[:, lanes], v_ref[:, lanes]
        grad = g_ref[:, lanes]
        both = grad.astype(F32) * c_ref[:, lanes].astype(F32)
        high = both.astype(BF)
        low = (both - high.astype(F32)).astype(BF)
        delta = (dot(ones, high, NT) + dot(ones, low, NT))[0:1, :]
        probs = jnp.exp(dot(key, query, NT) + bias_ref[...] - lse_ref[head : head + 1, :])
        d_scores = (probs * (dot(value, grad, NT) - delta)).astype(BF)
        dv_ref[:, lanes] = dot(probs.astype(BF), grad)
        dk_ref[:, lanes] = dot(d_scores, query)
        dq_ref[:, lanes] = dot(key.T, d_scores).T * HD**-0.5
    for part, (src, first, second) in enumerate(
        ((dq_ref, qa, qb), (dk_ref, ka, kb), (dv_ref, va, vb))
    ):
        if part < 2:
            made = jnp.concatenate(
                [
                    turn(src[:, half * 128 : (half + 1) * 128], cos_ref[...], -lo_ref[...], -hi_ref[...])
                    for half in range(2)
                ],
                axis=1,
            ).astype(BF)
        else:
            made = src[...].astype(BF)
        grad = dot(n_ref[...], made, TN).astype(BF)
        gw_ref[part, 0] = grad[:, :128]
        gw_ref[part, 1] = grad[:, 128:]
        dn_ref[...] += dot(made, jnp.concatenate([first[0], second[0]], axis=1), NT)

    @pl.when(step == pl.num_programs(0) - 1)
    def _():
        dg1_ref[...] = jnp.zeros_like(dg1_ref)

        @pl.loop(0, length // 128)
        def _(t):
            rows = pl.ds(pl.multiple_of(t * 128, 128), 128)
            gain = token_gain(seg_ref[rows, :], g1_ref)
            term, d_gain = norm_back(dn_ref[rows, :], s0_ref[rows, :], gain)
            dlow_ref[rows, :] = (ds1_ref[rows, :] + term).astype(BF)
            dg1_ref[...] += segment_sum(row_ref[:, rows], d_gain)


def plain_attend_back(
    normed, w_qkv, tables, seg_col, pad_col, seg_row, q, k, v, d_ctx, ctx, lse, stream0, gamma1, d_stream1
):
    length, width = normed.shape
    groups = width // 256
    units = [unit_spec(width, part * (width // 128) + e) for part in range(3) for e in range(2)]
    column = pl.BlockSpec((length, 256), lambda j: (0, j))
    full = whole((length, width))
    return pl.pallas_call(
        plain_attend_back_body,
        grid=(groups,),
        in_specs=[full]
        + units
        + [whole((length, 128))] * 3
        + [whole((length, 1))] * 2
        + [whole((1, length))]
        + [column] * 5
        + [pl.BlockSpec((8, length), lambda j: (j, 0)), full, whole((8, width)), full],
        out_specs=(
            pl.BlockSpec((3, 2, width, 128), lambda j: (0, j, 0, 0)),
            full,
            whole((8, width)),
        ),
        out_shape=(
            shaped((3, width // 128, width, 128), BF),
            shaped((length, width), BF),
            shaped((8, width), F32),
        ),
        scratch_shapes=[pltpu.VMEM((length, length), F32), pltpu.VMEM((length, width), F32)]
        + [pltpu.VMEM((length, 256), F32)] * 3,
        compiler_params=params(),
        name="attend_back",
    )(
        normed, *([w_qkv] * 6), *tables, seg_col, pad_col, seg_row, q, k, v, d_ctx, ctx, lse,
        stream0, gamma1, d_stream1,
    )


def plain_skip_back_body(x_ref, s_ref, d_ref, w_ref, gw_ref, dx_ref, ds_ref):
    low = d_ref[...]
    per = 256
    width = x_ref.shape[1]

    @pl.loop(0, width // per)
    def _(i):
        lanes = pl.ds(pl.multiple_of(i * per, per), per)
        part = d_ref[:, lanes]
        top = dot(x_ref[...], part, TN).astype(BF)
        end = dot(s_ref[...], part, TN).astype(BF)
        for e in range(2):
            gw_ref[2 * i + e, :width, :] = top[:, e * 128 : (e + 1) * 128]
            gw_ref[2 * i + e, width:, :] = end[:, e * 128 : (e + 1) * 128]

    tall = 256

    @pl.loop(0, width // tall)
    def _(i):
        rows = pl.ds(pl.multiple_of(i * tall, tall), tall)
        rest = pl.ds(pl.multiple_of(width + i * tall, tall), tall)
        dx_ref[:, rows] = dot(low, columns(w_ref, 0, NB, rows), NT)
        ds_ref[:, rows] = dot(low, columns(w_ref, 0, NB, rest), NT)


def plain_skip_back(inputs, skip_in, d_low, w_skip):
    length, width = inputs.shape
    return pl.pallas_call(
        plain_skip_back_body,
        out_shape=(
            shaped(w_skip.shape, BF),
            shaped((length, width), F32),
            shaped((length, width), F32),
        ),
        compiler_params=params(),
        name="skip_back",
    )(inputs, skip_in, d_low, w_skip)


class Place:
    def __init__(self):
        dp, fs = lax.axis_index("dp"), lax.axis_index("fsdp")
        self.y, self.x, self.z, self.c = dp // 2, dp % 2, fs // 2, fs % 2
        self.dp, self.fs = dp, fs

    def across_x(self):
        return (self.y * 2 + 1 - self.x, self.fs)

    def across_y(self):
        return ((1 - self.y) * 2 + self.x, self.fs)

    def sibling(self):
        return (self.dp, self.z * 2 + 1 - self.c)

    def along_z(self, hop):
        return (self.dp, ((self.z + hop) % 4) * 2 + self.c)

    def on_dp(self, index):
        return (index, self.fs)

    def on_fsdp(self, index):
        return (self.dp, index)

    def greet(self, wide=False):
        barrier = pltpu.get_barrier_semaphore()
        if wide:
            peers = [self.on_dp((self.dp + hop) % 4) for hop in range(1, 4)]
            peers += [self.on_fsdp((self.fs + hop) % NB) for hop in range(1, NB)]
        else:
            peers = [self.across_x(), self.across_y(), self.sibling()]
            peers += [self.along_z(hop) for hop in (1, 2, 3)]
        for peer in peers:
            pl.semaphore_signal(barrier, inc=1, device_id=peer, device_id_type=pl.DeviceIdType.MESH)
        pl.semaphore_wait(barrier, len(peers))


def remote(src, dst, send, recv, peer):
    return pltpu.make_async_remote_copy(
        src_ref=src, dst_ref=dst, send_sem=send, recv_sem=recv,
        device_id=peer, device_id_type=pl.DeviceIdType.MESH,
    )


class Lazy:
    def __init__(self, plan, send, recv):
        self.plan, self.send, self.recv = plan, send, recv

    def __len__(self):
        return len(self.plan)

    def __getitem__(self, i):
        if isinstance(i, slice):
            return [self[k] for k in range(*i.indices(len(self)))]
        if i >= len(self.plan):
            raise IndexError
        src, dst, peer = self.plan[i]
        return remote(src, dst, self.send.at[i], self.recv.at[i], peer)


def flow(*copy):
    return pltpu.make_async_copy(*copy)


class Gather:
    sems = 8

    def __init__(self, place, source, full, rows, flip):
        self.me, self.source, self.full, self.rows, self.flip = place, source, full, rows, flip

    def bind(self, send, recv, local):
        self.send, self.recv, self.local = send, recv, local

    def copies(self):
        me, full, rows = self.me, self.full, self.rows
        spot = full.at[me.z, me.c, me.y, me.x, rows, :]
        line = full.at[:, me.c, me.y, me.x, rows, :]
        if self.flip:
            pair = full.at[:, me.c, :, me.x, rows, :]
            near, far = me.across_y(), me.across_x()
            got = full.at[:, me.c, 1 - me.y, me.x, rows, :]
            late = full.at[:, me.c, :, 1 - me.x, rows, :]
        else:
            pair = full.at[:, me.c, me.y, :, rows, :]
            near, far = me.across_x(), me.across_y()
            got = full.at[:, me.c, me.y, 1 - me.x, rows, :]
            late = full.at[:, me.c, 1 - me.y, :, rows, :]
        sib = me.sibling()
        plan = [(self.source, spot, me.along_z(hop)) for hop in (1, 2, 3)]
        plan += [(line, line, near), (pair, pair, far), (line, line, sib), (got, got, sib), (late, late, sib)]
        return Lazy(plan, self.send, self.recv), (self.source, spot, self.local)

    def stage(self, number):
        made, keep = self.copies()
        if number == 0:
            flow(*keep).start()
            for copy in made[:3]:
                copy.start()
        elif number == 1:
            flow(*keep).wait()
            for copy in made[:3]:
                copy.wait_recv()
            made[3].start()
            made[5].start()
        elif number == 2:
            made[3].wait_recv()
            made[4].start()
            made[6].start()
        elif number == 3:
            made[4].wait_recv()
            made[7].start()
        else:
            for copy in made[5:]:
                copy.wait_recv()
            for copy in made[:]:
                copy.wait_send()


class Reduce:
    sems = 6

    def __init__(self, place, theirs, mine, own, room, out, flip, load):
        self.me, self.theirs, self.mine, self.own = place, theirs, mine, own
        self.other, self.half, self.quarter, self.parts = room
        self.out, self.flip, self.load = out, flip, load

    @staticmethod
    def room(count, per):
        return [
            pltpu.VMEM((4, 2, 2, count, per), BF),
            pltpu.VMEM((4, 2, count, per), BF),
            pltpu.VMEM((4, count, per), BF),
            pltpu.VMEM((3, count, per), BF),
        ]

    def bind(self, send, recv, local):
        self.send, self.recv, self.local = send, recv, local

    def copies(self):
        me = self.me
        if self.flip:
            give, near = self.own.at[:, :, 1 - me.x], me.across_x()
            give2, far = self.half.at[:, 1 - me.y], me.across_y()
        else:
            give, near = self.own.at[:, 1 - me.y], me.across_y()
            give2, far = self.half.at[:, 1 - me.x], me.across_x()
        plan = [(self.theirs, self.other, me.sibling()), (give, self.half, near), (give2, self.quarter, far)]
        plan += [
            (self.quarter.at[(me.z + hop) % 4], self.parts.at[hop - 1], me.along_z(hop)) for hop in (1, 2, 3)
        ]
        return Lazy(plan, self.send, self.recv), (self.mine, self.own, self.local)

    def stage(self, number):
        me = self.me
        made, load = self.copies()
        if number == 0:
            made[0].start()
            if self.load:
                flow(*load).start()
        elif number == 1:
            if self.load:
                flow(*load).wait()
            made[0].wait_recv()

            @pl.loop(0, 4)
            def _(z):
                self.own[z] = self.own[z] + self.other[z]

            made[1].start()
        elif number == 2:
            made[1].wait_recv()

            @pl.loop(0, 4)
            def _(z):
                kept = self.own[z, :, me.x] if self.flip else self.own[z, me.y]
                self.half[z] = self.half[z] + kept

            made[2].start()
        elif number == 3:
            made[0].wait_send()
            made[1].wait_send()
            made[2].wait_recv()
            kept = me.y if self.flip else me.x

            @pl.loop(0, 4)
            def _(z):
                self.quarter[z] = self.quarter[z] + self.half[z, kept]

            for copy in made[3:]:
                copy.start()
        else:
            for copy in made[3:]:
                copy.wait_recv()
            total = self.quarter[me.z].astype(F32)
            for i in range(3):
                total = total + self.parts[i].astype(F32)
            self.out[...] = total
            for copy in made[2:]:
                copy.wait_send()


class Swap:
    def __init__(self, place, axis, what, into, send, recv):
        count = 4 if axis == "dp" else NB
        at = place.dp if axis == "dp" else place.fs
        find = place.on_dp if axis == "dp" else place.on_fsdp
        self.at, self.what, self.into = at, what, into
        self.plan = []
        for hop in range(1, count):
            peer = (at + hop) % count
            self.plan.append((what(peer), into(at), send.at[hop - 1], recv.at[hop - 1], find(peer)))

    def start(self):
        for copy in self.plan:
            remote(*copy).start()

    def wait(self):
        for copy in self.plan:
            remote(*copy).wait()


class Traffic:
    def __init__(self):
        self.todo, self.pieces = {}, []

    def add(self, hooks, pieces):
        self.pieces += pieces
        for piece, places in zip(pieces, hooks, strict=True):
            for stage, hook in enumerate(places):
                self.todo.setdefault(hook, []).append((stage, piece))

    def bind(self, send, recv, local):
        for i, piece in enumerate(self.pieces):
            piece.bind(send.at[i], recv.at[i], local.at[i])

    def at(self, hook):
        for stage, piece in sorted(self.todo.pop(hook, []), key=lambda item: -item[0]):
            piece.stage(stage)

    def fire(self, step, steps, per, hook):
        for s in range(steps):
            if s * per + hook in self.todo:
                pl.when(step == s)(functools.partial(self.at, s * per + hook))

    def inside(self, index, first, count):
        for s in range(count):
            if first + s in self.todo:
                pl.when(index == s)(functools.partial(self.at, first + s))

    def drain(self):
        for hook in sorted(self.todo):
            self.at(hook)


def semaphores(count, kind):
    return [pltpu.SemaphoreType.DMA((count, kind))] * 2 + [pltpu.SemaphoreType.DMA((count,))]


def full_of(rows, per):
    return shaped((4, 2, 2, 2, rows, per), BF)


def halves(rows):
    return [(pl.ds(e * (rows // 2), rows // 2), e == 1) for e in range(2)]


def up_pair(me, shard, full, q):
    lanes = pl.ds(q * UNIT, UNIT)
    return [Gather(me, shard.at[rows, lanes], full, rows, flip) for rows, flip in halves(shard.shape[0])]


def down_pair(me, shard, full, q):
    tall = shard.shape[0] // 2
    step = tall // 4
    return [
        Gather(me, shard.at[pl.ds(e * tall + q * step, step), :], full, pl.ds(e * step, step), e == 1)
        for e in range(2)
    ]


def row_pieces(me, shard, full, count):
    tall = shard.shape[0] // count
    return [
        Gather(me, shard.at[pl.ds(i * tall, tall), :], full, pl.ds(i * tall, tall), i % 2 == 1)
        for i in range(count)
    ]


FRONT_HOOKS = (
    (1, 4, 7, 13, 14), (1, 4, 7, 13, 14),
    (4, 7, 10, 18, 19), (4, 7, 10, 18, 19),
    (0, 1, 3, 7, 8), (0, 1, 3, 7, 8),
    (3, 6, 9, 16, 18), (3, 6, 9, 16, 18),
    (9, 13, 18, 25, 28), (9, 13, 18, 25, 28),
    (6, 9, 15, 22, 25), (6, 9, 15, 22, 25),
    (0, 2, 5, 11, 13), (0, 2, 5, 10, 12),
    (13, 17, 21, 28, 31), (13, 17, 21, 28, 31),
)
FRONT_READY = 19
ATTEND_HOOKS = (
    (7, 10, 12, 15, 16), (7, 10, 12, 15, 16),
    (1, 4, 6, 9, 10), (1, 4, 6, 9, 10),
    (0, 1, 3, 5, 6), (0, 1, 3, 5, 6),
    (6, 9, 11, 14, 15), (6, 9, 11, 14, 15),
    (2, 5, 7, 10, 11), (2, 5, 7, 10, 11),
)
MLP_HOOKS = (
    (0, 1, 4, 7, 9), (0, 1, 4, 7, 9),
    (0, 1, 5, 9, 10), (0, 2, 5, 9, 10),
    (11, 14, 18, 22, 24), (11, 16, 18, 22, 24),
    (10, 13, 17, 21, 22), (10, 13, 17, 21, 22),
    (9, 10, 14, 17, 20), (9, 11, 14, 17, 21),
    (8, 9, 13, 16, 17), (8, 9, 13, 16, 18),
)
ATTEND_BACK_HOOKS = (
    (0, 1, 4, 8, 10), (0, 1, 4, 8, 10),
    (1, 2, 8, 11, 14), (1, 2, 8, 11, 14),
    (7, 8, 13, 16, 19), (7, 8, 13, 16, 19),
    (2, 3, 9, 12, 16), (2, 3, 9, 12, 16),
    (3, 4, 10, 13, 17), (3, 4, 10, 13, 17),
    (11, 12, 16, 18, 20), (11, 12, 16, 18, 20),
    (12, 13, 17, 19, 20), (12, 13, 17, 19, 20),
)
SKIP_BACK_HOOKS = (
    (5, 6, 11, 13, 16), (5, 6, 9, 12, 13),
    (7, 9, 13, 16, 19), (7, 9, 12, 14, 16),
    (2, 4, 7, 10, 12), (2, 4, 6, 9, 10),
    (5, 6, 11, 13, 16), (6, 7, 11, 13, 16),
    (0, 2, 5, 6, 8), (0, 2, 5, 7, 9),
    (2, 4, 7, 10, 12), (4, 5, 7, 10, 12),
    (11, 12, 16, 19, 20), (11, 12, 14, 17, 19),
    (12, 13, 18, 20, 22), (12, 13, 17, 19, 21),
    (13, 15, 19, 20, 23), (13, 15, 19, 20, 23),
    (7, 9, 13, 16, 19), (9, 10, 13, 16, 19),
)


def front_body(
    x_ref, s_ref, time_ref, seg_ref, ada_ref, skip_ref, qkv_ref,
    stream_ref, normed_ref, g1_ref, g2_ref, slots, fskip_ref, fqkv_ref,
    w_ref, part, got, summed, gam, w_sem, sends, recvs, send, recv, local,
):
    length, width = x_ref.shape
    per = ada_ref.shape[1] // 2
    me = Place()
    me.greet(True)
    traffic = Traffic()
    plan = row_pieces(me, skip_ref, fskip_ref, 8) + row_pieces(me, qkv_ref, fqkv_ref, 8)
    traffic.add(FRONT_HOOKS, plan)
    traffic.bind(send, recv, local)
    lay = functools.partial(pl.ds, 0)
    swaps = [
        Swap(me, "dp", lambda p: time_ref.at[p], lambda m: slots.at[m, me.fs], sends.at[0], recvs.at[0]),
        Swap(me, "fsdp", lambda p: slots.at[:, me.fs], lambda m: slots.at[:, m], sends.at[1], recvs.at[1]),
        Swap(me, "dp", lambda p: part.at[p, :, lay(8), :], lambda m: got.at[m], sends.at[2], recvs.at[2]),
        Swap(me, "fsdp", lambda p: summed.at[p], lambda m: gam.at[m], sends.at[3], recvs.at[3]),
    ]
    slots[me.dp, me.fs] = time_ref[me.dp]
    swaps[0].start()
    for hook in range(FRONT_READY + 1):
        traffic.at(hook)
        if hook == 4:
            swaps[0].wait()
            swaps[1].start()
        elif hook == 8:
            swaps[1].wait()
            made = dot(slots[...].reshape(4 * NB * 16, -1), ada_ref[...])
            part[...] = made.reshape(part.shape)
            got[me.dp] = part[me.dp, :, :8, :]
            swaps[2].start()
        elif hook == 12:
            swaps[2].wait()
            summed[...] = got[0] + got[1] + got[2] + got[3]
            gam[me.fs] = summed[me.fs]
            swaps[3].start()
    load = flow(fskip_ref, w_ref, w_sem)
    load.start()
    swaps[3].wait()
    for f in range(NB):
        g1_ref[:, f * per : (f + 1) * per] = gam[f, :, :per]
        g2_ref[:, f * per : (f + 1) * per] = gam[f, :, per:]
    load.wait()

    def stream(i):
        tile = jnp.concatenate([w_ref[i, c].reshape(2 * width, UNIT) for c in range(2)], axis=1)
        lanes = pl.ds(pl.multiple_of(i * 2 * UNIT, 2 * UNIT), 2 * UNIT)
        stream_ref[:, lanes] = dot(x_ref[...], tile[:width]) + dot(s_ref[...], tile[width:])

    def normalise(t):
        rows = pl.ds(pl.multiple_of(t * UNIT, UNIT), UNIT)
        gain = token_gain(seg_ref[rows, :], g1_ref)
        normed_ref[rows, :] = norm(stream_ref[rows, :], gain)

    @pl.loop(0, 4)
    def _(i):
        stream(i)
        traffic.inside(i, FRONT_READY + 1, 4)

    @pl.loop(0, length // UNIT)
    def _(t):
        normalise(t)
        traffic.inside(t, FRONT_READY + 5, 8)

    traffic.drain()


def front(inputs, skip_in, time_cut, seg_col, w_ada, w_skip, w_qkv):
    length, width = inputs.shape
    fulls = [full_of(*w.shape) for w in (w_skip, w_qkv)]
    vmem = pl.BlockSpec(memory_space=pltpu.VMEM)
    per = w_ada.shape[1]
    return pl.pallas_call(
        front_body,
        in_specs=[vmem] * 5 + [ANY] * 2,
        out_specs=(vmem,) * 5 + (ANY,) * 2,
        out_shape=(
            shaped((length, width), F32),
            shaped((length, width), BF),
            shaped((8, width), F32),
            shaped((8, width), F32),
            shaped((4, NB, 16, w_ada.shape[0]), BF),
            *fulls,
        ),
        scratch_shapes=[
            pltpu.VMEM(fulls[0].shape, BF),
            pltpu.VMEM((4, NB, 16, per), F32),
            pltpu.VMEM((4, NB, 8, per), F32),
            pltpu.VMEM((NB, 8, per), F32),
            pltpu.VMEM((NB, 8, per), F32),
            pltpu.SemaphoreType.DMA,
            pltpu.SemaphoreType.DMA((4, NB - 1)),
            pltpu.SemaphoreType.DMA((4, NB - 1)),
        ]
        + semaphores(16, Gather.sems),
        compiler_params=params(collective_id=0, has_side_effects=True),
        name="front",
    )(inputs, skip_in, time_cut, seg_col, w_ada, w_skip, w_qkv)


def attend_body(
    n_ref, qa, qb, ka, kb, va, vb, cos_ref, lo_ref, hi_ref, seg_ref, pad_ref, row_ref, out_ref, up_ref, down_ref,
    q_ref, k_ref, v_ref, c_ref, lse_ref, fout_ref, fup0_ref, fdn0_ref, fup1_ref, fdn1_ref,
    bias_ref, send, recv, local,
):
    step = pl.program_id(0)
    last = pl.num_programs(0) - 1
    me = Place()
    traffic = Traffic()
    pieces = (
        up_pair(me, up_ref, fup0_ref, 0)
        + down_pair(me, down_ref, fdn0_ref, 0)
        + up_pair(me, up_ref, fup1_ref, 1)
        + down_pair(me, down_ref, fdn1_ref, 1)
        + row_pieces(me, out_ref, fout_ref, 2)
    )
    traffic.add(ATTEND_HOOKS, pieces)
    traffic.bind(send, recv, local)
    fire = functools.partial(traffic.fire, step, 4, 4)

    @pl.when(step == 0)
    def _():
        me.greet()
        traffic.at(0)
        fill_bias(bias_ref, seg_ref, pad_ref, row_ref)

    normed = n_ref[...]
    for out, first, second, scale in ((q_ref, qa, qb, HD**-0.5), (k_ref, ka, kb, 1.0)):
        made = dot(normed, jnp.concatenate([first[0], second[0]], axis=1))
        for half in range(2):
            unit = made[:, half * 128 : (half + 1) * 128]
            turned = turn(unit, cos_ref[...], lo_ref[...], hi_ref[...])
            out[:, half * 128 : (half + 1) * 128] = (turned.astype(BF) * scale).astype(BF)
    v_ref[...] = dot(normed, jnp.concatenate([va[0], vb[0]], axis=1)).astype(BF)
    for head in range(4):
        fire(head)
        lanes = slice(head * HD, (head + 1) * HD)
        scores = dot(k_ref[:, lanes], q_ref[:, lanes], NT) + bias_ref[...]
        largest = jnp.max(scores, axis=0, keepdims=True)
        exponent = jnp.exp(scores - largest)
        total = jnp.sum(exponent, axis=0, keepdims=True)
        mixed = dot(v_ref[:, lanes].T, exponent.astype(BF)) * (1.0 / total)
        c_ref[:, lanes] = mixed.T.astype(BF)
        lse_ref[head : head + 1, :] = largest + jnp.log(total)
    pl.when(step == last)(traffic.drain)


def attend(normed, w_qkv, tables, seg_col, pad_col, seg_row, w_out, w_up, w_down):
    length, width = normed.shape
    groups = width // 256
    units = [unit_spec(width, part * (width // 128) + e) for part in range(3) for e in range(2)]
    column = pl.BlockSpec((length, 256), lambda j: (0, j))
    wide = shaped((length, width), BF)
    quarter = full_of(w_up.shape[0], UNIT)
    return pl.pallas_call(
        attend_body,
        grid=(groups,),
        in_specs=[whole((length, width))]
        + units
        + [whole((length, 128))] * 3
        + [whole((length, 1))] * 2
        + [whole((1, length))]
        + [ANY] * 3,
        out_specs=(column,) * 4 + (pl.BlockSpec((8, length), lambda j: (j, 0)),) + (ANY,) * 5,
        out_shape=(wide,) * 4
        + (shaped((8 * groups, length), F32), full_of(*w_out.shape)) + (quarter,) * 4,
        scratch_shapes=[pltpu.VMEM((length, length), F32)] + semaphores(10, Gather.sems),
        compiler_params=params(collective_id=1, has_side_effects=True),
        name="attend",
    )(normed, *([w_qkv] * 6), *tables, seg_col, pad_col, seg_row, w_out, w_up, w_down)


def mlp_body(
    stream0_ref, ctx_ref, wout_ref, g2_ref, seg_ref, row_ref, cot_ref,
    up_ref, down_ref, fup0, fdn0, fup1, fdn1,
    out_ref, gout_ref, ds1_ref, dctx_ref, dg2_ref, sup0, sdn0, gup1, gdn1, gup2, gdn2, gup3, gdn3,
    fup2, fdn2, fup3, fdn3,
    s1_ref, n2_ref, acc_ref, dn_ref, up_tile, dn_tile, act_ref, pre_ref, stage_up, stage_dn,
    sem, gsend, grecv, glocal, rsend, rrecv, rlocal, *room,
):
    step = pl.program_id(0)
    steps = 8
    length, width = ctx_ref.shape
    tiles = length // UNIT
    me = Place()
    gather, reduce = Traffic(), Traffic()
    pieces = (
        up_pair(me, up_ref, fup2, 2)
        + down_pair(me, down_ref, fdn2, 2)
        + up_pair(me, up_ref, fup3, 3)
        + down_pair(me, down_ref, fdn3, 3)
    )
    gather.add(MLP_HOOKS[:8], pieces)
    gather.bind(gsend, grecv, glocal)
    count = 0
    for q, (sup, sdn) in enumerate(((sup0, sdn0),)):
        made = []
        for rows, flip in halves(2 * UNIT):
            theirs = stage_up.at[q, 1 - me.c, :, :, :, rows, :]
            mine = stage_up.at[q, me.c, :, :, :, rows, :]
            made.append(Reduce(me, theirs, mine, mine, room[4 * count : 4 * count + 4], sup.at[rows, :], flip, False))
            count += 1
        for e in range(2):
            theirs = stage_dn.at[q, e, :, 1 - me.c]
            mine = stage_dn.at[q, e, :, me.c]
            rows = pl.ds(e * UNIT, UNIT)
            made.append(Reduce(me, theirs, mine, mine, room[4 * count : 4 * count + 4], sdn.at[rows, :], e == 1, False))
            count += 1
        reduce.add(MLP_HOOKS[8:], made)
    reduce.bind(rsend, rrecv, rlocal)
    ups, downs = (fup0, fup1, fup2, fup3), (fdn0, fdn1, fdn2, fdn3)
    saves = {2: (gup1, gdn1), 4: (gup2, gdn2), 6: (gup3, gdn3)}

    def tile_loads(s):
        q, e = s // 2, s % 2
        return (
            flow(ups[q].at[:, e], up_tile.at[s % 2], sem.at[0, s % 2]),
            flow(downs[q].at[:, :, :, :, pl.ds(e * UNIT, UNIT), :], dn_tile.at[s % 2], sem.at[1, s % 2]),
        )

    def grad_saves(s):
        q, e = s // 2, s % 2
        gup, gdn = saves[2 * q]
        return (
            flow(stage_up.at[q % 2, e], gup.at[e], sem.at[2, s - 2]),
            flow(stage_dn.at[q % 2, e], gdn.at[e], sem.at[3, s - 2]),
        )

    def hook(which):
        gather.fire(step, steps, 4, which)
        reduce.fire(step, steps, 4, which)

    @pl.when(step == 0)
    def _():
        me.greet()
        gather.at(0)
        for load in tile_loads(0):
            load.start()
        first = flow(stream0_ref, s1_ref, sem.at[2, 0])
        first.start()
        first.wait()
        for i in range(4):
            lanes = slice(i * 2 * UNIT, (i + 1) * 2 * UNIT)
            tile = jnp.concatenate([wout_ref[i, c].reshape(width, UNIT) for c in range(2)], axis=1)
            s1_ref[:, lanes] += dot(ctx_ref[...], tile)

        @pl.loop(0, tiles)
        def _(t):
            rows = pl.ds(pl.multiple_of(t * UNIT, UNIT), UNIT)
            n2_ref[rows, :] = norm(s1_ref[rows, :], token_gain(seg_ref[rows, :], g2_ref))

        acc_ref[...] = jnp.zeros_like(acc_ref)
        dn_ref[...] = jnp.zeros_like(dn_ref)

    hook(0)
    for s in range(steps):

        @pl.when(step == s)
        def _(s=s):
            if s in (2, 4, 6):
                for load in tile_loads(s):
                    load.start()
            for load in tile_loads(s):
                load.wait()
            if s % 2 == 0:
                for load in tile_loads(s + 1):
                    load.start()

    slot = step % 2
    up = jnp.concatenate([up_tile[slot, z].reshape(width, UNIT) for z in range(4)], axis=1)
    down = jnp.concatenate([dn_tile[slot, f // 2, f % 2].reshape(4 * UNIT, UNIT) for f in range(NB)], axis=1)
    hidden = dot(n2_ref[...], up)
    square = hidden * hidden
    half = 0.5 + 0.5 * jnp.tanh(hidden * (ROOT + ROOT * CUBE * square))
    act_ref[...] = (hidden * half).astype(BF)
    bend = hidden * (2.0 * ROOT + 6.0 * ROOT * CUBE * square)
    slope = half + half * (1.0 - half) * bend
    pre_ref[...] = (dot(cot_ref[...], down, NT) * slope).astype(BF)
    hook(1)
    acc_ref[...] += dot(act_ref[...], down)
    dn_ref[...] += dot(pre_ref[...], up, NT)
    hook(2)
    par = (step // 2) % 2
    grad = dot(act_ref[...], cot_ref[...], TN).astype(BF)
    for f in range(NB):
        stage_dn[par, slot, f // 2, f % 2] = grad[:, f * UNIT : (f + 1) * UNIT].reshape(2, 2, UNIT, UNIT)
    hook(3)
    grad = dot(n2_ref[...], pre_ref[...], TN).astype(BF)
    for z in range(4):
        stage_up[par, slot, z] = grad[:, z * UNIT : (z + 1) * UNIT].reshape(2, 2, 2 * UNIT, UNIT)
    for s in range(2, steps):

        @pl.when(step == s)
        def _(s=s):
            for save in grad_saves(s):
                save.start()
            if s == 5:
                for save in grad_saves(2) + grad_saves(3):
                    save.wait()

    @pl.when(step == steps - 1)
    def _():
        dg2_ref[...] = jnp.zeros_like(dg2_ref)

        @pl.loop(0, tiles)
        def _(t):
            rows = pl.ds(pl.multiple_of(t * UNIT, UNIT), UNIT)
            stream = s1_ref[rows, :]
            out_ref[rows, :] = (stream + acc_ref[rows, :]).astype(BF)
            gain = token_gain(seg_ref[rows, :], g2_ref)
            term, d_gain = norm_back(dn_ref[rows, :], stream, gain)
            d_stream = cot_ref[rows, :].astype(F32) + term
            s1_ref[rows, :] = d_stream
            n2_ref[rows, :] = d_stream.astype(BF)
            dg2_ref[...] += segment_sum(row_ref[:, rows], d_gain)

        keep = flow(s1_ref, ds1_ref, sem.at[0, 0])
        keep.start()
        for i in range(4):
            lanes = slice(i * 2 * UNIT, (i + 1) * 2 * UNIT)
            part = dot(ctx_ref[...], n2_ref[:, lanes], TN).astype(BF)
            for c in range(2):
                gout_ref[i, c] = part[:, c * UNIT : (c + 1) * UNIT].reshape(2, 2, 2 * UNIT, UNIT)
        for i in range(4):
            lanes = slice(i * 2 * UNIT, (i + 1) * 2 * UNIT)
            tile = jnp.concatenate([wout_ref[i, c].reshape(width, UNIT) for c in range(2)], axis=1)
            part = dot(n2_ref[:, lanes], tile, NT)
            acc_ref[...] = part if i == 0 else acc_ref[...] + part
        dctx_ref[...] = acc_ref[...].astype(BF)
        gather.drain()
        reduce.drain()
        for s in range(4, steps):
            for save in grad_saves(s):
                save.wait()
        keep.wait()


def mlp(stream0, ctx, w_out, gamma2, seg_col, seg_row, cotangent, s_up, s_down, fup0, fdn0, fup1, fdn1):
    length, width = ctx.shape
    full = whole((length, width))
    part = pl.BlockSpec((2 * UNIT, UNIT), lambda j: (0, 0))
    quarter = full_of(2 * UNIT, UNIT)
    grads = (shaped((2, 4, 2, 2, 2 * UNIT, UNIT), BF), shaped((2, 4, 2, 2, 2, UNIT, UNIT), BF))
    pieces = 4
    return pl.pallas_call(
        mlp_body,
        grid=(8,),
        in_specs=[
            ANY,
            full,
            whole(w_out.shape),
            whole((8, width)),
            whole((length, 1)),
            whole((1, length)),
            full,
        ]
        + [ANY] * 6,
        out_specs=(full, whole(w_out.shape), ANY, full, whole((8, width))) + (part,) * 2 + (ANY,) * 10,
        out_shape=(
            shaped((length, width), BF),
            shaped(w_out.shape, BF),
            shaped((length, width), F32),
            shaped((length, width), BF),
            shaped((8, width), F32),
        )
        + (shaped((2 * UNIT, UNIT), F32),) * 2
        + grads * 3
        + (quarter,) * 4,
        scratch_shapes=[
            pltpu.VMEM((length, width), F32),
            pltpu.VMEM((length, width), BF),
            pltpu.VMEM((length, width), F32),
            pltpu.VMEM((length, width), F32),
            pltpu.VMEM((2, 4, 2, 2, 2 * UNIT, UNIT), BF),
            pltpu.VMEM((2, 4, 2, 2, 2, UNIT, UNIT), BF),
            pltpu.VMEM((length, 4 * UNIT), BF),
            pltpu.VMEM((length, 4 * UNIT), BF),
            pltpu.VMEM((2, 2, 4, 2, 2, 2 * UNIT, UNIT), BF),
            pltpu.VMEM((2, 2, 4, 2, 2, 2, UNIT, UNIT), BF),
            pltpu.SemaphoreType.DMA((4, 6)),
        ]
        + semaphores(8, Gather.sems)
        + semaphores(pieces, Reduce.sems)
        + Reduce.room(UNIT, UNIT) * pieces,
        compiler_params=params(collective_id=2, has_side_effects=True),
        name="mlp",
    )(stream0, ctx, w_out, gamma2, seg_col, seg_row, cotangent, s_up, s_down, fup0, fdn0, fup1, fdn1)


def attend_back_body(
    n_ref, qa, qb, ka, kb, va, vb, cos_ref, lo_ref, hi_ref, seg_ref, pad_ref, row_ref,
    q_ref, k_ref, v_ref, g_ref, c_ref, lse_ref, g1_ref, s0_ref, ds1_ref, gup1, gdn1, gup2, gdn2, gup3, gdn3, gout,
    gw_ref, dlow_ref, dg1_ref, sup1, sdn1, sup2, sdn2, sup3, sdn3, sout,
    bias_ref, dn_ref, dq_ref, dk_ref, dv_ref, s0_buf, sem, send, recv, local, *room,
):
    step = pl.program_id(0)
    last = pl.num_programs(0) - 1
    length, width = n_ref.shape
    me = Place()
    traffic = Traffic()
    made = []

    def add(theirs, mine, out, e, own):
        count = len(made)
        rest = room[10 + 4 * count : 14 + 4 * count]
        made.append(Reduce(me, theirs, mine, room[own + e], rest, out, e == 1, True))

    for q, (gup, gdn, sup, sdn) in enumerate(
        ((gup1, gdn1, sup1, sdn1), (gup2, gdn2, sup2, sdn2), (gup3, gdn3, sup3, sdn3))
    ):
        for e, (rows, _) in enumerate(halves(2 * UNIT)):
            add(gup.at[1 - me.c, :, :, :, rows, :], gup.at[me.c, :, :, :, rows, :], sup.at[rows, :], e, (0, 4, 8)[q])
        for e in range(2):
            add(gdn.at[e, :, 1 - me.c], gdn.at[e, :, me.c], sdn.at[pl.ds(e * UNIT, UNIT), :], e, (2, 6, 0)[q])
    for e, (rows, _) in enumerate(halves(2 * UNIT)):
        theirs, mine = gout.at[:, 1 - me.c, :, :, rows, :], gout.at[:, me.c, :, :, rows, :]
        add(theirs, mine, sout.at[rows, :], e, 2)
    traffic.add(ATTEND_BACK_HOOKS, made)
    traffic.bind(send, recv, local)
    fire = functools.partial(traffic.fire, step, 4, 5)

    @pl.when(step == 0)
    def _():
        me.greet()
        traffic.at(0)
        flow(s0_ref, s0_buf, sem.at[0]).start()
        fill_bias(bias_ref, seg_ref, pad_ref, row_ref)
        dn_ref[...] = jnp.zeros_like(dn_ref)

    ones = jnp.ones((8, HD), BF)
    for head in range(4):
        fire(head)
        lanes = slice(head * HD, (head + 1) * HD)
        query, key, value = q_ref[:, lanes], k_ref[:, lanes], v_ref[:, lanes]
        grad = g_ref[:, lanes]
        both = grad.astype(F32) * c_ref[:, lanes].astype(F32)
        high = both.astype(BF)
        low = (both - high.astype(F32)).astype(BF)
        delta = (dot(ones, high, NT) + dot(ones, low, NT))[0:1, :]
        probs = jnp.exp(dot(key, query, NT) + bias_ref[...] - lse_ref[head : head + 1, :])
        d_scores = (probs * (dot(value, grad, NT) - delta)).astype(BF)
        dv_ref[:, lanes] = dot(probs.astype(BF), grad)
        dk_ref[:, lanes] = dot(d_scores, query)
        dq_ref[:, lanes] = dot(key.T, d_scores).T * HD**-0.5

    @pl.when(step == last)
    def _():
        flow(ds1_ref, bias_ref, sem.at[1]).start()

    fire(4)
    for part, (src, first, second) in enumerate(
        ((dq_ref, qa, qb), (dk_ref, ka, kb), (dv_ref, va, vb))
    ):
        if part < 2:
            made = jnp.concatenate(
                [
                    turn(src[:, half * 128 : (half + 1) * 128], cos_ref[...], -lo_ref[...], -hi_ref[...])
                    for half in range(2)
                ],
                axis=1,
            ).astype(BF)
        else:
            made = src[...].astype(BF)
        grad = dot(n_ref[...], made, TN).astype(BF)
        gw_ref[part, 0] = grad[:, :128]
        gw_ref[part, 1] = grad[:, 128:]
        dn_ref[...] += dot(made, jnp.concatenate([first[0], second[0]], axis=1), NT)

    @pl.when(step == last)
    def _():
        dg1_ref[...] = jnp.zeros_like(dg1_ref)
        flow(s0_ref, s0_buf, sem.at[0]).wait()
        flow(ds1_ref, bias_ref, sem.at[1]).wait()

        @pl.loop(0, length // UNIT)
        def _(t):
            rows = pl.ds(pl.multiple_of(t * UNIT, UNIT), UNIT)
            gain = token_gain(seg_ref[rows, :], g1_ref)
            term, d_gain = norm_back(dn_ref[rows, :], s0_buf[rows, :], gain)
            dlow_ref[rows, :] = (bias_ref[rows, :] + term).astype(BF)
            dg1_ref[...] += segment_sum(row_ref[:, rows], d_gain)

        traffic.drain()


def attend_back(
    normed, w_qkv, tables, seg_col, pad_col, seg_row, q, k, v, d_ctx, ctx, lse, gamma1, stream0, d_stream1, grads
):
    length, width = normed.shape
    groups = width // 256
    units = [unit_spec(width, part * (width // 128) + e) for part in range(3) for e in range(2)]
    column = pl.BlockSpec((length, 256), lambda j: (0, j))
    full = whole((length, width))
    part = whole((2 * UNIT, UNIT))
    pieces = 14
    return pl.pallas_call(
        attend_back_body,
        grid=(groups,),
        in_specs=[full]
        + units
        + [whole((length, 128))] * 3
        + [whole((length, 1))] * 2
        + [whole((1, length))]
        + [column] * 5
        + [pl.BlockSpec((8, length), lambda j: (j, 0)), whole((8, width))]
        + [ANY] * 9,
        out_specs=(
            pl.BlockSpec((3, 2, width, 128), lambda j: (0, j, 0, 0)),
            full,
            whole((8, width)),
        )
        + (part,) * 7,
        out_shape=(
            shaped((3, width // 128, width, 128), BF),
            shaped((length, width), BF),
            shaped((8, width), F32),
        )
        + (shaped((2 * UNIT, UNIT), F32),) * 7,
        scratch_shapes=[pltpu.VMEM((length, length), F32), pltpu.VMEM((length, width), F32)]
        + [pltpu.VMEM((length, 256), F32)] * 3
        + [pltpu.VMEM((length, width), F32), pltpu.SemaphoreType.DMA((2,))]
        + semaphores(pieces, Reduce.sems)
        + [pltpu.VMEM((4, 2, 2, UNIT, UNIT), BF)] * 10
        + Reduce.room(UNIT, UNIT) * pieces,
        compiler_params=params(collective_id=3, has_side_effects=True),
        name="attend_back",
    )(
        normed, *([w_qkv] * 6), *tables, seg_col, pad_col, seg_row, q, k, v, d_ctx, ctx, lse,
        gamma1, stream0, d_stream1, *grads,
    )


def skip_back_body(
    x_ref, s_ref, d_ref, w_ref, ada_ref, dg_ref, every_ref, gw_ref,
    dx_ref, ds_ref, time_ref, gada_ref, sskip, sqkv,
    stage, slots, part, got, summed, tim, sends, recvs, send, recv, local, *room,
):
    width = x_ref.shape[1]
    me = Place()
    me.greet(True)
    traffic = Traffic()
    made = []
    tall = 512

    def add(theirs, mine, out):
        own, *rest = room[5 * len(made) : 5 * len(made) + 5]
        made.append(Reduce(me, theirs, mine, own, rest, out, len(made) % 2 == 1, True))

    for sub in range(3):
        for i in range(4):
            rows = pl.ds(i * UNIT // 2, UNIT // 2)
            theirs, mine = gw_ref.at[:, 1 - me.c, sub, :, :, rows, :], gw_ref.at[:, me.c, sub, :, :, rows, :]
            add(theirs, mine, sqkv.at[rows, pl.ds(sub * UNIT, UNIT)])
    for i in range(8):
        rows = pl.ds(i * UNIT // 2, UNIT // 2)
        theirs, mine = stage.at[:, 1 - me.c, :, :, rows, :], stage.at[:, me.c, :, :, rows, :]
        add(theirs, mine, sskip.at[rows, :])
    traffic.add(SKIP_BACK_HOOKS, made)
    traffic.bind(send, recv, local)
    lay = functools.partial(pl.ds, 0)
    swaps = [
        Swap(me, "fsdp", lambda p: dg_ref.at[p], lambda m: slots.at[me.dp, m], sends.at[0], recvs.at[0]),
        Swap(me, "dp", lambda p: slots.at[me.dp], lambda m: slots.at[m], sends.at[1], recvs.at[1]),
        Swap(me, "fsdp", lambda p: part.at[:, p, lay(8), :], lambda m: got.at[m], sends.at[2], recvs.at[2]),
        Swap(me, "dp", lambda p: summed.at[p], lambda m: tim.at[m], sends.at[3], recvs.at[3]),
    ]
    slots[me.dp, me.fs] = dg_ref[me.fs]
    swaps[0].start()
    traffic.at(0)

    def grads(i):
        lanes = pl.ds(pl.multiple_of(i * 2 * UNIT, 2 * UNIT), 2 * UNIT)
        part = d_ref[:, lanes]
        top = dot(x_ref[...], part, TN).astype(BF)
        end = dot(s_ref[...], part, TN).astype(BF)
        for c in range(2):
            cols = slice(c * UNIT, (c + 1) * UNIT)
            stage[i, c, 0] = top[:, cols].reshape(2, tall, UNIT)
            stage[i, c, 1] = end[:, cols].reshape(2, tall, UNIT)

    def second():
        swaps[0].wait()
        swaps[1].start()

    @pl.loop(0, 4)
    def _(i):
        grads(i)
        traffic.inside(i, 1, 4)
        pl.when(i == 1)(second)

    traffic.at(5)
    swaps[1].wait()
    every = slots[...].reshape(4 * NB * 16, -1)
    gada_ref[...] = dot(every_ref[...].reshape(4 * NB * 16, -1), every, TN)
    part[...] = dot(every, ada_ref[...], NT).reshape(part.shape)
    got[me.fs] = part[:, me.fs, :8, :]
    swaps[2].start()

    def back(which, out, first):
        @pl.loop(0, 2)
        def _(i):
            traffic.inside(i, first, 2)
            rows = pl.ds(pl.multiple_of(i * tall, tall), tall)
            tile = jnp.concatenate([w_ref[f // 2, f % 2, which, i] for f in range(NB)], axis=1)
            out[:, rows] = dot(d_ref[...], tile, NT)

    back(0, dx_ref, 6)
    swaps[2].wait()
    total = got[0]
    for f in range(1, NB):
        total = total + got[f]
    summed[...] = total
    tim[me.dp] = summed[me.dp]
    swaps[3].start()
    back(1, ds_ref, 8)
    swaps[3].wait()
    for d in range(4):
        time_ref[:, d * 2 * UNIT : (d + 1) * 2 * UNIT] = tim[d]
    traffic.drain()


def skip_back(inputs, skip_in, d_low, w_skip, w_ada, dg_cut, every, g_qkv):
    length, width = inputs.shape
    vmem = pl.BlockSpec(memory_space=pltpu.VMEM)
    tall, per = w_ada.shape
    pieces = 20
    return pl.pallas_call(
        skip_back_body,
        in_specs=[vmem] * 7 + [ANY],
        out_shape=(
            shaped((length, width), F32),
            shaped((length, width), F32),
            shaped((8, width), F32),
            shaped((tall, per), F32),
            shaped((4 * UNIT, UNIT), F32),
            shaped((2 * UNIT, 3 * UNIT), F32),
        ),
        scratch_shapes=[
            pltpu.VMEM(w_skip.shape, BF),
            pltpu.VMEM((4, NB, 16, per), BF),
            pltpu.VMEM((4, NB, 16, tall), F32),
            pltpu.VMEM((NB, 4, 8, tall), F32),
            pltpu.VMEM((4, 8, tall), F32),
            pltpu.VMEM((4, 8, tall), F32),
            pltpu.SemaphoreType.DMA((4, NB - 1)),
            pltpu.SemaphoreType.DMA((4, NB - 1)),
        ]
        + semaphores(pieces, Reduce.sems)
        + ([pltpu.VMEM((4, 2, 2, UNIT // 2, UNIT), BF)] + Reduce.room(UNIT // 2, UNIT)) * pieces,
        compiler_params=params(collective_id=4, has_side_effects=True),
        name="skip_back",
    )(inputs, skip_in, d_low, w_skip, w_ada, dg_cut, every, g_qkv)


def rotary(positions):
    half = HD // 2
    lane = jnp.arange(128)
    frequency = 10000.0 ** (-2.0 * (lane % half).astype(F32) / HD)
    phase = positions.reshape(-1, 1).astype(F32) * frequency[None, :]
    cosine, sine = jnp.cos(phase), jnp.sin(phase)
    early = (lane % HD < half)[None, :]
    return cosine, jnp.where(early, -sine, 0.0), jnp.where(early, 0.0, sine)


def gathered(shard):
    blocks = lax.all_gather(shard, "fsdp", axis=0, tiled=False)
    blocks = lax.all_gather(blocks, "dp", axis=1, tiled=True)
    count, rows, per = blocks.shape
    if count == NB:
        return blocks
    flat = jnp.transpose(blocks, (1, 0, 2)).reshape(rows, count * per)
    return jnp.transpose(flat.reshape(rows, NB, count * per // NB), (1, 0, 2))


def scattered(blocks):
    count, rows, per = blocks.shape
    flat = jnp.transpose(blocks, (1, 0, 2)).reshape(rows, count * per)
    part = lax.psum_scatter(flat, "fsdp", scatter_dimension=1, tiled=True)
    return lax.psum_scatter(part, "dp", scatter_dimension=0, tiled=True).astype(F32)


def ada_grads(flat_time, d_gammas, tall, thin):
    every = lax.all_gather(flat_time, "fsdp", axis=0, tiled=True)
    every = lax.all_gather(every, "dp", axis=0, tiled=True)
    every = lax.dynamic_slice_in_dim(every, lax.axis_index("dp") * tall, tall, 1)
    gammas = lax.all_gather(d_gammas, "fsdp", axis=1, tiled=True)
    gammas = lax.all_gather(gammas, "dp", axis=1, tiled=True)
    gammas = lax.dynamic_slice_in_dim(gammas, lax.axis_index("fsdp") * thin, thin, 2)
    return [jnp.einsum("nd,ne->de", every, part, preferred_element_type=F32) for part in gammas]


def fused(
    inputs, skip_in, time_emb, seg_ids, positions, pad_mask,
    w_skip, w_ada1, w_qkv, w_out, w_ada2, w_up, w_down, cotangent,
):
    slots = time_emb.shape[1]
    length, width = inputs.shape
    seg_col, seg_row = seg_ids.reshape(-1, 1), seg_ids.reshape(1, -1)
    pad_col = pad_mask.reshape(-1, 1)
    tables = rotary(positions)
    flat_time = time_emb.reshape(slots, -1)
    time_cut = jnp.pad(flat_time, ((0, 16 - slots), (0, 0)))
    time_cut = jnp.transpose(time_cut.reshape(16, 4, -1), (1, 0, 2))
    w_ada = jnp.concatenate([w_ada1, w_ada2], axis=1)
    stream0, normed1, gamma1, gamma2, every, f_skip, f_qkv = front(
        inputs, skip_in, time_cut, seg_col, w_ada, w_skip, w_qkv
    )
    f_qkv = f_qkv.reshape(NB, width, -1)
    q, k, v, ctx, lse, f_out, fup0, fdn0, fup1, fdn1 = attend(
        normed1, f_qkv, tables, seg_col, pad_col, seg_row, w_out, w_up, w_down
    )
    output, g_out, d_stream1, d_ctx, d_gamma2, sup0, sdn0, *rest = mlp(
        stream0, ctx, f_out, gamma2, seg_col, seg_row, cotangent, w_up, w_down, fup0, fdn0, fup1, fdn1
    )
    g_qkv, d_low, d_gamma1, sup1, sdn1, sup2, sdn2, sup3, sdn3, s_out = attend_back(
        normed1, f_qkv, tables, seg_col, pad_col, seg_row, q, k, v, d_ctx, ctx, lse, gamma1,
        stream0, d_stream1, (*rest[:6], g_out),
    )
    dg_cut = jnp.concatenate([d.reshape(8, NB, -1) for d in (d_gamma1, d_gamma2)], axis=2)
    dg_cut = jnp.pad(jnp.transpose(dg_cut, (1, 0, 2)).astype(BF), ((0, 0), (0, 8), (0, 0)))
    d_input, d_skip, d_time, g_ada, s_skip, s_qkv = skip_back(
        inputs, skip_in, d_low, f_skip, w_ada, dg_cut, every, g_qkv.reshape(4, 2, 3, 2, 2, -1, UNIT)
    )
    s_up = jnp.concatenate([sup0, sup1, sup2, sup3], axis=1)
    s_down = jnp.stack([sdn0, sdn1, sdn2, sdn3]).reshape(4, 2, UNIT, UNIT)
    s_down = jnp.transpose(s_down, (1, 0, 2, 3)).reshape(w_down.shape)
    return (
        output, d_input, d_skip, d_time[:slots].reshape(time_emb.shape),
        s_skip, g_ada[:, :UNIT], s_qkv, s_out, g_ada[:, UNIT:], s_up, s_down,
    )


def plain(
    inputs, skip_in, time_emb, seg_ids, positions, pad_mask,
    w_skip, w_ada1, w_qkv, w_out, w_ada2, w_up, w_down, cotangent,
):
    slots = time_emb.shape[1]
    width = inputs.shape[1]
    seg_col, seg_row = seg_ids.reshape(-1, 1), seg_ids.reshape(1, -1)
    pad_col = pad_mask.reshape(-1, 1)
    tables = rotary(positions)
    flat_time = time_emb.reshape(slots, -1)
    time8 = jnp.pad(flat_time, ((0, 8 - slots), (0, 0)))
    f_skip, f_qkv, f_out, f_up, f_down, f_ada1, f_ada2 = [
        gathered(w) for w in (w_skip, w_qkv, w_out, w_up, w_down, w_ada1, w_ada2)
    ]
    ada = jnp.concatenate([f_ada1, f_ada2], axis=2)
    stream0, normed1, gamma1, gamma2 = plain_front(inputs, skip_in, f_skip, time8, ada, seg_col)
    q, k, v, ctx, lse = plain_attend(normed1, f_qkv, tables, seg_col, pad_col, seg_row)
    output, g_down, g_up, g_out, d_stream1, d_ctx, d_gamma2 = plain_mlp(
        stream0, ctx, f_out, gamma2, seg_col, seg_row, f_up, f_down, cotangent
    )
    g_qkv, d_low, d_gamma1 = plain_attend_back(
        normed1, f_qkv, tables, seg_col, pad_col, seg_row, q, k, v, d_ctx, ctx, lse,
        stream0, gamma1, d_stream1,
    )
    g_qkv = jnp.transpose(
        g_qkv.reshape(NB, 3, width, 128), (0, 2, 1, 3)
    ).reshape(NB, width, 3 * width // NB)
    g_skip, d_input, d_skip = plain_skip_back(inputs, skip_in, d_low, f_skip)
    d_gammas = jnp.stack([d_gamma1, d_gamma2]).astype(BF)[:, :slots]
    d_time = 0.0
    for d_gamma, part in zip(d_gammas, (f_ada1, f_ada2)):
        flat = jnp.transpose(part, (1, 0, 2)).reshape(width, width)
        d_time = d_time + jnp.einsum("ne,de->nd", d_gamma, flat, preferred_element_type=F32)
    g_ada = ada_grads(flat_time, d_gammas, *w_ada1.shape)
    return (
        output, d_input, d_skip, d_time.reshape(time_emb.shape),
        scattered(g_skip), g_ada[0], scattered(g_qkv), scattered(g_out), g_ada[1],
        scattered(g_up), scattered(g_down),
    )


def solution(mesh):
    rows = P(("dp", "fsdp"), None)
    cube = P(("dp", "fsdp"), None, None)
    tile = P("dp", "fsdp")
    fits = mesh.shape["dp"] == 4 and mesh.shape["fsdp"] == NB
    return jax.shard_map(
        fused if fits else plain,
        mesh=mesh,
        in_specs=(rows, rows, cube) + (rows,) * 3 + (tile,) * 7 + (rows,),
        out_specs=(rows, rows, rows, cube) + (tile,) * 7,
        check_vma=False,
    )
```

```python
import functools

import jax
import jax.numpy as jnp
from jax import lax
from jax.experimental import pallas as pl
from jax.experimental.pallas import tpu as pltpu
from jax.sharding import PartitionSpec as P

HD = 64
NB = 8
EPS = 1e-06
MASKED = -1e30
BF = jnp.bfloat16
F32 = jnp.float32
NN = (((1,), (0,)), ((), ()))
NT = (((1,), (1,)), ((), ()))
TN = (((0,), (0,)), ((), ()))
ROOT = 0.7978845608028654
CUBE = 0.044715


def dot(left, right, form=NN):
    return lax.dot_general(left, right, form, preferred_element_type=F32)


def params(**extra):
    return pltpu.CompilerParams(vmem_limit_bytes=60 << 20, **extra)


def whole(shape):
    return pl.BlockSpec(shape, lambda *_: (0,) * len(shape), pipeline_mode=pl.Buffered(1))


ANY = pl.BlockSpec(memory_space=pl.ANY)
UNIT = 128


def shaped(shape, kind):
    return jax.ShapeDtypeStruct(shape, kind)


def columns(ref, first, count, rows=slice(None)):
    return jnp.concatenate([ref[first + i, rows, :] for i in range(count)], axis=1)


def token_gain(seg, gamma):
    gain = gamma[0:1, :]
    for slot in range(1, 4):
        gain = jnp.where(seg == slot, gamma[slot : slot + 1, :], gain)
    return gain


def segment_sum(seg_row, values):
    slots = lax.broadcasted_iota(jnp.int32, (8, seg_row.shape[1]), 0)
    picked = (slots == seg_row).astype(BF)
    high = values.astype(BF)
    low = (values - high.astype(F32)).astype(BF)
    return dot(picked, high) + dot(picked, low)


def norm_back(grad, stream, gain):
    inverse = lax.rsqrt(jnp.mean(stream * stream, axis=-1, keepdims=True) + EPS)
    unit = stream * inverse
    scaled = grad * (1.0 + gain)
    d_stream = inverse * (scaled - unit * jnp.mean(scaled * unit, axis=-1, keepdims=True))
    return d_stream, grad * unit


def norm(stream, gain):
    inverse = lax.rsqrt(jnp.mean(stream * stream, axis=-1, keepdims=True) + EPS)
    return (stream * inverse * (1.0 + gain)).astype(BF)


def fill_bias(bias_ref, seg_ref, pad_ref, row_ref):
    length = seg_ref.shape[0]

    @pl.loop(0, length // UNIT)
    def _(t):
        rows = pl.ds(pl.multiple_of(t * UNIT, UNIT), UNIT)
        keys = lax.broadcasted_iota(jnp.int32, (UNIT, length), 0) + t * UNIT
        queries = lax.broadcasted_iota(jnp.int32, (UNIT, length), 1)
        allowed = (seg_ref[rows, :] == row_ref[0:1, :]) & (
            (pad_ref[rows, :] > 0) | (keys == queries)
        )
        bias_ref[rows, :] = jnp.where(allowed, 0.0, MASKED)


def turn(unit, cosine, before, after):
    return (
        unit * cosine
        + pltpu.roll(unit, 96, 1) * before
        + pltpu.roll(unit, 32, 1) * after
    )


def unit_spec(rows, base):
    def index(j):
        unit = base + 2 * j
        return (unit // 3, 0, unit % 3)

    return pl.BlockSpec((1, rows, 128), index)


def plain_front_body(x_ref, s_ref, w_ref, time_ref, ada_ref, seg_ref, stream_ref, normed_ref, g1_ref, g2_ref):
    length, width = x_ref.shape
    per = ada_ref.shape[2] // 2
    for f in range(NB):
        both = dot(time_ref[...], ada_ref[f])
        g1_ref[:, f * per : (f + 1) * per] = both[:, :per]
        g2_ref[:, f * per : (f + 1) * per] = both[:, per:]
    for i in range(NB // 2):
        tile = columns(w_ref, 2 * i, 2)
        part = dot(x_ref[...], tile[:width]) + dot(s_ref[...], tile[width:])
        stream_ref[:, i * part.shape[1] : (i + 1) * part.shape[1]] = part

    @pl.loop(0, length // 128)
    def _(t):
        rows = pl.ds(pl.multiple_of(t * 128, 128), 128)
        gain = token_gain(seg_ref[rows, :], g1_ref)
        normed_ref[rows, :] = norm(stream_ref[rows, :], gain)


def plain_front(inputs, skip_in, w_skip, time8, ada, seg_col):
    length, width = inputs.shape
    return pl.pallas_call(
        plain_front_body,
        out_shape=(
            shaped((length, width), F32),
            shaped((length, width), BF),
            shaped((8, width), F32),
            shaped((8, width), F32),
        ),
        compiler_params=params(),
        name="front",
    )(inputs, skip_in, w_skip, time8, ada, seg_col)


def plain_attend_body(
    n_ref, qa, qb, ka, kb, va, vb, cos_ref, lo_ref, hi_ref, seg_ref, pad_ref, row_ref,
    q_ref, k_ref, v_ref, c_ref, lse_ref, bias_ref,
):
    @pl.when(pl.program_id(0) == 0)
    def _():
        fill_bias(bias_ref, seg_ref, pad_ref, row_ref)

    normed = n_ref[...]
    for out, first, second, scale in ((q_ref, qa, qb, HD**-0.5), (k_ref, ka, kb, 1.0)):
        made = dot(normed, jnp.concatenate([first[0], second[0]], axis=1))
        for half in range(2):
            unit = made[:, half * 128 : (half + 1) * 128]
            turned = turn(unit, cos_ref[...], lo_ref[...], hi_ref[...])
            out[:, half * 128 : (half + 1) * 128] = (turned.astype(BF) * scale).astype(BF)
    v_ref[...] = dot(normed, jnp.concatenate([va[0], vb[0]], axis=1)).astype(BF)
    for head in range(4):
        lanes = slice(head * HD, (head + 1) * HD)
        scores = dot(k_ref[:, lanes], q_ref[:, lanes], NT) + bias_ref[...]
        largest = jnp.max(scores, axis=0, keepdims=True)
        exponent = jnp.exp(scores - largest)
        total = jnp.sum(exponent, axis=0, keepdims=True)
        mixed = dot(v_ref[:, lanes].T, exponent.astype(BF)) * (1.0 / total)
        c_ref[:, lanes] = mixed.T.astype(BF)
        lse_ref[head : head + 1, :] = largest + jnp.log(total)


def plain_attend(normed, w_qkv, tables, seg_col, pad_col, seg_row):
    length, width = normed.shape
    groups = width // 256
    units = [unit_spec(width, part * (width // 128) + e) for part in range(3) for e in range(2)]
    column = pl.BlockSpec((length, 256), lambda j: (0, j))
    wide = shaped((length, width), BF)
    return pl.pallas_call(
        plain_attend_body,
        grid=(groups,),
        in_specs=[whole((length, width))]
        + units
        + [whole((length, 128))] * 3
        + [whole((length, 1))] * 2
        + [whole((1, length))],
        out_specs=(column,) * 4 + (pl.BlockSpec((8, length), lambda j: (j, 0)),),
        out_shape=(wide,) * 4 + (shaped((8 * groups, length), F32),),
        scratch_shapes=[pltpu.VMEM((length, length), F32)],
        compiler_params=params(),
        name="attend",
    )(normed, *([w_qkv] * 6), *tables, seg_col, pad_col, seg_row)


def plain_mlp_body(
    stream0_ref, ctx_ref, wout_ref, g2_ref, seg_ref, row_ref, up_ref, down_ref, cot_ref,
    out_ref, gdown_ref, gup_ref, gout_ref, ds1_ref, dctx_ref, dg2_ref,
    s1_ref, n2_ref, acc_ref, dn_ref,
):
    step = pl.program_id(0)
    length, width = ctx_ref.shape
    tiles = length // 128

    @pl.when(step == 0)
    def _():
        @pl.loop(0, NB // 2)
        def _(i):
            lanes = pl.ds(pl.multiple_of(i * 256, 256), 256)
            s1_ref[:, lanes] = stream0_ref[:, lanes] + dot(ctx_ref[...], columns(wout_ref, 2 * i, 2))

        @pl.loop(0, tiles)
        def _(t):
            rows = pl.ds(pl.multiple_of(t * 128, 128), 128)
            n2_ref[rows, :] = norm(s1_ref[rows, :], token_gain(seg_ref[rows, :], g2_ref))

        acc_ref[...] = jnp.zeros_like(acc_ref)
        dn_ref[...] = jnp.zeros_like(dn_ref)

    cot = cot_ref[...]
    up = up_ref[0]
    down = columns(down_ref, 0, NB)
    hidden = dot(n2_ref[...], up)
    square = hidden * hidden
    tanh = jnp.tanh(ROOT * hidden * (1.0 + CUBE * square))
    active = (0.5 * hidden * (1.0 + tanh)).astype(BF)
    slope = 0.5 * (1.0 + tanh) + 0.5 * hidden * (1.0 - tanh * tanh) * (
        ROOT * (1.0 + 3.0 * CUBE * square)
    )
    d_pre = (dot(cot, down, NT) * slope).astype(BF)
    acc_ref[...] += dot(active, down)
    dn_ref[...] += dot(d_pre, up, NT)
    grad = dot(active, cot, TN).astype(BF)
    for f in range(NB):
        gdown_ref[f] = grad[:, f * gdown_ref.shape[2] : (f + 1) * gdown_ref.shape[2]]
    gup_ref[0] = dot(n2_ref[...], d_pre, TN).astype(BF)

    @pl.when(step == pl.num_programs(0) - 1)
    def _():
        dg2_ref[...] = jnp.zeros_like(dg2_ref)

        @pl.loop(0, tiles)
        def _(t):
            rows = pl.ds(pl.multiple_of(t * 128, 128), 128)
            stream = s1_ref[rows, :]
            out_ref[rows, :] = (stream + acc_ref[rows, :]).astype(BF)
            gain = token_gain(seg_ref[rows, :], g2_ref)
            term, d_gain = norm_back(dn_ref[rows, :], stream, gain)
            d_stream = cot_ref[rows, :].astype(F32) + term
            ds1_ref[rows, :] = d_stream
            n2_ref[rows, :] = d_stream.astype(BF)
            dg2_ref[...] += segment_sum(row_ref[:, rows], d_gain)

        @pl.loop(0, NB // 2)
        def _(i):
            lanes = pl.ds(pl.multiple_of(i * 256, 256), 256)
            part = dot(ctx_ref[...], n2_ref[:, lanes], TN).astype(BF)
            gout_ref[2 * i] = part[:, :128]
            gout_ref[2 * i + 1] = part[:, 128:]

        acc_ref[...] = jnp.zeros_like(acc_ref)

        @pl.loop(0, NB // 2)
        def _(i):
            lanes = pl.ds(pl.multiple_of(i * 256, 256), 256)
            acc_ref[...] += dot(n2_ref[:, lanes], columns(wout_ref, 2 * i, 2), NT)

        dctx_ref[...] = acc_ref[...].astype(BF)


def plain_mlp(stream0, ctx, w_out, gamma2, seg_col, seg_row, w_up, w_down, cotangent):
    length, width = ctx.shape
    hidden = w_down.shape[1]
    piece = hidden // NB
    per = width // NB
    full = whole((length, width))
    return pl.pallas_call(
        plain_mlp_body,
        grid=(NB,),
        in_specs=[
            full,
            full,
            whole((NB, width, per)),
            whole((8, width)),
            whole((length, 1)),
            whole((1, length)),
            pl.BlockSpec((1, width, piece), lambda j: (j, 0, 0)),
            pl.BlockSpec((NB, piece, per), lambda j: (0, j, 0)),
            full,
        ],
        out_specs=(
            full,
            pl.BlockSpec((NB, piece, per), lambda j: (0, j, 0)),
            pl.BlockSpec((1, width, piece), lambda j: (j, 0, 0)),
            whole((NB, width, per)),
            full,
            full,
            whole((8, width)),
        ),
        out_shape=(
            shaped((length, width), BF),
            shaped((NB, hidden, per), BF),
            shaped((NB, width, piece), BF),
            shaped((NB, width, per), BF),
            shaped((length, width), F32),
            shaped((length, width), BF),
            shaped((8, width), F32),
        ),
        scratch_shapes=[
            pltpu.VMEM((length, width), F32),
            pltpu.VMEM((length, width), BF),
            pltpu.VMEM((length, width), F32),
            pltpu.VMEM((length, width), F32),
        ],
        compiler_params=params(),
        name="mlp",
    )(stream0, ctx, w_out, gamma2, seg_col, seg_row, w_up, w_down, cotangent)


def plain_attend_back_body(
    n_ref, qa, qb, ka, kb, va, vb, cos_ref, lo_ref, hi_ref, seg_ref, pad_ref, row_ref,
    q_ref, k_ref, v_ref, g_ref, c_ref, lse_ref, s0_ref, g1_ref, ds1_ref,
    gw_ref, dlow_ref, dg1_ref, bias_ref, dn_ref, dq_ref, dk_ref, dv_ref,
):
    step = pl.program_id(0)
    length, width = n_ref.shape

    @pl.when(step == 0)
    def _():
        fill_bias(bias_ref, seg_ref, pad_ref, row_ref)
        dn_ref[...] = jnp.zeros_like(dn_ref)

    ones = jnp.ones((8, HD), BF)
    for head in range(4):
        lanes = slice(head * HD, (head + 1) * HD)
        query, key, value = q_ref[:, lanes], k_ref[:, lanes], v_ref[:, lanes]
        grad = g_ref[:, lanes]
        both = grad.astype(F32) * c_ref[:, lanes].astype(F32)
        high = both.astype(BF)
        low = (both - high.astype(F32)).astype(BF)
        delta = (dot(ones, high, NT) + dot(ones, low, NT))[0:1, :]
        probs = jnp.exp(dot(key, query, NT) + bias_ref[...] - lse_ref[head : head + 1, :])
        d_scores = (probs * (dot(value, grad, NT) - delta)).astype(BF)
        dv_ref[:, lanes] = dot(probs.astype(BF), grad)
        dk_ref[:, lanes] = dot(d_scores, query)
        dq_ref[:, lanes] = dot(key.T, d_scores).T * HD**-0.5
    for part, (src, first, second) in enumerate(
        ((dq_ref, qa, qb), (dk_ref, ka, kb), (dv_ref, va, vb))
    ):
        if part < 2:
            made = jnp.concatenate(
                [
                    turn(src[:, half * 128 : (half + 1) * 128], cos_ref[...], -lo_ref[...], -hi_ref[...])
                    for half in range(2)
                ],
                axis=1,
            ).astype(BF)
        else:
            made = src[...].astype(BF)
        grad = dot(n_ref[...], made, TN).astype(BF)
        gw_ref[part, 0] = grad[:, :128]
        gw_ref[part, 1] = grad[:, 128:]
        dn_ref[...] += dot(made, jnp.concatenate([first[0], second[0]], axis=1), NT)

    @pl.when(step == pl.num_programs(0) - 1)
    def _():
        dg1_ref[...] = jnp.zeros_like(dg1_ref)

        @pl.loop(0, length // 128)
        def _(t):
            rows = pl.ds(pl.multiple_of(t * 128, 128), 128)
            gain = token_gain(seg_ref[rows, :], g1_ref)
            term, d_gain = norm_back(dn_ref[rows, :], s0_ref[rows, :], gain)
            dlow_ref[rows, :] = (ds1_ref[rows, :] + term).astype(BF)
            dg1_ref[...] += segment_sum(row_ref[:, rows], d_gain)


def plain_attend_back(
    normed, w_qkv, tables, seg_col, pad_col, seg_row, q, k, v, d_ctx, ctx, lse, stream0, gamma1, d_stream1
):
    length, width = normed.shape
    groups = width // 256
    units = [unit_spec(width, part * (width // 128) + e) for part in range(3) for e in range(2)]
    column = pl.BlockSpec((length, 256), lambda j: (0, j))
    full = whole((length, width))
    return pl.pallas_call(
        plain_attend_back_body,
        grid=(groups,),
        in_specs=[full]
        + units
        + [whole((length, 128))] * 3
        + [whole((length, 1))] * 2
        + [whole((1, length))]
        + [column] * 5
        + [pl.BlockSpec((8, length), lambda j: (j, 0)), full, whole((8, width)), full],
        out_specs=(
            pl.BlockSpec((3, 2, width, 128), lambda j: (0, j, 0, 0)),
            full,
            whole((8, width)),
        ),
        out_shape=(
            shaped((3, width // 128, width, 128), BF),
            shaped((length, width), BF),
            shaped((8, width), F32),
        ),
        scratch_shapes=[pltpu.VMEM((length, length), F32), pltpu.VMEM((length, width), F32)]
        + [pltpu.VMEM((length, 256), F32)] * 3,
        compiler_params=params(),
        name="attend_back",
    )(
        normed, *([w_qkv] * 6), *tables, seg_col, pad_col, seg_row, q, k, v, d_ctx, ctx, lse,
        stream0, gamma1, d_stream1,
    )


def plain_skip_back_body(x_ref, s_ref, d_ref, w_ref, gw_ref, dx_ref, ds_ref):
    low = d_ref[...]
    per = 256
    width = x_ref.shape[1]

    @pl.loop(0, width // per)
    def _(i):
        lanes = pl.ds(pl.multiple_of(i * per, per), per)
        part = d_ref[:, lanes]
        top = dot(x_ref[...], part, TN).astype(BF)
        end = dot(s_ref[...], part, TN).astype(BF)
        for e in range(2):
            gw_ref[2 * i + e, :width, :] = top[:, e * 128 : (e + 1) * 128]
            gw_ref[2 * i + e, width:, :] = end[:, e * 128 : (e + 1) * 128]

    tall = 256

    @pl.loop(0, width // tall)
    def _(i):
        rows = pl.ds(pl.multiple_of(i * tall, tall), tall)
        rest = pl.ds(pl.multiple_of(width + i * tall, tall), tall)
        dx_ref[:, rows] = dot(low, columns(w_ref, 0, NB, rows), NT)
        ds_ref[:, rows] = dot(low, columns(w_ref, 0, NB, rest), NT)


def plain_skip_back(inputs, skip_in, d_low, w_skip):
    length, width = inputs.shape
    return pl.pallas_call(
        plain_skip_back_body,
        out_shape=(
            shaped(w_skip.shape, BF),
            shaped((length, width), F32),
            shaped((length, width), F32),
        ),
        compiler_params=params(),
        name="skip_back",
    )(inputs, skip_in, d_low, w_skip)


class Place:
    def __init__(self):
        dp, fs = lax.axis_index("dp"), lax.axis_index("fsdp")
        self.y, self.x, self.z, self.c = dp // 2, dp % 2, fs // 2, fs % 2
        self.dp, self.fs = dp, fs

    def across_x(self):
        return (self.y * 2 + 1 - self.x, self.fs)

    def across_y(self):
        return ((1 - self.y) * 2 + self.x, self.fs)

    def sibling(self):
        return (self.dp, self.z * 2 + 1 - self.c)

    def along_z(self, hop):
        return (self.dp, ((self.z + hop) % 4) * 2 + self.c)

    def on_dp(self, index):
        return (index, self.fs)

    def on_fsdp(self, index):
        return (self.dp, index)

    def greet(self, wide=False):
        barrier = pltpu.get_barrier_semaphore()
        if wide:
            peers = [self.on_dp((self.dp + hop) % 4) for hop in range(1, 4)]
            peers += [self.on_fsdp((self.fs + hop) % NB) for hop in range(1, NB)]
        else:
            peers = [self.across_x(), self.across_y(), self.sibling()]
            peers += [self.along_z(hop) for hop in (1, 2, 3)]
        for peer in peers:
            pl.semaphore_signal(barrier, inc=1, device_id=peer, device_id_type=pl.DeviceIdType.MESH)
        pl.semaphore_wait(barrier, len(peers))


def remote(src, dst, send, recv, peer):
    return pltpu.make_async_remote_copy(
        src_ref=src, dst_ref=dst, send_sem=send, recv_sem=recv,
        device_id=peer, device_id_type=pl.DeviceIdType.MESH,
    )


class Lazy:
    def __init__(self, plan, send, recv):
        self.plan, self.send, self.recv = plan, send, recv

    def __len__(self):
        return len(self.plan)

    def __getitem__(self, i):
        if isinstance(i, slice):
            return [self[k] for k in range(*i.indices(len(self)))]
        if i >= len(self.plan):
            raise IndexError
        src, dst, peer = self.plan[i]
        return remote(src, dst, self.send.at[i], self.recv.at[i], peer)


def flow(*copy):
    return pltpu.make_async_copy(*copy)


class Gather:
    sems = 8

    def __init__(self, place, source, full, rows, flip):
        self.me, self.source, self.full, self.rows, self.flip = place, source, full, rows, flip

    def bind(self, send, recv, local):
        self.send, self.recv, self.local = send, recv, local

    def copies(self):
        me, full, rows = self.me, self.full, self.rows
        spot = full.at[me.z, me.c, me.y, me.x, rows, :]
        line = full.at[:, me.c, me.y, me.x, rows, :]
        if self.flip:
            pair = full.at[:, me.c, :, me.x, rows, :]
            near, far = me.across_y(), me.across_x()
            got = full.at[:, me.c, 1 - me.y, me.x, rows, :]
            late = full.at[:, me.c, :, 1 - me.x, rows, :]
        else:
            pair = full.at[:, me.c, me.y, :, rows, :]
            near, far = me.across_x(), me.across_y()
            got = full.at[:, me.c, me.y, 1 - me.x, rows, :]
            late = full.at[:, me.c, 1 - me.y, :, rows, :]
        sib = me.sibling()
        plan = [(self.source, spot, me.along_z(hop)) for hop in (1, 2, 3)]
        plan += [(line, line, near), (pair, pair, far), (line, line, sib), (got, got, sib), (late, late, sib)]
        return Lazy(plan, self.send, self.recv), (self.source, spot, self.local)

    def stage(self, number):
        made, keep = self.copies()
        if number == 0:
            flow(*keep).start()
            for copy in made[:3]:
                copy.start()
        elif number == 1:
            flow(*keep).wait()
            for copy in made[:3]:
                copy.wait_recv()
            made[3].start()
            made[5].start()
        elif number == 2:
            made[3].wait_recv()
            made[4].start()
            made[6].start()
        elif number == 3:
            made[4].wait_recv()
            made[7].start()
        else:
            for copy in made[5:]:
                copy.wait_recv()
            for copy in made[:]:
                copy.wait_send()


class Reduce:
    sems = 6

    def __init__(self, place, theirs, mine, own, room, out, flip, load):
        self.me, self.theirs, self.mine, self.own = place, theirs, mine, own
        self.other, self.half, self.quarter, self.parts = room
        self.out, self.flip, self.load = out, flip, load

    @staticmethod
    def room(count, per):
        return [
            pltpu.VMEM((4, 2, 2, count, per), BF),
            pltpu.VMEM((4, 2, count, per), BF),
            pltpu.VMEM((4, count, per), BF),
            pltpu.VMEM((3, count, per), BF),
        ]

    def bind(self, send, recv, local):
        self.send, self.recv, self.local = send, recv, local

    def copies(self):
        me = self.me
        if self.flip:
            give, near = self.own.at[:, :, 1 - me.x], me.across_x()
            give2, far = self.half.at[:, 1 - me.y], me.across_y()
        else:
            give, near = self.own.at[:, 1 - me.y], me.across_y()
            give2, far = self.half.at[:, 1 - me.x], me.across_x()
        plan = [(self.theirs, self.other, me.sibling()), (give, self.half, near), (give2, self.quarter, far)]
        plan += [
            (self.quarter.at[(me.z + hop) % 4], self.parts.at[hop - 1], me.along_z(hop)) for hop in (1, 2, 3)
        ]
        return Lazy(plan, self.send, self.recv), (self.mine, self.own, self.local)

    def stage(self, number):
        me = self.me
        made, load = self.copies()
        if number == 0:
            made[0].start()
            if self.load:
                flow(*load).start()
        elif number == 1:
            if self.load:
                flow(*load).wait()
            made[0].wait_recv()

            @pl.loop(0, 4)
            def _(z):
                self.own[z] = self.own[z] + self.other[z]

            made[1].start()
        elif number == 2:
            made[1].wait_recv()

            @pl.loop(0, 4)
            def _(z):
                kept = self.own[z, :, me.x] if self.flip else self.own[z, me.y]
                self.half[z] = self.half[z] + kept

            made[2].start()
        elif number == 3:
            made[0].wait_send()
            made[1].wait_send()
            made[2].wait_recv()
            kept = me.y if self.flip else me.x

            @pl.loop(0, 4)
            def _(z):
                self.quarter[z] = self.quarter[z] + self.half[z, kept]

            for copy in made[3:]:
                copy.start()
        else:
            for copy in made[3:]:
                copy.wait_recv()
            total = self.quarter[me.z].astype(F32)
            for i in range(3):
                total = total + self.parts[i].astype(F32)
            self.out[...] = total
            for copy in made[2:]:
                copy.wait_send()


class Swap:
    def __init__(self, place, axis, what, into, send, recv):
        count = 4 if axis == "dp" else NB
        at = place.dp if axis == "dp" else place.fs
        find = place.on_dp if axis == "dp" else place.on_fsdp
        self.at, self.what, self.into = at, what, into
        self.plan = []
        for hop in range(1, count):
            peer = (at + hop) % count
            self.plan.append((what(peer), into(at), send.at[hop - 1], recv.at[hop - 1], find(peer)))

    def start(self):
        for copy in self.plan:
            remote(*copy).start()

    def wait(self):
        for copy in self.plan:
            remote(*copy).wait()


class Traffic:
    def __init__(self):
        self.todo, self.pieces = {}, []

    def add(self, hooks, pieces):
        self.pieces += pieces
        for piece, places in zip(pieces, hooks, strict=True):
            for stage, hook in enumerate(places):
                self.todo.setdefault(hook, []).append((stage, piece))

    def bind(self, send, recv, local):
        for i, piece in enumerate(self.pieces):
            piece.bind(send.at[i], recv.at[i], local.at[i])

    def at(self, hook):
        for stage, piece in sorted(self.todo.pop(hook, []), key=lambda item: -item[0]):
            piece.stage(stage)

    def fire(self, step, steps, per, hook):
        for s in range(steps):
            if s * per + hook in self.todo:
                pl.when(step == s)(functools.partial(self.at, s * per + hook))

    def inside(self, index, first, count):
        for s in range(count):
            if first + s in self.todo:
                pl.when(index == s)(functools.partial(self.at, first + s))

    def drain(self):
        for hook in sorted(self.todo):
            self.at(hook)


def semaphores(count, kind):
    return [pltpu.SemaphoreType.DMA((count, kind))] * 2 + [pltpu.SemaphoreType.DMA((count,))]


def full_of(rows, per):
    return shaped((4, 2, 2, 2, rows, per), BF)


def halves(rows):
    return [(pl.ds(e * (rows // 2), rows // 2), e == 1) for e in range(2)]


def up_pair(me, shard, full, q):
    lanes = pl.ds(q * UNIT, UNIT)
    return [Gather(me, shard.at[rows, lanes], full, rows, flip) for rows, flip in halves(shard.shape[0])]


def down_pair(me, shard, full, q):
    tall = shard.shape[0] // 2
    step = tall // 4
    return [
        Gather(me, shard.at[pl.ds(e * tall + q * step, step), :], full, pl.ds(e * step, step), e == 1)
        for e in range(2)
    ]


def row_pieces(me, shard, full, count):
    tall = shard.shape[0] // count
    return [
        Gather(me, shard.at[pl.ds(i * tall, tall), :], full, pl.ds(i * tall, tall), i % 2 == 1)
        for i in range(count)
    ]


FRONT_HOOKS = (
    (1, 4, 7, 13, 14), (1, 4, 7, 13, 14),
    (4, 7, 10, 18, 19), (4, 7, 10, 18, 19),
    (0, 1, 3, 7, 8), (0, 1, 3, 7, 8),
    (3, 6, 9, 16, 18), (3, 6, 9, 16, 18),
    (9, 13, 18, 25, 28), (9, 13, 18, 25, 28),
    (6, 9, 15, 22, 25), (6, 9, 15, 22, 25),
    (0, 2, 5, 11, 13), (0, 2, 5, 10, 12),
    (13, 17, 21, 28, 31), (13, 17, 21, 28, 31),
)
FRONT_READY = 19
ATTEND_HOOKS = (
    (7, 10, 12, 15, 16), (7, 10, 12, 15, 16),
    (1, 4, 6, 9, 10), (1, 4, 6, 9, 10),
    (0, 1, 3, 5, 6), (0, 1, 3, 5, 6),
    (6, 9, 11, 14, 15), (6, 9, 11, 14, 15),
    (2, 5, 7, 10, 11), (2, 5, 7, 10, 11),
)
MLP_HOOKS = (
    (0, 2, 5, 12, 13), (0, 2, 5, 12, 13),
    (0, 2, 5, 12, 13), (0, 2, 5, 12, 13),
    (14, 17, 20, 23, 24), (14, 17, 20, 23, 24),
    (12, 15, 17, 21, 23), (12, 15, 17, 21, 23),
    (8, 10, 16, 18, 23), (8, 10, 16, 18, 23),
    (8, 10, 16, 18, 23), (8, 10, 16, 18, 23),
)
ATTEND_BACK_HOOKS = (
    (0, 1, 4, 8, 10), (0, 1, 4, 8, 10),
    (1, 2, 8, 11, 14), (1, 2, 8, 11, 14),
    (7, 8, 13, 16, 19), (7, 8, 13, 16, 19),
    (2, 3, 9, 12, 16), (2, 3, 9, 12, 16),
    (3, 4, 10, 13, 17), (3, 4, 10, 13, 17),
    (11, 12, 16, 18, 20), (11, 12, 16, 18, 20),
    (12, 13, 17, 19, 20), (12, 13, 17, 19, 20),
)
SKIP_BACK_HOOKS = (
    (5, 6, 8, 10, 11), (5, 6, 8, 10, 11),
    (4, 5, 7, 8, 9), (4, 5, 7, 8, 9),
    (6, 7, 9, 11, 13), (6, 7, 9, 11, 13),
    (0, 2, 4, 6, 7), (0, 2, 4, 6, 7),
    (2, 4, 6, 7, 8), (2, 4, 6, 7, 8),
    (8, 9, 11, 13, 14), (8, 9, 11, 13, 14),
    (11, 12, 14, 15, 18), (11, 12, 14, 15, 18),
    (7, 8, 10, 12, 14), (7, 8, 10, 12, 14),
    (8, 9, 12, 14, 15), (8, 9, 12, 14, 15),
    (10, 11, 14, 15, 18), (10, 11, 14, 15, 18),
)


def front_body(
    x_ref, s_ref, time_ref, row_ref, freq_ref, ada_ref, skip_ref, qkv_ref,
    stream_ref, normed_ref, g1_ref, g2_ref, slots, seg_ref, pad_ref, cos_ref, lo_ref, hi_ref, fskip_ref, fqkv_ref,
    w_ref, part, got, summed, gam, w_sem, sends, recvs, send, recv, local,
):
    length, width = x_ref.shape
    per = ada_ref.shape[1] // 2
    me = Place()
    me.greet(True)
    traffic = Traffic()
    plan = row_pieces(me, skip_ref, fskip_ref, 8) + row_pieces(me, qkv_ref, fqkv_ref, 8)
    traffic.add(FRONT_HOOKS, plan)
    traffic.bind(send, recv, local)
    lay = functools.partial(pl.ds, 0)
    swaps = [
        Swap(me, "dp", lambda p: time_ref.at[p], lambda m: slots.at[m, me.fs], sends.at[0], recvs.at[0]),
        Swap(me, "fsdp", lambda p: slots.at[:, me.fs], lambda m: slots.at[:, m], sends.at[1], recvs.at[1]),
        Swap(me, "dp", lambda p: part.at[p, :, lay(8), :], lambda m: got.at[m], sends.at[2], recvs.at[2]),
        Swap(me, "fsdp", lambda p: summed.at[p], lambda m: gam.at[m], sends.at[3], recvs.at[3]),
    ]

    def prepare(t):
        rows = pl.ds(pl.multiple_of(t * UNIT, UNIT), UNIT)
        turned = row_ref[:, rows].T
        seg_ref[rows, :] = turned[:, 0:1]
        pad_ref[rows, :] = turned[:, 1:2]
        phase = turned[:, 2:3].astype(F32) * freq_ref[0:1, :]
        cosine, sine = jnp.cos(phase), jnp.sin(phase)
        early = lax.broadcasted_iota(jnp.int32, phase.shape, 1) % HD < HD // 2
        cos_ref[rows, :] = cosine
        lo_ref[rows, :] = jnp.where(early, -sine, 0.0)
        hi_ref[rows, :] = jnp.where(early, 0.0, sine)

    slots[me.dp, me.fs] = time_ref[me.dp]
    swaps[0].start()
    for hook in range(FRONT_READY + 1):
        traffic.at(hook)
        if hook == 2:
            pl.loop(0, length // UNIT)(prepare)
        elif hook == 4:
            swaps[0].wait()
            swaps[1].start()
        elif hook == 8:
            swaps[1].wait()
            made = dot(slots[...].reshape(4 * NB * 16, -1), ada_ref[...])
            part[...] = made.reshape(part.shape)
            got[me.dp] = part[me.dp, :, :8, :]
            swaps[2].start()
        elif hook == 12:
            swaps[2].wait()
            summed[...] = got[0] + got[1] + got[2] + got[3]
            gam[me.fs] = summed[me.fs]
            swaps[3].start()
    load = flow(fskip_ref, w_ref, w_sem)
    load.start()
    swaps[3].wait()
    for f in range(NB):
        g1_ref[:, f * per : (f + 1) * per] = gam[f, :, :per]
        g2_ref[:, f * per : (f + 1) * per] = gam[f, :, per:]
    load.wait()

    def stream(i):
        tile = jnp.concatenate([w_ref[i, c].reshape(2 * width, UNIT) for c in range(2)], axis=1)
        lanes = pl.ds(pl.multiple_of(i * 2 * UNIT, 2 * UNIT), 2 * UNIT)
        stream_ref[:, lanes] = dot(x_ref[...], tile[:width]) + dot(s_ref[...], tile[width:])

    def normalise(t):
        rows = pl.ds(pl.multiple_of(t * UNIT, UNIT), UNIT)
        gain = token_gain(seg_ref[rows, :], g1_ref)
        normed_ref[rows, :] = norm(stream_ref[rows, :], gain)

    @pl.loop(0, 4)
    def _(i):
        stream(i)
        traffic.inside(i, FRONT_READY + 1, 4)

    @pl.loop(0, length // UNIT)
    def _(t):
        normalise(t)
        traffic.inside(t, FRONT_READY + 5, 8)

    traffic.drain()


def front(inputs, skip_in, time_cut, rows, freq, w_ada, w_skip, w_qkv):
    length, width = inputs.shape
    fulls = [full_of(*w.shape) for w in (w_skip, w_qkv)]
    vmem = pl.BlockSpec(memory_space=pltpu.VMEM)
    per = w_ada.shape[1]
    return pl.pallas_call(
        front_body,
        in_specs=[vmem] * 6 + [ANY] * 2,
        out_specs=(vmem,) * 10 + (ANY,) * 2,
        out_shape=(
            shaped((length, width), F32),
            shaped((length, width), BF),
            shaped((8, width), F32),
            shaped((8, width), F32),
            shaped((4, NB, 16, w_ada.shape[0]), BF),
            shaped((length, 1), jnp.int32),
            shaped((length, 1), jnp.int32),
            shaped((length, UNIT), F32),
            shaped((length, UNIT), F32),
            shaped((length, UNIT), F32),
            *fulls,
        ),
        scratch_shapes=[
            pltpu.VMEM(fulls[0].shape, BF),
            pltpu.VMEM((4, NB, 16, per), F32),
            pltpu.VMEM((4, NB, 8, per), F32),
            pltpu.VMEM((NB, 8, per), F32),
            pltpu.VMEM((NB, 8, per), F32),
            pltpu.SemaphoreType.DMA,
            pltpu.SemaphoreType.DMA((4, NB - 1)),
            pltpu.SemaphoreType.DMA((4, NB - 1)),
        ]
        + semaphores(16, Gather.sems),
        compiler_params=params(collective_id=0, has_side_effects=True),
        name="front",
    )(inputs, skip_in, time_cut, rows, freq, w_ada, w_skip, w_qkv)


def attend_body(
    n_ref, qa, qb, ka, kb, va, vb, cos_ref, lo_ref, hi_ref, seg_ref, pad_ref, row_ref, out_ref, up_ref, down_ref,
    q_ref, k_ref, v_ref, c_ref, lse_ref, fout_ref, fup0_ref, fdn0_ref, fup1_ref, fdn1_ref,
    bias_ref, send, recv, local,
):
    step = pl.program_id(0)
    last = pl.num_programs(0) - 1
    me = Place()
    traffic = Traffic()
    pieces = (
        up_pair(me, up_ref, fup0_ref, 0)
        + down_pair(me, down_ref, fdn0_ref, 0)
        + up_pair(me, up_ref, fup1_ref, 1)
        + down_pair(me, down_ref, fdn1_ref, 1)
        + row_pieces(me, out_ref, fout_ref, 2)
    )
    traffic.add(ATTEND_HOOKS, pieces)
    traffic.bind(send, recv, local)
    fire = functools.partial(traffic.fire, step, 4, 4)

    @pl.when(step == 0)
    def _():
        me.greet()
        traffic.at(0)
        fill_bias(bias_ref, seg_ref, pad_ref, row_ref)

    normed = n_ref[...]
    for out, first, second, scale in ((q_ref, qa, qb, HD**-0.5), (k_ref, ka, kb, 1.0)):
        made = dot(normed, jnp.concatenate([first[0], second[0]], axis=1))
        for half in range(2):
            unit = made[:, half * 128 : (half + 1) * 128]
            turned = turn(unit, cos_ref[...], lo_ref[...], hi_ref[...])
            out[:, half * 128 : (half + 1) * 128] = (turned.astype(BF) * scale).astype(BF)
    v_ref[...] = dot(normed, jnp.concatenate([va[0], vb[0]], axis=1)).astype(BF)
    for head in range(4):
        fire(head)
        lanes = slice(head * HD, (head + 1) * HD)
        scores = dot(k_ref[:, lanes], q_ref[:, lanes], NT) + bias_ref[...]
        largest = jnp.max(scores, axis=0, keepdims=True)
        exponent = jnp.exp(scores - largest)
        total = jnp.sum(exponent, axis=0, keepdims=True)
        mixed = dot(v_ref[:, lanes].T, exponent.astype(BF)) * (1.0 / total)
        c_ref[:, lanes] = mixed.T.astype(BF)
        lse_ref[head : head + 1, :] = largest + jnp.log(total)
    pl.when(step == last)(traffic.drain)


def attend(normed, w_qkv, tables, seg_col, pad_col, seg_row, w_out, w_up, w_down):
    length, width = normed.shape
    groups = width // 256
    units = [unit_spec(width, part * (width // 128) + e) for part in range(3) for e in range(2)]
    column = pl.BlockSpec((length, 256), lambda j: (0, j))
    wide = shaped((length, width), BF)
    quarter = full_of(w_up.shape[0], UNIT)
    return pl.pallas_call(
        attend_body,
        grid=(groups,),
        in_specs=[whole((length, width))]
        + units
        + [whole((length, 128))] * 3
        + [whole((length, 1))] * 2
        + [whole((1, length))]
        + [ANY] * 3,
        out_specs=(column,) * 4 + (pl.BlockSpec((8, length), lambda j: (j, 0)),) + (ANY,) * 5,
        out_shape=(wide,) * 4
        + (shaped((8 * groups, length), F32), full_of(*w_out.shape)) + (quarter,) * 4,
        scratch_shapes=[pltpu.VMEM((length, length), F32)] + semaphores(10, Gather.sems),
        compiler_params=params(collective_id=1, has_side_effects=True),
        name="attend",
    )(normed, *([w_qkv] * 6), *tables, seg_col, pad_col, seg_row, w_out, w_up, w_down)


def mlp_body(
    stream0_ref, ctx_ref, wout_ref, g2_ref, seg_ref, row_ref, cot_ref,
    up_ref, down_ref, fup0, fdn0, fup1, fdn1,
    acts_ref, keep1_ref, gout_ref, ds1_ref, dctx_ref, dg2_ref, sup0, sdn0, gup1, gdn1, gup2, gdn2, gup3, gdn3,
    fup2, fdn2, fup3, fdn3,
    s1_ref, n2_ref, dn_ref, up_tile, dn_tile, act_ref, pre_ref, stage_up, stage_dn,
    sem, gsend, grecv, glocal, rsend, rrecv, rlocal, *room,
):
    step = pl.program_id(0)
    steps = 8
    length, width = ctx_ref.shape
    tiles = length // UNIT
    me = Place()
    gather, reduce = Traffic(), Traffic()
    pieces = (
        up_pair(me, up_ref, fup2, 2)
        + down_pair(me, down_ref, fdn2, 2)
        + up_pair(me, up_ref, fup3, 3)
        + down_pair(me, down_ref, fdn3, 3)
    )
    gather.add(MLP_HOOKS[:8], pieces)
    gather.bind(gsend, grecv, glocal)
    count = 0
    for q, (sup, sdn) in enumerate(((sup0, sdn0),)):
        made = []
        for rows, flip in halves(2 * UNIT):
            theirs = stage_up.at[q, 1 - me.c, :, :, :, rows, :]
            mine = stage_up.at[q, me.c, :, :, :, rows, :]
            made.append(Reduce(me, theirs, mine, mine, room[4 * count : 4 * count + 4], sup.at[rows, :], flip, False))
            count += 1
        for e in range(2):
            theirs = stage_dn.at[q, e, :, 1 - me.c]
            mine = stage_dn.at[q, e, :, me.c]
            rows = pl.ds(e * UNIT, UNIT)
            made.append(Reduce(me, theirs, mine, mine, room[4 * count : 4 * count + 4], sdn.at[rows, :], e == 1, False))
            count += 1
        reduce.add(MLP_HOOKS[8:], made)
    reduce.bind(rsend, rrecv, rlocal)
    ups, downs = (fup0, fup1, fup2, fup3), (fdn0, fdn1, fdn2, fdn3)
    saves = {2: (gup1, gdn1), 4: (gup2, gdn2), 6: (gup3, gdn3)}

    def tile_loads(s):
        q, e = s // 2, s % 2
        return (
            flow(ups[q].at[:, e], up_tile.at[s % 2], sem.at[0, s % 2]),
            flow(downs[q].at[:, :, :, :, pl.ds(e * UNIT, UNIT), :], dn_tile.at[s % 2], sem.at[1, s % 2]),
        )

    def grad_saves(s):
        q, e = s // 2, s % 2
        gup, gdn = saves[2 * q]
        return (
            flow(stage_up.at[q % 2, e], gup.at[e], sem.at[2, s - 2]),
            flow(stage_dn.at[q % 2, e], gdn.at[e], sem.at[3, s - 2]),
        )

    def act_save(s):
        return flow(act_ref.at[s % 2], acts_ref.at[s], sem.at[1, 2 + s % 2])

    def hook(which):
        gather.fire(step, steps, 4, which)
        reduce.fire(step, steps, 4, which)

    @pl.when(step == 0)
    def _():
        me.greet()
        gather.at(0)
        for load in tile_loads(0):
            load.start()
        first = flow(stream0_ref, s1_ref, sem.at[2, 0])
        first.start()
        first.wait()
        for i in range(4):
            lanes = slice(i * 2 * UNIT, (i + 1) * 2 * UNIT)
            tile = jnp.concatenate([wout_ref[i, c].reshape(width, UNIT) for c in range(2)], axis=1)
            s1_ref[:, lanes] += dot(ctx_ref[...], tile)

        @pl.loop(0, tiles)
        def _(t):
            rows = pl.ds(pl.multiple_of(t * UNIT, UNIT), UNIT)
            n2_ref[rows, :] = norm(s1_ref[rows, :], token_gain(seg_ref[rows, :], g2_ref))

        dn_ref[...] = jnp.zeros_like(dn_ref)
        flow(s1_ref, keep1_ref, sem.at[0, 2]).start()

    hook(0)
    for s in range(steps):

        @pl.when(step == s)
        def _(s=s):
            if s in (2, 4, 6):
                for load in tile_loads(s):
                    load.start()
            for load in tile_loads(s):
                load.wait()
            if s % 2 == 0:
                for load in tile_loads(s + 1):
                    load.start()
            if s >= 2:
                act_save(s - 2).wait()

    slot = step % 2
    up = jnp.concatenate([up_tile[slot, z].reshape(width, UNIT) for z in range(4)], axis=1)
    down = jnp.concatenate([dn_tile[slot, f // 2, f % 2].reshape(4 * UNIT, UNIT) for f in range(NB)], axis=1)
    hidden = dot(n2_ref[...], up)
    square = hidden * hidden
    half = 0.5 + 0.5 * jnp.tanh(hidden * (ROOT + ROOT * CUBE * square))
    act_ref[slot] = (hidden * half).astype(BF)
    bend = hidden * (2.0 * ROOT + 6.0 * ROOT * CUBE * square)
    slope = half + half * (1.0 - half) * bend
    pre_ref[...] = (dot(cot_ref[...], down, NT) * slope).astype(BF)
    for s in range(steps):

        @pl.when(step == s)
        def _(s=s):
            act_save(s).start()

    hook(1)
    dn_ref[...] += dot(pre_ref[...], up, NT)
    hook(2)
    par = (step // 2) % 2
    grad = dot(act_ref[slot], cot_ref[...], TN).astype(BF)
    for f in range(NB):
        stage_dn[par, slot, f // 2, f % 2] = grad[:, f * UNIT : (f + 1) * UNIT].reshape(2, 2, UNIT, UNIT)
    hook(3)
    grad = dot(n2_ref[...], pre_ref[...], TN).astype(BF)
    for z in range(4):
        stage_up[par, slot, z] = grad[:, z * UNIT : (z + 1) * UNIT].reshape(2, 2, 2 * UNIT, UNIT)
    for s in range(2, steps):

        @pl.when(step == s)
        def _(s=s):
            for save in grad_saves(s):
                save.start()
            if s == 5:
                for save in grad_saves(2) + grad_saves(3):
                    save.wait()

    @pl.when(step == steps - 1)
    def _():
        dg2_ref[...] = jnp.zeros_like(dg2_ref)
        flow(s1_ref, keep1_ref, sem.at[0, 2]).wait()

        @pl.loop(0, tiles)
        def _(t):
            rows = pl.ds(pl.multiple_of(t * UNIT, UNIT), UNIT)
            stream = s1_ref[rows, :]
            gain = token_gain(seg_ref[rows, :], g2_ref)
            term, d_gain = norm_back(dn_ref[rows, :], stream, gain)
            d_stream = cot_ref[rows, :].astype(F32) + term
            s1_ref[rows, :] = d_stream
            n2_ref[rows, :] = d_stream.astype(BF)
            dg2_ref[...] += segment_sum(row_ref[:, rows], d_gain)

        keep = flow(s1_ref, ds1_ref, sem.at[0, 0])
        keep.start()
        for i in range(4):
            lanes = slice(i * 2 * UNIT, (i + 1) * 2 * UNIT)
            part = dot(ctx_ref[...], n2_ref[:, lanes], TN).astype(BF)
            for c in range(2):
                gout_ref[i, c] = part[:, c * UNIT : (c + 1) * UNIT].reshape(2, 2, 2 * UNIT, UNIT)
        for i in range(4):
            lanes = slice(i * 2 * UNIT, (i + 1) * 2 * UNIT)
            tile = jnp.concatenate([wout_ref[i, c].reshape(width, UNIT) for c in range(2)], axis=1)
            part = dot(n2_ref[:, lanes], tile, NT)
            dn_ref[...] = part if i == 0 else dn_ref[...] + part
        dctx_ref[...] = dn_ref[...].astype(BF)
        gather.drain()
        reduce.drain()
        for s in range(4, steps):
            for save in grad_saves(s):
                save.wait()
        keep.wait()
        for s in (steps - 2, steps - 1):
            act_save(s).wait()


def mlp(stream0, ctx, w_out, gamma2, seg_col, seg_row, cotangent, s_up, s_down, fup0, fdn0, fup1, fdn1):
    length, width = ctx.shape
    full = whole((length, width))
    part = pl.BlockSpec((2 * UNIT, UNIT), lambda j: (0, 0))
    quarter = full_of(2 * UNIT, UNIT)
    grads = (shaped((2, 4, 2, 2, 2 * UNIT, UNIT), BF), shaped((2, 4, 2, 2, 2, UNIT, UNIT), BF))
    pieces = 4
    return pl.pallas_call(
        mlp_body,
        grid=(8,),
        in_specs=[
            ANY,
            full,
            whole(w_out.shape),
            whole((8, width)),
            whole((length, 1)),
            whole((1, length)),
            full,
        ]
        + [ANY] * 6,
        out_specs=(ANY, ANY, whole(w_out.shape), ANY, full, whole((8, width))) + (part,) * 2 + (ANY,) * 10,
        out_shape=(
            shaped((8, length, 4 * UNIT), BF),
            shaped((length, width), F32),
            shaped(w_out.shape, BF),
            shaped((length, width), F32),
            shaped((length, width), BF),
            shaped((8, width), F32),
        )
        + (shaped((2 * UNIT, UNIT), F32),) * 2
        + grads * 3
        + (quarter,) * 4,
        scratch_shapes=[
            pltpu.VMEM((length, width), F32),
            pltpu.VMEM((length, width), BF),
            pltpu.VMEM((length, width), F32),
            pltpu.VMEM((2, 4, 2, 2, 2 * UNIT, UNIT), BF),
            pltpu.VMEM((2, 4, 2, 2, 2, UNIT, UNIT), BF),
            pltpu.VMEM((2, length, 4 * UNIT), BF),
            pltpu.VMEM((length, 4 * UNIT), BF),
            pltpu.VMEM((2, 2, 4, 2, 2, 2 * UNIT, UNIT), BF),
            pltpu.VMEM((2, 2, 4, 2, 2, 2, UNIT, UNIT), BF),
            pltpu.SemaphoreType.DMA((4, 6)),
        ]
        + semaphores(8, Gather.sems)
        + semaphores(pieces, Reduce.sems)
        + Reduce.room(UNIT, UNIT) * pieces,
        compiler_params=params(collective_id=2, has_side_effects=True),
        name="mlp",
    )(stream0, ctx, w_out, gamma2, seg_col, seg_row, cotangent, s_up, s_down, fup0, fdn0, fup1, fdn1)


def attend_back_body(
    n_ref, qa, qb, ka, kb, va, vb, cos_ref, lo_ref, hi_ref, seg_ref, pad_ref, row_ref,
    q_ref, k_ref, v_ref, g_ref, c_ref, lse_ref, g1_ref, s0_ref, ds1_ref, gup1, gdn1, gup2, gdn2, gup3, gdn3, gout,
    gw_ref, dlow_ref, dg1_ref, sup1, sdn1, sup2, sdn2, sup3, sdn3, sout,
    bias_ref, dn_ref, dq_ref, dk_ref, dv_ref, s0_buf, sem, send, recv, local, *room,
):
    step = pl.program_id(0)
    last = pl.num_programs(0) - 1
    length, width = n_ref.shape
    me = Place()
    traffic = Traffic()
    made = []

    def add(theirs, mine, out, e, own):
        count = len(made)
        rest = room[10 + 4 * count : 14 + 4 * count]
        made.append(Reduce(me, theirs, mine, room[own + e], rest, out, e == 1, True))

    for q, (gup, gdn, sup, sdn) in enumerate(
        ((gup1, gdn1, sup1, sdn1), (gup2, gdn2, sup2, sdn2), (gup3, gdn3, sup3, sdn3))
    ):
        for e, (rows, _) in enumerate(halves(2 * UNIT)):
            add(gup.at[1 - me.c, :, :, :, rows, :], gup.at[me.c, :, :, :, rows, :], sup.at[rows, :], e, (0, 4, 8)[q])
        for e in range(2):
            add(gdn.at[e, :, 1 - me.c], gdn.at[e, :, me.c], sdn.at[pl.ds(e * UNIT, UNIT), :], e, (2, 6, 0)[q])
    for e, (rows, _) in enumerate(halves(2 * UNIT)):
        theirs, mine = gout.at[:, 1 - me.c, :, :, rows, :], gout.at[:, me.c, :, :, rows, :]
        add(theirs, mine, sout.at[rows, :], e, 2)
    traffic.add(ATTEND_BACK_HOOKS, made)
    traffic.bind(send, recv, local)
    fire = functools.partial(traffic.fire, step, 4, 5)

    @pl.when(step == 0)
    def _():
        me.greet()
        traffic.at(0)
        flow(s0_ref, s0_buf, sem.at[0]).start()
        fill_bias(bias_ref, seg_ref, pad_ref, row_ref)
        dn_ref[...] = jnp.zeros_like(dn_ref)

    ones = jnp.ones((8, HD), BF)
    for head in range(4):
        fire(head)
        lanes = slice(head * HD, (head + 1) * HD)
        query, key, value = q_ref[:, lanes], k_ref[:, lanes], v_ref[:, lanes]
        grad = g_ref[:, lanes]
        both = grad.astype(F32) * c_ref[:, lanes].astype(F32)
        high = both.astype(BF)
        low = (both - high.astype(F32)).astype(BF)
        delta = (dot(ones, high, NT) + dot(ones, low, NT))[0:1, :]
        probs = jnp.exp(dot(key, query, NT) + bias_ref[...] - lse_ref[head : head + 1, :])
        d_scores = (probs * (dot(value, grad, NT) - delta)).astype(BF)
        dv_ref[:, lanes] = dot(probs.astype(BF), grad)
        dk_ref[:, lanes] = dot(d_scores, query)
        dq_ref[:, lanes] = dot(key.T, d_scores).T * HD**-0.5

    @pl.when(step == last)
    def _():
        flow(ds1_ref, bias_ref, sem.at[1]).start()

    fire(4)
    for part, (src, first, second) in enumerate(
        ((dq_ref, qa, qb), (dk_ref, ka, kb), (dv_ref, va, vb))
    ):
        if part < 2:
            made = jnp.concatenate(
                [
                    turn(src[:, half * 128 : (half + 1) * 128], cos_ref[...], -lo_ref[...], -hi_ref[...])
                    for half in range(2)
                ],
                axis=1,
            ).astype(BF)
        else:
            made = src[...].astype(BF)
        grad = dot(n_ref[...], made, TN).astype(BF)
        gw_ref[part, 0] = grad[:, :128]
        gw_ref[part, 1] = grad[:, 128:]
        dn_ref[...] += dot(made, jnp.concatenate([first[0], second[0]], axis=1), NT)

    @pl.when(step == last)
    def _():
        dg1_ref[...] = jnp.zeros_like(dg1_ref)
        flow(s0_ref, s0_buf, sem.at[0]).wait()
        flow(ds1_ref, bias_ref, sem.at[1]).wait()

        @pl.loop(0, length // UNIT)
        def _(t):
            rows = pl.ds(pl.multiple_of(t * UNIT, UNIT), UNIT)
            gain = token_gain(seg_ref[rows, :], g1_ref)
            term, d_gain = norm_back(dn_ref[rows, :], s0_buf[rows, :], gain)
            dlow_ref[rows, :] = (bias_ref[rows, :] + term).astype(BF)
            dg1_ref[...] += segment_sum(row_ref[:, rows], d_gain)

        traffic.drain()


def attend_back(
    normed, w_qkv, tables, seg_col, pad_col, seg_row, q, k, v, d_ctx, ctx, lse, gamma1, stream0, d_stream1, grads
):
    length, width = normed.shape
    groups = width // 256
    units = [unit_spec(width, part * (width // 128) + e) for part in range(3) for e in range(2)]
    column = pl.BlockSpec((length, 256), lambda j: (0, j))
    full = whole((length, width))
    part = whole((2 * UNIT, UNIT))
    pieces = 14
    return pl.pallas_call(
        attend_back_body,
        grid=(groups,),
        in_specs=[full]
        + units
        + [whole((length, 128))] * 3
        + [whole((length, 1))] * 2
        + [whole((1, length))]
        + [column] * 5
        + [pl.BlockSpec((8, length), lambda j: (j, 0)), whole((8, width))]
        + [ANY] * 9,
        out_specs=(
            pl.BlockSpec((3, 2, width, 128), lambda j: (0, j, 0, 0)),
            full,
            whole((8, width)),
        )
        + (part,) * 7,
        out_shape=(
            shaped((3, width // 128, width, 128), BF),
            shaped((length, width), BF),
            shaped((8, width), F32),
        )
        + (shaped((2 * UNIT, UNIT), F32),) * 7,
        scratch_shapes=[pltpu.VMEM((length, length), F32), pltpu.VMEM((length, width), F32)]
        + [pltpu.VMEM((length, 256), F32)] * 3
        + [pltpu.VMEM((length, width), F32), pltpu.SemaphoreType.DMA((2,))]
        + semaphores(pieces, Reduce.sems)
        + [pltpu.VMEM((4, 2, 2, UNIT, UNIT), BF)] * 10
        + Reduce.room(UNIT, UNIT) * pieces,
        compiler_params=params(collective_id=3, has_side_effects=True),
        name="attend_back",
    )(
        normed, *([w_qkv] * 6), *tables, seg_col, pad_col, seg_row, q, k, v, d_ctx, ctx, lse,
        gamma1, stream0, d_stream1, *grads,
    )


def skip_back_body(
    x_ref, s_ref, d_ref, w_ref, ada_ref, dg_ref, every_ref, gw_ref, acts_ref, keep1_ref, fdn0, fdn1, fdn2, fdn3,
    out_ref, dx_ref, ds_ref, time_ref, gada_ref, sskip, sqkv,
    stage, acc_ref, act_tile, dn_tile, sem, slots, part, got, summed, tim, sends, recvs, send, recv, local, *room,
):
    width = x_ref.shape[1]
    me = Place()
    me.greet(True)
    traffic = Traffic()
    made = []
    tall = 512

    def add(theirs, mine, out):
        own, *rest = room[5 * len(made) : 5 * len(made) + 5]
        made.append(Reduce(me, theirs, mine, own, rest, out, len(made) % 2 == 1, True))

    for sub in range(3):
        for i in range(4):
            rows = pl.ds(i * UNIT // 2, UNIT // 2)
            theirs, mine = gw_ref.at[:, 1 - me.c, sub, :, :, rows, :], gw_ref.at[:, me.c, sub, :, :, rows, :]
            add(theirs, mine, sqkv.at[rows, pl.ds(sub * UNIT, UNIT)])
    for i in range(8):
        rows = pl.ds(i * UNIT // 2, UNIT // 2)
        theirs, mine = stage.at[:, 1 - me.c, :, :, rows, :], stage.at[:, me.c, :, :, rows, :]
        add(theirs, mine, sskip.at[rows, :])
    traffic.add(SKIP_BACK_HOOKS, made)
    traffic.bind(send, recv, local)
    lay = functools.partial(pl.ds, 0)
    swaps = [
        Swap(me, "fsdp", lambda p: dg_ref.at[p], lambda m: slots.at[me.dp, m], sends.at[0], recvs.at[0]),
        Swap(me, "dp", lambda p: slots.at[me.dp], lambda m: slots.at[m], sends.at[1], recvs.at[1]),
        Swap(me, "fsdp", lambda p: part.at[:, p, lay(8), :], lambda m: got.at[m], sends.at[2], recvs.at[2]),
        Swap(me, "dp", lambda p: summed.at[p], lambda m: tim.at[m], sends.at[3], recvs.at[3]),
    ]
    downs = (fdn0, fdn1, fdn2, fdn3)

    def tiles(s):
        return (
            flow(acts_ref.at[s], act_tile.at[s % 2], sem.at[0, s % 2]),
            flow(downs[s // 2].at[:, :, :, :, pl.ds(s % 2 * UNIT, UNIT), :], dn_tile.at[s % 2], sem.at[1, s % 2]),
        )

    start1 = flow(keep1_ref, acc_ref, sem.at[0, 2])
    slots[me.dp, me.fs] = dg_ref[me.fs]
    swaps[0].start()
    traffic.at(0)
    start1.start()
    for load in tiles(0):
        load.start()

    def add_down(slot):
        @pl.loop(0, 2)
        def _(half):
            tile = jnp.concatenate(
                [dn_tile[slot, 2 * half + i // 2, i % 2].reshape(4 * UNIT, UNIT) for i in range(4)], axis=1
            )
            lanes = pl.ds(pl.multiple_of(half * 4 * UNIT, 4 * UNIT), 4 * UNIT)
            acc_ref[:, lanes] += dot(act_tile[slot], tile)

    def grads(i):
        lanes = pl.ds(pl.multiple_of(i * 2 * UNIT, 2 * UNIT), 2 * UNIT)
        part = d_ref[:, lanes]
        top = dot(x_ref[...], part, TN).astype(BF)
        end = dot(s_ref[...], part, TN).astype(BF)
        for c in range(2):
            cols = slice(c * UNIT, (c + 1) * UNIT)
            stage[i, c, 0] = top[:, cols].reshape(2, tall, UNIT)
            stage[i, c, 1] = end[:, cols].reshape(2, tall, UNIT)

    def second():
        swaps[0].wait()
        swaps[1].start()

    @pl.loop(0, 4)
    def _(i):
        grads(i)
        traffic.inside(i, 1, 4)
        pl.when(i == 1)(second)

    traffic.at(5)
    swaps[1].wait()
    every = slots[...].reshape(4 * NB * 16, -1)
    gada_ref[...] = dot(every_ref[...].reshape(4 * NB * 16, -1), every, TN)
    part[...] = dot(every, ada_ref[...], NT).reshape(part.shape)
    got[me.fs] = part[:, me.fs, :8, :]
    swaps[2].start()

    def back(which, out, first):
        @pl.loop(0, 2)
        def _(i):
            traffic.inside(i, first, 2)
            rows = pl.ds(pl.multiple_of(i * tall, tall), tall)
            tile = jnp.concatenate([w_ref[f // 2, f % 2, which, i] for f in range(NB)], axis=1)
            out[:, rows] = dot(d_ref[...], tile, NT)

    back(0, dx_ref, 6)
    swaps[2].wait()
    total = got[0]
    for f in range(1, NB):
        total = total + got[f]
    summed[...] = total
    tim[me.dp] = summed[me.dp]
    swaps[3].start()
    back(1, ds_ref, 8)
    swaps[3].wait()
    for d in range(4):
        time_ref[:, d * 2 * UNIT : (d + 1) * 2 * UNIT] = tim[d]
    start1.wait()
    for s in range(8):
        if s < 7:
            for load in tiles(s + 1):
                load.start()
        for load in tiles(s):
            load.wait()
        add_down(s % 2)
        traffic.at(10 + s)
    out_ref[...] = acc_ref[...].astype(BF)
    traffic.drain()


def skip_back(inputs, skip_in, d_low, w_skip, w_ada, dg_cut, every, g_qkv, acts, stream1, fdowns):
    length, width = inputs.shape
    vmem = pl.BlockSpec(memory_space=pltpu.VMEM)
    tall, per = w_ada.shape
    pieces = 20
    return pl.pallas_call(
        skip_back_body,
        in_specs=[vmem] * 7 + [ANY] * 7,
        out_shape=(
            shaped((length, width), BF),
            shaped((length, width), F32),
            shaped((length, width), F32),
            shaped((8, width), F32),
            shaped((tall, per), F32),
            shaped((4 * UNIT, UNIT), F32),
            shaped((2 * UNIT, 3 * UNIT), F32),
        ),
        scratch_shapes=[
            pltpu.VMEM(w_skip.shape, BF),
            pltpu.VMEM((length, width), F32),
            pltpu.VMEM((2, *acts.shape[1:]), BF),
            pltpu.VMEM((2, 4, 2, 2, 2, UNIT, UNIT), BF),
            pltpu.SemaphoreType.DMA((2, 3)),
            pltpu.VMEM((4, NB, 16, per), BF),
            pltpu.VMEM((4, NB, 16, tall), F32),
            pltpu.VMEM((NB, 4, 8, tall), F32),
            pltpu.VMEM((4, 8, tall), F32),
            pltpu.VMEM((4, 8, tall), F32),
            pltpu.SemaphoreType.DMA((4, NB - 1)),
            pltpu.SemaphoreType.DMA((4, NB - 1)),
        ]
        + semaphores(pieces, Reduce.sems)
        + ([pltpu.VMEM((4, 2, 2, UNIT // 2, UNIT), BF)] + Reduce.room(UNIT // 2, UNIT)) * pieces,
        compiler_params=params(collective_id=4, has_side_effects=True),
        name="skip_back",
    )(inputs, skip_in, d_low, w_skip, w_ada, dg_cut, every, g_qkv, acts, stream1, *fdowns)


def frequencies():
    lane = jnp.arange(128) % (HD // 2)
    return 10000.0 ** (-2.0 * lane.astype(F32) / HD)


def rotary(positions):
    half = HD // 2
    lane = jnp.arange(128)
    phase = positions.reshape(-1, 1).astype(F32) * frequencies()[None, :]
    cosine, sine = jnp.cos(phase), jnp.sin(phase)
    early = (lane % HD < half)[None, :]
    return cosine, jnp.where(early, -sine, 0.0), jnp.where(early, 0.0, sine)


def gathered(shard):
    blocks = lax.all_gather(shard, "fsdp", axis=0, tiled=False)
    blocks = lax.all_gather(blocks, "dp", axis=1, tiled=True)
    count, rows, per = blocks.shape
    if count == NB:
        return blocks
    flat = jnp.transpose(blocks, (1, 0, 2)).reshape(rows, count * per)
    return jnp.transpose(flat.reshape(rows, NB, count * per // NB), (1, 0, 2))


def scattered(blocks):
    count, rows, per = blocks.shape
    flat = jnp.transpose(blocks, (1, 0, 2)).reshape(rows, count * per)
    part = lax.psum_scatter(flat, "fsdp", scatter_dimension=1, tiled=True)
    return lax.psum_scatter(part, "dp", scatter_dimension=0, tiled=True).astype(F32)


def ada_grads(flat_time, d_gammas, tall, thin):
    every = lax.all_gather(flat_time, "fsdp", axis=0, tiled=True)
    every = lax.all_gather(every, "dp", axis=0, tiled=True)
    every = lax.dynamic_slice_in_dim(every, lax.axis_index("dp") * tall, tall, 1)
    gammas = lax.all_gather(d_gammas, "fsdp", axis=1, tiled=True)
    gammas = lax.all_gather(gammas, "dp", axis=1, tiled=True)
    gammas = lax.dynamic_slice_in_dim(gammas, lax.axis_index("fsdp") * thin, thin, 2)
    return [jnp.einsum("nd,ne->de", every, part, preferred_element_type=F32) for part in gammas]


def fused(
    inputs, skip_in, time_emb, seg_ids, positions, pad_mask,
    w_skip, w_ada1, w_qkv, w_out, w_ada2, w_up, w_down, cotangent,
):
    slots = time_emb.shape[1]
    length, width = inputs.shape
    seg_row = seg_ids.reshape(1, -1)
    rows = jnp.concatenate([seg_row, pad_mask.reshape(1, -1), positions.reshape(1, -1)])
    rows = jnp.pad(rows, ((0, 5), (0, 0)))
    freq = jnp.broadcast_to(frequencies(), (8, UNIT))
    flat_time = time_emb.reshape(slots, -1)
    time_cut = jnp.pad(flat_time, ((0, 16 - slots), (0, 0)))
    time_cut = jnp.transpose(time_cut.reshape(16, 4, -1), (1, 0, 2))
    w_ada = jnp.concatenate([w_ada1, w_ada2], axis=1)
    stream0, normed1, gamma1, gamma2, every, seg_col, pad_col, *tables, f_skip, f_qkv = front(
        inputs, skip_in, time_cut, rows, freq, w_ada, w_skip, w_qkv
    )
    f_qkv = f_qkv.reshape(NB, width, -1)
    q, k, v, ctx, lse, f_out, fup0, fdn0, fup1, fdn1 = attend(
        normed1, f_qkv, tables, seg_col, pad_col, seg_row, w_out, w_up, w_down
    )
    acts, stream1, g_out, d_stream1, d_ctx, d_gamma2, sup0, sdn0, *rest = mlp(
        stream0, ctx, f_out, gamma2, seg_col, seg_row, cotangent, w_up, w_down, fup0, fdn0, fup1, fdn1
    )
    g_qkv, d_low, d_gamma1, sup1, sdn1, sup2, sdn2, sup3, sdn3, s_out = attend_back(
        normed1, f_qkv, tables, seg_col, pad_col, seg_row, q, k, v, d_ctx, ctx, lse, gamma1,
        stream0, d_stream1, (*rest[:6], g_out),
    )
    dg_cut = jnp.concatenate([d.reshape(8, NB, -1) for d in (d_gamma1, d_gamma2)], axis=2)
    dg_cut = jnp.pad(jnp.transpose(dg_cut, (1, 0, 2)).astype(BF), ((0, 0), (0, 8), (0, 0)))
    output, d_input, d_skip, d_time, g_ada, s_skip, s_qkv = skip_back(
        inputs, skip_in, d_low, f_skip, w_ada, dg_cut, every, g_qkv.reshape(4, 2, 3, 2, 2, -1, UNIT),
        acts, stream1, (fdn0, fdn1, rest[7], rest[9]),
    )
    s_up = jnp.concatenate([sup0, sup1, sup2, sup3], axis=1)
    s_down = jnp.stack([sdn0, sdn1, sdn2, sdn3]).reshape(4, 2, UNIT, UNIT)
    s_down = jnp.transpose(s_down, (1, 0, 2, 3)).reshape(w_down.shape)
    return (
        output, d_input, d_skip, d_time[:slots].reshape(time_emb.shape),
        s_skip, g_ada[:, :UNIT], s_qkv, s_out, g_ada[:, UNIT:], s_up, s_down,
    )


def plain(
    inputs, skip_in, time_emb, seg_ids, positions, pad_mask,
    w_skip, w_ada1, w_qkv, w_out, w_ada2, w_up, w_down, cotangent,
):
    slots = time_emb.shape[1]
    width = inputs.shape[1]
    seg_col, seg_row = seg_ids.reshape(-1, 1), seg_ids.reshape(1, -1)
    pad_col = pad_mask.reshape(-1, 1)
    tables = rotary(positions)
    flat_time = time_emb.reshape(slots, -1)
    time8 = jnp.pad(flat_time, ((0, 8 - slots), (0, 0)))
    f_skip, f_qkv, f_out, f_up, f_down, f_ada1, f_ada2 = [
        gathered(w) for w in (w_skip, w_qkv, w_out, w_up, w_down, w_ada1, w_ada2)
    ]
    ada = jnp.concatenate([f_ada1, f_ada2], axis=2)
    stream0, normed1, gamma1, gamma2 = plain_front(inputs, skip_in, f_skip, time8, ada, seg_col)
    q, k, v, ctx, lse = plain_attend(normed1, f_qkv, tables, seg_col, pad_col, seg_row)
    output, g_down, g_up, g_out, d_stream1, d_ctx, d_gamma2 = plain_mlp(
        stream0, ctx, f_out, gamma2, seg_col, seg_row, f_up, f_down, cotangent
    )
    g_qkv, d_low, d_gamma1 = plain_attend_back(
        normed1, f_qkv, tables, seg_col, pad_col, seg_row, q, k, v, d_ctx, ctx, lse,
        stream0, gamma1, d_stream1,
    )
    g_qkv = jnp.transpose(
        g_qkv.reshape(NB, 3, width, 128), (0, 2, 1, 3)
    ).reshape(NB, width, 3 * width // NB)
    g_skip, d_input, d_skip = plain_skip_back(inputs, skip_in, d_low, f_skip)
    d_gammas = jnp.stack([d_gamma1, d_gamma2]).astype(BF)[:, :slots]
    d_time = 0.0
    for d_gamma, part in zip(d_gammas, (f_ada1, f_ada2)):
        flat = jnp.transpose(part, (1, 0, 2)).reshape(width, width)
        d_time = d_time + jnp.einsum("ne,de->nd", d_gamma, flat, preferred_element_type=F32)
    g_ada = ada_grads(flat_time, d_gammas, *w_ada1.shape)
    return (
        output, d_input, d_skip, d_time.reshape(time_emb.shape),
        scattered(g_skip), g_ada[0], scattered(g_qkv), scattered(g_out), g_ada[1],
        scattered(g_up), scattered(g_down),
    )


def solution(mesh):
    rows = P(("dp", "fsdp"), None)
    cube = P(("dp", "fsdp"), None, None)
    tile = P("dp", "fsdp")
    fits = mesh.shape["dp"] == 4 and mesh.shape["fsdp"] == NB
    return jax.shard_map(
        fused if fits else plain,
        mesh=mesh,
        in_specs=(rows, rows, cube) + (rows,) * 3 + (tile,) * 7 + (rows,),
        out_specs=(rows, rows, rows, cube) + (tile,) * 7,
        check_vma=False,
    )
```

```python
import functools

import jax
import jax.numpy as jnp
from jax import lax
from jax.experimental import pallas as pl
from jax.experimental.pallas import tpu as pltpu
from jax.sharding import PartitionSpec as P

HD = 64
NB = 8
EPS = 1e-06
MASKED = -1e30
BF = jnp.bfloat16
F32 = jnp.float32
NN = (((1,), (0,)), ((), ()))
NT = (((1,), (1,)), ((), ()))
TN = (((0,), (0,)), ((), ()))
ROOT = 0.7978845608028654
CUBE = 0.044715


def dot(left, right, form=NN):
    return lax.dot_general(left, right, form, preferred_element_type=F32)


def params(**extra):
    return pltpu.CompilerParams(vmem_limit_bytes=60 << 20, **extra)


def whole(shape):
    return pl.BlockSpec(shape, lambda *_: (0,) * len(shape), pipeline_mode=pl.Buffered(1))


ANY = pl.BlockSpec(memory_space=pl.ANY)
UNIT = 128


def shaped(shape, kind):
    return jax.ShapeDtypeStruct(shape, kind)


def columns(ref, first, count, rows=slice(None)):
    return jnp.concatenate([ref[first + i, rows, :] for i in range(count)], axis=1)


def token_gain(seg, gamma):
    gain = gamma[0:1, :]
    for slot in range(1, 4):
        gain = jnp.where(seg == slot, gamma[slot : slot + 1, :], gain)
    return gain


def segment_sum(seg_row, values):
    slots = lax.broadcasted_iota(jnp.int32, (8, seg_row.shape[1]), 0)
    picked = (slots == seg_row).astype(BF)
    high = values.astype(BF)
    low = (values - high.astype(F32)).astype(BF)
    return dot(picked, high) + dot(picked, low)


def norm_back(grad, stream, gain):
    inverse = lax.rsqrt(jnp.mean(stream * stream, axis=-1, keepdims=True) + EPS)
    unit = stream * inverse
    scaled = grad * (1.0 + gain)
    d_stream = inverse * (scaled - unit * jnp.mean(scaled * unit, axis=-1, keepdims=True))
    return d_stream, grad * unit


def norm(stream, gain):
    inverse = lax.rsqrt(jnp.mean(stream * stream, axis=-1, keepdims=True) + EPS)
    return (stream * inverse * (1.0 + gain)).astype(BF)


def fill_bias(bias_ref, seg_ref, pad_ref, row_ref):
    length = seg_ref.shape[0]

    @pl.loop(0, length // UNIT)
    def _(t):
        rows = pl.ds(pl.multiple_of(t * UNIT, UNIT), UNIT)
        keys = lax.broadcasted_iota(jnp.int32, (UNIT, length), 0) + t * UNIT
        queries = lax.broadcasted_iota(jnp.int32, (UNIT, length), 1)
        allowed = (seg_ref[rows, :] == row_ref[0:1, :]) & (
            (pad_ref[rows, :] > 0) | (keys == queries)
        )
        bias_ref[rows, :] = jnp.where(allowed, 0.0, MASKED)


def turn(unit, cosine, before, after):
    return (
        unit * cosine
        + pltpu.roll(unit, 96, 1) * before
        + pltpu.roll(unit, 32, 1) * after
    )


def unit_spec(rows, base):
    def index(j):
        unit = base + 2 * j
        return (unit // 3, 0, unit % 3)

    return pl.BlockSpec((1, rows, 128), index)


def plain_front_body(x_ref, s_ref, w_ref, time_ref, ada_ref, seg_ref, stream_ref, normed_ref, g1_ref, g2_ref):
    length, width = x_ref.shape
    per = ada_ref.shape[2] // 2
    for f in range(NB):
        both = dot(time_ref[...], ada_ref[f])
        g1_ref[:, f * per : (f + 1) * per] = both[:, :per]
        g2_ref[:, f * per : (f + 1) * per] = both[:, per:]
    for i in range(NB // 2):
        tile = columns(w_ref, 2 * i, 2)
        part = dot(x_ref[...], tile[:width]) + dot(s_ref[...], tile[width:])
        stream_ref[:, i * part.shape[1] : (i + 1) * part.shape[1]] = part

    @pl.loop(0, length // 128)
    def _(t):
        rows = pl.ds(pl.multiple_of(t * 128, 128), 128)
        gain = token_gain(seg_ref[rows, :], g1_ref)
        normed_ref[rows, :] = norm(stream_ref[rows, :], gain)


def plain_front(inputs, skip_in, w_skip, time8, ada, seg_col):
    length, width = inputs.shape
    return pl.pallas_call(
        plain_front_body,
        out_shape=(
            shaped((length, width), F32),
            shaped((length, width), BF),
            shaped((8, width), F32),
            shaped((8, width), F32),
        ),
        compiler_params=params(),
        name="front",
    )(inputs, skip_in, w_skip, time8, ada, seg_col)


def plain_attend_body(
    n_ref, qa, qb, ka, kb, va, vb, cos_ref, lo_ref, hi_ref, seg_ref, pad_ref, row_ref,
    q_ref, k_ref, v_ref, c_ref, lse_ref, bias_ref,
):
    @pl.when(pl.program_id(0) == 0)
    def _():
        fill_bias(bias_ref, seg_ref, pad_ref, row_ref)

    normed = n_ref[...]
    for out, first, second, scale in ((q_ref, qa, qb, HD**-0.5), (k_ref, ka, kb, 1.0)):
        made = dot(normed, jnp.concatenate([first[0], second[0]], axis=1))
        for half in range(2):
            unit = made[:, half * 128 : (half + 1) * 128]
            turned = turn(unit, cos_ref[...], lo_ref[...], hi_ref[...])
            out[:, half * 128 : (half + 1) * 128] = (turned.astype(BF) * scale).astype(BF)
    v_ref[...] = dot(normed, jnp.concatenate([va[0], vb[0]], axis=1)).astype(BF)
    for head in range(4):
        lanes = slice(head * HD, (head + 1) * HD)
        scores = dot(k_ref[:, lanes], q_ref[:, lanes], NT) + bias_ref[...]
        largest = jnp.max(scores, axis=0, keepdims=True)
        exponent = jnp.exp(scores - largest)
        total = jnp.sum(exponent, axis=0, keepdims=True)
        mixed = dot(v_ref[:, lanes].T, exponent.astype(BF)) * (1.0 / total)
        c_ref[:, lanes] = mixed.T.astype(BF)
        lse_ref[head : head + 1, :] = largest + jnp.log(total)


def plain_attend(normed, w_qkv, tables, seg_col, pad_col, seg_row):
    length, width = normed.shape
    groups = width // 256
    units = [unit_spec(width, part * (width // 128) + e) for part in range(3) for e in range(2)]
    column = pl.BlockSpec((length, 256), lambda j: (0, j))
    wide = shaped((length, width), BF)
    return pl.pallas_call(
        plain_attend_body,
        grid=(groups,),
        in_specs=[whole((length, width))]
        + units
        + [whole((length, 128))] * 3
        + [whole((length, 1))] * 2
        + [whole((1, length))],
        out_specs=(column,) * 4 + (pl.BlockSpec((8, length), lambda j: (j, 0)),),
        out_shape=(wide,) * 4 + (shaped((8 * groups, length), F32),),
        scratch_shapes=[pltpu.VMEM((length, length), F32)],
        compiler_params=params(),
        name="attend",
    )(normed, *([w_qkv] * 6), *tables, seg_col, pad_col, seg_row)


def plain_mlp_body(
    stream0_ref, ctx_ref, wout_ref, g2_ref, seg_ref, row_ref, up_ref, down_ref, cot_ref,
    out_ref, gdown_ref, gup_ref, gout_ref, ds1_ref, dctx_ref, dg2_ref,
    s1_ref, n2_ref, acc_ref, dn_ref,
):
    step = pl.program_id(0)
    length, width = ctx_ref.shape
    tiles = length // 128

    @pl.when(step == 0)
    def _():
        @pl.loop(0, NB // 2)
        def _(i):
            lanes = pl.ds(pl.multiple_of(i * 256, 256), 256)
            s1_ref[:, lanes] = stream0_ref[:, lanes] + dot(ctx_ref[...], columns(wout_ref, 2 * i, 2))

        @pl.loop(0, tiles)
        def _(t):
            rows = pl.ds(pl.multiple_of(t * 128, 128), 128)
            n2_ref[rows, :] = norm(s1_ref[rows, :], token_gain(seg_ref[rows, :], g2_ref))

        acc_ref[...] = jnp.zeros_like(acc_ref)
        dn_ref[...] = jnp.zeros_like(dn_ref)

    cot = cot_ref[...]
    up = up_ref[0]
    down = columns(down_ref, 0, NB)
    hidden = dot(n2_ref[...], up)
    square = hidden * hidden
    tanh = jnp.tanh(ROOT * hidden * (1.0 + CUBE * square))
    active = (0.5 * hidden * (1.0 + tanh)).astype(BF)
    slope = 0.5 * (1.0 + tanh) + 0.5 * hidden * (1.0 - tanh * tanh) * (
        ROOT * (1.0 + 3.0 * CUBE * square)
    )
    d_pre = (dot(cot, down, NT) * slope).astype(BF)
    acc_ref[...] += dot(active, down)
    dn_ref[...] += dot(d_pre, up, NT)
    grad = dot(active, cot, TN).astype(BF)
    for f in range(NB):
        gdown_ref[f] = grad[:, f * gdown_ref.shape[2] : (f + 1) * gdown_ref.shape[2]]
    gup_ref[0] = dot(n2_ref[...], d_pre, TN).astype(BF)

    @pl.when(step == pl.num_programs(0) - 1)
    def _():
        dg2_ref[...] = jnp.zeros_like(dg2_ref)

        @pl.loop(0, tiles)
        def _(t):
            rows = pl.ds(pl.multiple_of(t * 128, 128), 128)
            stream = s1_ref[rows, :]
            out_ref[rows, :] = (stream + acc_ref[rows, :]).astype(BF)
            gain = token_gain(seg_ref[rows, :], g2_ref)
            term, d_gain = norm_back(dn_ref[rows, :], stream, gain)
            d_stream = cot_ref[rows, :].astype(F32) + term
            ds1_ref[rows, :] = d_stream
            n2_ref[rows, :] = d_stream.astype(BF)
            dg2_ref[...] += segment_sum(row_ref[:, rows], d_gain)

        @pl.loop(0, NB // 2)
        def _(i):
            lanes = pl.ds(pl.multiple_of(i * 256, 256), 256)
            part = dot(ctx_ref[...], n2_ref[:, lanes], TN).astype(BF)
            gout_ref[2 * i] = part[:, :128]
            gout_ref[2 * i + 1] = part[:, 128:]

        acc_ref[...] = jnp.zeros_like(acc_ref)

        @pl.loop(0, NB // 2)
        def _(i):
            lanes = pl.ds(pl.multiple_of(i * 256, 256), 256)
            acc_ref[...] += dot(n2_ref[:, lanes], columns(wout_ref, 2 * i, 2), NT)

        dctx_ref[...] = acc_ref[...].astype(BF)


def plain_mlp(stream0, ctx, w_out, gamma2, seg_col, seg_row, w_up, w_down, cotangent):
    length, width = ctx.shape
    hidden = w_down.shape[1]
    piece = hidden // NB
    per = width // NB
    full = whole((length, width))
    return pl.pallas_call(
        plain_mlp_body,
        grid=(NB,),
        in_specs=[
            full,
            full,
            whole((NB, width, per)),
            whole((8, width)),
            whole((length, 1)),
            whole((1, length)),
            pl.BlockSpec((1, width, piece), lambda j: (j, 0, 0)),
            pl.BlockSpec((NB, piece, per), lambda j: (0, j, 0)),
            full,
        ],
        out_specs=(
            full,
            pl.BlockSpec((NB, piece, per), lambda j: (0, j, 0)),
            pl.BlockSpec((1, width, piece), lambda j: (j, 0, 0)),
            whole((NB, width, per)),
            full,
            full,
            whole((8, width)),
        ),
        out_shape=(
            shaped((length, width), BF),
            shaped((NB, hidden, per), BF),
            shaped((NB, width, piece), BF),
            shaped((NB, width, per), BF),
            shaped((length, width), F32),
            shaped((length, width), BF),
            shaped((8, width), F32),
        ),
        scratch_shapes=[
            pltpu.VMEM((length, width), F32),
            pltpu.VMEM((length, width), BF),
            pltpu.VMEM((length, width), F32),
            pltpu.VMEM((length, width), F32),
        ],
        compiler_params=params(),
        name="mlp",
    )(stream0, ctx, w_out, gamma2, seg_col, seg_row, w_up, w_down, cotangent)


def plain_attend_back_body(
    n_ref, qa, qb, ka, kb, va, vb, cos_ref, lo_ref, hi_ref, seg_ref, pad_ref, row_ref,
    q_ref, k_ref, v_ref, g_ref, c_ref, lse_ref, s0_ref, g1_ref, ds1_ref,
    gw_ref, dlow_ref, dg1_ref, bias_ref, dn_ref, dq_ref, dk_ref, dv_ref,
):
    step = pl.program_id(0)
    length, width = n_ref.shape

    @pl.when(step == 0)
    def _():
        fill_bias(bias_ref, seg_ref, pad_ref, row_ref)
        dn_ref[...] = jnp.zeros_like(dn_ref)

    ones = jnp.ones((8, HD), BF)
    for head in range(4):
        lanes = slice(head * HD, (head + 1) * HD)
        query, key, value = q_ref[:, lanes], k_ref[:, lanes], v_ref[:, lanes]
        grad = g_ref[:, lanes]
        both = grad.astype(F32) * c_ref[:, lanes].astype(F32)
        high = both.astype(BF)
        low = (both - high.astype(F32)).astype(BF)
        delta = (dot(ones, high, NT) + dot(ones, low, NT))[0:1, :]
        probs = jnp.exp(dot(key, query, NT) + bias_ref[...] - lse_ref[head : head + 1, :])
        d_scores = (probs * (dot(value, grad, NT) - delta)).astype(BF)
        dv_ref[:, lanes] = dot(probs.astype(BF), grad)
        dk_ref[:, lanes] = dot(d_scores, query)
        dq_ref[:, lanes] = dot(key.T, d_scores).T * HD**-0.5
    for part, (src, first, second) in enumerate(
        ((dq_ref, qa, qb), (dk_ref, ka, kb), (dv_ref, va, vb))
    ):
        if part < 2:
            made = jnp.concatenate(
                [
                    turn(src[:, half * 128 : (half + 1) * 128], cos_ref[...], -lo_ref[...], -hi_ref[...])
                    for half in range(2)
                ],
                axis=1,
            ).astype(BF)
        else:
            made = src[...].astype(BF)
        grad = dot(n_ref[...], made, TN).astype(BF)
        gw_ref[part, 0] = grad[:, :128]
        gw_ref[part, 1] = grad[:, 128:]
        dn_ref[...] += dot(made, jnp.concatenate([first[0], second[0]], axis=1), NT)

    @pl.when(step == pl.num_programs(0) - 1)
    def _():
        dg1_ref[...] = jnp.zeros_like(dg1_ref)

        @pl.loop(0, length // 128)
        def _(t):
            rows = pl.ds(pl.multiple_of(t * 128, 128), 128)
            gain = token_gain(seg_ref[rows, :], g1_ref)
            term, d_gain = norm_back(dn_ref[rows, :], s0_ref[rows, :], gain)
            dlow_ref[rows, :] = (ds1_ref[rows, :] + term).astype(BF)
            dg1_ref[...] += segment_sum(row_ref[:, rows], d_gain)


def plain_attend_back(
    normed, w_qkv, tables, seg_col, pad_col, seg_row, q, k, v, d_ctx, ctx, lse, stream0, gamma1, d_stream1
):
    length, width = normed.shape
    groups = width // 256
    units = [unit_spec(width, part * (width // 128) + e) for part in range(3) for e in range(2)]
    column = pl.BlockSpec((length, 256), lambda j: (0, j))
    full = whole((length, width))
    return pl.pallas_call(
        plain_attend_back_body,
        grid=(groups,),
        in_specs=[full]
        + units
        + [whole((length, 128))] * 3
        + [whole((length, 1))] * 2
        + [whole((1, length))]
        + [column] * 5
        + [pl.BlockSpec((8, length), lambda j: (j, 0)), full, whole((8, width)), full],
        out_specs=(
            pl.BlockSpec((3, 2, width, 128), lambda j: (0, j, 0, 0)),
            full,
            whole((8, width)),
        ),
        out_shape=(
            shaped((3, width // 128, width, 128), BF),
            shaped((length, width), BF),
            shaped((8, width), F32),
        ),
        scratch_shapes=[pltpu.VMEM((length, length), F32), pltpu.VMEM((length, width), F32)]
        + [pltpu.VMEM((length, 256), F32)] * 3,
        compiler_params=params(),
        name="attend_back",
    )(
        normed, *([w_qkv] * 6), *tables, seg_col, pad_col, seg_row, q, k, v, d_ctx, ctx, lse,
        stream0, gamma1, d_stream1,
    )


def plain_skip_back_body(x_ref, s_ref, d_ref, w_ref, gw_ref, dx_ref, ds_ref):
    low = d_ref[...]
    per = 256
    width = x_ref.shape[1]

    @pl.loop(0, width // per)
    def _(i):
        lanes = pl.ds(pl.multiple_of(i * per, per), per)
        part = d_ref[:, lanes]
        top = dot(x_ref[...], part, TN).astype(BF)
        end = dot(s_ref[...], part, TN).astype(BF)
        for e in range(2):
            gw_ref[2 * i + e, :width, :] = top[:, e * 128 : (e + 1) * 128]
            gw_ref[2 * i + e, width:, :] = end[:, e * 128 : (e + 1) * 128]

    tall = 256

    @pl.loop(0, width // tall)
    def _(i):
        rows = pl.ds(pl.multiple_of(i * tall, tall), tall)
        rest = pl.ds(pl.multiple_of(width + i * tall, tall), tall)
        dx_ref[:, rows] = dot(low, columns(w_ref, 0, NB, rows), NT)
        ds_ref[:, rows] = dot(low, columns(w_ref, 0, NB, rest), NT)


def plain_skip_back(inputs, skip_in, d_low, w_skip):
    length, width = inputs.shape
    return pl.pallas_call(
        plain_skip_back_body,
        out_shape=(
            shaped(w_skip.shape, BF),
            shaped((length, width), F32),
            shaped((length, width), F32),
        ),
        compiler_params=params(),
        name="skip_back",
    )(inputs, skip_in, d_low, w_skip)


class Place:
    def __init__(self):
        dp, fs = lax.axis_index("dp"), lax.axis_index("fsdp")
        self.y, self.x, self.z, self.c = dp // 2, dp % 2, fs // 2, fs % 2
        self.dp, self.fs = dp, fs

    def across_x(self):
        return (self.y * 2 + 1 - self.x, self.fs)

    def across_y(self):
        return ((1 - self.y) * 2 + self.x, self.fs)

    def sibling(self):
        return (self.dp, self.z * 2 + 1 - self.c)

    def along_z(self, hop):
        return (self.dp, ((self.z + hop) % 4) * 2 + self.c)

    def on_dp(self, index):
        return (index, self.fs)

    def on_fsdp(self, index):
        return (self.dp, index)

    def greet(self, wide=False):
        barrier = pltpu.get_barrier_semaphore()
        if wide:
            peers = [self.on_dp((self.dp + hop) % 4) for hop in range(1, 4)]
            peers += [self.on_fsdp((self.fs + hop) % NB) for hop in range(1, NB)]
        else:
            peers = [self.across_x(), self.across_y(), self.sibling()]
            peers += [self.along_z(hop) for hop in (1, 2, 3)]
        for peer in peers:
            pl.semaphore_signal(barrier, inc=1, device_id=peer, device_id_type=pl.DeviceIdType.MESH)
        pl.semaphore_wait(barrier, len(peers))


def remote(src, dst, send, recv, peer):
    return pltpu.make_async_remote_copy(
        src_ref=src, dst_ref=dst, send_sem=send, recv_sem=recv,
        device_id=peer, device_id_type=pl.DeviceIdType.MESH,
    )


class Lazy:
    def __init__(self, plan, send, recv):
        self.plan, self.send, self.recv = plan, send, recv

    def __len__(self):
        return len(self.plan)

    def __getitem__(self, i):
        if isinstance(i, slice):
            return [self[k] for k in range(*i.indices(len(self)))]
        if i >= len(self.plan):
            raise IndexError
        src, dst, peer = self.plan[i]
        return remote(src, dst, self.send.at[i], self.recv.at[i], peer)


def flow(*copy):
    return pltpu.make_async_copy(*copy)


class Gather:
    sems = 8

    def __init__(self, place, source, full, rows, flip):
        self.me, self.source, self.full, self.rows, self.flip = place, source, full, rows, flip

    def bind(self, send, recv, local):
        self.send, self.recv, self.local = send, recv, local

    def copies(self):
        me, full, rows = self.me, self.full, self.rows
        spot = full.at[me.z, me.c, me.y, me.x, rows, :]
        line = full.at[:, me.c, me.y, me.x, rows, :]
        if self.flip:
            pair = full.at[:, me.c, :, me.x, rows, :]
            near, far = me.across_y(), me.across_x()
            got = full.at[:, me.c, 1 - me.y, me.x, rows, :]
            late = full.at[:, me.c, :, 1 - me.x, rows, :]
        else:
            pair = full.at[:, me.c, me.y, :, rows, :]
            near, far = me.across_x(), me.across_y()
            got = full.at[:, me.c, me.y, 1 - me.x, rows, :]
            late = full.at[:, me.c, 1 - me.y, :, rows, :]
        sib = me.sibling()
        plan = [(self.source, spot, me.along_z(hop)) for hop in (1, 2, 3)]
        plan += [(line, line, near), (pair, pair, far), (line, line, sib), (got, got, sib), (late, late, sib)]
        return Lazy(plan, self.send, self.recv), (self.source, spot, self.local)

    def stage(self, number):
        made, keep = self.copies()
        if number == 0:
            flow(*keep).start()
            for copy in made[:3]:
                copy.start()
        elif number == 1:
            flow(*keep).wait()
            for copy in made[:3]:
                copy.wait_recv()
            made[3].start()
            made[5].start()
        elif number == 2:
            made[3].wait_recv()
            made[4].start()
            made[6].start()
        elif number == 3:
            made[4].wait_recv()
            made[7].start()
        else:
            for copy in made[5:]:
                copy.wait_recv()
            for copy in made[:]:
                copy.wait_send()


class Reduce:
    sems = 6

    def __init__(self, place, theirs, mine, own, room, out, flip, load):
        self.me, self.theirs, self.mine, self.own = place, theirs, mine, own
        self.other, self.half, self.quarter, self.parts = room
        self.out, self.flip, self.load = out, flip, load

    @staticmethod
    def room(count, per):
        return [
            pltpu.VMEM((4, 2, 2, count, per), BF),
            pltpu.VMEM((4, 2, count, per), BF),
            pltpu.VMEM((4, count, per), BF),
            pltpu.VMEM((3, count, per), BF),
        ]

    def bind(self, send, recv, local):
        self.send, self.recv, self.local = send, recv, local

    def copies(self):
        me = self.me
        if self.flip:
            give, near = self.own.at[:, :, 1 - me.x], me.across_x()
            give2, far = self.half.at[:, 1 - me.y], me.across_y()
        else:
            give, near = self.own.at[:, 1 - me.y], me.across_y()
            give2, far = self.half.at[:, 1 - me.x], me.across_x()
        plan = [(self.theirs, self.other, me.sibling()), (give, self.half, near), (give2, self.quarter, far)]
        plan += [
            (self.quarter.at[(me.z + hop) % 4], self.parts.at[hop - 1], me.along_z(hop)) for hop in (1, 2, 3)
        ]
        return Lazy(plan, self.send, self.recv), (self.mine, self.own, self.local)

    def stage(self, number):
        me = self.me
        made, load = self.copies()
        if number == 0:
            made[0].start()
            if self.load:
                flow(*load).start()
        elif number == 1:
            if self.load:
                flow(*load).wait()
            made[0].wait_recv()

            @pl.loop(0, 4)
            def _(z):
                self.own[z] = self.own[z] + self.other[z]

            made[1].start()
        elif number == 2:
            made[1].wait_recv()

            @pl.loop(0, 4)
            def _(z):
                kept = self.own[z, :, me.x] if self.flip else self.own[z, me.y]
                self.half[z] = self.half[z] + kept

            made[2].start()
        elif number == 3:
            made[0].wait_send()
            made[1].wait_send()
            made[2].wait_recv()
            kept = me.y if self.flip else me.x

            @pl.loop(0, 4)
            def _(z):
                self.quarter[z] = self.quarter[z] + self.half[z, kept]

            for copy in made[3:]:
                copy.start()
        else:
            for copy in made[3:]:
                copy.wait_recv()
            total = self.quarter[me.z].astype(F32)
            for i in range(3):
                total = total + self.parts[i].astype(F32)
            self.out[...] = total
            for copy in made[2:]:
                copy.wait_send()


class Swap:
    def __init__(self, place, axis, what, into, send, recv):
        count = 4 if axis == "dp" else NB
        at = place.dp if axis == "dp" else place.fs
        find = place.on_dp if axis == "dp" else place.on_fsdp
        self.at, self.what, self.into = at, what, into
        self.plan = []
        for hop in range(1, count):
            peer = (at + hop) % count
            self.plan.append((what(peer), into(at), send.at[hop - 1], recv.at[hop - 1], find(peer)))

    def start(self):
        for copy in self.plan:
            remote(*copy).start()

    def wait(self):
        for copy in self.plan:
            remote(*copy).wait()


class Traffic:
    def __init__(self):
        self.todo, self.pieces = {}, []

    def add(self, hooks, pieces):
        self.pieces += pieces
        for piece, places in zip(pieces, hooks, strict=True):
            for stage, hook in enumerate(places):
                self.todo.setdefault(hook, []).append((stage, piece))

    def bind(self, send, recv, local):
        for i, piece in enumerate(self.pieces):
            piece.bind(send.at[i], recv.at[i], local.at[i])

    def at(self, hook):
        for stage, piece in sorted(self.todo.pop(hook, []), key=lambda item: -item[0]):
            piece.stage(stage)

    def fire(self, step, steps, per, hook):
        for s in range(steps):
            if s * per + hook in self.todo:
                pl.when(step == s)(functools.partial(self.at, s * per + hook))

    def inside(self, index, first, count):
        for s in range(count):
            if first + s in self.todo:
                pl.when(index == s)(functools.partial(self.at, first + s))

    def drain(self):
        for hook in sorted(self.todo):
            self.at(hook)


def semaphores(count, kind):
    return [pltpu.SemaphoreType.DMA((count, kind))] * 2 + [pltpu.SemaphoreType.DMA((count,))]


def full_of(rows, per):
    return shaped((4, 2, 2, 2, rows, per), BF)


def halves(rows):
    return [(pl.ds(e * (rows // 2), rows // 2), e == 1) for e in range(2)]


def up_pair(me, shard, full, q):
    lanes = pl.ds(q * UNIT, UNIT)
    return [Gather(me, shard.at[rows, lanes], full, rows, flip) for rows, flip in halves(shard.shape[0])]


def down_pair(me, shard, full, q):
    tall = shard.shape[0] // 2
    step = tall // 4
    return [
        Gather(me, shard.at[pl.ds(e * tall + q * step, step), :], full, pl.ds(e * step, step), e == 1)
        for e in range(2)
    ]


def row_pieces(me, shard, full, count):
    tall = shard.shape[0] // count
    return [
        Gather(me, shard.at[pl.ds(i * tall, tall), :], full, pl.ds(i * tall, tall), i % 2 == 1)
        for i in range(count)
    ]


FRONT_HOOKS = (
    (1, 4, 7, 13, 14), (1, 4, 7, 13, 14),
    (4, 7, 10, 18, 19), (4, 7, 10, 18, 19),
    (0, 1, 3, 7, 8), (0, 1, 3, 7, 8),
    (3, 6, 9, 16, 18), (3, 6, 9, 16, 18),
    (9, 13, 18, 25, 28), (9, 13, 18, 25, 28),
    (6, 9, 15, 22, 25), (6, 9, 15, 22, 25),
    (0, 2, 5, 11, 13), (0, 2, 5, 10, 12),
    (13, 17, 21, 28, 31), (13, 17, 21, 28, 31),
)
FRONT_READY = 19
ATTEND_HOOKS = (
    (7, 10, 12, 15, 16), (7, 10, 12, 15, 16),
    (1, 4, 6, 9, 10), (1, 4, 6, 9, 10),
    (0, 1, 3, 5, 6), (0, 1, 3, 5, 6),
    (6, 9, 11, 14, 15), (6, 9, 11, 14, 15),
    (2, 5, 7, 10, 11), (2, 5, 7, 10, 11),
)
MLP_HOOKS = (
    (0, 2, 5, 12, 13), (0, 2, 5, 12, 13),
    (0, 2, 5, 12, 13), (0, 2, 5, 12, 13),
    (14, 17, 20, 23, 24), (14, 17, 20, 23, 24),
    (12, 15, 17, 21, 23), (12, 15, 17, 21, 23),
    (8, 10, 16, 18, 23), (8, 10, 16, 18, 23),
    (8, 10, 16, 18, 23), (8, 10, 16, 18, 23),
)
ATTEND_BACK_HOOKS = (
    (0, 1, 4, 8, 10), (0, 1, 4, 8, 10),
    (1, 2, 8, 11, 14), (1, 2, 8, 11, 14),
    (7, 8, 13, 16, 19), (7, 8, 13, 16, 19),
    (2, 3, 9, 12, 16), (2, 3, 9, 12, 16),
    (3, 4, 10, 13, 17), (3, 4, 10, 13, 17),
    (11, 12, 16, 18, 20), (11, 12, 16, 18, 20),
    (12, 13, 17, 19, 20), (12, 13, 17, 19, 20),
)
SKIP_BACK_HOOKS = (
    (5, 6, 8, 10, 11), (5, 6, 8, 10, 11),
    (4, 5, 7, 8, 9), (4, 5, 7, 8, 9),
    (6, 7, 9, 11, 13), (6, 7, 9, 11, 13),
    (0, 2, 4, 6, 7), (0, 2, 4, 6, 7),
    (2, 4, 6, 7, 8), (2, 4, 6, 7, 8),
    (8, 9, 11, 13, 14), (8, 9, 11, 13, 14),
    (11, 12, 14, 15, 18), (11, 12, 14, 15, 18),
    (7, 8, 10, 12, 14), (7, 8, 10, 12, 14),
    (8, 9, 12, 14, 15), (8, 9, 12, 14, 15),
    (10, 11, 14, 15, 18), (10, 11, 14, 15, 18),
)


def front_body(
    x_hbm, s_hbm, time_ref, row_ref, freq_ref, ada_ref, skip_ref, qkv_ref,
    stream_hbm, normed_ref, g1_ref, g2_ref, slots, seg_ref, pad_ref, cos_ref, lo_ref, hi_ref, fskip_ref, fqkv_ref,
    x_ref, s_ref, stream_ref, near_sem, w_ref, part, got, summed, gam, w_sem, sends, recvs, send, recv, local,
):
    length, width = x_ref.shape
    ahead = [flow(x_hbm, x_ref, near_sem.at[0]), flow(s_hbm, s_ref, near_sem.at[1])]
    for load in ahead:
        load.start()
    per = ada_ref.shape[1] // 2
    me = Place()
    me.greet(True)
    traffic = Traffic()
    plan = row_pieces(me, skip_ref, fskip_ref, 8) + row_pieces(me, qkv_ref, fqkv_ref, 8)
    traffic.add(FRONT_HOOKS, plan)
    traffic.bind(send, recv, local)
    lay = functools.partial(pl.ds, 0)
    swaps = [
        Swap(me, "dp", lambda p: time_ref.at[p], lambda m: slots.at[m, me.fs], sends.at[0], recvs.at[0]),
        Swap(me, "fsdp", lambda p: slots.at[:, me.fs], lambda m: slots.at[:, m], sends.at[1], recvs.at[1]),
        Swap(me, "dp", lambda p: part.at[p, :, lay(8), :], lambda m: got.at[m], sends.at[2], recvs.at[2]),
        Swap(me, "fsdp", lambda p: summed.at[p], lambda m: gam.at[m], sends.at[3], recvs.at[3]),
    ]

    def prepare(t):
        rows = pl.ds(pl.multiple_of(t * UNIT, UNIT), UNIT)
        turned = row_ref[:, rows].T
        seg_ref[rows, :] = turned[:, 0:1]
        pad_ref[rows, :] = turned[:, 1:2]
        phase = turned[:, 2:3].astype(F32) * freq_ref[0:1, :]
        cosine, sine = jnp.cos(phase), jnp.sin(phase)
        early = lax.broadcasted_iota(jnp.int32, phase.shape, 1) % HD < HD // 2
        cos_ref[rows, :] = cosine
        lo_ref[rows, :] = jnp.where(early, -sine, 0.0)
        hi_ref[rows, :] = jnp.where(early, 0.0, sine)

    slots[me.dp, me.fs] = time_ref[me.dp]
    swaps[0].start()
    for hook in range(FRONT_READY + 1):
        traffic.at(hook)
        if hook == 2:
            pl.loop(0, length // UNIT)(prepare)
        elif hook == 4:
            swaps[0].wait()
            swaps[1].start()
        elif hook == 8:
            swaps[1].wait()
            made = dot(slots[...].reshape(4 * NB * 16, -1), ada_ref[...])
            part[...] = made.reshape(part.shape)
            got[me.dp] = part[me.dp, :, :8, :]
            swaps[2].start()
        elif hook == 12:
            swaps[2].wait()
            summed[...] = got[0] + got[1] + got[2] + got[3]
            gam[me.fs] = summed[me.fs]
            swaps[3].start()
    load = flow(fskip_ref, w_ref, w_sem)
    load.start()
    swaps[3].wait()
    for f in range(NB):
        g1_ref[:, f * per : (f + 1) * per] = gam[f, :, :per]
        g2_ref[:, f * per : (f + 1) * per] = gam[f, :, per:]
    load.wait()
    for load in ahead:
        load.wait()

    def stream(i):
        tile = jnp.concatenate([w_ref[i, c].reshape(2 * width, UNIT) for c in range(2)], axis=1)
        lanes = pl.ds(pl.multiple_of(i * 2 * UNIT, 2 * UNIT), 2 * UNIT)
        stream_ref[:, lanes] = dot(x_ref[...], tile[:width]) + dot(s_ref[...], tile[width:])

    def normalise(t):
        rows = pl.ds(pl.multiple_of(t * UNIT, UNIT), UNIT)
        gain = token_gain(seg_ref[rows, :], g1_ref)
        normed_ref[rows, :] = norm(stream_ref[rows, :], gain)

    @pl.loop(0, 4)
    def _(i):
        stream(i)
        traffic.inside(i, FRONT_READY + 1, 4)

    away = flow(stream_ref, stream_hbm, near_sem.at[2])
    away.start()

    @pl.loop(0, length // UNIT)
    def _(t):
        normalise(t)
        traffic.inside(t, FRONT_READY + 5, 8)

    traffic.drain()
    away.wait()


def front(inputs, skip_in, time_cut, rows, freq, w_ada, w_skip, w_qkv):
    length, width = inputs.shape
    fulls = [full_of(*w.shape) for w in (w_skip, w_qkv)]
    vmem = pl.BlockSpec(memory_space=pltpu.VMEM)
    per = w_ada.shape[1]
    return pl.pallas_call(
        front_body,
        in_specs=[ANY] * 2 + [vmem] * 4 + [ANY] * 2,
        out_specs=(ANY,) + (vmem,) * 9 + (ANY,) * 2,
        out_shape=(
            shaped((length, width), F32),
            shaped((length, width), BF),
            shaped((8, width), F32),
            shaped((8, width), F32),
            shaped((4, NB, 16, w_ada.shape[0]), BF),
            shaped((length, 1), jnp.int32),
            shaped((length, 1), jnp.int32),
            shaped((length, UNIT), F32),
            shaped((length, UNIT), F32),
            shaped((length, UNIT), F32),
            *fulls,
        ),
        scratch_shapes=[
            pltpu.VMEM((length, width), BF),
            pltpu.VMEM((length, width), BF),
            pltpu.VMEM((length, width), F32),
            pltpu.SemaphoreType.DMA((3,)),
            pltpu.VMEM(fulls[0].shape, BF),
            pltpu.VMEM((4, NB, 16, per), F32),
            pltpu.VMEM((4, NB, 8, per), F32),
            pltpu.VMEM((NB, 8, per), F32),
            pltpu.VMEM((NB, 8, per), F32),
            pltpu.SemaphoreType.DMA,
            pltpu.SemaphoreType.DMA((4, NB - 1)),
            pltpu.SemaphoreType.DMA((4, NB - 1)),
        ]
        + semaphores(16, Gather.sems),
        compiler_params=params(collective_id=0, has_side_effects=True),
        name="front",
    )(inputs, skip_in, time_cut, rows, freq, w_ada, w_skip, w_qkv)


def attend_body(
    n_ref, qa, qb, ka, kb, va, vb, cos_ref, lo_ref, hi_ref, seg_ref, pad_ref, row_ref, out_ref, up_ref, down_ref,
    q_ref, k_ref, v_ref, c_ref, lse_ref, fout_ref, fup0_ref, fdn0_ref, fup1_ref, fdn1_ref,
    bias_ref, send, recv, local,
):
    step = pl.program_id(0)
    last = pl.num_programs(0) - 1
    me = Place()
    traffic = Traffic()
    pieces = (
        up_pair(me, up_ref, fup0_ref, 0)
        + down_pair(me, down_ref, fdn0_ref, 0)
        + up_pair(me, up_ref, fup1_ref, 1)
        + down_pair(me, down_ref, fdn1_ref, 1)
        + row_pieces(me, out_ref, fout_ref, 2)
    )
    traffic.add(ATTEND_HOOKS, pieces)
    traffic.bind(send, recv, local)
    fire = functools.partial(traffic.fire, step, 4, 4)

    @pl.when(step == 0)
    def _():
        me.greet()
        traffic.at(0)
        fill_bias(bias_ref, seg_ref, pad_ref, row_ref)

    normed = n_ref[...]
    for out, first, second, scale in ((q_ref, qa, qb, HD**-0.5), (k_ref, ka, kb, 1.0)):
        made = dot(normed, jnp.concatenate([first[0], second[0]], axis=1))
        for half in range(2):
            unit = made[:, half * 128 : (half + 1) * 128]
            turned = turn(unit, cos_ref[...], lo_ref[...], hi_ref[...])
            out[:, half * 128 : (half + 1) * 128] = (turned.astype(BF) * scale).astype(BF)
    v_ref[...] = dot(normed, jnp.concatenate([va[0], vb[0]], axis=1)).astype(BF)
    for head in range(4):
        fire(head)
        lanes = slice(head * HD, (head + 1) * HD)
        scores = dot(k_ref[:, lanes], q_ref[:, lanes], NT) + bias_ref[...]
        largest = jnp.max(scores, axis=0, keepdims=True)
        exponent = jnp.exp(scores - largest)
        total = jnp.sum(exponent, axis=0, keepdims=True)
        mixed = dot(v_ref[:, lanes].T, exponent.astype(BF)) * (1.0 / total)
        c_ref[:, lanes] = mixed.T.astype(BF)
        lse_ref[head : head + 1, :] = largest + jnp.log(total)
    pl.when(step == last)(traffic.drain)


def attend(normed, w_qkv, tables, seg_col, pad_col, seg_row, w_out, w_up, w_down):
    length, width = normed.shape
    groups = width // 256
    units = [unit_spec(width, part * (width // 128) + e) for part in range(3) for e in range(2)]
    column = pl.BlockSpec((length, 256), lambda j: (0, j))
    wide = shaped((length, width), BF)
    quarter = full_of(w_up.shape[0], UNIT)
    return pl.pallas_call(
        attend_body,
        grid=(groups,),
        in_specs=[whole((length, width))]
        + units
        + [whole((length, 128))] * 3
        + [whole((length, 1))] * 2
        + [whole((1, length))]
        + [ANY] * 3,
        out_specs=(column,) * 4 + (pl.BlockSpec((8, length), lambda j: (j, 0)),) + (ANY,) * 5,
        out_shape=(wide,) * 4
        + (shaped((8 * groups, length), F32), full_of(*w_out.shape)) + (quarter,) * 4,
        scratch_shapes=[pltpu.VMEM((length, length), F32)] + semaphores(10, Gather.sems),
        compiler_params=params(collective_id=1, has_side_effects=True),
        name="attend",
    )(normed, *([w_qkv] * 6), *tables, seg_col, pad_col, seg_row, w_out, w_up, w_down)


def mlp_body(
    stream0_ref, ctx_ref, wout_ref, g2_ref, seg_ref, row_ref, cot_ref,
    up_ref, down_ref, fup0, fdn0, fup1, fdn1,
    acts_ref, keep1_ref, gout_ref, ds1_ref, dctx_ref, dg2_ref, sup0, sdn0, gup1, gdn1, gup2, gdn2, gup3, gdn3,
    fup2, fdn2, fup3, fdn3,
    s1_ref, n2_ref, dn_ref, up_tile, dn_tile, act_ref, pre_ref, stage_up, stage_dn,
    sem, gsend, grecv, glocal, rsend, rrecv, rlocal, *room,
):
    step = pl.program_id(0)
    steps = 8
    length, width = ctx_ref.shape
    tiles = length // UNIT
    me = Place()
    gather, reduce = Traffic(), Traffic()
    pieces = (
        up_pair(me, up_ref, fup2, 2)
        + down_pair(me, down_ref, fdn2, 2)
        + up_pair(me, up_ref, fup3, 3)
        + down_pair(me, down_ref, fdn3, 3)
    )
    gather.add(MLP_HOOKS[:8], pieces)
    gather.bind(gsend, grecv, glocal)
    count = 0
    for q, (sup, sdn) in enumerate(((sup0, sdn0),)):
        made = []
        for rows, flip in halves(2 * UNIT):
            theirs = stage_up.at[q, 1 - me.c, :, :, :, rows, :]
            mine = stage_up.at[q, me.c, :, :, :, rows, :]
            made.append(Reduce(me, theirs, mine, mine, room[4 * count : 4 * count + 4], sup.at[rows, :], flip, False))
            count += 1
        for e in range(2):
            theirs = stage_dn.at[q, e, :, 1 - me.c]
            mine = stage_dn.at[q, e, :, me.c]
            rows = pl.ds(e * UNIT, UNIT)
            made.append(Reduce(me, theirs, mine, mine, room[4 * count : 4 * count + 4], sdn.at[rows, :], e == 1, False))
            count += 1
        reduce.add(MLP_HOOKS[8:], made)
    reduce.bind(rsend, rrecv, rlocal)
    ups, downs = (fup0, fup1, fup2, fup3), (fdn0, fdn1, fdn2, fdn3)
    saves = {2: (gup1, gdn1), 4: (gup2, gdn2), 6: (gup3, gdn3)}

    def tile_loads(s):
        q, e = s // 2, s % 2
        return (
            flow(ups[q].at[:, e], up_tile.at[s % 2], sem.at[0, s % 2]),
            flow(downs[q].at[:, :, :, :, pl.ds(e * UNIT, UNIT), :], dn_tile.at[s % 2], sem.at[1, s % 2]),
        )

    def grad_saves(s):
        q, e = s // 2, s % 2
        gup, gdn = saves[2 * q]
        return (
            flow(stage_up.at[q % 2, e], gup.at[e], sem.at[2, s - 2]),
            flow(stage_dn.at[q % 2, e], gdn.at[e], sem.at[3, s - 2]),
        )

    def act_save(s):
        return flow(act_ref.at[s % 2], acts_ref.at[s], sem.at[1, 2 + s % 2])

    def hook(which):
        gather.fire(step, steps, 4, which)
        reduce.fire(step, steps, 4, which)

    @pl.when(step == 0)
    def _():
        me.greet()
        gather.at(0)
        for load in tile_loads(0):
            load.start()
        first = flow(stream0_ref, s1_ref, sem.at[2, 0])
        first.start()
        first.wait()
        for i in range(4):
            lanes = slice(i * 2 * UNIT, (i + 1) * 2 * UNIT)
            tile = jnp.concatenate([wout_ref[i, c].reshape(width, UNIT) for c in range(2)], axis=1)
            s1_ref[:, lanes] += dot(ctx_ref[...], tile)

        @pl.loop(0, tiles)
        def _(t):
            rows = pl.ds(pl.multiple_of(t * UNIT, UNIT), UNIT)
            n2_ref[rows, :] = norm(s1_ref[rows, :], token_gain(seg_ref[rows, :], g2_ref))

        dn_ref[...] = jnp.zeros_like(dn_ref)
        flow(s1_ref, keep1_ref, sem.at[0, 2]).start()

    hook(0)
    for s in range(steps):

        @pl.when(step == s)
        def _(s=s):
            if s in (2, 4, 6):
                for load in tile_loads(s):
                    load.start()
            for load in tile_loads(s):
                load.wait()
            if s % 2 == 0:
                for load in tile_loads(s + 1):
                    load.start()
            if s >= 2:
                act_save(s - 2).wait()

    slot = step % 2
    up = jnp.concatenate([up_tile[slot, z].reshape(width, UNIT) for z in range(4)], axis=1)
    down = jnp.concatenate([dn_tile[slot, f // 2, f % 2].reshape(4 * UNIT, UNIT) for f in range(NB)], axis=1)
    hidden = dot(n2_ref[...], up)
    square = hidden * hidden
    half = 0.5 + 0.5 * jnp.tanh(hidden * (ROOT + ROOT * CUBE * square))
    act_ref[slot] = (hidden * half).astype(BF)
    bend = hidden * (2.0 * ROOT + 6.0 * ROOT * CUBE * square)
    slope = half + half * (1.0 - half) * bend
    pre_ref[...] = (dot(cot_ref[...], down, NT) * slope).astype(BF)
    for s in range(steps):

        @pl.when(step == s)
        def _(s=s):
            act_save(s).start()

    hook(1)
    dn_ref[...] += dot(pre_ref[...], up, NT)
    hook(2)
    par = (step // 2) % 2
    grad = dot(act_ref[slot], cot_ref[...], TN).astype(BF)
    for f in range(NB):
        stage_dn[par, slot, f // 2, f % 2] = grad[:, f * UNIT : (f + 1) * UNIT].reshape(2, 2, UNIT, UNIT)
    hook(3)
    grad = dot(n2_ref[...], pre_ref[...], TN).astype(BF)
    for z in range(4):
        stage_up[par, slot, z] = grad[:, z * UNIT : (z + 1) * UNIT].reshape(2, 2, 2 * UNIT, UNIT)
    for s in range(2, steps):

        @pl.when(step == s)
        def _(s=s):
            for save in grad_saves(s):
                save.start()
            if s == 5:
                for save in grad_saves(2) + grad_saves(3):
                    save.wait()

    @pl.when(step == steps - 1)
    def _():
        dg2_ref[...] = jnp.zeros_like(dg2_ref)
        flow(s1_ref, keep1_ref, sem.at[0, 2]).wait()

        @pl.loop(0, tiles)
        def _(t):
            rows = pl.ds(pl.multiple_of(t * UNIT, UNIT), UNIT)
            stream = s1_ref[rows, :]
            gain = token_gain(seg_ref[rows, :], g2_ref)
            term, d_gain = norm_back(dn_ref[rows, :], stream, gain)
            d_stream = cot_ref[rows, :].astype(F32) + term
            s1_ref[rows, :] = d_stream
            n2_ref[rows, :] = d_stream.astype(BF)
            dg2_ref[...] += segment_sum(row_ref[:, rows], d_gain)

        keep = flow(s1_ref, ds1_ref, sem.at[0, 0])
        keep.start()
        for i in range(4):
            lanes = slice(i * 2 * UNIT, (i + 1) * 2 * UNIT)
            part = dot(ctx_ref[...], n2_ref[:, lanes], TN).astype(BF)
            for c in range(2):
                gout_ref[i, c] = part[:, c * UNIT : (c + 1) * UNIT].reshape(2, 2, 2 * UNIT, UNIT)
        for i in range(4):
            lanes = slice(i * 2 * UNIT, (i + 1) * 2 * UNIT)
            tile = jnp.concatenate([wout_ref[i, c].reshape(width, UNIT) for c in range(2)], axis=1)
            part = dot(n2_ref[:, lanes], tile, NT)
            dn_ref[...] = part if i == 0 else dn_ref[...] + part
        dctx_ref[...] = dn_ref[...].astype(BF)
        gather.drain()
        reduce.drain()
        for s in range(4, steps):
            for save in grad_saves(s):
                save.wait()
        keep.wait()
        for s in (steps - 2, steps - 1):
            act_save(s).wait()


def mlp(stream0, ctx, w_out, gamma2, seg_col, seg_row, cotangent, s_up, s_down, fup0, fdn0, fup1, fdn1):
    length, width = ctx.shape
    full = whole((length, width))
    part = pl.BlockSpec((2 * UNIT, UNIT), lambda j: (0, 0))
    quarter = full_of(2 * UNIT, UNIT)
    grads = (shaped((2, 4, 2, 2, 2 * UNIT, UNIT), BF), shaped((2, 4, 2, 2, 2, UNIT, UNIT), BF))
    pieces = 4
    return pl.pallas_call(
        mlp_body,
        grid=(8,),
        in_specs=[
            ANY,
            full,
            whole(w_out.shape),
            whole((8, width)),
            whole((length, 1)),
            whole((1, length)),
            full,
        ]
        + [ANY] * 6,
        out_specs=(ANY, ANY, whole(w_out.shape), ANY, full, whole((8, width))) + (part,) * 2 + (ANY,) * 10,
        out_shape=(
            shaped((8, length, 4 * UNIT), BF),
            shaped((length, width), F32),
            shaped(w_out.shape, BF),
            shaped((length, width), F32),
            shaped((length, width), BF),
            shaped((8, width), F32),
        )
        + (shaped((2 * UNIT, UNIT), F32),) * 2
        + grads * 3
        + (quarter,) * 4,
        scratch_shapes=[
            pltpu.VMEM((length, width), F32),
            pltpu.VMEM((length, width), BF),
            pltpu.VMEM((length, width), F32),
            pltpu.VMEM((2, 4, 2, 2, 2 * UNIT, UNIT), BF),
            pltpu.VMEM((2, 4, 2, 2, 2, UNIT, UNIT), BF),
            pltpu.VMEM((2, length, 4 * UNIT), BF),
            pltpu.VMEM((length, 4 * UNIT), BF),
            pltpu.VMEM((2, 2, 4, 2, 2, 2 * UNIT, UNIT), BF),
            pltpu.VMEM((2, 2, 4, 2, 2, 2, UNIT, UNIT), BF),
            pltpu.SemaphoreType.DMA((4, 6)),
        ]
        + semaphores(8, Gather.sems)
        + semaphores(pieces, Reduce.sems)
        + Reduce.room(UNIT, UNIT) * pieces,
        compiler_params=params(collective_id=2, has_side_effects=True),
        name="mlp",
    )(stream0, ctx, w_out, gamma2, seg_col, seg_row, cotangent, s_up, s_down, fup0, fdn0, fup1, fdn1)


def attend_back_body(
    n_ref, qa, qb, ka, kb, va, vb, cos_ref, lo_ref, hi_ref, seg_ref, pad_ref, row_ref,
    q_ref, k_ref, v_ref, g_ref, c_ref, lse_ref, g1_ref, s0_ref, ds1_ref, gup1, gdn1, gup2, gdn2, gup3, gdn3, gout,
    gw_ref, dlow_ref, dg1_ref, sup1, sdn1, sup2, sdn2, sup3, sdn3, sout,
    bias_ref, dn_ref, dq_ref, dk_ref, dv_ref, s0_buf, sem, send, recv, local, *room,
):
    step = pl.program_id(0)
    last = pl.num_programs(0) - 1
    length, width = n_ref.shape
    me = Place()
    traffic = Traffic()
    made = []

    def add(theirs, mine, out, e, own):
        count = len(made)
        rest = room[10 + 4 * count : 14 + 4 * count]
        made.append(Reduce(me, theirs, mine, room[own + e], rest, out, e == 1, True))

    for q, (gup, gdn, sup, sdn) in enumerate(
        ((gup1, gdn1, sup1, sdn1), (gup2, gdn2, sup2, sdn2), (gup3, gdn3, sup3, sdn3))
    ):
        for e, (rows, _) in enumerate(halves(2 * UNIT)):
            add(gup.at[1 - me.c, :, :, :, rows, :], gup.at[me.c, :, :, :, rows, :], sup.at[rows, :], e, (0, 4, 8)[q])
        for e in range(2):
            add(gdn.at[e, :, 1 - me.c], gdn.at[e, :, me.c], sdn.at[pl.ds(e * UNIT, UNIT), :], e, (2, 6, 0)[q])
    for e, (rows, _) in enumerate(halves(2 * UNIT)):
        theirs, mine = gout.at[:, 1 - me.c, :, :, rows, :], gout.at[:, me.c, :, :, rows, :]
        add(theirs, mine, sout.at[rows, :], e, 2)
    traffic.add(ATTEND_BACK_HOOKS, made)
    traffic.bind(send, recv, local)
    fire = functools.partial(traffic.fire, step, 4, 5)

    @pl.when(step == 0)
    def _():
        me.greet()
        traffic.at(0)
        flow(s0_ref, s0_buf, sem.at[0]).start()
        fill_bias(bias_ref, seg_ref, pad_ref, row_ref)
        dn_ref[...] = jnp.zeros_like(dn_ref)

    ones = jnp.ones((8, HD), BF)
    for head in range(4):
        fire(head)
        lanes = slice(head * HD, (head + 1) * HD)
        query, key, value = q_ref[:, lanes], k_ref[:, lanes], v_ref[:, lanes]
        grad = g_ref[:, lanes]
        both = grad.astype(F32) * c_ref[:, lanes].astype(F32)
        high = both.astype(BF)
        low = (both - high.astype(F32)).astype(BF)
        delta = (dot(ones, high, NT) + dot(ones, low, NT))[0:1, :]
        probs = jnp.exp(dot(key, query, NT) + bias_ref[...] - lse_ref[head : head + 1, :])
        d_scores = (probs * (dot(value, grad, NT) - delta)).astype(BF)
        dv_ref[:, lanes] = dot(probs.astype(BF), grad)
        dk_ref[:, lanes] = dot(d_scores, query)
        dq_ref[:, lanes] = dot(key.T, d_scores).T * HD**-0.5

    @pl.when(step == last)
    def _():
        flow(ds1_ref, bias_ref, sem.at[1]).start()

    fire(4)
    for part, (src, first, second) in enumerate(
        ((dq_ref, qa, qb), (dk_ref, ka, kb), (dv_ref, va, vb))
    ):
        if part < 2:
            made = jnp.concatenate(
                [
                    turn(src[:, half * 128 : (half + 1) * 128], cos_ref[...], -lo_ref[...], -hi_ref[...])
                    for half in range(2)
                ],
                axis=1,
            ).astype(BF)
        else:
            made = src[...].astype(BF)
        grad = dot(n_ref[...], made, TN).astype(BF)
        gw_ref[part, 0] = grad[:, :128]
        gw_ref[part, 1] = grad[:, 128:]
        dn_ref[...] += dot(made, jnp.concatenate([first[0], second[0]], axis=1), NT)

    @pl.when(step == last)
    def _():
        dg1_ref[...] = jnp.zeros_like(dg1_ref)
        flow(s0_ref, s0_buf, sem.at[0]).wait()
        flow(ds1_ref, bias_ref, sem.at[1]).wait()

        @pl.loop(0, length // UNIT)
        def _(t):
            rows = pl.ds(pl.multiple_of(t * UNIT, UNIT), UNIT)
            gain = token_gain(seg_ref[rows, :], g1_ref)
            term, d_gain = norm_back(dn_ref[rows, :], s0_buf[rows, :], gain)
            dlow_ref[rows, :] = (bias_ref[rows, :] + term).astype(BF)
            dg1_ref[...] += segment_sum(row_ref[:, rows], d_gain)

        traffic.drain()


def attend_back(
    normed, w_qkv, tables, seg_col, pad_col, seg_row, q, k, v, d_ctx, ctx, lse, gamma1, stream0, d_stream1, grads
):
    length, width = normed.shape
    groups = width // 256
    units = [unit_spec(width, part * (width // 128) + e) for part in range(3) for e in range(2)]
    column = pl.BlockSpec((length, 256), lambda j: (0, j))
    full = whole((length, width))
    part = whole((2 * UNIT, UNIT))
    pieces = 14
    return pl.pallas_call(
        attend_back_body,
        grid=(groups,),
        in_specs=[full]
        + units
        + [whole((length, 128))] * 3
        + [whole((length, 1))] * 2
        + [whole((1, length))]
        + [column] * 5
        + [pl.BlockSpec((8, length), lambda j: (j, 0)), whole((8, width))]
        + [ANY] * 9,
        out_specs=(
            pl.BlockSpec((3, 2, width, 128), lambda j: (0, j, 0, 0)),
            full,
            whole((8, width)),
        )
        + (part,) * 7,
        out_shape=(
            shaped((3, width // 128, width, 128), BF),
            shaped((length, width), BF),
            shaped((8, width), F32),
        )
        + (shaped((2 * UNIT, UNIT), F32),) * 7,
        scratch_shapes=[pltpu.VMEM((length, length), F32), pltpu.VMEM((length, width), F32)]
        + [pltpu.VMEM((length, 256), F32)] * 3
        + [pltpu.VMEM((length, width), F32), pltpu.SemaphoreType.DMA((2,))]
        + semaphores(pieces, Reduce.sems)
        + [pltpu.VMEM((4, 2, 2, UNIT, UNIT), BF)] * 10
        + Reduce.room(UNIT, UNIT) * pieces,
        compiler_params=params(collective_id=3, has_side_effects=True),
        name="attend_back",
    )(
        normed, *([w_qkv] * 6), *tables, seg_col, pad_col, seg_row, q, k, v, d_ctx, ctx, lse,
        gamma1, stream0, d_stream1, *grads,
    )


def skip_back_body(
    x_hbm, s_hbm, d_ref, w_hbm, ada_ref, dg_ref, every_ref, gw_ref, acts_ref, keep1_ref, fdn0, fdn1, fdn2, fdn3,
    out_ref, dx_hbm, ds_hbm, time_ref, gada_ref, sskip, sqkv,
    x_ref, s_ref, w_ref, dx_ref, ds_ref, near_sem, stage, acc_ref, act_tile, dn_tile, sem, slots, part, got, summed, tim, sends, recvs, send, recv, local, *room,
):
    width = x_ref.shape[1]
    ahead = [
        flow(x_hbm, x_ref, near_sem.at[0]),
        flow(s_hbm, s_ref, near_sem.at[1]),
        flow(w_hbm, w_ref, near_sem.at[2]),
    ]
    for load in ahead:
        load.start()
    me = Place()
    me.greet(True)
    traffic = Traffic()
    made = []
    tall = 512

    def add(theirs, mine, out):
        own, *rest = room[5 * len(made) : 5 * len(made) + 5]
        made.append(Reduce(me, theirs, mine, own, rest, out, len(made) % 2 == 1, True))

    for sub in range(3):
        for i in range(4):
            rows = pl.ds(i * UNIT // 2, UNIT // 2)
            theirs, mine = gw_ref.at[:, 1 - me.c, sub, :, :, rows, :], gw_ref.at[:, me.c, sub, :, :, rows, :]
            add(theirs, mine, sqkv.at[rows, pl.ds(sub * UNIT, UNIT)])
    for i in range(8):
        rows = pl.ds(i * UNIT // 2, UNIT // 2)
        theirs, mine = stage.at[:, 1 - me.c, :, :, rows, :], stage.at[:, me.c, :, :, rows, :]
        add(theirs, mine, sskip.at[rows, :])
    traffic.add(SKIP_BACK_HOOKS, made)
    traffic.bind(send, recv, local)
    lay = functools.partial(pl.ds, 0)
    swaps = [
        Swap(me, "fsdp", lambda p: dg_ref.at[p], lambda m: slots.at[me.dp, m], sends.at[0], recvs.at[0]),
        Swap(me, "dp", lambda p: slots.at[me.dp], lambda m: slots.at[m], sends.at[1], recvs.at[1]),
        Swap(me, "fsdp", lambda p: part.at[:, p, lay(8), :], lambda m: got.at[m], sends.at[2], recvs.at[2]),
        Swap(me, "dp", lambda p: summed.at[p], lambda m: tim.at[m], sends.at[3], recvs.at[3]),
    ]
    downs = (fdn0, fdn1, fdn2, fdn3)

    def tiles(s):
        return (
            flow(acts_ref.at[s], act_tile.at[s % 2], sem.at[0, s % 2]),
            flow(downs[s // 2].at[:, :, :, :, pl.ds(s % 2 * UNIT, UNIT), :], dn_tile.at[s % 2], sem.at[1, s % 2]),
        )

    start1 = flow(keep1_ref, acc_ref, sem.at[0, 2])
    slots[me.dp, me.fs] = dg_ref[me.fs]
    swaps[0].start()
    traffic.at(0)
    start1.start()
    for load in tiles(0):
        load.start()
    ahead[0].wait()
    ahead[1].wait()

    def add_down(slot):
        @pl.loop(0, 2)
        def _(half):
            tile = jnp.concatenate(
                [dn_tile[slot, 2 * half + i // 2, i % 2].reshape(4 * UNIT, UNIT) for i in range(4)], axis=1
            )
            lanes = pl.ds(pl.multiple_of(half * 4 * UNIT, 4 * UNIT), 4 * UNIT)
            acc_ref[:, lanes] += dot(act_tile[slot], tile)

    def grads(i):
        lanes = pl.ds(pl.multiple_of(i * 2 * UNIT, 2 * UNIT), 2 * UNIT)
        part = d_ref[:, lanes]
        top = dot(x_ref[...], part, TN).astype(BF)
        end = dot(s_ref[...], part, TN).astype(BF)
        for c in range(2):
            cols = slice(c * UNIT, (c + 1) * UNIT)
            stage[i, c, 0] = top[:, cols].reshape(2, tall, UNIT)
            stage[i, c, 1] = end[:, cols].reshape(2, tall, UNIT)

    def second():
        swaps[0].wait()
        swaps[1].start()

    @pl.loop(0, 4)
    def _(i):
        grads(i)
        traffic.inside(i, 1, 4)
        pl.when(i == 1)(second)

    traffic.at(5)
    swaps[1].wait()
    every = slots[...].reshape(4 * NB * 16, -1)
    gada_ref[...] = dot(every_ref[...].reshape(4 * NB * 16, -1), every, TN)
    part[...] = dot(every, ada_ref[...], NT).reshape(part.shape)
    got[me.fs] = part[:, me.fs, :8, :]
    swaps[2].start()

    def back(which, out, first):
        @pl.loop(0, 2)
        def _(i):
            traffic.inside(i, first, 2)
            rows = pl.ds(pl.multiple_of(i * tall, tall), tall)
            tile = jnp.concatenate([w_ref[f // 2, f % 2, which, i] for f in range(NB)], axis=1)
            out[:, rows] = dot(d_ref[...], tile, NT)

    ahead[2].wait()
    back(0, dx_ref, 6)
    away = [flow(dx_ref, dx_hbm, near_sem.at[3]), flow(ds_ref, ds_hbm, near_sem.at[4])]
    away[0].start()
    swaps[2].wait()
    total = got[0]
    for f in range(1, NB):
        total = total + got[f]
    summed[...] = total
    tim[me.dp] = summed[me.dp]
    swaps[3].start()
    back(1, ds_ref, 8)
    away[1].start()
    swaps[3].wait()
    for d in range(4):
        time_ref[:, d * 2 * UNIT : (d + 1) * 2 * UNIT] = tim[d]
    start1.wait()
    for s in range(8):
        if s < 7:
            for load in tiles(s + 1):
                load.start()
        for load in tiles(s):
            load.wait()
        add_down(s % 2)
        traffic.at(10 + s)
    out_ref[...] = acc_ref[...].astype(BF)
    traffic.drain()
    for copy in away:
        copy.wait()


def skip_back(inputs, skip_in, d_low, w_skip, w_ada, dg_cut, every, g_qkv, acts, stream1, fdowns):
    length, width = inputs.shape
    vmem = pl.BlockSpec(memory_space=pltpu.VMEM)
    tall, per = w_ada.shape
    pieces = 20
    return pl.pallas_call(
        skip_back_body,
        in_specs=[ANY] * 2 + [vmem, ANY] + [vmem] * 3 + [ANY] * 7,
        out_specs=(vmem, ANY, ANY) + (vmem,) * 4,
        out_shape=(
            shaped((length, width), BF),
            shaped((length, width), F32),
            shaped((length, width), F32),
            shaped((8, width), F32),
            shaped((tall, per), F32),
            shaped((4 * UNIT, UNIT), F32),
            shaped((2 * UNIT, 3 * UNIT), F32),
        ),
        scratch_shapes=[
            pltpu.VMEM((length, width), BF),
            pltpu.VMEM((length, width), BF),
            pltpu.VMEM(w_skip.shape, BF),
            pltpu.VMEM((length, width), F32),
            pltpu.VMEM((length, width), F32),
            pltpu.SemaphoreType.DMA((5,)),
            pltpu.VMEM(w_skip.shape, BF),
            pltpu.VMEM((length, width), F32),
            pltpu.VMEM((2, *acts.shape[1:]), BF),
            pltpu.VMEM((2, 4, 2, 2, 2, UNIT, UNIT), BF),
            pltpu.SemaphoreType.DMA((2, 3)),
            pltpu.VMEM((4, NB, 16, per), BF),
            pltpu.VMEM((4, NB, 16, tall), F32),
            pltpu.VMEM((NB, 4, 8, tall), F32),
            pltpu.VMEM((4, 8, tall), F32),
            pltpu.VMEM((4, 8, tall), F32),
            pltpu.SemaphoreType.DMA((4, NB - 1)),
            pltpu.SemaphoreType.DMA((4, NB - 1)),
        ]
        + semaphores(pieces, Reduce.sems)
        + ([pltpu.VMEM((4, 2, 2, UNIT // 2, UNIT), BF)] + Reduce.room(UNIT // 2, UNIT)) * pieces,
        compiler_params=params(collective_id=4, has_side_effects=True),
        name="skip_back",
    )(inputs, skip_in, d_low, w_skip, w_ada, dg_cut, every, g_qkv, acts, stream1, *fdowns)


def frequencies():
    lane = jnp.arange(128) % (HD // 2)
    return 10000.0 ** (-2.0 * lane.astype(F32) / HD)


def rotary(positions):
    half = HD // 2
    lane = jnp.arange(128)
    phase = positions.reshape(-1, 1).astype(F32) * frequencies()[None, :]
    cosine, sine = jnp.cos(phase), jnp.sin(phase)
    early = (lane % HD < half)[None, :]
    return cosine, jnp.where(early, -sine, 0.0), jnp.where(early, 0.0, sine)


def gathered(shard):
    blocks = lax.all_gather(shard, "fsdp", axis=0, tiled=False)
    blocks = lax.all_gather(blocks, "dp", axis=1, tiled=True)
    count, rows, per = blocks.shape
    if count == NB:
        return blocks
    flat = jnp.transpose(blocks, (1, 0, 2)).reshape(rows, count * per)
    return jnp.transpose(flat.reshape(rows, NB, count * per // NB), (1, 0, 2))


def scattered(blocks):
    count, rows, per = blocks.shape
    flat = jnp.transpose(blocks, (1, 0, 2)).reshape(rows, count * per)
    part = lax.psum_scatter(flat, "fsdp", scatter_dimension=1, tiled=True)
    return lax.psum_scatter(part, "dp", scatter_dimension=0, tiled=True).astype(F32)


def ada_grads(flat_time, d_gammas, tall, thin):
    every = lax.all_gather(flat_time, "fsdp", axis=0, tiled=True)
    every = lax.all_gather(every, "dp", axis=0, tiled=True)
    every = lax.dynamic_slice_in_dim(every, lax.axis_index("dp") * tall, tall, 1)
    gammas = lax.all_gather(d_gammas, "fsdp", axis=1, tiled=True)
    gammas = lax.all_gather(gammas, "dp", axis=1, tiled=True)
    gammas = lax.dynamic_slice_in_dim(gammas, lax.axis_index("fsdp") * thin, thin, 2)
    return [jnp.einsum("nd,ne->de", every, part, preferred_element_type=F32) for part in gammas]


def fused(
    inputs, skip_in, time_emb, seg_ids, positions, pad_mask,
    w_skip, w_ada1, w_qkv, w_out, w_ada2, w_up, w_down, cotangent,
):
    slots = time_emb.shape[1]
    length, width = inputs.shape
    seg_row = seg_ids.reshape(1, -1)
    rows = jnp.concatenate([seg_row, pad_mask.reshape(1, -1), positions.reshape(1, -1)])
    rows = jnp.pad(rows, ((0, 5), (0, 0)))
    freq = jnp.broadcast_to(frequencies(), (8, UNIT))
    flat_time = time_emb.reshape(slots, -1)
    time_cut = jnp.pad(flat_time, ((0, 16 - slots), (0, 0)))
    time_cut = jnp.transpose(time_cut.reshape(16, 4, -1), (1, 0, 2))
    w_ada = jnp.concatenate([w_ada1, w_ada2], axis=1)
    stream0, normed1, gamma1, gamma2, every, seg_col, pad_col, *tables, f_skip, f_qkv = front(
        inputs, skip_in, time_cut, rows, freq, w_ada, w_skip, w_qkv
    )
    f_qkv = f_qkv.reshape(NB, width, -1)
    q, k, v, ctx, lse, f_out, fup0, fdn0, fup1, fdn1 = attend(
        normed1, f_qkv, tables, seg_col, pad_col, seg_row, w_out, w_up, w_down
    )
    acts, stream1, g_out, d_stream1, d_ctx, d_gamma2, sup0, sdn0, *rest = mlp(
        stream0, ctx, f_out, gamma2, seg_col, seg_row, cotangent, w_up, w_down, fup0, fdn0, fup1, fdn1
    )
    g_qkv, d_low, d_gamma1, sup1, sdn1, sup2, sdn2, sup3, sdn3, s_out = attend_back(
        normed1, f_qkv, tables, seg_col, pad_col, seg_row, q, k, v, d_ctx, ctx, lse, gamma1,
        stream0, d_stream1, (*rest[:6], g_out),
    )
    dg_cut = jnp.concatenate([d.reshape(8, NB, -1) for d in (d_gamma1, d_gamma2)], axis=2)
    dg_cut = jnp.pad(jnp.transpose(dg_cut, (1, 0, 2)).astype(BF), ((0, 0), (0, 8), (0, 0)))
    output, d_input, d_skip, d_time, g_ada, s_skip, s_qkv = skip_back(
        inputs, skip_in, d_low, f_skip, w_ada, dg_cut, every, g_qkv.reshape(4, 2, 3, 2, 2, -1, UNIT),
        acts, stream1, (fdn0, fdn1, rest[7], rest[9]),
    )
    s_up = jnp.concatenate([sup0, sup1, sup2, sup3], axis=1)
    s_down = jnp.stack([sdn0, sdn1, sdn2, sdn3]).reshape(4, 2, UNIT, UNIT)
    s_down = jnp.transpose(s_down, (1, 0, 2, 3)).reshape(w_down.shape)
    return (
        output, d_input, d_skip, d_time[:slots].reshape(time_emb.shape),
        s_skip, g_ada[:, :UNIT], s_qkv, s_out, g_ada[:, UNIT:], s_up, s_down,
    )


def plain(
    inputs, skip_in, time_emb, seg_ids, positions, pad_mask,
    w_skip, w_ada1, w_qkv, w_out, w_ada2, w_up, w_down, cotangent,
):
    slots = time_emb.shape[1]
    width = inputs.shape[1]
    seg_col, seg_row = seg_ids.reshape(-1, 1), seg_ids.reshape(1, -1)
    pad_col = pad_mask.reshape(-1, 1)
    tables = rotary(positions)
    flat_time = time_emb.reshape(slots, -1)
    time8 = jnp.pad(flat_time, ((0, 8 - slots), (0, 0)))
    f_skip, f_qkv, f_out, f_up, f_down, f_ada1, f_ada2 = [
        gathered(w) for w in (w_skip, w_qkv, w_out, w_up, w_down, w_ada1, w_ada2)
    ]
    ada = jnp.concatenate([f_ada1, f_ada2], axis=2)
    stream0, normed1, gamma1, gamma2 = plain_front(inputs, skip_in, f_skip, time8, ada, seg_col)
    q, k, v, ctx, lse = plain_attend(normed1, f_qkv, tables, seg_col, pad_col, seg_row)
    output, g_down, g_up, g_out, d_stream1, d_ctx, d_gamma2 = plain_mlp(
        stream0, ctx, f_out, gamma2, seg_col, seg_row, f_up, f_down, cotangent
    )
    g_qkv, d_low, d_gamma1 = plain_attend_back(
        normed1, f_qkv, tables, seg_col, pad_col, seg_row, q, k, v, d_ctx, ctx, lse,
        stream0, gamma1, d_stream1,
    )
    g_qkv = jnp.transpose(
        g_qkv.reshape(NB, 3, width, 128), (0, 2, 1, 3)
    ).reshape(NB, width, 3 * width // NB)
    g_skip, d_input, d_skip = plain_skip_back(inputs, skip_in, d_low, f_skip)
    d_gammas = jnp.stack([d_gamma1, d_gamma2]).astype(BF)[:, :slots]
    d_time = 0.0
    for d_gamma, part in zip(d_gammas, (f_ada1, f_ada2)):
        flat = jnp.transpose(part, (1, 0, 2)).reshape(width, width)
        d_time = d_time + jnp.einsum("ne,de->nd", d_gamma, flat, preferred_element_type=F32)
    g_ada = ada_grads(flat_time, d_gammas, *w_ada1.shape)
    return (
        output, d_input, d_skip, d_time.reshape(time_emb.shape),
        scattered(g_skip), g_ada[0], scattered(g_qkv), scattered(g_out), g_ada[1],
        scattered(g_up), scattered(g_down),
    )


def solution(mesh):
    rows = P(("dp", "fsdp"), None)
    cube = P(("dp", "fsdp"), None, None)
    tile = P("dp", "fsdp")
    fits = mesh.shape["dp"] == 4 and mesh.shape["fsdp"] == NB
    return jax.shard_map(
        fused if fits else plain,
        mesh=mesh,
        in_specs=(rows, rows, cube) + (rows,) * 3 + (tile,) * 7 + (rows,),
        out_specs=(rows, rows, rows, cube) + (tile,) * 7,
        check_vma=False,
    )
```
